32 devices in a mesh: section: 2 (over y), nodes: 16 (over z, x, core).
Axes of the slice: x: 2, y: 2, z: 4, core: 2. Of those that a mesh axis runs over, the one named last changes fastest.
Arguments:
- inputs: bfloat16 [4, 2048, 512], P(None, 'nodes'), may hold values from -6 to 6
- cotangent: bfloat16 [4, 2048, 512], P(None, 'nodes'), may hold values from -6 to 6
- neighbours: int32 [2048, 16], P('nodes'), may hold values from -1 to 2047, as said below
- mesh_ids: int32 [2048], P('nodes'), may hold values from 0 to 1, as said below
- noise_sigma: float32 [4, 2], replicated, may hold values from 0.02 to 80
- w_qkv: bfloat16 [2, 512, 1536], P('section'), may hold values from -0.25 to 0.25
- w_out: bfloat16 [2, 512, 512], P('section'), may hold values from -0.5 to 0.5
- w_up: bfloat16 [2, 512, 2048], P('section'), may hold values from -0.25 to 0.25
- b_up: float32 [2, 2048], P('section'), may hold values from -3 to 3
- w_down: bfloat16 [2, 2048, 512], P('section'), may hold values from -0.125 to 0.125
- b_down: float32 [2, 512], P('section'), may hold values from -3 to 3
- w_mod: bfloat16 [2, 512, 2048], P('section'), may hold values from -0.125 to 0.125
- b_mod: float32 [2, 2048], P('section'), may hold values from -2 to 2
Outputs:
- layer_outputs: bfloat16 [2, 4, 2048, 512], P('section', None, 'nodes')
- input_grads: bfloat16 [2, 4, 2048, 512], P('section', None, 'nodes')
- grad_qkv: float32 [2, 512, 1536], P('section', 'nodes')
- grad_out: float32 [2, 512, 512], P('section', 'nodes')
- grad_up: float32 [2, 512, 2048], P('section', 'nodes')
- grad_up_bias: float32 [2, 2048], P('section', 'nodes')
- grad_down: float32 [2, 2048, 512], P('section', 'nodes')
- grad_down_bias: float32 [2, 512], P('section', 'nodes')
- grad_mod: float32 [2, 512, 2048], P('section', 'nodes')
- grad_mod_bias: float32 [2, 2048], P('section', 'nodes')
The draws below stay inside these ranges and needn't reach their ends.
Inputs may be any that keep to these rules, and one draw needn't show every extreme that they name: `neighbours`: entry 0 of node i's row is i itself; every other entry is -1 or a node j with |j - i| <= 32, and some entry of every node is exactly 32 away. `mesh_ids`: never falls from one node to the next.
All inputs are finite; a program needn't handle non-finite values.
Results may differ from the reference program's by a relative error of at most 0.02.
Values may be sent and summed in bfloat16 or wider, within the bound.
A program may use at most 192 MiB of HBM per device.

```python
import math
import jax
import jax.numpy as jnp
from jax import lax

D = 512
HEADS = 4
HEAD = 128
FF = 2048
NEIGH = 16
MB = 4
MESHES_MB = 2
REACH = 32
NODES = 2048
LAYERS = 2


def draw_neighbours(key, part):
    key = jax.random.fold_in(key, 11)
    key_offset, key_pad = jax.random.split(key)
    node_no = jnp.arange(NODES, dtype=jnp.int32)[:, None]
    slot_no = jnp.arange(NEIGH, dtype=jnp.int32)[None, :]
    offset = jax.random.randint(key_offset, (NODES, NEIGH), -REACH, REACH + 1).astype(jnp.int32)
    offset = jnp.where(slot_no == 0, 0, offset)
    far_step = jnp.where(node_no >= REACH, -REACH, REACH).astype(jnp.int32)
    offset = jnp.where(slot_no == 1, far_step, offset)
    target = node_no + offset
    target = jnp.where((target < 0) | (target >= NODES), node_no - offset, target)
    padded = (jax.random.randint(key_pad, (NODES, NEIGH), 0, 8) == 0) & (slot_no >= 2)
    return jnp.where(padded, -1, target).astype(jnp.int32)


def draw_mesh_ids(key, part):
    key = jax.random.fold_in(key, 23)
    boundaries = jnp.sort(jax.random.randint(key, (MESHES_MB - 1,), NODES // 4, NODES - NODES // 4))
    node_no = jnp.arange(NODES, dtype=jnp.int32)
    return jnp.sum((node_no[:, None] >= boundaries[None, :]).astype(jnp.int32), axis=1).astype(jnp.int32)


def level_of(key, extent, shards, smallest, high):
    loudness = 1.0
    for axis_at, blocks in shards:
        draws = jax.random.uniform(jax.random.fold_in(jax.random.fold_in(key, 6), axis_at), (blocks,), jnp.float32, smallest / len(shards), high / len(shards))
        loudness = loudness * jnp.repeat(jnp.exp(draws), extent[axis_at] // blocks).reshape((-1,) + (1,) * (len(extent) - 1 - axis_at))
    return loudness


def gaussian(own_key, shape, deviation, reach, cuts=(), kind=jnp.bfloat16):
    array = jax.random.normal(own_key, shape, jnp.float32) * deviation
    if len(cuts) > 0:
        array = level_of(own_key, shape, cuts, -0.22, 0.18) * array
    return jnp.clip(array, min=-reach, max=reach).astype(kind)


def setup_inputs(seed: int = 0) -> dict:
    key_list = jax.random.split(jax.random.key(seed), 14)
    inputs = gaussian(key_list[0], (MB, NODES, D), 1.0, 6.0, ((1, 16),))
    cotangent = gaussian(key_list[1], (MB, NODES, D), 1.0, 6.0, ((1, 16),))
    neighbours = draw_neighbours(jax.random.fold_in(key_list[13], 71), 0)
    mesh_ids = draw_mesh_ids(jax.random.fold_in(key_list[13], 71), 0)
    noise_sigma = jnp.clip(jnp.exp(jax.random.uniform(key_list[4], (MB, MESHES_MB), jnp.float32, math.log(0.02), math.log(80.0))), 0.02, 80.0)
    w_qkv = gaussian(key_list[5], (LAYERS, D, 3 * D), D ** -0.5, 0.25, ((0, 2),))
    w_out = gaussian(key_list[6], (LAYERS, D, D), (D // 4) ** -0.5, 0.5, ((0, 2),))
    w_up = gaussian(key_list[7], (LAYERS, D, FF), D ** -0.5, 0.25, ((0, 2),))
    b_up = gaussian(key_list[8], (LAYERS, FF), 0.5, 3.0, ((0, 2),), jnp.float32)
    w_down = gaussian(key_list[9], (LAYERS, FF, D), FF ** -0.5, 0.125, ((0, 2),))
    b_down = gaussian(key_list[10], (LAYERS, D), 0.5, 3.0, ((0, 2),), jnp.float32)
    w_mod = gaussian(key_list[11], (LAYERS, D, 4 * D), (4 * D) ** -0.5, 0.125, ((0, 2),))
    b_mod = gaussian(key_list[12], (LAYERS, 4 * D), 0.3, 2.0, ((0, 2),), jnp.float32)
    return dict(inputs=inputs, cotangent=cotangent, neighbours=neighbours, mesh_ids=mesh_ids, noise_sigma=noise_sigma, w_qkv=w_qkv, w_out=w_out, w_up=w_up, b_up=b_up, w_down=w_down, b_down=b_down, w_mod=w_mod, b_mod=b_mod)


PRECISE = lax.Precision.HIGHEST
EPSILON = 1e-06

@jax.custom_vjp
def low(v):
    return lax.optimization_barrier(v.astype(jnp.bfloat16)).astype(jnp.float32)

@jax.custom_vjp
def low_back(v):
    return v

def low_keep(v):
    return (low(v), None)

def low_pass(kept, grad):
    return (grad,)

def back_keep(v):
    return (v, None)

def back_low(kept, grad):
    return (low(grad),)
low.defvjp(low_keep, low_pass)
low_back.defvjp(back_keep, back_low)

def matmul(former, latter):
    return jnp.dot(former, latter, precision=PRECISE, preferred_element_type=jnp.float32)

def embed_noise(noise_row, model_width):
    half_width = model_width // 2
    frequency = 3.0 * jnp.exp(-jnp.log(100.0) * jnp.arange(half_width, dtype=jnp.float32) / half_width)
    angles = jnp.log(noise_row)[:, None] * frequency[None, :]
    return jnp.concatenate([jnp.sin(angles), jnp.cos(angles)], axis=1)

def adaptive_norm(values, scale_rows, shift_rows):
    centred = values - lax.optimization_barrier(jnp.mean(values, axis=-1, keepdims=True))
    variance = lax.optimization_barrier(jnp.mean(centred * centred, axis=-1, keepdims=True))
    return centred * lax.rsqrt(variance + EPSILON) * (1.0 + scale_rows) + shift_rows

def attend_block(queries, index_block, valid_block, keys_values):
    row_count = queries.shape[0]
    gathered = jnp.take(keys_values, index_block, axis=0)
    key_rows = gathered[:, :, :D].reshape(row_count, NEIGH, HEADS, HEAD)
    value_rows = gathered[:, :, D:].reshape(row_count, NEIGH, HEADS, HEAD)
    heads_query = queries.reshape(row_count, HEADS, HEAD)
    scores = low_back(jnp.einsum('bhd,bnhd->bhn', heads_query, key_rows, precision=PRECISE) * HEAD ** (-0.5))
    scores = jnp.where(valid_block[:, None, :], scores, -1000000000.0)
    raised = jnp.exp(scores - lax.optimization_barrier(jnp.max(scores, axis=-1, keepdims=True)))
    weights = low(raised / lax.optimization_barrier(jnp.sum(raised, axis=-1, keepdims=True)))
    return jnp.einsum('bhn,bnhd->bhd', weights, value_rows, precision=PRECISE).reshape(row_count, D)

def attend(queries, neighbour_index, slot_valid, keys_values):
    node_count = queries.shape[0]
    block_rows = 2048 if node_count % 2048 == 0 else node_count
    blocks = node_count // block_rows

    def one_block(pieces):
        return attend_block(pieces[0], pieces[1], pieces[2], keys_values)
    result = lax.map(jax.checkpoint(one_block), (queries.reshape(blocks, block_rows, D), neighbour_index.reshape(blocks, block_rows, NEIGH), slot_valid.reshape(blocks, block_rows, NEIGH)))
    return result.reshape(node_count, D)

def processor_layer(values, neighbour_index, slot_valid, selector, noise_row, w_qkv, w_out, w_up, b_up, w_down, b_down, w_mod, b_mod):
    mod_table = matmul(low(embed_noise(noise_row, D)), w_mod) + b_mod
    per_node = matmul(selector, mod_table)
    normed = low(adaptive_norm(values, per_node[:, :D], per_node[:, D:2 * D]))
    qkv_all = low_back(low(matmul(normed, w_qkv)))
    attended = low_back(low(attend(qkv_all[:, :D], neighbour_index, slot_valid, qkv_all[:, D:])))
    middle = values + low_back(matmul(attended, w_out))
    normed_b = low(adaptive_norm(middle, per_node[:, 2 * D:3 * D], per_node[:, 3 * D:]))
    before = low_back(matmul(normed_b, w_up) + b_up)
    hidden = low(before * jax.nn.sigmoid(before))
    return middle + low_back(matmul(hidden, w_down) + b_down)

def reference(inputs, cotangent, neighbours, mesh_ids, noise_sigma, w_qkv, w_out, w_up, b_up, w_down, b_down, w_mod, b_mod):
    slot_valid = neighbours >= 0
    neighbour_index = jnp.where(slot_valid, neighbours, 0).astype(jnp.int32)
    selector = (mesh_ids[:, None] == jnp.arange(MESHES_MB, dtype=jnp.int32)[None, :]).astype(jnp.float32)
    params = tuple((weight.astype(jnp.float32) for weight in (w_qkv, w_out, w_up, b_up, w_down, b_down, w_mod, b_mod)))

    def forward(values_in, offset_in, weights_in, noise_row):
        first_layer = processor_layer(values_in, neighbour_index, slot_valid, selector, noise_row, *[weight[0] for weight in weights_in])
        handed = low(first_layer)
        second = processor_layer(low_back(handed) + offset_in, neighbour_index, slot_valid, selector, noise_row, *[weight[1] for weight in weights_in])
        return (second, handed)

    def one_batch(running, batch_in):
        values, seed_grad, noise_row = batch_in

        def bound_forward(values_in, offset_in, weights_in):
            return forward(values_in, offset_in, weights_in, noise_row)
        output, pullback, handed = jax.vjp(bound_forward, values, jnp.zeros_like(values), params, has_aux=True)
        grad_in, grad_mid, grad_params = pullback(seed_grad)
        running = jax.tree.map(lambda acc_a, acc_b: acc_a + acc_b, running, grad_params)
        return (running, (handed.astype(jnp.bfloat16), output.astype(jnp.bfloat16), grad_in.astype(jnp.bfloat16), grad_mid.astype(jnp.bfloat16)))
    initial = jax.tree.map(jnp.zeros_like, params)
    totals, (first_out, second_out, first_grad, second_grad) = lax.scan(one_batch, initial, (inputs.astype(jnp.float32), cotangent.astype(jnp.float32), noise_sigma))
    layer_outputs = jnp.stack([first_out, second_out])
    input_grads = jnp.stack([first_grad, second_grad])
    return (layer_outputs, input_grads, totals[0], totals[1], totals[2], totals[3], totals[4], totals[5], totals[6], totals[7])
```

```python
import jax
import jax.numpy as jnp
from jax import lax
from jax.experimental import pallas as pl
from jax.experimental.pallas import tpu as pltpu
from jax.sharding import PartitionSpec as P

HEADS = 4
REACH = 32
EPSILON = 1e-06
MASKED = -1e9
ABSENT = -2e38
TILE = 512
MESH = pl.DeviceIdType.MESH
F32, LOW = jnp.float32, jnp.bfloat16


def dot(a, b):
    return lax.dot_general(a, b, (((1,), (0,)), ((), ())), preferred_element_type=F32)


def dot_nt(a, b):
    return lax.dot_general(a, b, (((1,), (1,)), ((), ())), preferred_element_type=F32)


def dot_tn(a, b):
    return lax.dot_general(a, b, (((0,), (0,)), ((), ())), preferred_element_type=F32)


class Sizes:
    def __init__(self, inputs, neighbours, noise, w_up, shards):
        self.batches, self.rows, self.width = inputs.shape
        self.slots = neighbours.shape[1]
        self.meshes = noise.shape[1]
        self.hidden = w_up.shape[2]
        self.shards = shards
        self.ext = self.rows + 2 * REACH
        self.window = (self.ext // 128 + 1) * 128
        self.groups = self.hidden // TILE
        self.own = self.width // shards
        self.scatter = self.own % 16 == 0
        self.pieces = [(3 + q, 0, "down", q) for q in range(self.groups)]
        self.pieces += [(2, 1 + q, "up", q) for q in range(self.groups)]
        self.pieces += [(1, 1 + self.groups, "out", 0)]
        self.pieces += [(0, 2 + self.groups + q, "qkv", q) for q in range(3)]
        self.lefts = 3 + self.groups
        self.rights = 2 + self.groups + 3
        self.rings = max(shards.bit_length() - 1, 1)
        self.line = max(shards // 4, 1)


def kernel_of(z):
    batches, rows, width, ext, window = z.batches, z.rows, z.width, z.ext, z.window
    groups, shards, own = z.groups, z.shards, z.own
    head = width // HEADS
    score_scale = head ** (-0.5)
    npiece = len(z.pieces)
    half, quarter = TILE // 2, TILE // 4

    def position(owner):
        if not z.scatter:
            return owner
        return (owner % 2) * (shards // 2) + (owner // 2 % 2) * z.line + owner // 4

    def kernel(
        inputs, cotangent, neighbours, mesh_ids, sigma,
        w_qkv, w_out, w_up, b_up, w_down, b_down, w_mod, b_mod,
        lo, ig, *rest,
    ):
        if z.scatter:
            o_qkv, o_out, o_up, o_upb, o_down, o_downb, o_mod, o_modb = rest[:8]
            rest = rest[8:]
            left_t, right_t = rest[:2]
            rest = rest[2:]
        else:
            left_t, right_t, small_out, table_out = rest[:4]
            rest = rest[4:]
        (
            wq, wo, wu, wd, wm, xext, dybuf, sel, cnt, bias, mod, emb,
            n1, ua, ia, qb, kvext, af, ca, ob, n2, ub, ib, fp, dx1, dkv, hsend, hrecv, sm,
            lsem, hx_s, hx_r, hm_s, hm_r, fx_s, fx_r, bh_s, bh_r, bx_s, bx_r,
        ) = rest[:40]
        rest = rest[40:]

        sec = lax.axis_index("section")
        me = lax.axis_index("nodes")
        up = lax.rem(me + 1, shards)
        down = lax.rem(me + shards - 1, shards)
        other = 1 - sec
        if z.scatter:
            core, xpos, zpos = me % 2, me // 2 % 2, me // 4
            core_mate = me + 1 - 2 * core
            x_mate = me + 2 - 4 * xpos

            def z_mate(k):
                return lax.rem(zpos + k, z.line) * 4 + xpos * 2 + core

        def local(src, dst, k):
            return pltpu.make_async_copy(src, dst, lsem.at[k])

        loads = [
            local(w_mod.at[0], wm, 0),
            local(w_qkv.at[0], wq, 1),
            local(w_out.at[0], wo, 2),
            local(w_up.at[0], wu, 3),
            local(w_down.at[0], wd, 4),
        ]
        own_rows = pl.ds(REACH, rows)
        first_load = local(inputs, xext.at[:, own_rows, :], 5)
        last_load = local(cotangent, dybuf, 6)
        for copy in loads:
            copy.start()

        @pl.when(sec == 0)
        def _():
            first_load.start()

        @pl.when(sec == 1)
        def _():
            last_load.start()

        barrier = pltpu.get_barrier_semaphore()
        mates = [(sec, up), (sec, down), (other, me), (other, up), (other, down)]
        if z.scatter:
            mates += [(sec, x_mate)] + [(sec, z_mate(k)) for k in range(1, z.line)]
        for mate in mates:
            pl.semaphore_signal(barrier, inc=1, device_id=mate, device_id_type=MESH)
        pl.semaphore_wait(barrier, len(mates))

        def remote(src, dst, s_sem, r_sem, mate):
            return pltpu.make_async_remote_copy(
                src_ref=src, dst_ref=dst, send_sem=s_sem, recv_sem=r_sem, device_id=mate, device_id_type=MESH
            )

        low_rows, top_rows = pl.ds(0, REACH), pl.ds(REACH + rows, REACH)
        head_rows, tail_rows = pl.ds(REACH, REACH), pl.ds(rows, REACH)
        x_down = remote(inputs.at[:, pl.ds(0, REACH), :], xext.at[:, top_rows, :], hx_s.at[0], hx_r.at[0], (sec, down))
        x_up = remote(inputs.at[:, pl.ds(rows - REACH, REACH), :], xext.at[:, low_rows, :], hx_s.at[1], hx_r.at[1], (sec, up))

        @pl.when(sec == 0)
        def _():
            x_down.start()
            x_up.start()

        ids = jnp.broadcast_to(mesh_ids[...].astype(F32), (128, rows))
        sel[own_rows, :] = ids.T
        m_down = remote(sel.at[head_rows, :], sel.at[top_rows, :], hm_s.at[0], hm_r.at[0], (sec, down))
        m_up = remote(sel.at[tail_rows, :], sel.at[low_rows, :], hm_s.at[1], hm_r.at[1], (sec, up))
        m_down.start()
        m_up.start()

        slots = neighbours[...]
        slots = jnp.where(slots >= 0, slots - (me * rows - REACH), ext)
        column = lax.broadcasted_iota(jnp.int32, (rows, window), 1)
        counts = jnp.zeros((rows, window), F32)
        for n in range(z.slots):
            counts = counts + jnp.where(slots[:, n : n + 1] == column, 1.0, 0.0)
        cnt[...] = counts
        bias[...] = jnp.where(counts > 0, jnp.where(column == ext, MASKED, 0.0), ABSENT)

        row_no = lax.broadcasted_iota(jnp.int32, (16, width // 2), 0)
        level = jnp.ones((16, width // 2), F32)
        for b in range(batches):
            for m in range(z.meshes):
                level = jnp.where(row_no == b * z.meshes + m, sigma[b, m], level)
        place = lax.broadcasted_iota(jnp.int32, (16, width // 2), 1).astype(F32)
        frequency = 3.0 * jnp.exp(-jnp.log(100.0) * place / (width // 2))
        angles = jnp.log(level) * frequency
        embedded = jnp.concatenate([jnp.sin(angles), jnp.cos(angles)], axis=1).astype(LOW)
        padded = jnp.concatenate([embedded.astype(F32), jnp.zeros((112, width), F32)], axis=0)
        emb[...] = padded.T
        loads[0].wait()
        for g in range(4):
            cols = pl.ds(g * width, width)
            table = dot(embedded, wm[:, cols]) + b_mod[:, cols]
            for b in range(batches):
                mod[b, 0 : z.meshes, cols] = table[b * z.meshes : (b + 1) * z.meshes]

        def mod_rows(b, part, ids_rows):
            cols = pl.ds(part * width, width)
            value = jnp.broadcast_to(mod[b, 0:1, cols], (ids_rows.shape[0], width))
            for m in range(1, z.meshes):
                value = jnp.where(ids_rows > m - 0.5, mod[b, m : m + 1, cols], value)
            return value

        def wide(ids_rows):
            return jnp.concatenate([ids_rows] * (width // 128), axis=1)

        def unit(x):
            centred = x - jnp.mean(x, axis=-1, keepdims=True)
            inv = lax.rsqrt(jnp.mean(centred * centred, axis=-1, keepdims=True) + EPSILON)
            return centred * inv, inv

        def batch_cols(b):
            return pl.ds(pl.multiple_of(b * rows, rows), rows)

        def put_left(first, b, value, span):
            turned = value.T
            for owner in range(TILE // span):
                at = position(owner) * span
                left_t[first, at : at + span, batch_cols(b)] = turned[owner * span : (owner + 1) * span]

        def put_left_hidden(b, value, group):
            turned = value.T
            run = z.hidden // (TILE // 32) if not z.scatter else z.hidden // shards
            span = run // groups
            for k in range(TILE // span):
                at = group * TILE + k * span
                owner, part = at // run, at % run // span
                to = position(owner) * span
                left_t[3 + part, to : to + span, batch_cols(b)] = turned[k * span : (k + 1) * span]

        span = own if z.scatter else 32

        def forward(b):
            ids_rows = wide(sel[0:ext, :])
            u, inv = unit(xext[b].astype(F32))
            normed = (u * (1.0 + mod_rows(b, 0, ids_rows)) + mod_rows(b, 1, ids_rows)).astype(LOW)
            n1[...] = normed
            ua[b] = u[REACH : REACH + rows]
            ia[b] = jnp.broadcast_to(inv[REACH : REACH + rows], (rows, 128))
            put_left(0, b, normed[REACH : REACH + rows], span)
            qb[b] = dot(n1[own_rows, :], wq[:, 0:width]).astype(LOW)
            for g in range(2):
                part = dot(n1[...], wq[:, (g + 1) * width : (g + 2) * width]).astype(LOW)
                kvext[b, 0:ext, g * width : (g + 1) * width] = part
            for h in range(HEADS):
                hs = slice(h * head, (h + 1) * head)
                vs = slice(width + h * head, width + (h + 1) * head)
                s = dot_nt(qb[b, :, hs], kvext[b, :, hs]) * score_scale + bias[...]
                e = jnp.exp(s - jnp.max(s, axis=-1, keepdims=True))
                a = e / jnp.sum(e * cnt[...], axis=-1, keepdims=True)
                af[b, h] = a
                c = (a.astype(LOW).astype(F32) * cnt[...]).astype(LOW)
                ca[b, h] = c
                ob[:, hs] = dot(c, kvext[b, :, vs]).astype(LOW)
            put_left(1, b, ob[...], span)
            x1 = xext[b, own_rows, :].astype(F32) + dot(ob[...], wo[...])
            u, inv = unit(x1)
            ub[b] = u
            ib[b] = jnp.broadcast_to(inv, (rows, 128))
            ids_rows = wide(sel[own_rows, :])
            normed = (u * (1.0 + mod_rows(b, 2, ids_rows)) + mod_rows(b, 3, ids_rows)).astype(LOW)
            n2[...] = normed
            put_left(2, b, normed, span)
            total = x1 + b_down[...]
            for g in range(groups):
                gs = slice(g * TILE, (g + 1) * TILE)
                gate = dot(n2[...], wu[:, gs]) + b_up[:, gs]
                s = 1.0 / (1.0 + jnp.exp(-gate))
                fp[b, :, gs] = s + gate * s * (1.0 - s)
                hid = (gate * s).astype(LOW)
                put_left_hidden(b, hid, g)
                total = total + dot(hid, wd[gs, :])
            lo[0, b] = total.astype(LOW)

        def relay(b):
            return [
                remote(lo.at[0, b], xext.at[b, own_rows, :], fx_s.at[b, 0], fx_r.at[b, 0], (other, me)),
                remote(lo.at[0, b, pl.ds(0, REACH), :], xext.at[b, top_rows, :], fx_s.at[b, 1], fx_r.at[b, 1], (other, down)),
                remote(lo.at[0, b, pl.ds(rows - REACH, REACH), :], xext.at[b, low_rows, :], fx_s.at[b, 2], fx_r.at[b, 2], (other, up)),
            ]

        def norm_back(d, u, inv, scale):
            scaled = d * (1.0 + scale)
            return inv * (
                scaled
                - jnp.mean(scaled, axis=-1, keepdims=True)
                - u * jnp.mean(scaled * u, axis=-1, keepdims=True)
            )

        def mod_sums(b, part, d, u, ids_rows):
            for m in range(z.meshes):
                chosen = jnp.where(jnp.abs(ids_rows - m) < 0.5, d, 0.0)
                sm[b, m : m + 1, part * width : (part + 1) * width] = jnp.sum(chosen * u, axis=0, keepdims=True)
                sm[b, m : m + 1, (part + 1) * width : (part + 2) * width] = jnp.sum(chosen, axis=0, keepdims=True)

        def halos(b):
            return [
                remote(hsend.at[b, 0], hrecv.at[b, 1], bh_s.at[b, 0], bh_r.at[b, 0], (sec, down)),
                remote(hsend.at[b, 1], hrecv.at[b, 0], bh_s.at[b, 1], bh_r.at[b, 1], (sec, up)),
            ]

        def back_first(b):
            at = batch_cols(b)
            ids_rows = wide(sel[own_rows, :])
            dr = dybuf[b]
            right_t[0, at, :] = dr
            dy = dr.astype(F32)
            sm[b, 7:8, 0:width] = jnp.sum(dy, axis=0, keepdims=True)
            dn = jnp.zeros((rows, width), F32)
            for g in range(groups):
                gs = slice(g * TILE, (g + 1) * TILE)
                dg = (dot_nt(dr, wd[gs, :]) * fp[b, :, gs]).astype(LOW)
                right_t[1 + g, at, :] = dg
                sm[b, 6:7, gs] = jnp.sum(dg.astype(F32), axis=0, keepdims=True)
                dn = dn + dot_nt(dg, wu[:, gs])
            u = ub[b]
            grad = dy + norm_back(dn, u, ib[b][:, 0:1], mod_rows(b, 2, ids_rows))
            mod_sums(b, 2, dn, u, ids_rows)
            dx1[b] = grad
            db = grad.astype(LOW)
            right_t[1 + groups, at, :] = db
            ob[...] = dot_nt(db, wo[...]).astype(LOW)
            for h in range(HEADS):
                hs = slice(h * head, (h + 1) * head)
                vs = slice(width + h * head, width + (h + 1) * head)
                da = dot_nt(ob[:, hs], kvext[b, :, vs])
                a = af[b, h]
                ds = a * (da - jnp.sum(a * cnt[...] * da, axis=-1, keepdims=True))
                ds = (ds.astype(LOW).astype(F32) * cnt[...]).astype(LOW)
                right_t[2 + groups, at, hs] = (dot(ds, kvext[b, :, hs]) * score_scale).astype(LOW)
                dk = dot_tn(ds, qb[b, :, hs]) * score_scale
                dv = dot_tn(ca[b, h], ob[:, hs])
                for part, cols in ((dk, hs), (dv, vs)):
                    hsend[b, 0, :, cols] = part[0:REACH].astype(LOW)
                    dkv[b, :, cols] = part[REACH : REACH + rows]
                    hsend[b, 1, :, cols] = part[REACH + rows : ext].astype(LOW)

        def back_second(b):
            at = batch_cols(b)
            ids_rows = wide(sel[own_rows, :])
            edge = rows - REACH
            dkv[b, 0:REACH, :] += hrecv[b, 0].astype(F32)
            dkv[b, edge:rows, :] += hrecv[b, 1].astype(F32)
            dn = dot_nt(right_t[2 + groups, at, :], wq[:, 0:width])
            for g in range(2):
                part = dkv[b, :, g * width : (g + 1) * width].astype(LOW)
                right_t[3 + groups + g, at, :] = part
                dn = dn + dot_nt(part, wq[:, (g + 1) * width : (g + 2) * width])
            u = ua[b]
            grad = dx1[b] + norm_back(dn, u, ia[b][:, 0:1], mod_rows(b, 0, ids_rows))
            mod_sums(b, 0, dn, u, ids_rows)
            ig[0, b] = grad.astype(LOW)

        def relay_back(b):
            return remote(ig.at[0, b], dybuf.at[b], bx_s.at[b], bx_r.at[b], (other, me))

        kvext[:, ext:window, :] = jnp.zeros((batches, window - ext, 2 * width), LOW)
        sm[...] = jnp.zeros(sm.shape, F32)
        for copy in loads[1:]:
            copy.wait()
        for copy in (m_down, m_up):
            copy.wait()

        @pl.when(sec == 0)
        def _():
            first_load.wait()
            x_down.wait()
            x_up.wait()

        @pl.when(sec == 1)
        def _():
            last_load.wait()

        def forward_step(b, carry):
            @pl.when(sec == 1)
            def _():
                for copy in relay(b):
                    copy.wait_recv()

            forward(b)

            @pl.when(sec == 0)
            def _():
                for copy in relay(b):
                    copy.start()

            return carry

        lax.fori_loop(0, batches, forward_step, 0)

        def first_step(b):
            @pl.when(sec == 0)
            def _():
                relay_back(b).wait_recv()

            back_first(b)
            for copy in halos(b):
                copy.start()

        def second_step(b):
            for copy in halos(b):
                copy.wait_recv()
            back_second(b)

            @pl.when(sec == 1)
            def _():
                relay_back(b).start()

        def backward_step(k, carry):
            b = batches - 1 - k
            first_step(b)

            @pl.when(k > 0)
            def _():
                second_step(b + 1)

            return carry

        lax.fori_loop(0, batches, backward_step, 0)
        second_step(0)

        def finish(b, carry):
            @pl.when(sec == 0)
            def _():
                for copy in relay(b):
                    copy.wait_send()

            @pl.when(sec == 1)
            def _():
                relay_back(b).wait_send()

            for copy in halos(b):
                copy.wait_send()
            return carry

        lines = [sm[b, m : m + 1, :] for b in range(batches) for m in range(z.meshes)]
        for line in (6, 7):
            lines.append(sum(sm[b, line : line + 1, :] for b in range(batches)))
        lines.append(jnp.zeros((16 - len(lines), sm.shape[2]), F32))
        small = jnp.concatenate(lines, axis=0)

        if not z.scatter:
            small_out[...] = small
            table_out[...] = emb[...]
            lax.fori_loop(0, batches, finish, 0)
            return

        (
            cs, cr, xs, xr, xk, zs, zr, zk, acc, msend, mrecv, tot,
            c_s, c_r, x_s, x_r, z_s, z_r, m_s, m_r,
        ) = rest

        def core_copy(p):
            return remote(cs.at[p], cr.at[p], c_s.at[p], c_r.at[p], (sec, core_mate))

        def x_copy(p):
            return remote(xs.at[p], xr.at[p], x_s.at[p], x_r.at[p], (sec, x_mate))

        def z_copies(p):
            return [
                remote(zs.at[p, lax.rem(zpos + k, z.line)], zr.at[p, k - 1], z_s.at[p, k - 1], z_r.at[p, k - 1], (sec, z_mate(k)))
                for k in range(1, z.line)
            ]

        def half_rows(c):
            return pl.ds(pl.multiple_of(c * half, half), half)

        def piece_start(p):
            left, right, _, _ = z.pieces[p]
            cs[p] = dot(left_t[left, half_rows(1 - core), :], right_t[right]).astype(LOW)
            core_copy(p).start()

        def piece_core(p):
            left, right, _, _ = z.pieces[p]
            mine = dot(left_t[left, half_rows(core), :], right_t[right])
            core_copy(p).wait_recv()
            acc[...] = mine + cr[p].astype(F32)
            give = pl.ds(pl.multiple_of((1 - xpos) * quarter, quarter), quarter)
            keep = pl.ds(pl.multiple_of(xpos * quarter, quarter), quarter)
            xs[p] = acc[give, :].astype(LOW)
            xk[p] = acc[keep, :]
            x_copy(p).start()

        def piece_x(p):
            x_copy(p).wait_recv()
            value = xk[p] + xr[p].astype(F32)
            for k in range(z.line):
                zs[p, k] = value[k * own : (k + 1) * own].astype(LOW)
                zk[p, k] = value[k * own : (k + 1) * own]
            for copy in z_copies(p):
                copy.start()

        def piece_z(p):
            value = zk[p, zpos]
            for k, copy in enumerate(z_copies(p)):
                copy.wait_recv()
                value = value + zr[p, k].astype(F32)
            _, _, name, q = z.pieces[p]
            if name == "down":
                o_down[0, q * own : (q + 1) * own, :] = value
            elif name == "up":
                o_up[0, :, q * TILE : (q + 1) * TILE] = value
            elif name == "out":
                o_out[0] = value
            else:
                o_qkv[0, :, q * TILE : (q + 1) * TILE] = value

        def ring_copy(k):
            bit = 1 << k
            mate = me + bit - 2 * bit * (me // bit % 2)
            return remote(msend.at[k], mrecv.at[k], m_s.at[k], m_r.at[k], (sec, mate))

        def ring_start(k, value):
            msend[k] = value.astype(LOW)
            ring_copy(k).start()

        def ring_end(k):
            ring_copy(k).wait_recv()
            return msend[k].astype(F32) + mrecv[k].astype(F32)

        ring_start(0, small)
        for p in range(npiece + 4):
            if p < npiece:
                piece_start(p)
            if 1 <= p <= npiece:
                piece_core(p - 1)
            if 2 <= p < npiece + 2:
                piece_x(p - 2)
            if 4 <= p:
                piece_z(p - 4)
            k = p - 1
            if 0 <= k < z.rings:
                value = ring_end(k)
                if k + 1 < z.rings:
                    ring_start(k + 1, value)
                else:
                    tot[...] = value

        count = batches * z.meshes
        table = emb[pl.ds(pl.multiple_of(me * own, own), own), :]
        grad = jnp.zeros((own, 4 * width), F32)
        for k in range(count):
            grad = grad + table[:, k : k + 1] * tot[k : k + 1, :]
        o_mod[0] = grad
        cols = 4 * width // shards
        mine = tot[:, pl.ds(pl.multiple_of(me * cols, cols), cols)]
        o_modb[...] = jnp.sum(mine[0:count], axis=0, keepdims=True)
        o_upb[...] = mine[count : count + 1]
        ratio = 128 // own
        line = tot[:, pl.ds(pl.multiple_of(me // ratio * 128, 128), 128)][count + 1 : count + 2]
        value = line[:, 0:own]
        for k in range(1, ratio):
            value = jnp.where(me % ratio == k, line[:, k * own : (k + 1) * own], value)
        o_downb[...] = value

        lax.fori_loop(0, batches, finish, 0)
        for p in range(npiece):
            core_copy(p).wait_send()
            x_copy(p).wait_send()
            for copy in z_copies(p):
                copy.wait_send()
        for k in range(z.rings):
            ring_copy(k).wait_send()

    def whole(*refs):
        kernel(*refs)

    return whole


def body(
    inputs,
    cotangent,
    neighbours,
    mesh_ids,
    noise_sigma,
    w_qkv,
    w_out,
    w_up,
    b_up,
    w_down,
    b_down,
    w_mod,
    b_mod,
):
    shards = lax.axis_size("nodes")
    z = Sizes(inputs, neighbours, noise_sigma, w_up, shards)
    batches, rows, width, hidden = z.batches, z.rows, z.width, z.hidden
    own, npiece = z.own, len(z.pieces)
    shape = jax.ShapeDtypeStruct
    outs = [shape((1, batches, rows, width), LOW), shape((1, batches, rows, width), LOW)]
    sides = [(z.lefts, TILE, batches * rows), (z.rights, batches * rows, TILE)]
    if z.scatter:
        outs += [
            shape((1, own, 3 * width), F32),
            shape((1, own, width), F32),
            shape((1, own, hidden), F32),
            shape((1, hidden // shards), F32),
            shape((1, hidden // shards, width), F32),
            shape((1, own), F32),
            shape((1, own, 4 * width), F32),
            shape((1, 4 * width // shards), F32),
        ]
        scratch = [pltpu.VMEM(s, LOW) for s in sides]
    else:
        outs += [shape(s, LOW) for s in sides] + [shape((16, hidden), F32), shape((width, 128), F32)]
        scratch = []
    dma = pltpu.SemaphoreType.DMA
    scratch += [
        pltpu.VMEM((width, 3 * width), LOW),
        pltpu.VMEM((width, width), LOW),
        pltpu.VMEM((width, hidden), LOW),
        pltpu.VMEM((hidden, width), LOW),
        pltpu.VMEM((width, 4 * width), LOW),
        pltpu.VMEM((batches, z.ext, width), LOW),
        pltpu.VMEM((batches, rows, width), LOW),
        pltpu.VMEM((z.ext, 128), F32),
        pltpu.VMEM((rows, z.window), F32),
        pltpu.VMEM((rows, z.window), F32),
        pltpu.VMEM((batches, 8, 4 * width), F32),
        pltpu.VMEM((width, 128), F32),
        pltpu.VMEM((z.ext, width), LOW),
        pltpu.VMEM((batches, rows, width), F32),
        pltpu.VMEM((batches, rows, 128), F32),
        pltpu.VMEM((batches, rows, width), LOW),
        pltpu.VMEM((batches, z.window, 2 * width), LOW),
        pltpu.VMEM((batches, HEADS, rows, z.window), F32),
        pltpu.VMEM((batches, HEADS, rows, z.window), LOW),
        pltpu.VMEM((rows, width), LOW),
        pltpu.VMEM((rows, width), LOW),
        pltpu.VMEM((batches, rows, width), F32),
        pltpu.VMEM((batches, rows, 128), F32),
        pltpu.VMEM((batches, rows, hidden), F32),
        pltpu.VMEM((batches, rows, width), F32),
        pltpu.VMEM((batches, rows, 2 * width), F32),
        pltpu.VMEM((batches, 2, REACH, 2 * width), LOW),
        pltpu.VMEM((batches, 2, REACH, 2 * width), LOW),
        pltpu.VMEM((batches, 8, hidden), F32),
        dma((7,)),
        dma((2,)),
        dma((2,)),
        dma((2,)),
        dma((2,)),
        dma((batches, 3)),
        dma((batches, 3)),
        dma((batches, 2)),
        dma((batches, 2)),
        dma((batches,)),
        dma((batches,)),
    ]
    if z.scatter:
        half, quarter, line = TILE // 2, TILE // 4, z.line
        scratch += [
            pltpu.VMEM((npiece, half, TILE), LOW),
            pltpu.VMEM((npiece, half, TILE), LOW),
            pltpu.VMEM((npiece, quarter, TILE), LOW),
            pltpu.VMEM((npiece, quarter, TILE), LOW),
            pltpu.VMEM((npiece, quarter, TILE), F32),
            pltpu.VMEM((npiece, line, own, TILE), LOW),
            pltpu.VMEM((npiece, line, own, TILE), LOW),
            pltpu.VMEM((npiece, line, own, TILE), F32),
            pltpu.VMEM((half, TILE), F32),
            pltpu.VMEM((z.rings, 16, hidden), LOW),
            pltpu.VMEM((z.rings, 16, hidden), LOW),
            pltpu.VMEM((16, hidden), F32),
            dma((npiece,)),
            dma((npiece,)),
            dma((npiece,)),
            dma((npiece,)),
            dma((npiece, line)),
            dma((npiece, line)),
            dma((z.rings,)),
            dma((z.rings,)),
        ]
    hbm = pl.BlockSpec(memory_space=pl.ANY)
    vmem = pl.BlockSpec(memory_space=pltpu.VMEM)
    smem = pl.BlockSpec(memory_space=pltpu.SMEM)
    got = pl.pallas_call(
        kernel_of(z),
        out_shape=outs,
        in_specs=[hbm, hbm, vmem, vmem, smem, hbm, hbm, hbm, vmem, hbm, vmem, hbm, vmem],
        out_specs=[vmem] * len(outs),
        scratch_shapes=scratch,
        compiler_params=pltpu.CompilerParams(
            collective_id=0, has_side_effects=True, vmem_limit_bytes=60 * 2**20
        ),
    )(
        inputs,
        cotangent,
        neighbours,
        mesh_ids.reshape(1, rows),
        noise_sigma,
        w_qkv,
        w_out,
        w_up,
        b_up,
        w_down,
        b_down,
        w_mod,
        b_mod,
    )
    if z.scatter:
        return tuple(got)
    lo, ig, left_t, right_t, small, table = got

    def summed(value):
        return lax.psum_scatter(value, "nodes", scatter_dimension=0, tiled=True)

    def gathered(name):
        return [dot(left_t[left], right_t[right]) for left, right, kind, _ in z.pieces if kind == name]

    down = jnp.stack([v.reshape(TILE // 32, 32, TILE) for v in gathered("down")], axis=1)
    count = batches * z.meshes
    small = lax.psum(small, "nodes")
    me = lax.axis_index("nodes")
    mod = jnp.dot(table[:, :count], small[:count], precision=lax.Precision.HIGHEST)

    def mine(value):
        size = value.shape[0] // shards
        return lax.dynamic_slice_in_dim(value, me * size, size, axis=0)[None]

    return (
        lo,
        ig,
        summed(jnp.concatenate(gathered("qkv"), axis=1))[None],
        summed(gathered("out")[0])[None],
        summed(jnp.concatenate(gathered("up"), axis=1))[None],
        mine(small[count]),
        summed(down.reshape(hidden, width))[None],
        mine(small[count + 1, :width]),
        mine(mod),
        mine(jnp.sum(small[:count], axis=0)),
    )


def solution(mesh):
    return jax.shard_map(
        body,
        mesh=mesh,
        in_specs=(
            P(None, "nodes", None),
            P(None, "nodes", None),
            P("nodes", None),
            P("nodes"),
            P(),
            P("section", None, None),
            P("section", None, None),
            P("section", None, None),
            P("section", None),
            P("section", None, None),
            P("section", None),
            P("section", None, None),
            P("section", None),
        ),
        out_specs=(
            P("section", None, "nodes", None),
            P("section", None, "nodes", None),
            P("section", "nodes", None),
            P("section", "nodes", None),
            P("section", "nodes", None),
            P("section", "nodes"),
            P("section", "nodes", None),
            P("section", "nodes"),
            P("section", "nodes", None),
            P("section", "nodes"),
        ),
        check_vma=False,
    )
```

```python
import jax
import jax.numpy as jnp
from jax import lax
from jax.experimental import pallas as pl
from jax.experimental.pallas import tpu as pltpu
from jax.sharding import PartitionSpec as P

HEADS = 4
REACH = 32
EPSILON = 1e-06
MASKED = -1e9
ABSENT = -2e38
TILE = 512
TOGETHER = 2
MESH = pl.DeviceIdType.MESH
F32, LOW = jnp.float32, jnp.bfloat16


def dot(a, b):
    return lax.dot_general(a, b, (((1,), (0,)), ((), ())), preferred_element_type=F32)


def dot_nt(a, b):
    return lax.dot_general(a, b, (((1,), (1,)), ((), ())), preferred_element_type=F32)


def dot_tn(a, b):
    return lax.dot_general(a, b, (((0,), (0,)), ((), ())), preferred_element_type=F32)


class Sizes:
    def __init__(self, inputs, neighbours, noise, w_up, shards):
        self.batches, self.rows, self.width = inputs.shape
        self.together = TOGETHER if self.batches % TOGETHER == 0 else 1
        self.turns = self.batches // self.together
        self.slots = neighbours.shape[1]
        self.meshes = noise.shape[1]
        self.hidden = w_up.shape[2]
        self.shards = shards
        self.ext = self.rows + 2 * REACH
        self.window = (self.ext // 128 + 1) * 128
        self.groups = self.hidden // TILE
        self.own = self.width // shards
        self.scatter = self.own % 16 == 0
        self.pieces = 2 * self.groups + 4
        self.lefts = 3 + self.groups
        self.rights = 2 + self.groups + 3
        self.rings = max(shards.bit_length() - 1, 1)
        self.line = max(shards // 4, 1)

    def left(self, p):
        n = self.groups
        return jnp.minimum(p, n) + lax.div(p, 2 * n) + lax.div(p, 2 * n + 1)

    def right(self, p):
        return jnp.maximum(p - (self.groups - 1), 0)


def kernel_of(z):
    batches, rows, width, ext, window = z.batches, z.rows, z.width, z.ext, z.window
    groups, shards, own, many = z.groups, z.shards, z.own, z.together
    head = width // HEADS
    score_scale = head ** (-0.5)
    npiece = z.pieces
    half, quarter = TILE // 2, TILE // 4
    g_out, g_q, g_k = 1 + groups, 2 + groups, 3 + groups

    def position(owner):
        if not z.scatter:
            return owner
        return (owner % 2) * (shards // 2) + (owner // 2 % 2) * z.line + owner // 4

    def kernel(
        inputs, cotangent, neighbours, mesh_ids, sigma,
        w_qkv, w_out, w_up, b_up, w_down, b_down, w_mod, b_mod,
        lo, ig, *rest,
    ):
        if z.scatter:
            o_piece, o_mod, o_line = rest[:3]
            rest = rest[3:]
            left_t, right_t = rest[:2]
            rest = rest[2:]
        else:
            left_t, right_t, small_out, table_out = rest[:4]
            rest = rest[4:]
        (
            wq, wo, wu, wd, wm, xext, dybuf, sel, cnt, bias, mod, emb,
            n1, n1s, ua, ia, qb, kvext, sbuf, af, ca, obs, n2s, ub, ib, tb, fp, hs,
            ob, cds, dx1, dkv, hsend, hrecv, sm,
            lsem, hx_s, hx_r, hm_s, hm_r, fx_s, fx_r, bh_s, bh_r, bx_s, bx_r,
        ) = rest[:46]
        rest = rest[46:]

        sec = lax.axis_index("section")
        me = lax.axis_index("nodes")
        up = lax.rem(me + 1, shards)
        down = lax.rem(me + shards - 1, shards)
        other = 1 - sec
        if z.scatter:
            core, xpos, zpos = me % 2, me // 2 % 2, me // 4
            core_mate = me + 1 - 2 * core
            x_mate = me + 2 - 4 * xpos

            def z_mate(k):
                return lax.rem(zpos + k, z.line) * 4 + xpos * 2 + core

        def local(src, dst, k):
            return pltpu.make_async_copy(src, dst, lsem.at[k])

        loads = [
            local(w_mod.at[0], wm, 0),
            local(w_qkv.at[0], wq, 1),
            local(w_out.at[0], wo, 2),
            local(w_up.at[0], wu, 3),
            local(w_down.at[0], wd, 4),
        ]
        own_rows = pl.ds(REACH, rows)
        first_load = local(inputs, xext.at[:, own_rows, :], 5)
        last_load = local(cotangent, dybuf, 6)
        loads[0].start()

        @pl.when(sec == 0)
        def _():
            first_load.start()

        for copy in loads[1:]:
            copy.start()

        @pl.when(sec == 1)
        def _():
            last_load.start()

        barrier = pltpu.get_barrier_semaphore()
        mates = [(sec, up), (sec, down), (other, me), (other, up), (other, down)]
        if z.scatter:
            mates += [(sec, x_mate)] + [(sec, z_mate(k)) for k in range(1, z.line)]
        for mate in mates:
            pl.semaphore_signal(barrier, inc=1, device_id=mate, device_id_type=MESH)
        pl.semaphore_wait(barrier, len(mates))

        def remote(src, dst, s_sem, r_sem, mate):
            return pltpu.make_async_remote_copy(
                src_ref=src, dst_ref=dst, send_sem=s_sem, recv_sem=r_sem, device_id=mate, device_id_type=MESH
            )

        low_rows, top_rows = pl.ds(0, REACH), pl.ds(REACH + rows, REACH)
        head_rows, tail_rows = pl.ds(REACH, REACH), pl.ds(rows, REACH)
        x_down = remote(inputs.at[:, pl.ds(0, REACH), :], xext.at[:, top_rows, :], hx_s.at[0], hx_r.at[0], (sec, down))
        x_up = remote(inputs.at[:, pl.ds(rows - REACH, REACH), :], xext.at[:, low_rows, :], hx_s.at[1], hx_r.at[1], (sec, up))

        @pl.when(sec == 0)
        def _():
            x_down.start()
            x_up.start()

        ids = jnp.broadcast_to(mesh_ids[...].astype(F32), (128, rows))
        sel[own_rows, :] = ids.T
        m_down = remote(sel.at[head_rows, :], sel.at[top_rows, :], hm_s.at[0], hm_r.at[0], (sec, down))
        m_up = remote(sel.at[tail_rows, :], sel.at[low_rows, :], hm_s.at[1], hm_r.at[1], (sec, up))
        m_down.start()
        m_up.start()

        row_no = lax.broadcasted_iota(jnp.int32, (16, width // 2), 0)
        level = jnp.ones((16, width // 2), F32)
        for b in range(batches):
            for m in range(z.meshes):
                level = jnp.where(row_no == b * z.meshes + m, sigma[m, b], level)
        place = lax.broadcasted_iota(jnp.int32, (16, width // 2), 1).astype(F32)
        frequency = 3.0 * jnp.exp(-jnp.log(100.0) * place / (width // 2))
        angles = jnp.log(level) * frequency
        embedded = jnp.concatenate([jnp.sin(angles), jnp.cos(angles)], axis=1).astype(LOW)
        padded = jnp.concatenate([embedded.astype(F32), jnp.zeros((112, width), F32)], axis=0)
        emb[...] = padded.T
        loads[0].wait()
        for g in range(4):
            cols = pl.ds(g * width, width)
            table = dot(embedded, wm[:, cols]) + b_mod[:, cols]
            for b in range(batches):
                mod[b, 0 : z.meshes, cols] = table[b * z.meshes : (b + 1) * z.meshes]

        slots = neighbours[...].astype(F32)
        slots = jnp.concatenate([slots, jnp.zeros((128 - z.slots, rows), F32)], axis=0).T
        slots = jnp.where(slots >= 0, slots - (me * rows - REACH).astype(F32), float(ext))
        column = lax.broadcasted_iota(jnp.int32, (rows, window), 1).astype(F32)
        counts = jnp.zeros((rows, window), F32)
        for n in range(z.slots):
            counts = counts + jnp.where(slots[:, n : n + 1] == column, 1.0, 0.0)
        cnt[...] = counts
        bias[...] = jnp.where(counts > 0, jnp.where(column == ext, MASKED, 0.0), ABSENT)

        def mod_rows(b, part, ids_rows):
            cols = pl.ds(part * width, width)
            value = jnp.broadcast_to(mod[b, 0:1, cols], (ids_rows.shape[0], width))
            for m in range(1, z.meshes):
                value = jnp.where(ids_rows > m - 0.5, mod[b, m : m + 1, cols], value)
            return value

        def wide(ids_rows):
            return jnp.concatenate([ids_rows] * (width // 128), axis=1)

        def unit(x):
            centred = x - jnp.mean(x, axis=-1, keepdims=True)
            inv = lax.rsqrt(jnp.mean(centred * centred, axis=-1, keepdims=True) + EPSILON)
            return centred * inv, inv

        def batch_cols(b):
            return pl.ds(pl.multiple_of(b * rows, rows), rows)

        def turn_cols(t):
            return pl.ds(pl.multiple_of(t * many * rows, many * rows), many * rows)

        def turn_of(ref, t):
            return ref[pl.ds(t * many, many)].reshape(many * rows, ref.shape[2])

        span = own if z.scatter else 32

        def transposes(b, carry):
            for first, ref in ((groups, n2s), (groups + 1, obs), (groups + 2, n1s)):
                turned = ref[b].T
                for owner in range(TILE // span):
                    at = position(owner) * span
                    left_t[first, at : at + span, batch_cols(b)] = turned[owner * span : (owner + 1) * span]
            run = groups * span
            for g in range(groups):
                turned = hs[b, :, g * TILE : (g + 1) * TILE].T
                for k in range(TILE // span):
                    at = g * TILE + k * span
                    owner, part = at // run, at % run // span
                    to = position(owner) * span
                    left_t[part, to : to + span, batch_cols(b)] = turned[k * span : (k + 1) * span]
            return carry

        def forward(t):
            for i in range(many):
                b = t * many + i
                ids_rows = wide(sel[0:ext, :])
                u, inv = unit(xext[b].astype(F32))
                normed = (u * (1.0 + mod_rows(b, 0, ids_rows)) + mod_rows(b, 1, ids_rows)).astype(LOW)
                n1[i * ext : (i + 1) * ext, :] = normed
                n1s[b] = normed[REACH : REACH + rows]
                ua[b] = u[REACH : REACH + rows]
                ia[b] = jnp.broadcast_to(inv[REACH : REACH + rows], (rows, 128))
            part = dot(turn_of(n1s, t), wq[:, 0:width]).astype(LOW)
            qb[pl.ds(t * many, many)] = part.reshape(many, rows, width)
            for g in range(2):
                part = dot(n1[...], wq[:, (g + 1) * width : (g + 2) * width]).astype(LOW)
                for i in range(many):
                    kvext[t * many + i, 0:ext, g * width : (g + 1) * width] = part[i * ext : (i + 1) * ext]
            for i in range(many):
                b = t * many + i
                for h in range(HEADS):
                    hd = slice(h * head, (h + 1) * head)
                    sbuf[h] = dot_nt(qb[b, :, hd], kvext[b, :, hd]) * score_scale + bias[...]
                for h in range(HEADS):
                    s = sbuf[h]
                    e = jnp.exp(s - jnp.max(s, axis=-1, keepdims=True))
                    a = e / jnp.sum(e * cnt[...], axis=-1, keepdims=True)
                    af[b, h] = a
                    ca[b, h] = (a.astype(LOW).astype(F32) * cnt[...]).astype(LOW)
                for h in range(HEADS):
                    hd = slice(h * head, (h + 1) * head)
                    vd = slice(width + h * head, width + (h + 1) * head)
                    obs[b, :, hd] = dot(ca[b, h], kvext[b, :, vd]).astype(LOW)
            branch = dot(turn_of(obs, t), wo[...])
            for i in range(many):
                b = t * many + i
                x1 = xext[b, own_rows, :].astype(F32) + branch[i * rows : (i + 1) * rows]
                u, inv = unit(x1)
                ub[b] = u
                ib[b] = jnp.broadcast_to(inv, (rows, 128))
                ids_rows = wide(sel[own_rows, :])
                n2s[b] = (u * (1.0 + mod_rows(b, 2, ids_rows)) + mod_rows(b, 3, ids_rows)).astype(LOW)
                tb[i * rows : (i + 1) * rows, :] = x1 + b_down[...]
            for g in range(groups):
                gs = slice(g * TILE, (g + 1) * TILE)
                gate = dot(turn_of(n2s, t), wu[:, gs]) + b_up[:, gs]
                s = 1.0 / (1.0 + jnp.exp(-gate))
                hid = (gate * s).astype(LOW)
                slope = (s + gate * s * (1.0 - s)).astype(LOW)
                for i in range(many):
                    fp[t * many + i, :, gs] = slope[i * rows : (i + 1) * rows]
                    hs[t * many + i, :, gs] = hid[i * rows : (i + 1) * rows]
                tb[...] += dot(hid, wd[gs, :])
            for i in range(many):
                lo[0, t * many + i] = tb[i * rows : (i + 1) * rows, :].astype(LOW)

        def relay(b):
            return [
                remote(lo.at[0, b], xext.at[b, own_rows, :], fx_s.at[b, 0], fx_r.at[b, 0], (other, me)),
                remote(lo.at[0, b, pl.ds(0, REACH), :], xext.at[b, top_rows, :], fx_s.at[b, 1], fx_r.at[b, 1], (other, down)),
                remote(lo.at[0, b, pl.ds(rows - REACH, REACH), :], xext.at[b, low_rows, :], fx_s.at[b, 2], fx_r.at[b, 2], (other, up)),
            ]

        def norm_back(d, u, inv, scale):
            scaled = d * (1.0 + scale)
            return inv * (
                scaled
                - jnp.mean(scaled, axis=-1, keepdims=True)
                - u * jnp.mean(scaled * u, axis=-1, keepdims=True)
            )

        def mod_sums(b, part, d, u, ids_rows):
            for m in range(z.meshes):
                chosen = jnp.where(jnp.abs(ids_rows - m) < 0.5, d, 0.0)
                sm[b, m : m + 1, part * width : (part + 1) * width] = jnp.sum(chosen * u, axis=0, keepdims=True)
                sm[b, m : m + 1, (part + 1) * width : (part + 2) * width] = jnp.sum(chosen, axis=0, keepdims=True)

        def halos(b):
            return [
                remote(hsend.at[b, 0], hrecv.at[b, 1], bh_s.at[b, 0], bh_r.at[b, 0], (sec, down)),
                remote(hsend.at[b, 1], hrecv.at[b, 0], bh_s.at[b, 1], bh_r.at[b, 1], (sec, up)),
            ]

        def given(t):
            at = turn_cols(t)
            dr = turn_of(dybuf, t)
            right_t[0, at, :] = dr
            for i in range(many):
                total = jnp.sum(dr[i * rows : (i + 1) * rows].astype(F32), axis=0, keepdims=True)
                sm[t * many + i, 7:8, 0:width] = total
            for g in range(groups):
                right_t[1 + g, at, :] = dot_nt(dr, wd[g * TILE : (g + 1) * TILE, :]).astype(LOW)

        def back_ffn(t):
            at = turn_cols(t)
            dn = jnp.zeros((many * rows, width), F32)
            for g in range(groups):
                gs = slice(g * TILE, (g + 1) * TILE)
                dg = right_t[1 + g, at, :].astype(F32) * turn_of(fp, t)[:, gs].astype(F32)
                sm[t * many, 6:7, gs] = jnp.sum(dg, axis=0, keepdims=True)
                dg = dg.astype(LOW)
                right_t[1 + g, at, :] = dg
                dn = dn + dot_nt(dg, wu[:, gs])
            ids_rows = wide(sel[own_rows, :])
            for i in range(many):
                b = t * many + i
                d = dn[i * rows : (i + 1) * rows]
                u = ub[b]
                grad = dybuf[b].astype(F32) + norm_back(d, u, ib[b][:, 0:1], mod_rows(b, 2, ids_rows))
                mod_sums(b, 2, d, u, ids_rows)
                dx1[b] = grad
                right_t[g_out, batch_cols(b), :] = grad.astype(LOW)
            ob[...] = dot_nt(right_t[g_out, at, :], wo[...]).astype(LOW)

        def back_attention(t):
            for i in range(many):
                b = t * many + i
                at = batch_cols(b)
                here = slice(i * rows, (i + 1) * rows)
                for h in range(HEADS):
                    hd = slice(h * head, (h + 1) * head)
                    vd = slice(width + h * head, width + (h + 1) * head)
                    sbuf[h] = dot_nt(ob[here, hd], kvext[b, :, vd])
                for h in range(HEADS):
                    a, da = af[b, h], sbuf[h]
                    ds = a * (da - jnp.sum(a * cnt[...] * da, axis=-1, keepdims=True))
                    cds[h] = (ds.astype(LOW).astype(F32) * cnt[...]).astype(LOW)
                for h in range(HEADS):
                    hd = slice(h * head, (h + 1) * head)
                    vd = slice(width + h * head, width + (h + 1) * head)
                    dk = dot_tn(cds[h], qb[b, :, hd]) * score_scale
                    dv = dot_tn(ca[b, h], ob[here, hd])
                    for part, cols in ((dk, hd), (dv, vd)):
                        hsend[b, 0, :, cols] = part[0:REACH].astype(LOW)
                        dkv[b, :, cols] = part[REACH : REACH + rows]
                        hsend[b, 1, :, cols] = part[REACH + rows : ext].astype(LOW)
                for copy in halos(b):
                    copy.start()
                for h in range(HEADS):
                    hd = slice(h * head, (h + 1) * head)
                    right_t[g_q, at, hd] = (dot(cds[h], kvext[b, :, hd]) * score_scale).astype(LOW)

        def back_second(t):
            at = turn_cols(t)
            ids_rows = wide(sel[own_rows, :])
            edge = rows - REACH
            dn = dot_nt(right_t[g_q, at, :], wq[:, 0:width])
            for i in range(many):
                b = t * many + i
                for copy in halos(b):
                    copy.wait_recv()
                dkv[b, 0:REACH, :] += hrecv[b, 0].astype(F32)
                dkv[b, edge:rows, :] += hrecv[b, 1].astype(F32)
                for g in range(2):
                    right_t[g_k + g, batch_cols(b), :] = dkv[b, :, g * width : (g + 1) * width].astype(LOW)
            for g in range(2):
                dn = dn + dot_nt(right_t[g_k + g, at, :], wq[:, (g + 1) * width : (g + 2) * width])
            for i in range(many):
                b = t * many + i
                d = dn[i * rows : (i + 1) * rows]
                u = ua[b]
                grad = dx1[b] + norm_back(d, u, ia[b][:, 0:1], mod_rows(b, 0, ids_rows))
                ig[0, b] = grad.astype(LOW)

                @pl.when(sec == 1)
                def _():
                    relay_back(b).start()

                mod_sums(b, 0, d, u, ids_rows)

        def relay_back(b):
            return remote(ig.at[0, b], dybuf.at[b], bx_s.at[b], bx_r.at[b], (other, me))

        kvext[:, ext:window, :] = jnp.zeros((batches, window - ext, 2 * width), LOW)
        sm[...] = jnp.zeros(sm.shape, F32)
        for copy in loads[1:]:
            copy.wait()
        for copy in (m_down, m_up):
            copy.wait()

        @pl.when(sec == 0)
        def _():
            first_load.wait()
            x_down.wait()
            x_up.wait()

        @pl.when(sec == 1)
        def _():
            last_load.wait()

            @pl.loop(0, z.turns)
            def _(t):
                given(t)

        @pl.loop(0, z.turns)
        def _(t):
            @pl.when(sec == 1)
            def _():
                for i in range(many):
                    for copy in relay(t * many + i):
                        copy.wait_recv()

            forward(t)

            @pl.when(sec == 0)
            def _():
                for i in range(many):
                    for copy in relay(t * many + i):
                        copy.start()

        @pl.when(sec == 0)
        def _():
            lax.fori_loop(0, batches, transposes, 0)

        if z.scatter:
            (
                cs, cr, xs, xr, xk, zs, zr, acc, msend, mrecv, tot,
                c_s, c_r, x_s, x_r, z_s, z_r, m_s, m_r,
            ) = rest

            def core_copy(p):
                return remote(cs.at[p], cr.at[p], c_s.at[p], c_r.at[p], (sec, core_mate))

            def x_copy(p):
                return remote(xs.at[p], xr.at[p], x_s.at[p], x_r.at[p], (sec, x_mate))

            def z_copies(p):
                return [
                    remote(zs.at[p, lax.rem(zpos + k, z.line)], zr.at[p, k - 1], z_s.at[p, k - 1], z_r.at[p, k - 1], (sec, z_mate(k)))
                    for k in range(1, z.line)
                ]

            def half_rows(c):
                return pl.ds(pl.multiple_of(c * half, half), half)

            def quarter_rows(c):
                return pl.ds(pl.multiple_of(c * quarter, quarter), quarter)

            def piece_start(p):
                cs[p] = dot(left_t[z.left(p), half_rows(1 - core), :], right_t[z.right(p)]).astype(LOW)
                core_copy(p).start()

            def piece_core(p):
                mine = dot(left_t[z.left(p), half_rows(core), :], right_t[z.right(p)])
                core_copy(p).wait_recv()
                acc[...] = mine + cr[p].astype(F32)
                xs[p] = acc[quarter_rows(1 - xpos), :].astype(LOW)
                x_copy(p).start()
                xk[p] = acc[quarter_rows(xpos), :]

            def piece_x(p):
                x_copy(p).wait_recv()
                value = xk[p] + xr[p].astype(F32)
                for k in range(z.line):
                    zs[p, k] = value[k * own : (k + 1) * own].astype(LOW)
                for copy in z_copies(p):
                    copy.start()
                xk[p] = value

            def piece_z(p):
                value = xk[p, pl.ds(pl.multiple_of(zpos * own, own), own), :]
                for k, copy in enumerate(z_copies(p)):
                    copy.wait_recv()
                    value = value + zr[p, k].astype(F32)
                o_piece[p] = value

            def pieces(step, first, last):
                @pl.loop(first, last)
                def _(p):
                    step(p)

        @pl.loop(0, z.turns)
        def _(k):
            t = z.turns - 1 - k

            @pl.when(sec == 0)
            def _():
                for i in range(many):
                    relay_back(t * many + i).wait_recv()
                given(t)

            if z.scatter:

                @pl.when((sec == 0) & (t == 0))
                def _():
                    pieces(piece_start, 0, groups)

            back_ffn(t)
            if z.scatter:

                @pl.when((sec == 0) & (t == 0))
                def _():
                    pieces(piece_start, groups, 2 * groups + 1)
                    pieces(piece_core, 0, groups)

            back_attention(t)
            if z.scatter:

                @pl.when((sec == 0) & (t == 0))
                def _():
                    pieces(piece_core, groups, 2 * groups + 1)

            back_second(t)

        @pl.when(sec == 1)
        def _():
            lax.fori_loop(0, batches, transposes, 0)

        lines = [sm[b, m : m + 1, :] for b in range(batches) for m in range(z.meshes)]
        for line in (6, 7):
            lines.append(sum(sm[b, line : line + 1, :] for b in range(batches)))
        lines.append(jnp.zeros((16 - len(lines), sm.shape[2]), F32))
        small = jnp.concatenate(lines, axis=0)

        def finish():
            @pl.loop(0, batches)
            def _(b):
                @pl.when(sec == 0)
                def _():
                    for copy in relay(b):
                        copy.wait_send()

                @pl.when(sec == 1)
                def _():
                    relay_back(b).wait_send()

                for copy in halos(b):
                    copy.wait_send()

        if not z.scatter:
            small_out[...] = small
            table_out[...] = emb[...]
            finish()
            return

        def ring_copy(k):
            bit = 1 << k
            mate = me + bit - 2 * bit * (me // bit % 2)
            return remote(msend.at[k], mrecv.at[k], m_s.at[k], m_r.at[k], (sec, mate))

        def ring_start(k, value):
            msend[k] = value.astype(LOW)
            ring_copy(k).start()

        def ring_end(k):
            ring_copy(k).wait_recv()
            value = msend[k].astype(F32) + mrecv[k].astype(F32)
            if k + 1 < z.rings:
                ring_start(k + 1, value)
            else:
                tot[...] = value

        ring_start(0, small)
        early = 2 * groups + 1
        first = (1 - sec) * early
        pieces(piece_start, first, npiece)
        ring_end(0)
        pieces(piece_core, first, npiece)
        if z.rings > 1:
            ring_end(1)
        pieces(piece_x, 0, groups)
        if z.rings > 2:
            ring_end(2)
        pieces(piece_x, groups, early)
        for k in range(3, z.rings):
            ring_end(k)

        count = batches * z.meshes
        table = emb[pl.ds(pl.multiple_of(me * own, own), own), :]
        grad = jnp.zeros((own, 4 * width), F32)
        for k in range(count):
            grad = grad + table[:, k : k + 1] * tot[k : k + 1, :]
        o_mod[0] = grad
        cols = 4 * width // shards
        mine = tot[:, pl.ds(pl.multiple_of(me * cols, cols), cols)]
        o_line[0:1, :] = jnp.sum(mine[0:count], axis=0, keepdims=True)
        o_line[1:2, :] = mine[count : count + 1]
        ratio = 128 // own
        line = tot[:, pl.ds(pl.multiple_of(me // ratio * 128, 128), 128)][count + 1 : count + 2]
        value = line
        for k in range(1, ratio):
            turned = jnp.concatenate([line[:, k * own :], line[:, : k * own]], axis=1)
            value = jnp.where(me % ratio == k, turned, value)
        o_line[2:3, :] = value

        pieces(piece_x, early, npiece)
        pieces(piece_z, 0, npiece)
        finish()

        @pl.loop(0, npiece)
        def _(p):
            core_copy(p).wait_send()
            x_copy(p).wait_send()
            for copy in z_copies(p):
                copy.wait_send()

        for k in range(z.rings):
            ring_copy(k).wait_send()

    def whole(*refs):
        kernel(*refs)

    return whole


def layout_of(z):
    own, groups = z.own, z.groups

    def kernel(
        lo, ig, piece, mod, line,
        o_lo, o_ig, o_qkv, o_out, o_up, o_upb, o_down, o_downb, o_mod, o_modb, sems,
    ):
        moves = [(lo, o_lo), (ig, o_ig), (mod, o_mod)]
        for q in range(groups):
            moves.append((piece.at[q], o_down.at[0, pl.ds(q * own, own), :]))
            moves.append((piece.at[groups + q], o_up.at[0, :, pl.ds(q * TILE, TILE)]))
        moves.append((piece.at[2 * groups], o_out.at[0]))
        for q in range(3):
            moves.append((piece.at[2 * groups + 1 + q], o_qkv.at[0, :, pl.ds(q * TILE, TILE)]))
        copies = [pltpu.make_async_copy(src, dst, sems.at[k]) for k, (src, dst) in enumerate(moves)]
        for copy in copies:
            copy.start()
        o_modb[...] = line[0:1, :]
        o_upb[...] = line[1:2, :]
        o_downb[...] = line[2:3, 0:own]
        for copy in copies:
            copy.wait()

    return kernel, 3 + 2 * groups + 4


def body(
    inputs,
    cotangent,
    neighbours,
    mesh_ids,
    noise_sigma,
    w_qkv,
    w_out,
    w_up,
    b_up,
    w_down,
    b_down,
    w_mod,
    b_mod,
):
    shards = lax.axis_size("nodes")
    z = Sizes(inputs, neighbours, noise_sigma, w_up, shards)
    batches, rows, width, hidden, many = z.batches, z.rows, z.width, z.hidden, z.together
    own, npiece = z.own, z.pieces
    shape = jax.ShapeDtypeStruct
    stack = shape((1, batches, rows, width), LOW)
    outs = [stack, stack]
    sides = [(z.lefts, TILE, batches * rows), (z.rights, batches * rows, TILE)]
    if z.scatter:
        outs += [shape((npiece, own, TILE), F32), shape((1, own, 4 * width), F32), shape((8, 128), F32)]
        scratch = [pltpu.VMEM(s, LOW) for s in sides]
    else:
        outs += [shape(s, LOW) for s in sides] + [shape((16, hidden), F32), shape((width, 128), F32)]
        scratch = []
    dma = pltpu.SemaphoreType.DMA
    scratch += [
        pltpu.VMEM((width, 3 * width), LOW),
        pltpu.VMEM((width, width), LOW),
        pltpu.VMEM((width, hidden), LOW),
        pltpu.VMEM((hidden, width), LOW),
        pltpu.VMEM((width, 4 * width), LOW),
        pltpu.VMEM((batches, z.ext, width), LOW),
        pltpu.VMEM((batches, rows, width), LOW),
        pltpu.VMEM((z.ext, 128), F32),
        pltpu.VMEM((rows, z.window), F32),
        pltpu.VMEM((rows, z.window), F32),
        pltpu.VMEM((batches, 8, 4 * width), F32),
        pltpu.VMEM((width, 128), F32),
        pltpu.VMEM((many * z.ext, width), LOW),
        pltpu.VMEM((batches, rows, width), LOW),
        pltpu.VMEM((batches, rows, width), F32),
        pltpu.VMEM((batches, rows, 128), F32),
        pltpu.VMEM((batches, rows, width), LOW),
        pltpu.VMEM((batches, z.window, 2 * width), LOW),
        pltpu.VMEM((HEADS, rows, z.window), F32),
        pltpu.VMEM((batches, HEADS, rows, z.window), F32),
        pltpu.VMEM((batches, HEADS, rows, z.window), LOW),
        pltpu.VMEM((batches, rows, width), LOW),
        pltpu.VMEM((batches, rows, width), LOW),
        pltpu.VMEM((batches, rows, width), F32),
        pltpu.VMEM((batches, rows, 128), F32),
        pltpu.VMEM((many * rows, width), F32),
        pltpu.VMEM((batches, rows, hidden), LOW),
        pltpu.VMEM((batches, rows, hidden), LOW),
        pltpu.VMEM((many * rows, width), LOW),
        pltpu.VMEM((HEADS, rows, z.window), LOW),
        pltpu.VMEM((batches, rows, width), F32),
        pltpu.VMEM((batches, rows, 2 * width), F32),
        pltpu.VMEM((batches, 2, REACH, 2 * width), LOW),
        pltpu.VMEM((batches, 2, REACH, 2 * width), LOW),
        pltpu.VMEM((batches, 8, hidden), F32),
        dma((7,)),
        dma((2,)),
        dma((2,)),
        dma((2,)),
        dma((2,)),
        dma((batches, 3)),
        dma((batches, 3)),
        dma((batches, 2)),
        dma((batches, 2)),
        dma((batches,)),
        dma((batches,)),
    ]
    if z.scatter:
        half, quarter, line = TILE // 2, TILE // 4, z.line
        scratch += [
            pltpu.VMEM((npiece, half, TILE), LOW),
            pltpu.VMEM((npiece, half, TILE), LOW),
            pltpu.VMEM((npiece, quarter, TILE), LOW),
            pltpu.VMEM((npiece, quarter, TILE), LOW),
            pltpu.VMEM((npiece, quarter, TILE), F32),
            pltpu.VMEM((npiece, line, own, TILE), LOW),
            pltpu.VMEM((npiece, line, own, TILE), LOW),
            pltpu.VMEM((half, TILE), F32),
            pltpu.VMEM((z.rings, 16, hidden), LOW),
            pltpu.VMEM((z.rings, 16, hidden), LOW),
            pltpu.VMEM((16, hidden), F32),
            dma((npiece,)),
            dma((npiece,)),
            dma((npiece,)),
            dma((npiece,)),
            dma((npiece, line)),
            dma((npiece, line)),
            dma((z.rings,)),
            dma((z.rings,)),
        ]
    hbm = pl.BlockSpec(memory_space=pl.ANY)
    vmem = pl.BlockSpec(memory_space=pltpu.VMEM)
    smem = pl.BlockSpec(memory_space=pltpu.SMEM)
    got = pl.pallas_call(
        kernel_of(z),
        out_shape=outs,
        in_specs=[hbm, hbm, vmem, vmem, smem, hbm, hbm, hbm, vmem, hbm, vmem, hbm, vmem],
        out_specs=[vmem] * len(outs),
        scratch_shapes=scratch,
        compiler_params=pltpu.CompilerParams(
            collective_id=0, has_side_effects=True, vmem_limit_bytes=62 * 2**20
        ),
    )(
        inputs,
        cotangent,
        neighbours.T,
        mesh_ids.reshape(1, rows),
        noise_sigma.T,
        w_qkv,
        w_out,
        w_up,
        b_up,
        w_down,
        b_down,
        w_mod,
        b_mod,
    )
    if z.scatter:
        kernel, moves = layout_of(z)
        return tuple(
            pl.pallas_call(
                kernel,
                out_shape=[
                    stack,
                    stack,
                    shape((1, own, 3 * width), F32),
                    shape((1, own, width), F32),
                    shape((1, own, hidden), F32),
                    shape((1, hidden // shards), F32),
                    shape((1, hidden // shards, width), F32),
                    shape((1, own), F32),
                    shape((1, own, 4 * width), F32),
                    shape((1, 4 * width // shards), F32),
                ],
                in_specs=[hbm, hbm, hbm, hbm, vmem],
                out_specs=[hbm, hbm, hbm, hbm, hbm, vmem, hbm, vmem, hbm, vmem],
                scratch_shapes=[dma((moves,))],
                compiler_params=pltpu.CompilerParams(vmem_limit_bytes=62 * 2**20),
            )(*got)
        )
    lo, ig, left_t, right_t, small, table = got
    groups = z.groups

    def summed(value):
        return lax.psum_scatter(value, "nodes", scatter_dimension=0, tiled=True)

    def wide_sum(left, first, last):
        return summed(jnp.concatenate([dot(left_t[left], right_t[r]) for r in range(first, last)], axis=1))[None]

    down = [dot(left_t[q], right_t[0]).reshape(TILE // 32, 32, TILE) for q in range(groups)]
    down = jnp.stack(down, axis=1)
    count = batches * z.meshes
    small = lax.psum(small, "nodes")
    me = lax.axis_index("nodes")
    mod = jnp.dot(table[:, :count], small[:count], precision=lax.Precision.HIGHEST)

    def mine(value):
        size = value.shape[0] // shards
        return lax.dynamic_slice_in_dim(value, me * size, size, axis=0)[None]

    return (
        lo,
        ig,
        wide_sum(groups + 2, 2 + groups, 5 + groups),
        wide_sum(groups + 1, 1 + groups, 2 + groups),
        wide_sum(groups, 1, 1 + groups),
        mine(small[count]),
        summed(down.reshape(hidden, width))[None],
        mine(small[count + 1, :width]),
        mine(mod),
        mine(jnp.sum(small[:count], axis=0)),
    )


def solution(mesh):
    return jax.shard_map(
        body,
        mesh=mesh,
        in_specs=(
            P(None, "nodes", None),
            P(None, "nodes", None),
            P("nodes", None),
            P("nodes"),
            P(),
            P("section", None, None),
            P("section", None, None),
            P("section", None, None),
            P("section", None),
            P("section", None, None),
            P("section", None),
            P("section", None, None),
            P("section", None),
        ),
        out_specs=(
            P("section", None, "nodes", None),
            P("section", None, "nodes", None),
            P("section", "nodes", None),
            P("section", "nodes", None),
            P("section", "nodes", None),
            P("section", "nodes"),
            P("section", "nodes", None),
            P("section", "nodes"),
            P("section", "nodes", None),
            P("section", "nodes"),
        ),
        check_vma=False,
    )
```

```python
import jax
import jax.numpy as jnp
from jax import lax
from jax.experimental import pallas as pl
from jax.experimental.pallas import tpu as pltpu
from jax.sharding import PartitionSpec as P

HEADS = 4
REACH = 32
EPSILON = 1e-06
MASKED = -1e9
ABSENT = -2e38
TILE = 512
TOGETHER = 2
MESH = pl.DeviceIdType.MESH
F32, LOW = jnp.float32, jnp.bfloat16


def dot(a, b):
    return lax.dot_general(a, b, (((1,), (0,)), ((), ())), preferred_element_type=F32)


def dot_nt(a, b):
    return lax.dot_general(a, b, (((1,), (1,)), ((), ())), preferred_element_type=F32)


def dot_tn(a, b):
    return lax.dot_general(a, b, (((0,), (0,)), ((), ())), preferred_element_type=F32)


class Sizes:
    def __init__(self, inputs, neighbours, noise, w_up, shards):
        self.batches, self.rows, self.width = inputs.shape
        self.together = TOGETHER if self.batches % TOGETHER == 0 else 1
        self.turns = self.batches // self.together
        self.slots = neighbours.shape[1]
        self.meshes = noise.shape[1]
        self.hidden = w_up.shape[2]
        self.shards = shards
        self.ext = self.rows + 2 * REACH
        self.window = (self.ext // 128 + 1) * 128
        self.groups = self.hidden // TILE
        self.own = self.width // shards
        self.scatter = self.own % 16 == 0
        self.pieces = 2 * self.groups + 4
        self.lefts = 3 + self.groups
        self.rights = 2 + self.groups + 3
        self.rings = max(shards.bit_length() - 1, 1)
        self.line = max(shards // 4, 1)

    def left(self, p):
        n = self.groups
        return jnp.minimum(p, n) + lax.div(p, 2 * n) + lax.div(p, 2 * n + 1)

    def right(self, p):
        return jnp.maximum(p - (self.groups - 1), 0)


def kernel_of(z):
    batches, rows, width, ext, window = z.batches, z.rows, z.width, z.ext, z.window
    groups, shards, own, many = z.groups, z.shards, z.own, z.together
    head = width // HEADS
    score_scale = head ** (-0.5)
    npiece = z.pieces
    half, quarter = TILE // 2, TILE // 4
    g_out, g_q, g_k = 1 + groups, 2 + groups, 3 + groups

    def position(owner):
        if not z.scatter:
            return owner
        return (owner % 2) * (shards // 2) + (owner // 2 % 2) * z.line + owner // 4

    def kernel(
        inputs, cotangent, neighbours, mesh_ids, sigma,
        w_qkv, w_out, w_up, b_up, w_down, b_down, w_mod, b_mod,
        lo, ig, *rest,
    ):
        left_t, right_t, small_out, table_out = rest[:4]
        rest = rest[4:]
        (
            wq, wo, wu, wd, wm, xext, dybuf, sel, cnt, bias, mod, emb,
            n1, n1s, ua, ia, qb, kvext, sbuf, af, ca, obs, n2s, ub, ib, tb, fp, hs,
            ob, cds, dx1, dkv, hsend, hrecv, sm,
            lsem, hx_s, hx_r, hm_s, hm_r, fx_s, fx_r, bh_s, bh_r, bx_s, bx_r,
        ) = rest

        sec = lax.axis_index("section")
        me = lax.axis_index("nodes")
        up = lax.rem(me + 1, shards)
        down = lax.rem(me + shards - 1, shards)
        other = 1 - sec
        def local(src, dst, k):
            return pltpu.make_async_copy(src, dst, lsem.at[k])

        loads = [
            local(w_mod.at[0], wm, 0),
            local(w_qkv.at[0], wq, 1),
            local(w_out.at[0], wo, 2),
            local(w_up.at[0], wu, 3),
            local(w_down.at[0], wd, 4),
        ]
        own_rows = pl.ds(REACH, rows)
        first_load = local(inputs, xext.at[:, own_rows, :], 5)
        last_load = local(cotangent, dybuf, 6)
        loads[0].start()

        @pl.when(sec == 0)
        def _():
            first_load.start()

        for copy in loads[1:]:
            copy.start()

        @pl.when(sec == 1)
        def _():
            last_load.start()

        barrier = pltpu.get_barrier_semaphore()
        mates = [(sec, up), (sec, down), (other, me), (other, up), (other, down)]
        for mate in mates:
            pl.semaphore_signal(barrier, inc=1, device_id=mate, device_id_type=MESH)
        pl.semaphore_wait(barrier, len(mates))

        def remote(src, dst, s_sem, r_sem, mate):
            return pltpu.make_async_remote_copy(
                src_ref=src, dst_ref=dst, send_sem=s_sem, recv_sem=r_sem, device_id=mate, device_id_type=MESH
            )

        low_rows, top_rows = pl.ds(0, REACH), pl.ds(REACH + rows, REACH)
        head_rows, tail_rows = pl.ds(REACH, REACH), pl.ds(rows, REACH)
        x_down = remote(inputs.at[:, pl.ds(0, REACH), :], xext.at[:, top_rows, :], hx_s.at[0], hx_r.at[0], (sec, down))
        x_up = remote(inputs.at[:, pl.ds(rows - REACH, REACH), :], xext.at[:, low_rows, :], hx_s.at[1], hx_r.at[1], (sec, up))

        @pl.when(sec == 0)
        def _():
            x_down.start()
            x_up.start()

        ids = jnp.broadcast_to(mesh_ids[...].astype(F32), (128, rows))
        sel[own_rows, :] = ids.T
        m_down = remote(sel.at[head_rows, :], sel.at[top_rows, :], hm_s.at[0], hm_r.at[0], (sec, down))
        m_up = remote(sel.at[tail_rows, :], sel.at[low_rows, :], hm_s.at[1], hm_r.at[1], (sec, up))
        m_down.start()
        m_up.start()

        row_no = lax.broadcasted_iota(jnp.int32, (16, width // 2), 0)
        level = jnp.ones((16, width // 2), F32)
        for b in range(batches):
            for m in range(z.meshes):
                level = jnp.where(row_no == b * z.meshes + m, sigma[m, b], level)
        place = lax.broadcasted_iota(jnp.int32, (16, width // 2), 1).astype(F32)
        frequency = 3.0 * jnp.exp(-jnp.log(100.0) * place / (width // 2))
        angles = jnp.log(level) * frequency
        embedded = jnp.concatenate([jnp.sin(angles), jnp.cos(angles)], axis=1).astype(LOW)
        padded = jnp.concatenate([embedded.astype(F32), jnp.zeros((112, width), F32)], axis=0)
        emb[...] = padded.T
        loads[0].wait()
        for g in range(4):
            cols = pl.ds(g * width, width)
            table = dot(embedded, wm[:, cols]) + b_mod[:, cols]
            for b in range(batches):
                mod[b, 0 : z.meshes, cols] = table[b * z.meshes : (b + 1) * z.meshes]

        slots = neighbours[...].astype(F32)
        slots = jnp.concatenate([slots, jnp.zeros((128 - z.slots, rows), F32)], axis=0).T
        slots = jnp.where(slots >= 0, slots - (me * rows - REACH).astype(F32), float(ext))
        column = lax.broadcasted_iota(jnp.int32, (rows, window), 1).astype(F32)
        counts = jnp.zeros((rows, window), F32)
        for n in range(z.slots):
            counts = counts + jnp.where(slots[:, n : n + 1] == column, 1.0, 0.0)
        cnt[...] = counts
        bias[...] = jnp.where(counts > 0, jnp.where(column == ext, MASKED, 0.0), ABSENT)

        def mod_rows(b, part, ids_rows):
            cols = pl.ds(part * width, width)
            value = jnp.broadcast_to(mod[b, 0:1, cols], (ids_rows.shape[0], width))
            for m in range(1, z.meshes):
                value = jnp.where(ids_rows > m - 0.5, mod[b, m : m + 1, cols], value)
            return value

        def wide(ids_rows):
            return jnp.concatenate([ids_rows] * (width // 128), axis=1)

        def unit(x):
            centred = x - jnp.mean(x, axis=-1, keepdims=True)
            inv = lax.rsqrt(jnp.mean(centred * centred, axis=-1, keepdims=True) + EPSILON)
            return centred * inv, inv

        def batch_cols(b):
            return pl.ds(pl.multiple_of(b * rows, rows), rows)

        def turn_cols(t):
            return pl.ds(pl.multiple_of(t * many * rows, many * rows), many * rows)

        def turn_of(ref, t):
            return ref[pl.ds(t * many, many)].reshape(many * rows, ref.shape[2])

        span = own if z.scatter else 32

        def transposes(b, carry):
            for first, ref in ((groups, n2s), (groups + 1, obs), (groups + 2, n1s)):
                turned = ref[b].T
                for owner in range(TILE // span):
                    at = position(owner) * span
                    left_t[first, at : at + span, batch_cols(b)] = turned[owner * span : (owner + 1) * span]
            run = groups * span
            for g in range(groups):
                turned = hs[b, :, g * TILE : (g + 1) * TILE].T
                for k in range(TILE // span):
                    at = g * TILE + k * span
                    owner, part = at // run, at % run // span
                    to = position(owner) * span
                    left_t[part, to : to + span, batch_cols(b)] = turned[k * span : (k + 1) * span]
            return carry

        def forward(t):
            for i in range(many):
                b = t * many + i
                ids_rows = wide(sel[0:ext, :])
                u, inv = unit(xext[b].astype(F32))
                normed = (u * (1.0 + mod_rows(b, 0, ids_rows)) + mod_rows(b, 1, ids_rows)).astype(LOW)
                n1[i * ext : (i + 1) * ext, :] = normed
                n1s[b] = normed[REACH : REACH + rows]
                ua[b] = u[REACH : REACH + rows]
                ia[b] = jnp.broadcast_to(inv[REACH : REACH + rows], (rows, 128))
            part = dot(turn_of(n1s, t), wq[:, 0:width]).astype(LOW)
            qb[pl.ds(t * many, many)] = part.reshape(many, rows, width)
            for g in range(2):
                part = dot(n1[...], wq[:, (g + 1) * width : (g + 2) * width]).astype(LOW)
                for i in range(many):
                    kvext[t * many + i, 0:ext, g * width : (g + 1) * width] = part[i * ext : (i + 1) * ext]
            for i in range(many):
                b = t * many + i
                for h in range(HEADS):
                    hd = slice(h * head, (h + 1) * head)
                    sbuf[h] = dot_nt(qb[b, :, hd], kvext[b, :, hd]) * score_scale + bias[...]
                for h in range(HEADS):
                    s = sbuf[h]
                    e = jnp.exp(s - jnp.max(s, axis=-1, keepdims=True))
                    a = e * (1.0 / jnp.sum(e * cnt[...], axis=-1, keepdims=True))
                    af[b, h] = a
                    ca[b, h] = (a.astype(LOW).astype(F32) * cnt[...]).astype(LOW)
                for h in range(HEADS):
                    hd = slice(h * head, (h + 1) * head)
                    vd = slice(width + h * head, width + (h + 1) * head)
                    obs[b, :, hd] = dot(ca[b, h], kvext[b, :, vd]).astype(LOW)
            branch = dot(turn_of(obs, t), wo[...])
            for i in range(many):
                b = t * many + i
                x1 = xext[b, own_rows, :].astype(F32) + branch[i * rows : (i + 1) * rows]
                u, inv = unit(x1)
                ub[b] = u
                ib[b] = jnp.broadcast_to(inv, (rows, 128))
                ids_rows = wide(sel[own_rows, :])
                n2s[b] = (u * (1.0 + mod_rows(b, 2, ids_rows)) + mod_rows(b, 3, ids_rows)).astype(LOW)
                tb[i * rows : (i + 1) * rows, :] = x1 + b_down[...]
            for g in range(groups):
                gs = slice(g * TILE, (g + 1) * TILE)
                gate = dot(turn_of(n2s, t), wu[:, gs]) + b_up[:, gs]
                s = 0.5 + 0.5 * jnp.tanh(0.5 * gate)
                hid = (gate * s).astype(LOW)
                slope = (s + gate * s * (1.0 - s)).astype(LOW)
                for i in range(many):
                    fp[t * many + i, :, gs] = slope[i * rows : (i + 1) * rows]
                    hs[t * many + i, :, gs] = hid[i * rows : (i + 1) * rows]
                tb[...] += dot(hid, wd[gs, :])
            for i in range(many):
                lo[0, t * many + i] = tb[i * rows : (i + 1) * rows, :].astype(LOW)

        def relay(b):
            return [
                remote(lo.at[0, b], xext.at[b, own_rows, :], fx_s.at[b, 0], fx_r.at[b, 0], (other, me)),
                remote(lo.at[0, b, pl.ds(0, REACH), :], xext.at[b, top_rows, :], fx_s.at[b, 1], fx_r.at[b, 1], (other, down)),
                remote(lo.at[0, b, pl.ds(rows - REACH, REACH), :], xext.at[b, low_rows, :], fx_s.at[b, 2], fx_r.at[b, 2], (other, up)),
            ]

        def norm_back(d, u, inv, scale):
            scaled = d * (1.0 + scale)
            return inv * (
                scaled
                - jnp.mean(scaled, axis=-1, keepdims=True)
                - u * jnp.mean(scaled * u, axis=-1, keepdims=True)
            )

        def mod_sums(b, part, d, u, ids_rows):
            for m in range(z.meshes):
                chosen = jnp.where(jnp.abs(ids_rows - m) < 0.5, d, 0.0)
                sm[b, m : m + 1, part * width : (part + 1) * width] = jnp.sum(chosen * u, axis=0, keepdims=True)
                sm[b, m : m + 1, (part + 1) * width : (part + 2) * width] = jnp.sum(chosen, axis=0, keepdims=True)

        def halos(b):
            return [
                remote(hsend.at[b, 0], hrecv.at[b, 1], bh_s.at[b, 0], bh_r.at[b, 0], (sec, down)),
                remote(hsend.at[b, 1], hrecv.at[b, 0], bh_s.at[b, 1], bh_r.at[b, 1], (sec, up)),
            ]

        def given(t):
            at = turn_cols(t)
            dr = turn_of(dybuf, t)
            right_t[0, at, :] = dr
            for i in range(many):
                total = jnp.sum(dr[i * rows : (i + 1) * rows].astype(F32), axis=0, keepdims=True)
                sm[t * many + i, 7:8, 0:width] = total
            for g in range(groups):
                right_t[1 + g, at, :] = dot_nt(dr, wd[g * TILE : (g + 1) * TILE, :]).astype(LOW)

        def back_ffn(t):
            at = turn_cols(t)
            dn = jnp.zeros((many * rows, width), F32)
            for g in range(groups):
                gs = slice(g * TILE, (g + 1) * TILE)
                dg = right_t[1 + g, at, :].astype(F32) * turn_of(fp, t)[:, gs].astype(F32)
                sm[t * many, 6:7, gs] = jnp.sum(dg, axis=0, keepdims=True)
                dg = dg.astype(LOW)
                right_t[1 + g, at, :] = dg
                dn = dn + dot_nt(dg, wu[:, gs])
            ids_rows = wide(sel[own_rows, :])
            for i in range(many):
                b = t * many + i
                d = dn[i * rows : (i + 1) * rows]
                u = ub[b]
                grad = dybuf[b].astype(F32) + norm_back(d, u, ib[b][:, 0:1], mod_rows(b, 2, ids_rows))
                mod_sums(b, 2, d, u, ids_rows)
                dx1[b] = grad
                right_t[g_out, batch_cols(b), :] = grad.astype(LOW)
            ob[...] = dot_nt(right_t[g_out, at, :], wo[...]).astype(LOW)

        def back_attention(t):
            for i in range(many):
                b = t * many + i
                at = batch_cols(b)
                here = slice(i * rows, (i + 1) * rows)
                for h in range(HEADS):
                    hd = slice(h * head, (h + 1) * head)
                    vd = slice(width + h * head, width + (h + 1) * head)
                    sbuf[h] = dot_nt(ob[here, hd], kvext[b, :, vd])
                for h in range(HEADS):
                    a, da = af[b, h], sbuf[h]
                    ds = a * (da - jnp.sum(a * cnt[...] * da, axis=-1, keepdims=True))
                    cds[h] = (ds.astype(LOW).astype(F32) * cnt[...]).astype(LOW)
                for h in range(HEADS):
                    hd = slice(h * head, (h + 1) * head)
                    vd = slice(width + h * head, width + (h + 1) * head)
                    dk = dot_tn(cds[h], qb[b, :, hd]) * score_scale
                    dv = dot_tn(ca[b, h], ob[here, hd])
                    for part, cols in ((dk, hd), (dv, vd)):
                        hsend[b, 0, :, cols] = part[0:REACH].astype(LOW)
                        dkv[b, :, cols] = part[REACH : REACH + rows]
                        hsend[b, 1, :, cols] = part[REACH + rows : ext].astype(LOW)
                for copy in halos(b):
                    copy.start()
                for h in range(HEADS):
                    hd = slice(h * head, (h + 1) * head)
                    right_t[g_q, at, hd] = (dot(cds[h], kvext[b, :, hd]) * score_scale).astype(LOW)

        def back_second(t):
            at = turn_cols(t)
            ids_rows = wide(sel[own_rows, :])
            edge = rows - REACH
            dn = dot_nt(right_t[g_q, at, :], wq[:, 0:width])
            for i in range(many):
                b = t * many + i
                for copy in halos(b):
                    copy.wait_recv()
                dkv[b, 0:REACH, :] += hrecv[b, 0].astype(F32)
                dkv[b, edge:rows, :] += hrecv[b, 1].astype(F32)
                for g in range(2):
                    right_t[g_k + g, batch_cols(b), :] = dkv[b, :, g * width : (g + 1) * width].astype(LOW)
            for g in range(2):
                dn = dn + dot_nt(right_t[g_k + g, at, :], wq[:, (g + 1) * width : (g + 2) * width])
            for i in range(many):
                b = t * many + i
                d = dn[i * rows : (i + 1) * rows]
                u = ua[b]
                grad = dx1[b] + norm_back(d, u, ia[b][:, 0:1], mod_rows(b, 0, ids_rows))
                ig[0, b] = grad.astype(LOW)

                @pl.when(sec == 1)
                def _():
                    relay_back(b).start()

                mod_sums(b, 0, d, u, ids_rows)

        def relay_back(b):
            return remote(ig.at[0, b], dybuf.at[b], bx_s.at[b], bx_r.at[b], (other, me))

        kvext[:, ext:window, :] = jnp.zeros((batches, window - ext, 2 * width), LOW)
        sm[...] = jnp.zeros(sm.shape, F32)
        for copy in loads[1:]:
            copy.wait()
        for copy in (m_down, m_up):
            copy.wait()

        @pl.when(sec == 0)
        def _():
            first_load.wait()
            x_down.wait()
            x_up.wait()

        @pl.when(sec == 1)
        def _():
            last_load.wait()

            @pl.loop(0, z.turns)
            def _(t):
                given(t)

        @pl.loop(0, z.turns)
        def _(t):
            @pl.when(sec == 1)
            def _():
                for i in range(many):
                    for copy in relay(t * many + i):
                        copy.wait_recv()

            forward(t)

            @pl.when(sec == 0)
            def _():
                for i in range(many):
                    for copy in relay(t * many + i):
                        copy.start()

        @pl.when(sec == 0)
        def _():
            lax.fori_loop(0, batches, transposes, 0)

        @pl.loop(0, z.turns)
        def _(k):
            t = z.turns - 1 - k

            @pl.when(sec == 0)
            def _():
                for i in range(many):
                    relay_back(t * many + i).wait_recv()
                given(t)

            back_ffn(t)
            back_attention(t)
            back_second(t)

        @pl.when(sec == 1)
        def _():
            lax.fori_loop(0, batches, transposes, 0)

        lines = [sm[b, m : m + 1, :] for b in range(batches) for m in range(z.meshes)]
        for line in (6, 7):
            lines.append(sum(sm[b, line : line + 1, :] for b in range(batches)))
        lines.append(jnp.zeros((16 - len(lines), sm.shape[2]), F32))
        small = jnp.concatenate(lines, axis=0)

        def finish():
            @pl.loop(0, batches)
            def _(b):
                @pl.when(sec == 0)
                def _():
                    for copy in relay(b):
                        copy.wait_send()

                @pl.when(sec == 1)
                def _():
                    relay_back(b).wait_send()

                for copy in halos(b):
                    copy.wait_send()

        small_out[...] = small
        table_out[...] = emb[...]
        finish()

    return kernel


def scatter_of(z):
    shards, own, groups, npiece, batches, width = z.shards, z.own, z.groups, z.pieces, z.batches, z.width
    half, quarter = TILE // 2, TILE // 4

    def kernel(
        left_t, right_t, small, emb, o_piece, o_mod, o_line,
        cs, cr, xs, xr, xk, zs, zr, acc, msend, mrecv, tot,
        c_s, c_r, x_s, x_r, z_s, z_r, m_s, m_r,
    ):
        sec = lax.axis_index("section")
        me = lax.axis_index("nodes")
        core, xpos, zpos = me % 2, me // 2 % 2, me // 4
        core_mate = me + 1 - 2 * core
        x_mate = me + 2 - 4 * xpos

        def z_mate(k):
            return lax.rem(zpos + k, z.line) * 4 + xpos * 2 + core

        barrier = pltpu.get_barrier_semaphore()
        mates = [(sec, core_mate), (sec, x_mate)] + [(sec, z_mate(k)) for k in range(1, z.line)]
        for mate in mates:
            pl.semaphore_signal(barrier, inc=1, device_id=mate, device_id_type=MESH)
        pl.semaphore_wait(barrier, len(mates))

        def remote(src, dst, s_sem, r_sem, mate):
            return pltpu.make_async_remote_copy(
                src_ref=src, dst_ref=dst, send_sem=s_sem, recv_sem=r_sem, device_id=mate, device_id_type=MESH
            )

        def core_copy(p):
            return remote(cs.at[p], cr.at[p], c_s.at[p], c_r.at[p], (sec, core_mate))

        def x_copy(p):
            return remote(xs.at[p], xr.at[p], x_s.at[p], x_r.at[p], (sec, x_mate))

        def z_copies(p):
            return [
                remote(zs.at[p, lax.rem(zpos + k, z.line)], zr.at[p, k - 1], z_s.at[p, k - 1], z_r.at[p, k - 1], (sec, z_mate(k)))
                for k in range(1, z.line)
            ]

        def half_rows(c):
            return pl.ds(pl.multiple_of(c * half, half), half)

        def quarter_rows(c):
            return pl.ds(pl.multiple_of(c * quarter, quarter), quarter)

        def piece_start(p):
            cs[p] = dot(left_t[z.left(p), half_rows(1 - core), :], right_t[z.right(p)]).astype(LOW)
            core_copy(p).start()

        def piece_core(p):
            mine = dot(left_t[z.left(p), half_rows(core), :], right_t[z.right(p)])
            core_copy(p).wait_recv()
            acc[...] = mine + cr[p].astype(F32)
            xs[p] = acc[quarter_rows(1 - xpos), :].astype(LOW)
            x_copy(p).start()
            xk[p] = acc[quarter_rows(xpos), :]

        def piece_x(p):
            x_copy(p).wait_recv()
            value = xk[p] + xr[p].astype(F32)
            for k in range(z.line):
                zs[p, k] = value[k * own : (k + 1) * own].astype(LOW)
            for copy in z_copies(p):
                copy.start()
            xk[p] = value

        def piece_z(p):
            value = xk[p, pl.ds(pl.multiple_of(zpos * own, own), own), :]
            for k, copy in enumerate(z_copies(p)):
                copy.wait_recv()
                value = value + zr[p, k].astype(F32)
            o_piece[p] = value

        def ring_copy(k):
            bit = 1 << k
            mate = me + bit - 2 * bit * (me // bit % 2)
            return remote(msend.at[k], mrecv.at[k], m_s.at[k], m_r.at[k], (sec, mate))

        def ring_start(k, value):
            msend[k] = value.astype(LOW)
            ring_copy(k).start()

        def ring_end(k):
            ring_copy(k).wait_recv()
            value = msend[k].astype(F32) + mrecv[k].astype(F32)
            if k + 1 < z.rings:
                ring_start(k + 1, value)
            else:
                tot[...] = value

        ring_start(0, small[...])

        @pl.loop(0, npiece + 6)
        def _(p):
            for step, lag in ((piece_start, 0), (piece_core, 1), (piece_x, 3), (piece_z, 6)):

                @pl.when((p >= lag) & (p < npiece + lag))
                def _(step=step, lag=lag):
                    step(p - lag)

            for k in range(z.rings):

                @pl.when(p == 2 + 2 * k)
                def _(k=k):
                    ring_end(k)

        count = batches * z.meshes
        table = emb[pl.ds(pl.multiple_of(me * own, own), own), :]
        grad = jnp.zeros((own, 4 * width), F32)
        for k in range(count):
            grad = grad + table[:, k : k + 1] * tot[k : k + 1, :]
        o_mod[0] = grad
        cols = 4 * width // shards
        mine = tot[:, pl.ds(pl.multiple_of(me * cols, cols), cols)]
        o_line[0:1, :] = jnp.sum(mine[0:count], axis=0, keepdims=True)
        o_line[1:2, :] = mine[count : count + 1]
        ratio = 128 // own
        line = tot[:, pl.ds(pl.multiple_of(me // ratio * 128, 128), 128)][count + 1 : count + 2]
        value = line
        for k in range(1, ratio):
            turned = jnp.concatenate([line[:, k * own :], line[:, : k * own]], axis=1)
            value = jnp.where(me % ratio == k, turned, value)
        o_line[2:3, :] = value

        @pl.loop(0, npiece)
        def _(p):
            core_copy(p).wait_send()
            x_copy(p).wait_send()
            for copy in z_copies(p):
                copy.wait_send()

        for k in range(z.rings):
            ring_copy(k).wait_send()

    return kernel


def layout_of(z):
    own, groups = z.own, z.groups

    def kernel(
        lo, ig, piece, mod, line,
        o_lo, o_ig, o_qkv, o_out, o_up, o_upb, o_down, o_downb, o_mod, o_modb,
        v_lo, v_ig, v_piece, v_mod, into, back,
    ):
        moves = [(lo, v_lo, o_lo), (ig, v_ig, o_ig)]
        targets = [o_down.at[0, pl.ds(q * own, own), :] for q in range(groups)]
        targets += [o_up.at[0, :, pl.ds(q * TILE, TILE)] for q in range(groups)]
        targets += [o_out.at[0]] + [o_qkv.at[0, :, pl.ds(q * TILE, TILE)] for q in range(3)]
        moves += [(piece.at[k], v_piece.at[k], target) for k, target in enumerate(targets)]
        moves += [(mod, v_mod, o_mod)]
        firsts = [pltpu.make_async_copy(a, b, into.at[k]) for k, (a, b, _) in enumerate(moves)]
        lasts = [pltpu.make_async_copy(b, c, back.at[k]) for k, (_, b, c) in enumerate(moves)]
        for copy in firsts:
            copy.start()
        o_modb[...] = line[0:1, :]
        o_upb[...] = line[1:2, :]
        o_downb[...] = line[2:3, 0:own]
        for first, last in zip(firsts, lasts):
            first.wait()
            last.start()
        for copy in lasts:
            copy.wait()

    return kernel


def body(
    inputs,
    cotangent,
    neighbours,
    mesh_ids,
    noise_sigma,
    w_qkv,
    w_out,
    w_up,
    b_up,
    w_down,
    b_down,
    w_mod,
    b_mod,
):
    shards = lax.axis_size("nodes")
    z = Sizes(inputs, neighbours, noise_sigma, w_up, shards)
    batches, rows, width, hidden, many = z.batches, z.rows, z.width, z.hidden, z.together
    own, npiece = z.own, z.pieces
    shape = jax.ShapeDtypeStruct
    stack = shape((1, batches, rows, width), LOW)
    outs = [stack, stack]
    outs += [shape((z.lefts, TILE, batches * rows), LOW), shape((z.rights, batches * rows, TILE), LOW)]
    outs += [shape((16, hidden), F32), shape((width, 128), F32)]
    dma = pltpu.SemaphoreType.DMA
    scratch = [
        pltpu.VMEM((width, 3 * width), LOW),
        pltpu.VMEM((width, width), LOW),
        pltpu.VMEM((width, hidden), LOW),
        pltpu.VMEM((hidden, width), LOW),
        pltpu.VMEM((width, 4 * width), LOW),
        pltpu.VMEM((batches, z.ext, width), LOW),
        pltpu.VMEM((batches, rows, width), LOW),
        pltpu.VMEM((z.ext, 128), F32),
        pltpu.VMEM((rows, z.window), F32),
        pltpu.VMEM((rows, z.window), F32),
        pltpu.VMEM((batches, 8, 4 * width), F32),
        pltpu.VMEM((width, 128), F32),
        pltpu.VMEM((many * z.ext, width), LOW),
        pltpu.VMEM((batches, rows, width), LOW),
        pltpu.VMEM((batches, rows, width), F32),
        pltpu.VMEM((batches, rows, 128), F32),
        pltpu.VMEM((batches, rows, width), LOW),
        pltpu.VMEM((batches, z.window, 2 * width), LOW),
        pltpu.VMEM((HEADS, rows, z.window), F32),
        pltpu.VMEM((batches, HEADS, rows, z.window), F32),
        pltpu.VMEM((batches, HEADS, rows, z.window), LOW),
        pltpu.VMEM((batches, rows, width), LOW),
        pltpu.VMEM((batches, rows, width), LOW),
        pltpu.VMEM((batches, rows, width), F32),
        pltpu.VMEM((batches, rows, 128), F32),
        pltpu.VMEM((many * rows, width), F32),
        pltpu.VMEM((batches, rows, hidden), LOW),
        pltpu.VMEM((batches, rows, hidden), LOW),
        pltpu.VMEM((many * rows, width), LOW),
        pltpu.VMEM((HEADS, rows, z.window), LOW),
        pltpu.VMEM((batches, rows, width), F32),
        pltpu.VMEM((batches, rows, 2 * width), F32),
        pltpu.VMEM((batches, 2, REACH, 2 * width), LOW),
        pltpu.VMEM((batches, 2, REACH, 2 * width), LOW),
        pltpu.VMEM((batches, 8, hidden), F32),
        dma((7,)),
        dma((2,)),
        dma((2,)),
        dma((2,)),
        dma((2,)),
        dma((batches, 3)),
        dma((batches, 3)),
        dma((batches, 2)),
        dma((batches, 2)),
        dma((batches,)),
        dma((batches,)),
    ]
    hbm = pl.BlockSpec(memory_space=pl.ANY)
    vmem = pl.BlockSpec(memory_space=pltpu.VMEM)
    smem = pl.BlockSpec(memory_space=pltpu.SMEM)
    got = pl.pallas_call(
        kernel_of(z),
        out_shape=outs,
        in_specs=[hbm, hbm, vmem, vmem, smem, hbm, hbm, hbm, vmem, hbm, vmem, hbm, vmem],
        out_specs=[vmem] * len(outs),
        scratch_shapes=scratch,
        compiler_params=pltpu.CompilerParams(
            collective_id=0, has_side_effects=True, vmem_limit_bytes=62 * 2**20
        ),
    )(
        inputs,
        cotangent,
        neighbours.T,
        mesh_ids.reshape(1, rows),
        noise_sigma.T,
        w_qkv,
        w_out,
        w_up,
        b_up,
        w_down,
        b_down,
        w_mod,
        b_mod,
    )
    lo, ig, left_t, right_t, small, table = got
    if z.scatter:
        half, quarter, line = TILE // 2, TILE // 4, z.line
        sums = [
            pltpu.VMEM((npiece, half, TILE), LOW),
            pltpu.VMEM((npiece, half, TILE), LOW),
            pltpu.VMEM((npiece, quarter, TILE), LOW),
            pltpu.VMEM((npiece, quarter, TILE), LOW),
            pltpu.VMEM((npiece, quarter, TILE), F32),
            pltpu.VMEM((npiece, line, own, TILE), LOW),
            pltpu.VMEM((npiece, line, own, TILE), LOW),
            pltpu.VMEM((half, TILE), F32),
            pltpu.VMEM((z.rings, 16, hidden), LOW),
            pltpu.VMEM((z.rings, 16, hidden), LOW),
            pltpu.VMEM((16, hidden), F32),
            dma((npiece,)),
            dma((npiece,)),
            dma((npiece,)),
            dma((npiece,)),
            dma((npiece, line)),
            dma((npiece, line)),
            dma((z.rings,)),
            dma((z.rings,)),
        ]
        piece, mod, line = pl.pallas_call(
            scatter_of(z),
            out_shape=[shape((npiece, own, TILE), F32), shape((1, own, 4 * width), F32), shape((8, 128), F32)],
            in_specs=[vmem] * 4,
            out_specs=[vmem] * 3,
            scratch_shapes=sums,
            compiler_params=pltpu.CompilerParams(
                collective_id=1, has_side_effects=True, vmem_limit_bytes=62 * 2**20
            ),
        )(left_t, right_t, small, table)
        return tuple(
            pl.pallas_call(
                layout_of(z),
                out_shape=[
                    stack,
                    stack,
                    shape((1, own, 3 * width), F32),
                    shape((1, own, width), F32),
                    shape((1, own, hidden), F32),
                    shape((1, hidden // shards), F32),
                    shape((1, hidden // shards, width), F32),
                    shape((1, own), F32),
                    shape((1, own, 4 * width), F32),
                    shape((1, 4 * width // shards), F32),
                ],
                in_specs=[hbm, hbm, hbm, hbm, vmem],
                out_specs=[hbm, hbm, hbm, hbm, hbm, vmem, hbm, vmem, hbm, vmem],
                scratch_shapes=[
                    pltpu.VMEM(stack.shape, LOW),
                    pltpu.VMEM(stack.shape, LOW),
                    pltpu.VMEM((npiece, own, TILE), F32),
                    pltpu.VMEM((1, own, 4 * width), F32),
                    dma((npiece + 3,)),
                    dma((npiece + 3,)),
                ],
                compiler_params=pltpu.CompilerParams(vmem_limit_bytes=62 * 2**20),
            )(lo, ig, piece, mod, line)
        )
    groups = z.groups

    def summed(value):
        return lax.psum_scatter(value, "nodes", scatter_dimension=0, tiled=True)

    def wide_sum(left, first, last):
        return summed(jnp.concatenate([dot(left_t[left], right_t[r]) for r in range(first, last)], axis=1))[None]

    down = [dot(left_t[q], right_t[0]).reshape(TILE // 32, 32, TILE) for q in range(groups)]
    down = jnp.stack(down, axis=1)
    count = batches * z.meshes
    small = lax.psum(small, "nodes")
    me = lax.axis_index("nodes")
    mod = jnp.dot(table[:, :count], small[:count], precision=lax.Precision.HIGHEST)

    def mine(value):
        size = value.shape[0] // shards
        return lax.dynamic_slice_in_dim(value, me * size, size, axis=0)[None]

    return (
        lo,
        ig,
        wide_sum(groups + 2, 2 + groups, 5 + groups),
        wide_sum(groups + 1, 1 + groups, 2 + groups),
        wide_sum(groups, 1, 1 + groups),
        mine(small[count]),
        summed(down.reshape(hidden, width))[None],
        mine(small[count + 1, :width]),
        mine(mod),
        mine(jnp.sum(small[:count], axis=0)),
    )


def solution(mesh):
    return jax.shard_map(
        body,
        mesh=mesh,
        in_specs=(
            P(None, "nodes", None),
            P(None, "nodes", None),
            P("nodes", None),
            P("nodes"),
            P(),
            P("section", None, None),
            P("section", None, None),
            P("section", None, None),
            P("section", None),
            P("section", None, None),
            P("section", None),
            P("section", None, None),
            P("section", None),
        ),
        out_specs=(
            P("section", None, "nodes", None),
            P("section", None, "nodes", None),
            P("section", "nodes", None),
            P("section", "nodes", None),
            P("section", "nodes", None),
            P("section", "nodes"),
            P("section", "nodes", None),
            P("section", "nodes"),
            P("section", "nodes", None),
            P("section", "nodes"),
        ),
        check_vma=False,
    )
```

```python
import jax
import jax.numpy as jnp
from jax import lax
from jax.experimental import pallas as pl
from jax.experimental.pallas import tpu as pltpu
from jax.sharding import PartitionSpec as P

HEADS = 4
REACH = 32
EPSILON = 1e-06
MASKED = -1e9
ABSENT = -2e38
TILE = 512
TOGETHER = 2
MESH = pl.DeviceIdType.MESH
F32, LOW = jnp.float32, jnp.bfloat16


def dot(a, b):
    return lax.dot_general(a, b, (((1,), (0,)), ((), ())), preferred_element_type=F32)


def dot_nt(a, b):
    return lax.dot_general(a, b, (((1,), (1,)), ((), ())), preferred_element_type=F32)


def dot_tn(a, b):
    return lax.dot_general(a, b, (((0,), (0,)), ((), ())), preferred_element_type=F32)


class Sizes:
    def __init__(self, inputs, neighbours, noise, w_up, shards):
        self.batches, self.rows, self.width = inputs.shape
        self.together = TOGETHER if self.batches % TOGETHER == 0 else 1
        self.turns = self.batches // self.together
        self.slots = neighbours.shape[1]
        self.meshes = noise.shape[1]
        self.hidden = w_up.shape[2]
        self.shards = shards
        self.ext = self.rows + 2 * REACH
        self.window = (self.ext // 128 + 1) * 128
        self.groups = self.hidden // TILE
        self.own = self.width // shards
        self.scatter = self.own % 16 == 0
        self.pieces = 2 * self.groups + 4
        self.lefts = 3 + self.groups
        self.rights = 2 + self.groups + 3
        self.rings = max(shards.bit_length() - 1, 1)

        self.bits = [1 << k for k in range(shards.bit_length() - 1)]

    def left(self, p):
        n = self.groups
        return jnp.minimum(p, n) + lax.div(p, 2 * n) + lax.div(p, 2 * n + 1)

    def order(self, swapped):
        bits = list(self.bits)
        if swapped and len(bits) > 2:
            bits[1], bits[2] = bits[2], bits[1]
        return bits

    def right(self, p):
        return jnp.maximum(p - (self.groups - 1), 0)


def kernel_of(z):
    batches, rows, width, ext, window = z.batches, z.rows, z.width, z.ext, z.window
    groups, shards, own, many = z.groups, z.shards, z.own, z.together
    head = width // HEADS
    score_scale = head ** (-0.5)
    log2e = 1.4426950408889634
    npiece = z.pieces
    half, quarter = TILE // 2, TILE // 4
    g_out, g_q, g_k = 1 + groups, 2 + groups, 3 + groups

    def position(owner, first):
        if not z.scatter:
            return owner
        place = 0
        for bit in z.order(first == groups + 2):
            place = 2 * place + owner // bit % 2
        return place

    def kernel(
        inputs, cotangent, neighbours, mesh_ids, sigma,
        w_qkv, w_out, w_up, b_up, w_down, b_down, w_mod, b_mod,
        lo, ig, *rest,
    ):
        left_t, right_t, small_out, table_out = rest[:4]
        rest = rest[4:]
        (
            wq, wo, wu, wd, wm, xext, dybuf, sel, pick, cnt, few, bias, mod, emb,
            n1, n1s, ua, ia, qb, kvext, sbuf, af, ca, obs, n2s, ub, ib, tb, fp, hs,
            ob, cds, dx1, dkv, hsend, hrecv, sm,
            lsem, hx_s, hx_r, hm_s, hm_r, fx_s, fx_r, bh_s, bh_r, bx_s, bx_r,
        ) = rest

        sec = lax.axis_index("section")
        me = lax.axis_index("nodes")
        up = lax.rem(me + 1, shards)
        down = lax.rem(me + shards - 1, shards)
        other = 1 - sec
        def local(src, dst, k):
            return pltpu.make_async_copy(src, dst, lsem.at[k])

        loads = [
            local(w_mod.at[0], wm, 0),
            local(w_qkv.at[0], wq, 1),
            local(w_out.at[0], wo, 2),
            local(w_up.at[0], wu, 3),
            local(w_down.at[0], wd, 4),
        ]
        own_rows = pl.ds(REACH, rows)
        first_load = local(inputs, xext.at[:, own_rows, :], 5)
        last_load = local(cotangent, dybuf, 6)
        loads[0].start()

        @pl.when(sec == 0)
        def _():
            first_load.start()

        for copy in loads[1:]:
            copy.start()

        @pl.when(sec == 1)
        def _():
            last_load.start()

        barrier = pltpu.get_barrier_semaphore()
        mates = [(sec, up), (sec, down), (other, me), (other, up), (other, down)]
        for mate in mates:
            pl.semaphore_signal(barrier, inc=1, device_id=mate, device_id_type=MESH)
        pl.semaphore_wait(barrier, len(mates))

        def remote(src, dst, s_sem, r_sem, mate):
            return pltpu.make_async_remote_copy(
                src_ref=src, dst_ref=dst, send_sem=s_sem, recv_sem=r_sem, device_id=mate, device_id_type=MESH
            )

        low_rows, top_rows = pl.ds(0, REACH), pl.ds(REACH + rows, REACH)
        head_rows, tail_rows = pl.ds(REACH, REACH), pl.ds(rows, REACH)
        x_down = remote(inputs.at[:, pl.ds(0, REACH), :], xext.at[:, top_rows, :], hx_s.at[0], hx_r.at[0], (sec, down))
        x_up = remote(inputs.at[:, pl.ds(rows - REACH, REACH), :], xext.at[:, low_rows, :], hx_s.at[1], hx_r.at[1], (sec, up))

        @pl.when(sec == 0)
        def _():
            x_down.start()
            x_up.start()

        ids = jnp.broadcast_to(mesh_ids[...].astype(F32), (128, rows))
        sel[own_rows, :] = ids.T
        sample = lax.broadcasted_iota(jnp.int32, (16, rows), 0).astype(F32)
        pick[...] = jnp.where(ids[0:16] == sample, 1.0, 0.0).astype(LOW)
        m_down = remote(sel.at[head_rows, :], sel.at[top_rows, :], hm_s.at[0], hm_r.at[0], (sec, down))
        m_up = remote(sel.at[tail_rows, :], sel.at[low_rows, :], hm_s.at[1], hm_r.at[1], (sec, up))
        m_down.start()
        m_up.start()

        row_no = lax.broadcasted_iota(jnp.int32, (16, width // 2), 0)
        level = jnp.ones((16, width // 2), F32)
        for b in range(batches):
            for m in range(z.meshes):
                level = jnp.where(row_no == b * z.meshes + m, sigma[m, b], level)
        place = lax.broadcasted_iota(jnp.int32, (16, width // 2), 1).astype(F32)
        frequency = 3.0 * jnp.exp(-jnp.log(100.0) * place / (width // 2))
        angles = jnp.log(level) * frequency
        embedded = jnp.concatenate([jnp.sin(angles), jnp.cos(angles)], axis=1).astype(LOW)
        padded = jnp.concatenate([embedded.astype(F32), jnp.zeros((112, width), F32)], axis=0)
        emb[...] = padded.T
        loads[0].wait()
        for g in range(4):
            cols = pl.ds(g * width, width)
            table = dot(embedded, wm[:, cols]) + b_mod[:, cols] + (1.0 - g % 2)
            for b in range(batches):
                mod[b, 0 : z.meshes, cols] = table[b * z.meshes : (b + 1) * z.meshes]

        slots = neighbours[...].astype(F32)
        slots = jnp.concatenate([slots, jnp.zeros((128 - z.slots, rows), F32)], axis=0).T
        slots = jnp.where(slots >= 0, slots - (me * rows - REACH).astype(F32), float(ext))
        column = lax.broadcasted_iota(jnp.int32, (rows, window), 1).astype(F32)
        counts = jnp.zeros((rows, window), F32)
        for n in range(z.slots):
            counts = counts + jnp.where(slots[:, n : n + 1] == column, 1.0, 0.0)
        cnt[...] = counts
        few[...] = counts.astype(LOW)
        bias[...] = jnp.where(counts > 0, jnp.where(column == ext, MASKED * log2e, 0.0), ABSENT)

        def mod_rows(b, part, ids_rows):
            cols = pl.ds(part * width, width)
            value = jnp.broadcast_to(mod[b, 0:1, cols], (ids_rows.shape[0], width))
            for m in range(1, z.meshes):
                value = jnp.where(ids_rows > m - 0.5, mod[b, m : m + 1, cols], value)
            return value

        def wide(ids_rows):
            return jnp.concatenate([ids_rows] * (width // 128), axis=1)

        def unit(x):
            centred = x - jnp.mean(x, axis=-1, keepdims=True)
            inv = lax.rsqrt(jnp.mean(centred * centred, axis=-1, keepdims=True) + EPSILON)
            return centred * inv, inv

        def span_of(start, size):
            if isinstance(start, int):
                return pl.ds(start, size)
            return pl.ds(pl.multiple_of(start, size), size)

        def batch_cols(b):
            return span_of(b * rows, rows)

        def turn_cols(t):
            return span_of(t * many * rows, many * rows)

        def turn_of(ref, t):
            return ref[pl.ds(t * many, many)].reshape(many * rows, ref.shape[2])

        span = own if z.scatter else 32

        def transposes(b, carry):
            for first, ref in ((groups, n2s), (groups + 1, obs), (groups + 2, n1s)):
                turned = ref[b].T
                for owner in range(TILE // span):
                    at = position(owner, first) * span
                    left_t[first, at : at + span, batch_cols(b)] = turned[owner * span : (owner + 1) * span]
            run = groups * span
            for g in range(groups):
                turned = hs[b, :, g * TILE : (g + 1) * TILE].T
                for k in range(TILE // span):
                    at = g * TILE + k * span
                    owner, part = at // run, at % run // span
                    to = position(owner, part) * span
                    left_t[part, to : to + span, batch_cols(b)] = turned[k * span : (k + 1) * span]
            return carry

        def forward(t):
            for i in range(many):
                b = t * many + i
                ids_rows = wide(sel[0:ext, :])
                u, inv = unit(xext[b].astype(F32))
                normed = (u * mod_rows(b, 0, ids_rows) + mod_rows(b, 1, ids_rows)).astype(LOW)
                n1[i * ext : (i + 1) * ext, :] = normed
                n1s[b] = normed[REACH : REACH + rows]
                ua[b] = u[REACH : REACH + rows]
                ia[b] = jnp.broadcast_to(inv[REACH : REACH + rows], (rows, 128))
            part = dot(turn_of(n1s, t), wq[:, 0:width]).astype(LOW)
            qb[pl.ds(t * many, many)] = part.reshape(many, rows, width)
            for g in range(2):
                part = dot(n1[...], wq[:, (g + 1) * width : (g + 2) * width]).astype(LOW)
                for i in range(many):
                    kvext[t * many + i, 0:ext, g * width : (g + 1) * width] = part[i * ext : (i + 1) * ext]
            for i in range(many):
                b = t * many + i
                for h in range(HEADS):
                    hd = slice(h * head, (h + 1) * head)
                    sbuf[h] = dot_nt(qb[b, :, hd], kvext[b, :, hd]) * (score_scale * log2e) + bias[...]
                for h in range(HEADS):
                    s = sbuf[h]
                    e = jnp.exp2(s - jnp.max(s, axis=-1, keepdims=True))
                    a = e * (1.0 / jnp.sum(e * cnt[...], axis=-1, keepdims=True))
                    af[b, h] = a
                    ca[b, h] = a.astype(LOW) * few[...]
                for h in range(HEADS):
                    hd = slice(h * head, (h + 1) * head)
                    vd = slice(width + h * head, width + (h + 1) * head)
                    obs[b, :, hd] = dot(ca[b, h], kvext[b, :, vd]).astype(LOW)
            branch = dot(turn_of(obs, t), wo[...])
            for i in range(many):
                b = t * many + i
                x1 = xext[b, own_rows, :].astype(F32) + branch[i * rows : (i + 1) * rows]
                u, inv = unit(x1)
                ub[b] = u
                ib[b] = jnp.broadcast_to(inv, (rows, 128))
                ids_rows = wide(sel[own_rows, :])
                n2s[b] = (u * mod_rows(b, 2, ids_rows) + mod_rows(b, 3, ids_rows)).astype(LOW)
                tb[i * rows : (i + 1) * rows, :] = x1 + b_down[...]
            for g in range(groups):
                gs = slice(g * TILE, (g + 1) * TILE)
                gate = dot(turn_of(n2s, t), wu[:, gs]) + b_up[:, gs]
                s = 0.5 + 0.5 * jnp.tanh(0.5 * gate)
                hid = (gate * s).astype(LOW)
                slope = (s + gate * s * (1.0 - s)).astype(LOW)
                for i in range(many):
                    fp[t * many + i, :, gs] = slope[i * rows : (i + 1) * rows]
                    hs[t * many + i, :, gs] = hid[i * rows : (i + 1) * rows]
                tb[...] += dot(hid, wd[gs, :])
            for i in range(many):
                lo[0, t * many + i] = tb[i * rows : (i + 1) * rows, :].astype(LOW)

        def relay(b):
            return [
                remote(lo.at[0, b], xext.at[b, own_rows, :], fx_s.at[b, 0], fx_r.at[b, 0], (other, me)),
                remote(lo.at[0, b, pl.ds(0, REACH), :], xext.at[b, top_rows, :], fx_s.at[b, 1], fx_r.at[b, 1], (other, down)),
                remote(lo.at[0, b, pl.ds(rows - REACH, REACH), :], xext.at[b, low_rows, :], fx_s.at[b, 2], fx_r.at[b, 2], (other, up)),
            ]

        def norm_back(d, u, inv, scale):
            scaled = d * scale
            return inv * (
                scaled
                - jnp.mean(scaled, axis=-1, keepdims=True)
                - u * jnp.mean(scaled * u, axis=-1, keepdims=True)
            )

        def mod_sums(b, part, d, u):
            for k, value in enumerate((d * u, d)):
                total = dot(pick[...], value.astype(LOW))
                sm[b, 0 : z.meshes, (part + k) * width : (part + k + 1) * width] = total[0 : z.meshes]

        def halos(b):
            return [
                remote(hsend.at[b, 0], hrecv.at[b, 1], bh_s.at[b, 0], bh_r.at[b, 0], (sec, down)),
                remote(hsend.at[b, 1], hrecv.at[b, 0], bh_s.at[b, 1], bh_r.at[b, 1], (sec, up)),
            ]

        def given(t):
            at = turn_cols(t)
            dr = turn_of(dybuf, t)
            right_t[0, at, :] = dr
            for i in range(many):
                total = jnp.sum(dr[i * rows : (i + 1) * rows].astype(F32), axis=0, keepdims=True)
                sm[t * many + i, 7:8, 0:width] = total
            for g in range(groups):
                right_t[1 + g, at, :] = dot_nt(dr, wd[g * TILE : (g + 1) * TILE, :]).astype(LOW)

        def back_ffn(t):
            at = turn_cols(t)
            dn = jnp.zeros((many * rows, width), F32)
            for g in range(groups):
                gs = slice(g * TILE, (g + 1) * TILE)
                dg = right_t[1 + g, at, :].astype(F32) * turn_of(fp, t)[:, gs].astype(F32)
                sm[t * many, 6:7, gs] = jnp.sum(dg, axis=0, keepdims=True)
                dg = dg.astype(LOW)
                right_t[1 + g, at, :] = dg
                dn = dn + dot_nt(dg, wu[:, gs])
            ids_rows = wide(sel[own_rows, :])
            for i in range(many):
                b = t * many + i
                d = dn[i * rows : (i + 1) * rows]
                u = ub[b]
                grad = dybuf[b].astype(F32) + norm_back(d, u, ib[b][:, 0:1], mod_rows(b, 2, ids_rows))
                mod_sums(b, 2, d, u)
                dx1[b] = grad
                right_t[g_out, batch_cols(b), :] = grad.astype(LOW)
            ob[...] = dot_nt(right_t[g_out, at, :], wo[...]).astype(LOW)

        def back_attention(t):
            for i in range(many):
                b = t * many + i
                at = batch_cols(b)
                here = slice(i * rows, (i + 1) * rows)
                for h in range(HEADS):
                    hd = slice(h * head, (h + 1) * head)
                    vd = slice(width + h * head, width + (h + 1) * head)
                    sbuf[h] = dot_nt(ob[here, hd], kvext[b, :, vd])
                for h in range(HEADS):
                    a, da = af[b, h], sbuf[h]
                    ds = a * (da - jnp.sum(a * cnt[...] * da, axis=-1, keepdims=True))
                    cds[h] = ds.astype(LOW) * few[...]
                for h in range(HEADS):
                    hd = slice(h * head, (h + 1) * head)
                    vd = slice(width + h * head, width + (h + 1) * head)
                    dk = dot_tn(cds[h], qb[b, :, hd]) * score_scale
                    dv = dot_tn(ca[b, h], ob[here, hd])
                    for part, cols in ((dk, hd), (dv, vd)):
                        hsend[b, 0, :, cols] = part[0:REACH].astype(LOW)
                        dkv[b, :, cols] = part[REACH : REACH + rows]
                        hsend[b, 1, :, cols] = part[REACH + rows : ext].astype(LOW)
                for copy in halos(b):
                    copy.start()
                for h in range(HEADS):
                    hd = slice(h * head, (h + 1) * head)
                    right_t[g_q, at, hd] = (dot(cds[h], kvext[b, :, hd]) * score_scale).astype(LOW)

        def back_second(t):
            at = turn_cols(t)
            ids_rows = wide(sel[own_rows, :])
            edge = rows - REACH
            dn = dot_nt(right_t[g_q, at, :], wq[:, 0:width])
            for i in range(many):
                b = t * many + i
                for copy in halos(b):
                    copy.wait_recv()
                dkv[b, 0:REACH, :] += hrecv[b, 0].astype(F32)
                dkv[b, edge:rows, :] += hrecv[b, 1].astype(F32)
                for g in range(2):
                    right_t[g_k + g, batch_cols(b), :] = dkv[b, :, g * width : (g + 1) * width].astype(LOW)
            for g in range(2):
                dn = dn + dot_nt(right_t[g_k + g, at, :], wq[:, (g + 1) * width : (g + 2) * width])
            for i in range(many):
                b = t * many + i
                d = dn[i * rows : (i + 1) * rows]
                u = ua[b]
                grad = dx1[b] + norm_back(d, u, ia[b][:, 0:1], mod_rows(b, 0, ids_rows))
                ig[0, b] = grad.astype(LOW)

                @pl.when(sec == 1)
                def _(b=b):
                    relay_back(b).start()

                mod_sums(b, 0, d, u)

        def relay_back(b):
            return remote(ig.at[0, b], dybuf.at[b], bx_s.at[b], bx_r.at[b], (other, me))

        kvext[:, ext:window, :] = jnp.zeros((batches, window - ext, 2 * width), LOW)
        sm[...] = jnp.zeros(sm.shape, F32)
        for copy in loads[1:]:
            copy.wait()
        for copy in (m_down, m_up):
            copy.wait()

        @pl.when(sec == 0)
        def _():
            first_load.wait()
            x_down.wait()
            x_up.wait()

        @pl.when(sec == 1)
        def _():
            last_load.wait()

            @pl.loop(0, z.turns)
            def _(t):
                given(t)

        for t in range(z.turns):

            @pl.when(sec == 1)
            def _(t=t):
                for i in range(many):
                    for copy in relay(t * many + i):
                        copy.wait_recv()

            forward(t)

            @pl.when(sec == 0)
            def _(t=t):
                for i in range(many):
                    for copy in relay(t * many + i):
                        copy.start()

        @pl.when(sec == 0)
        def _():
            lax.fori_loop(0, batches, transposes, 0)

        for t in reversed(range(z.turns)):

            @pl.when(sec == 0)
            def _(t=t):
                for i in range(many):
                    relay_back(t * many + i).wait_recv()
                given(t)

            back_ffn(t)
            back_attention(t)
            back_second(t)

        @pl.when(sec == 1)
        def _():
            lax.fori_loop(0, batches, transposes, 0)

        lines = [sm[b, m : m + 1, :] for b in range(batches) for m in range(z.meshes)]
        for line in (6, 7):
            lines.append(sum(sm[b, line : line + 1, :] for b in range(batches)))
        lines.append(jnp.zeros((16 - len(lines), sm.shape[2]), F32))
        small = jnp.concatenate(lines, axis=0)

        def finish():
            @pl.loop(0, batches)
            def _(b):
                @pl.when(sec == 0)
                def _():
                    for copy in relay(b):
                        copy.wait_send()

                @pl.when(sec == 1)
                def _():
                    relay_back(b).wait_send()

                for copy in halos(b):
                    copy.wait_send()

        small_out[...] = small
        table_out[...] = emb[...]
        finish()

    return kernel


def scatter_of(z):
    shards, own, groups, npiece, batches, width = z.shards, z.own, z.groups, z.pieces, z.batches, z.width
    half = TILE // 2
    stages = len(z.bits)

    def kernel(left_t, right_t, small, emb, o_piece, o_mod, o_line, *rest):
        gives, gets, keeps = rest[:stages], rest[stages : 2 * stages], rest[2 * stages : 3 * stages - 1]
        acc, msend, mrecv, tot, p_s, p_r, m_s, m_r = rest[3 * stages - 1 :]
        sec = lax.axis_index("section")
        me = lax.axis_index("nodes")

        def bit_of(p, k):
            plain, swapped = z.order(False)[k], z.order(True)[k]
            return plain + (swapped - plain) * lax.div(p, 2 * groups + 1)

        def side(bit):
            return lax.rem(lax.div(me, bit), 2)

        def mate(bit):
            return me + bit - 2 * bit * side(bit)

        barrier = pltpu.get_barrier_semaphore()
        for bit in z.bits:
            pl.semaphore_signal(barrier, inc=1, device_id=(sec, mate(bit)), device_id_type=MESH)
        pl.semaphore_wait(barrier, stages)

        def remote(src, dst, s_sem, r_sem, mate):
            return pltpu.make_async_remote_copy(
                src_ref=src, dst_ref=dst, send_sem=s_sem, recv_sem=r_sem, device_id=mate, device_id_type=MESH
            )

        def copy(p, k):
            return remote(gives[k].at[p], gets[k].at[p], p_s.at[p, k], p_r.at[p, k], (sec, mate(bit_of(p, k))))

        def rows_of(c, size):
            return pl.ds(pl.multiple_of(c * size, size), size)

        def piece_start(p):
            away = 1 - side(1)
            gives[0][p] = dot(left_t[z.left(p), rows_of(away, half), :], right_t[z.right(p)]).astype(LOW)
            copy(p, 0).start()

        def piece_step(p, k):
            size = half >> k
            if k == 0:
                mine = dot(left_t[z.left(p), rows_of(side(1), half), :], right_t[z.right(p)])
            else:
                mine = keeps[k - 1][p]
            copy(p, k).wait_recv()
            value = mine + gets[k][p].astype(F32)
            if k == stages - 1:
                o_piece[p] = value
                return
            here = side(bit_of(p, k + 1))
            acc[0:size, :] = value
            gives[k + 1][p] = acc[rows_of(1 - here, size // 2), :].astype(LOW)
            copy(p, k + 1).start()
            keeps[k][p] = acc[rows_of(here, size // 2), :]

        def ring_copy(k):
            return remote(msend.at[k], mrecv.at[k], m_s.at[k], m_r.at[k], (sec, mate(1 << k)))

        def ring_start(k, value):
            msend[k] = value.astype(LOW)
            ring_copy(k).start()

        def ring_end(k):
            ring_copy(k).wait_recv()
            value = msend[k].astype(F32) + mrecv[k].astype(F32)
            if k + 1 < z.rings:
                ring_start(k + 1, value)
            else:
                tot[...] = value

        ring_start(0, small[...])

        @pl.loop(0, npiece + 2 * stages - 1)
        def _(p):
            @pl.when(p < npiece)
            def _():
                piece_start(p)

            for k in range(stages):
                lag = 2 * k + 1

                @pl.when((p >= lag) & (p < npiece + lag))
                def _(k=k, lag=lag):
                    piece_step(p - lag, k)

            for k in range(z.rings):

                @pl.when(p == 2 + 2 * k)
                def _(k=k):
                    ring_end(k)

        count = batches * z.meshes
        table = emb[pl.ds(pl.multiple_of(me * own, own), own), :]
        grad = jnp.zeros((own, 4 * width), F32)
        for k in range(count):
            grad = grad + table[:, k : k + 1] * tot[k : k + 1, :]
        o_mod[0] = grad
        cols = 4 * width // shards
        mine = tot[:, pl.ds(pl.multiple_of(me * cols, cols), cols)]
        o_line[0:1, :] = jnp.sum(mine[0:count], axis=0, keepdims=True)
        o_line[1:2, :] = mine[count : count + 1]
        ratio = 128 // own
        line = tot[:, pl.ds(pl.multiple_of(me // ratio * 128, 128), 128)][count + 1 : count + 2]
        value = line
        for k in range(1, ratio):
            turned = jnp.concatenate([line[:, k * own :], line[:, : k * own]], axis=1)
            value = jnp.where(me % ratio == k, turned, value)
        o_line[2:3, :] = value

        @pl.loop(0, npiece)
        def _(p):
            for k in range(stages):
                copy(p, k).wait_send()

        for k in range(z.rings):
            ring_copy(k).wait_send()

    return kernel


def layout_of(z):
    own, groups = z.own, z.groups

    def kernel(
        lo, ig, piece, mod, line,
        o_lo, o_ig, o_qkv, o_out, o_up, o_upb, o_down, o_downb, o_mod, o_modb,
        v_lo, v_ig, v_piece, v_mod, into, back,
    ):
        moves = [(lo, v_lo, o_lo), (ig, v_ig, o_ig)]
        targets = [o_down.at[0, pl.ds(q * own, own), :] for q in range(groups)]
        targets += [o_up.at[0, :, pl.ds(q * TILE, TILE)] for q in range(groups)]
        targets += [o_out.at[0]] + [o_qkv.at[0, :, pl.ds(q * TILE, TILE)] for q in range(3)]
        moves += [(piece.at[k], v_piece.at[k], target) for k, target in enumerate(targets)]
        moves += [(mod, v_mod, o_mod)]
        firsts = [pltpu.make_async_copy(a, b, into.at[k]) for k, (a, b, _) in enumerate(moves)]
        lasts = [pltpu.make_async_copy(b, c, back.at[k]) for k, (_, b, c) in enumerate(moves)]
        for copy in firsts:
            copy.start()
        o_modb[...] = line[0:1, :]
        o_upb[...] = line[1:2, :]
        o_downb[...] = line[2:3, 0:own]
        for first, last in zip(firsts, lasts):
            first.wait()
            last.start()
        for copy in lasts:
            copy.wait()

    return kernel


def body(
    inputs,
    cotangent,
    neighbours,
    mesh_ids,
    noise_sigma,
    w_qkv,
    w_out,
    w_up,
    b_up,
    w_down,
    b_down,
    w_mod,
    b_mod,
):
    shards = lax.axis_size("nodes")
    z = Sizes(inputs, neighbours, noise_sigma, w_up, shards)
    batches, rows, width, hidden, many = z.batches, z.rows, z.width, z.hidden, z.together
    own, npiece = z.own, z.pieces
    shape = jax.ShapeDtypeStruct
    stack = shape((1, batches, rows, width), LOW)
    outs = [stack, stack]
    outs += [shape((z.lefts, TILE, batches * rows), LOW), shape((z.rights, batches * rows, TILE), LOW)]
    outs += [shape((16, hidden), F32), shape((width, 128), F32)]
    dma = pltpu.SemaphoreType.DMA
    scratch = [
        pltpu.VMEM((width, 3 * width), LOW),
        pltpu.VMEM((width, width), LOW),
        pltpu.VMEM((width, hidden), LOW),
        pltpu.VMEM((hidden, width), LOW),
        pltpu.VMEM((width, 4 * width), LOW),
        pltpu.VMEM((batches, z.ext, width), LOW),
        pltpu.VMEM((batches, rows, width), LOW),
        pltpu.VMEM((z.ext, 128), F32),
        pltpu.VMEM((16, rows), LOW),
        pltpu.VMEM((rows, z.window), F32),
        pltpu.VMEM((rows, z.window), LOW),
        pltpu.VMEM((rows, z.window), F32),
        pltpu.VMEM((batches, 8, 4 * width), F32),
        pltpu.VMEM((width, 128), F32),
        pltpu.VMEM((many * z.ext, width), LOW),
        pltpu.VMEM((batches, rows, width), LOW),
        pltpu.VMEM((batches, rows, width), F32),
        pltpu.VMEM((batches, rows, 128), F32),
        pltpu.VMEM((batches, rows, width), LOW),
        pltpu.VMEM((batches, z.window, 2 * width), LOW),
        pltpu.VMEM((HEADS, rows, z.window), F32),
        pltpu.VMEM((batches, HEADS, rows, z.window), F32),
        pltpu.VMEM((batches, HEADS, rows, z.window), LOW),
        pltpu.VMEM((batches, rows, width), LOW),
        pltpu.VMEM((batches, rows, width), LOW),
        pltpu.VMEM((batches, rows, width), F32),
        pltpu.VMEM((batches, rows, 128), F32),
        pltpu.VMEM((many * rows, width), F32),
        pltpu.VMEM((batches, rows, hidden), LOW),
        pltpu.VMEM((batches, rows, hidden), LOW),
        pltpu.VMEM((many * rows, width), LOW),
        pltpu.VMEM((HEADS, rows, z.window), LOW),
        pltpu.VMEM((batches, rows, width), F32),
        pltpu.VMEM((batches, rows, 2 * width), F32),
        pltpu.VMEM((batches, 2, REACH, 2 * width), LOW),
        pltpu.VMEM((batches, 2, REACH, 2 * width), LOW),
        pltpu.VMEM((batches, 8, hidden), F32),
        dma((7,)),
        dma((2,)),
        dma((2,)),
        dma((2,)),
        dma((2,)),
        dma((batches, 3)),
        dma((batches, 3)),
        dma((batches, 2)),
        dma((batches, 2)),
        dma((batches,)),
        dma((batches,)),
    ]
    hbm = pl.BlockSpec(memory_space=pl.ANY)
    vmem = pl.BlockSpec(memory_space=pltpu.VMEM)
    smem = pl.BlockSpec(memory_space=pltpu.SMEM)
    got = pl.pallas_call(
        kernel_of(z),
        out_shape=outs,
        in_specs=[hbm, hbm, vmem, vmem, smem, hbm, hbm, hbm, vmem, hbm, vmem, hbm, vmem],
        out_specs=[vmem] * len(outs),
        scratch_shapes=scratch,
        compiler_params=pltpu.CompilerParams(
            collective_id=0, has_side_effects=True, vmem_limit_bytes=62 * 2**20
        ),
    )(
        inputs,
        cotangent,
        neighbours.T,
        mesh_ids.reshape(1, rows),
        noise_sigma.T,
        w_qkv,
        w_out,
        w_up,
        b_up,
        w_down,
        b_down,
        w_mod,
        b_mod,
    )
    lo, ig, left_t, right_t, small, table = got
    if z.scatter:
        stages = len(z.bits)
        sizes = [TILE >> (k + 1) for k in range(stages)]
        sums = [pltpu.VMEM((npiece, size, TILE), LOW) for size in sizes + sizes]
        sums += [pltpu.VMEM((npiece, size, TILE), F32) for size in sizes[1:]]
        sums += [
            pltpu.VMEM((sizes[0], TILE), F32),
            pltpu.VMEM((z.rings, 16, hidden), LOW),
            pltpu.VMEM((z.rings, 16, hidden), LOW),
            pltpu.VMEM((16, hidden), F32),
            dma((npiece, stages)),
            dma((npiece, stages)),
            dma((z.rings,)),
            dma((z.rings,)),
        ]
        piece, mod, line = pl.pallas_call(
            scatter_of(z),
            out_shape=[shape((npiece, own, TILE), F32), shape((1, own, 4 * width), F32), shape((8, 128), F32)],
            in_specs=[vmem] * 4,
            out_specs=[vmem] * 3,
            scratch_shapes=sums,
            compiler_params=pltpu.CompilerParams(
                collective_id=1, has_side_effects=True, vmem_limit_bytes=62 * 2**20
            ),
        )(left_t, right_t, small, table)
        return tuple(
            pl.pallas_call(
                layout_of(z),
                out_shape=[
                    stack,
                    stack,
                    shape((1, own, 3 * width), F32),
                    shape((1, own, width), F32),
                    shape((1, own, hidden), F32),
                    shape((1, hidden // shards), F32),
                    shape((1, hidden // shards, width), F32),
                    shape((1, own), F32),
                    shape((1, own, 4 * width), F32),
                    shape((1, 4 * width // shards), F32),
                ],
                in_specs=[hbm, hbm, hbm, hbm, vmem],
                out_specs=[hbm, hbm, hbm, hbm, hbm, vmem, hbm, vmem, hbm, vmem],
                scratch_shapes=[
                    pltpu.VMEM(stack.shape, LOW),
                    pltpu.VMEM(stack.shape, LOW),
                    pltpu.VMEM((npiece, own, TILE), F32),
                    pltpu.VMEM((1, own, 4 * width), F32),
                    dma((npiece + 3,)),
                    dma((npiece + 3,)),
                ],
                compiler_params=pltpu.CompilerParams(vmem_limit_bytes=62 * 2**20),
            )(lo, ig, piece, mod, line)
        )
    groups = z.groups

    def summed(value):
        return lax.psum_scatter(value, "nodes", scatter_dimension=0, tiled=True)

    def wide_sum(left, first, last):
        return summed(jnp.concatenate([dot(left_t[left], right_t[r]) for r in range(first, last)], axis=1))[None]

    down = [dot(left_t[q], right_t[0]).reshape(TILE // 32, 32, TILE) for q in range(groups)]
    down = jnp.stack(down, axis=1)
    count = batches * z.meshes
    small = lax.psum(small, "nodes")
    me = lax.axis_index("nodes")
    mod = jnp.dot(table[:, :count], small[:count], precision=lax.Precision.HIGHEST)

    def mine(value):
        size = value.shape[0] // shards
        return lax.dynamic_slice_in_dim(value, me * size, size, axis=0)[None]

    return (
        lo,
        ig,
        wide_sum(groups + 2, 2 + groups, 5 + groups),
        wide_sum(groups + 1, 1 + groups, 2 + groups),
        wide_sum(groups, 1, 1 + groups),
        mine(small[count]),
        summed(down.reshape(hidden, width))[None],
        mine(small[count + 1, :width]),
        mine(mod),
        mine(jnp.sum(small[:count], axis=0)),
    )


def solution(mesh):
    return jax.shard_map(
        body,
        mesh=mesh,
        in_specs=(
            P(None, "nodes", None),
            P(None, "nodes", None),
            P("nodes", None),
            P("nodes"),
            P(),
            P("section", None, None),
            P("section", None, None),
            P("section", None, None),
            P("section", None),
            P("section", None, None),
            P("section", None),
            P("section", None, None),
            P("section", None),
        ),
        out_specs=(
            P("section", None, "nodes", None),
            P("section", None, "nodes", None),
            P("section", "nodes", None),
            P("section", "nodes", None),
            P("section", "nodes", None),
            P("section", "nodes"),
            P("section", "nodes", None),
            P("section", "nodes"),
            P("section", "nodes", None),
            P("section", "nodes"),
        ),
        check_vma=False,
    )
```

```python
import jax
import jax.numpy as jnp
from jax import lax
from jax.experimental import pallas as pl
from jax.experimental.pallas import tpu as pltpu
from jax.sharding import PartitionSpec as P

HEADS = 4
REACH = 32
EPSILON = 1e-06
MASKED = -1e9
ABSENT = -2e38
TILE = 512
MESH = pl.DeviceIdType.MESH
F32, LOW = jnp.float32, jnp.bfloat16


def dot(a, b):
    return lax.dot_general(a, b, (((1,), (0,)), ((), ())), preferred_element_type=F32)


def dot_nt(a, b):
    return lax.dot_general(a, b, (((1,), (1,)), ((), ())), preferred_element_type=F32)


def dot_tn(a, b):
    return lax.dot_general(a, b, (((0,), (0,)), ((), ())), preferred_element_type=F32)


class Sizes:
    def __init__(self, inputs, neighbours, noise, w_up, shards):
        self.batches, self.rows, self.width = inputs.shape
        self.slots = neighbours.shape[1]
        self.meshes = noise.shape[1]
        self.hidden = w_up.shape[2]
        self.shards = shards
        self.ext = self.rows + 2 * REACH
        self.window = (self.ext // 128 + 1) * 128
        self.groups = self.hidden // TILE
        self.own = self.width // shards
        self.scatter = self.own % 16 == 0
        self.pieces = 2 * self.groups + 4
        self.lefts = 3 + self.groups
        self.rights = 2 + self.groups + 3
        self.rings = max(shards.bit_length() - 1, 1)

        self.bits = [1 << k for k in range(shards.bit_length() - 1)]

    def left(self, p):
        n = self.groups
        return jnp.minimum(p, n) + lax.div(p, 2 * n) + lax.div(p, 2 * n + 1)

    def order(self, swapped):
        bits = list(self.bits)
        if swapped and len(bits) > 2:
            bits[1], bits[2] = bits[2], bits[1]
        return bits

    def right(self, p):
        return jnp.maximum(p - (self.groups - 1), 0)


def weave(*chains):
    chains = list(chains)
    while chains:
        for chain in list(chains):
            try:
                next(chain)
            except StopIteration:
                chains.remove(chain)


def kernel_of(z):
    batches, rows, width, ext, window = z.batches, z.rows, z.width, z.ext, z.window
    groups, shards, own = z.groups, z.shards, z.own
    head = width // HEADS
    score_scale = head ** (-0.5)
    log2e = 1.4426950408889634
    npiece = z.pieces
    half = TILE // 2
    stages = len(z.bits)
    g_out, g_q, g_k = 1 + groups, 2 + groups, 3 + groups

    def position(owner, first):
        if not z.scatter:
            return owner
        place = 0
        for bit in z.order(1 <= first < groups):
            place = 2 * place + owner // bit % 2
        return place

    def kernel(
        inputs, cotangent, neighbours, mesh_ids, sigma,
        w_qkv, w_out, w_up, b_up, w_down, b_down, w_mod, b_mod,
        lo, ig, *rest,
    ):
        if z.scatter:
            o_piece, o_mod, o_line, left_t, right_t = rest[:5]
            rest = rest[5:]
        else:
            left_t, right_t, small_out, table_out = rest[:4]
            rest = rest[4:]
        (
            wq, wo, wu, wd, wm, xext, dybuf, sel, pick, cnt, few, bias, mod, emb,
            n1, n1s, ua, ia, qb, kvext, sbuf, af, ca, obs, n2s, ub, ib, tb, fp, hs,
            ob, dbuf, cds, dx1, dkv, hsend, hrecv, sm,
            lsem, hx_s, hx_r, hm_s, hm_r, fx_s, fx_r, bh_s, bh_r, bx_s, bx_r,
        ) = rest[:49]
        rest = rest[49:]
        if z.scatter:
            gives, gets, keeps = rest[:stages], rest[stages : 2 * stages], rest[2 * stages : 3 * stages - 1]
            acc, msend, mrecv, tot, p_s, p_r, m_s, m_r = rest[3 * stages - 1 :]

        sec = lax.axis_index("section")
        me = lax.axis_index("nodes")
        up = lax.rem(me + 1, shards)
        down = lax.rem(me + shards - 1, shards)
        other = 1 - sec

        def local(src, dst, k):
            return pltpu.make_async_copy(src, dst, lsem.at[k])

        loads = [
            local(w_mod.at[0], wm, 0),
            local(w_qkv.at[0], wq, 1),
            local(w_out.at[0], wo, 2),
            local(w_up.at[0], wu, 3),
            local(w_down.at[0], wd, 4),
        ]
        own_rows = pl.ds(REACH, rows)
        first_load = local(inputs, xext.at[:, own_rows, :], 5)
        last_load = local(cotangent, dybuf, 6)
        loads[0].start()

        @pl.when(sec == 0)
        def _():
            first_load.start()

        for copy in loads[1:]:
            copy.start()

        @pl.when(sec == 1)
        def _():
            last_load.start()

        def side(bit):
            return lax.rem(lax.div(me, bit), 2)

        def mate(bit):
            return me + bit - 2 * bit * side(bit)

        barrier = pltpu.get_barrier_semaphore()
        mates = [(sec, up), (sec, down), (other, me), (other, up), (other, down)]
        if z.scatter:
            mates += [(sec, mate(bit)) for bit in z.bits[1:]]
        for peer in mates:
            pl.semaphore_signal(barrier, inc=1, device_id=peer, device_id_type=MESH)
        pl.semaphore_wait(barrier, len(mates))

        def remote(src, dst, s_sem, r_sem, peer):
            return pltpu.make_async_remote_copy(
                src_ref=src, dst_ref=dst, send_sem=s_sem, recv_sem=r_sem, device_id=peer, device_id_type=MESH
            )

        low_rows, top_rows = pl.ds(0, REACH), pl.ds(REACH + rows, REACH)
        head_rows, tail_rows = pl.ds(REACH, REACH), pl.ds(rows, REACH)
        x_down = remote(inputs.at[:, pl.ds(0, REACH), :], xext.at[:, top_rows, :], hx_s.at[0], hx_r.at[0], (sec, down))
        x_up = remote(inputs.at[:, pl.ds(rows - REACH, REACH), :], xext.at[:, low_rows, :], hx_s.at[1], hx_r.at[1], (sec, up))

        @pl.when(sec == 0)
        def _():
            x_down.start()
            x_up.start()

        ids = jnp.broadcast_to(mesh_ids[...].astype(F32), (128, rows))
        sel[own_rows, :] = ids.T
        m_down = remote(sel.at[head_rows, :], sel.at[top_rows, :], hm_s.at[0], hm_r.at[0], (sec, down))
        m_up = remote(sel.at[tail_rows, :], sel.at[low_rows, :], hm_s.at[1], hm_r.at[1], (sec, up))
        m_down.start()
        m_up.start()
        sample = lax.broadcasted_iota(jnp.int32, (16, rows), 0).astype(F32)
        pick[...] = jnp.where(ids[0:16] == sample, 1.0, 0.0).astype(LOW)

        row_no = lax.broadcasted_iota(jnp.int32, (16, width // 2), 0)
        level = jnp.ones((16, width // 2), F32)
        for b in range(batches):
            for m in range(z.meshes):
                level = jnp.where(row_no == b * z.meshes + m, sigma[m, b], level)
        place = lax.broadcasted_iota(jnp.int32, (16, width // 2), 1).astype(F32)
        frequency = 3.0 * jnp.exp(-jnp.log(100.0) * place / (width // 2))
        angles = jnp.log(level) * frequency
        embedded = jnp.concatenate([jnp.sin(angles), jnp.cos(angles)], axis=1).astype(LOW)
        padded = jnp.concatenate([embedded.astype(F32), jnp.zeros((112, width), F32)], axis=0)
        emb[...] = padded.T
        loads[0].wait()
        for g in range(4):
            cols = pl.ds(g * width, width)
            table = dot(embedded, wm[:, cols]) + b_mod[:, cols] + (1.0 - g % 2)
            for b in range(batches):
                mod[b, 0 : z.meshes, cols] = table[b * z.meshes : (b + 1) * z.meshes]

        slots = neighbours[...].astype(F32)
        slots = jnp.concatenate([slots, jnp.zeros((128 - z.slots, rows), F32)], axis=0).T
        slots = jnp.where(slots >= 0, slots - (me * rows - REACH).astype(F32), float(ext))
        column = lax.broadcasted_iota(jnp.int32, (rows, window), 1).astype(F32)
        counts = jnp.zeros((rows, window), F32)
        for n in range(z.slots):
            counts = counts + jnp.where(slots[:, n : n + 1] == column, 1.0, 0.0)
        cnt[...] = counts
        few[...] = counts.astype(LOW)
        bias[...] = jnp.where(counts > 0, jnp.where(column == ext, MASKED * log2e, 0.0), ABSENT)

        def mod_rows(b, part, ids_rows):
            cols = pl.ds(part * width, width)
            value = jnp.broadcast_to(mod[b, 0:1, cols], (ids_rows.shape[0], width))
            for m in range(1, z.meshes):
                value = jnp.where(ids_rows > m - 0.5, mod[b, m : m + 1, cols], value)
            return value

        def wide(ids_rows):
            return jnp.concatenate([ids_rows] * (width // 128), axis=1)

        def unit(x):
            centred = x - jnp.mean(x, axis=-1, keepdims=True)
            inv = lax.rsqrt(jnp.mean(centred * centred, axis=-1, keepdims=True) + EPSILON)
            return centred * inv, inv

        def batch_cols(b):
            return pl.ds(b * rows, rows) if isinstance(b, int) else pl.ds(pl.multiple_of(b * rows, rows), rows)

        span = own if z.scatter else 32

        def transposes(b, carry):
            for first, ref in ((groups, n2s), (groups + 1, obs), (groups + 2, n1s)):
                turned = ref[b].T
                for owner in range(TILE // span):
                    at = position(owner, first) * span
                    left_t[first, at : at + span, batch_cols(b)] = turned[owner * span : (owner + 1) * span]
            run = groups * span
            for g in range(groups):
                turned = hs[b, :, g * TILE : (g + 1) * TILE].T
                for k in range(TILE // span):
                    at = g * TILE + k * span
                    owner, part = at // run, at % run // span
                    to = position(owner, part) * span
                    left_t[part, to : to + span, batch_cols(b)] = turned[k * span : (k + 1) * span]
            return carry

        heads = [slice(h * head, (h + 1) * head) for h in range(HEADS)]
        heads_v = [slice(width + h * head, width + (h + 1) * head) for h in range(HEADS)]
        tiles = [slice(g * TILE, (g + 1) * TILE) for g in range(groups)]
        thirds = [slice(g * width, (g + 1) * width) for g in range(3)]

        def forward_first(b):
            ids_rows = wide(sel[0:ext, :])
            u, inv = unit(xext[b].astype(F32))
            normed = (u * mod_rows(b, 0, ids_rows) + mod_rows(b, 1, ids_rows)).astype(LOW)
            n1[...] = normed
            n1s[b] = normed[REACH : REACH + rows]
            ua[b] = u[REACH : REACH + rows]
            ia[b] = jnp.broadcast_to(inv[REACH : REACH + rows], (rows, 128))
            yield
            kvext[b, 0:ext, thirds[0]] = dot(n1[...], wq[:, thirds[1]]).astype(LOW)
            qb[b] = dot(n1s[b], wq[:, thirds[0]]).astype(LOW)
            yield
            for h in range(HEADS):
                sbuf[h] = dot_nt(qb[b, :, heads[h]], kvext[b, :, heads[h]]) * (score_scale * log2e) + bias[...]
            kvext[b, 0:ext, thirds[1]] = dot(n1[...], wq[:, thirds[2]]).astype(LOW)
            yield
            for h in range(HEADS):
                s = sbuf[h]
                e = jnp.exp2(s - jnp.max(s, axis=-1, keepdims=True))
                a = e * (1.0 / jnp.sum(e * cnt[...], axis=-1, keepdims=True))
                af[b, h] = a
                ca[b, h] = a.astype(LOW) * few[...]
                if h % 2 == 1:
                    yield
            for h in range(HEADS):
                obs[b, :, heads[h]] = dot(ca[b, h], kvext[b, :, heads_v[h]]).astype(LOW)
            yield

        def forward_second(b):
            x1 = xext[b, own_rows, :].astype(F32) + dot(obs[b], wo[...])
            u, inv = unit(x1)
            ub[b] = u
            ib[b] = jnp.broadcast_to(inv, (rows, 128))
            ids_rows = wide(sel[own_rows, :])
            n2s[b] = (u * mod_rows(b, 2, ids_rows) + mod_rows(b, 3, ids_rows)).astype(LOW)
            tb[...] = x1 + b_down[...]
            yield
            for gs in tiles:
                gate = dot(n2s[b], wu[:, gs]) + b_up[:, gs]
                s = 0.5 + 0.5 * jnp.tanh(0.5 * gate)
                hid = gate * s
                fp[b, :, gs] = (s + hid * (1.0 - s)).astype(LOW)
                hid = hid.astype(LOW)
                hs[b, :, gs] = hid
                tb[...] += dot(hid, wd[gs, :])
                yield
            lo[0, b] = tb[...].astype(LOW)
            yield

        def relay(b):
            return [
                remote(lo.at[0, b], xext.at[b, own_rows, :], fx_s.at[b, 0], fx_r.at[b, 0], (other, me)),
                remote(lo.at[0, b, pl.ds(0, REACH), :], xext.at[b, top_rows, :], fx_s.at[b, 1], fx_r.at[b, 1], (other, down)),
                remote(lo.at[0, b, pl.ds(rows - REACH, REACH), :], xext.at[b, low_rows, :], fx_s.at[b, 2], fx_r.at[b, 2], (other, up)),
            ]

        def norm_back(d, u, inv, scale):
            scaled = d * scale
            return inv * (
                scaled
                - jnp.mean(scaled, axis=-1, keepdims=True)
                - u * jnp.mean(scaled * u, axis=-1, keepdims=True)
            )

        def mod_sums(b, part, d, u):
            for k, value in enumerate((d * u, d)):
                total = dot(pick[...], value.astype(LOW))
                sm[b, 0 : z.meshes, (part + k) * width : (part + k + 1) * width] = total[0 : z.meshes]

        def halos(b):
            return [
                remote(hsend.at[b, 0], hrecv.at[b, 1], bh_s.at[b, 0], bh_r.at[b, 0], (sec, down)),
                remote(hsend.at[b, 1], hrecv.at[b, 0], bh_s.at[b, 1], bh_r.at[b, 1], (sec, up)),
            ]

        def given(b):
            at = batch_cols(b)
            dr = dybuf[b]
            right_t[0, at, :] = dr
            sm[b, 7:8, 0:width] = jnp.sum(dr.astype(F32), axis=0, keepdims=True)
            for g in range(groups):
                right_t[1 + g, at, :] = dot_nt(dr, wd[tiles[g], :]).astype(LOW)

        def back_ffn(b):
            at = batch_cols(b)
            for g in range(groups):
                gs = tiles[g]
                dg = right_t[1 + g, at, :].astype(F32) * fp[b, :, gs].astype(F32)
                sm[b, 6:7, gs] = jnp.sum(dg, axis=0, keepdims=True)
                dg = dg.astype(LOW)
                right_t[1 + g, at, :] = dg
                part = dot_nt(dg, wu[:, gs])
                if g == 0:
                    dbuf[...] = part
                else:
                    dbuf[...] += part
                yield

        def back_middle(b):
            at = batch_cols(b)
            ids_rows = wide(sel[own_rows, :])
            d, u = dbuf[...], ub[b]
            grad = dybuf[b].astype(F32) + norm_back(d, u, ib[b][:, 0:1], mod_rows(b, 2, ids_rows))
            dx1[b] = grad
            right_t[g_out, at, :] = grad.astype(LOW)
            yield
            ob[...] = dot_nt(right_t[g_out, at, :], wo[...]).astype(LOW)
            mod_sums(b, 2, d, u)
            yield

        def back_attention(b):
            at = batch_cols(b)
            for h in range(HEADS):
                sbuf[h] = dot_nt(ob[:, heads[h]], kvext[b, :, heads_v[h]])
            for h in range(HEADS):
                dv = dot_tn(ca[b, h], ob[:, heads[h]])
                hsend[b, 0, :, heads_v[h]] = dv[0:REACH].astype(LOW)
                dkv[b, :, heads_v[h]] = dv[REACH : REACH + rows]
                hsend[b, 1, :, heads_v[h]] = dv[REACH + rows : ext].astype(LOW)
            yield
            for h in range(HEADS):
                a, da = af[b, h], sbuf[h]
                ds = a * (da - jnp.sum(a * cnt[...] * da, axis=-1, keepdims=True))
                cds[h] = ds.astype(LOW) * few[...]
            yield
            for h in range(HEADS):
                dk = dot_tn(cds[h], qb[b, :, heads[h]]) * score_scale
                hsend[b, 0, :, heads[h]] = dk[0:REACH].astype(LOW)
                dkv[b, :, heads[h]] = dk[REACH : REACH + rows]
                hsend[b, 1, :, heads[h]] = dk[REACH + rows : ext].astype(LOW)
            yield
            for h in range(HEADS):
                right_t[g_q, at, heads[h]] = (dot(cds[h], kvext[b, :, heads[h]]) * score_scale).astype(LOW)
            yield

        def back_second(b):
            at = batch_cols(b)
            edge = rows - REACH
            dkv[b, 0:REACH, :] += hrecv[b, 0].astype(F32)
            dkv[b, edge:rows, :] += hrecv[b, 1].astype(F32)
            for g in range(2):
                right_t[g_k + g, at, :] = dkv[b, :, thirds[g]].astype(LOW)
            yield
            d = dot_nt(right_t[g_q, at, :], wq[:, thirds[0]])
            for g in range(2):
                d = d + dot_nt(right_t[g_k + g, at, :], wq[:, thirds[g + 1]])
            tb[...] = d
            yield
            d, u = tb[...], ua[b]
            ids_rows = wide(sel[own_rows, :])
            grad = dx1[b] + norm_back(d, u, ia[b][:, 0:1], mod_rows(b, 0, ids_rows))
            ig[0, b] = grad.astype(LOW)
            mod_sums(b, 0, d, u)
            yield

        def relay_back(b):
            return remote(ig.at[0, b], dybuf.at[b], bx_s.at[b], bx_r.at[b], (other, me))

        def take(b):
            @pl.when(sec == 1)
            def _():
                for copy in relay(b):
                    copy.wait_recv()

        def hand(b):
            @pl.when(sec == 0)
            def _():
                for copy in relay(b):
                    copy.start()

        kvext[:, ext:window, :] = jnp.zeros((batches, window - ext, 2 * width), LOW)
        sm[...] = jnp.zeros(sm.shape, F32)
        for copy in loads[1:]:
            copy.wait()
        for copy in (m_down, m_up):
            copy.wait()

        @pl.when(sec == 0)
        def _():
            first_load.wait()
            x_down.wait()
            x_up.wait()

        @pl.when(sec == 1)
        def _():
            last_load.wait()

            @pl.loop(0, batches)
            def _(b):
                given(b)

        take(0)
        weave(forward_first(0))

        @pl.loop(0, batches - 1)
        def _(b):
            take(b + 1)
            weave(forward_second(b), forward_first(b + 1))
            hand(b)

        weave(forward_second(batches - 1))
        hand(batches - 1)

        @pl.when(sec == 0)
        def _():
            lax.fori_loop(0, batches, transposes, 0)

        def bit_of(p, k):
            plain, swapped = z.order(False)[k], z.order(True)[k]
            trades = jnp.minimum(p, 1) - jnp.minimum(lax.div(p, groups), 1)
            return plain + (swapped - plain) * trades

        def piece_copy(p, k):
            return remote(gives[k].at[p], gets[k].at[p], p_s.at[p, k], p_r.at[p, k], (sec, mate(bit_of(p, k))))

        def rows_of(c, size):
            return pl.ds(pl.multiple_of(c * size, size), size)

        def piece_start(p):
            away = 1 - side(1)
            gives[0][p] = dot(left_t[z.left(p), rows_of(away, half), :], right_t[z.right(p)]).astype(LOW)
            piece_copy(p, 0).start()

        def piece_step(p, k):
            size = half >> k
            if k == 0:
                mine = dot(left_t[z.left(p), rows_of(side(1), half), :], right_t[z.right(p)])
            else:
                mine = keeps[k - 1][p]
            piece_copy(p, k).wait_recv()
            value = mine + gets[k][p].astype(F32)
            if k == stages - 1:
                o_piece[p] = value
                return
            here = side(bit_of(p, k + 1))
            acc[0:size, :] = value
            gives[k + 1][p] = acc[rows_of(1 - here, size // 2), :].astype(LOW)
            piece_copy(p, k + 1).start()
            keeps[k][p] = acc[rows_of(here, size // 2), :]

        def pieces(first, last, step=None):
            @pl.loop(first, last)
            def _(p):
                if step is None:
                    piece_start(p)
                else:
                    piece_step(p, step)

        early = 2 * groups + 1

        def arrive(b):
            relay_back(b).wait_recv()
            given(b)

        def send_halos(b):
            for copy in halos(b):
                copy.start()

        def get_halos(b):
            for copy in halos(b):
                copy.wait_recv()

        def send_back(b):
            @pl.when(sec == 1)
            def _():
                relay_back(b).start()

        @pl.when(sec == 0)
        def _():
            arrive(batches - 1)

        weave(back_ffn(batches - 1))
        weave(back_middle(batches - 1))
        weave(back_attention(batches - 1))
        send_halos(batches - 1)

        @pl.loop(0, batches - 2 + sec)
        def _(k):
            b = batches - 2 - k

            @pl.when(sec == 0)
            def _():
                arrive(b)

            get_halos(b + 1)
            weave(back_second(b + 1), back_ffn(b))
            send_back(b + 1)
            weave(back_middle(b))
            weave(back_attention(b))
            send_halos(b)

        @pl.when(sec == 0)
        def _():
            get_halos(1)
            weave(back_second(1))
            arrive(0)
            if z.scatter:
                pieces(0, groups)
            weave(back_ffn(0))
            if z.scatter:
                pieces(0, groups, 0)
                pieces(groups, 2 * groups)
            weave(back_middle(0))
            if z.scatter:
                pieces(2 * groups, early)
            weave(back_attention(0))
            send_halos(0)
            if z.scatter:
                pieces(groups, early, 0)

        get_halos(0)
        weave(back_second(0))
        send_back(0)

        @pl.when(sec == 1)
        def _():
            lax.fori_loop(0, batches, transposes, 0)

        lines = [sm[b, m : m + 1, :] for b in range(batches) for m in range(z.meshes)]
        for line in (6, 7):
            lines.append(sum(sm[b, line : line + 1, :] for b in range(batches)))
        lines.append(jnp.zeros((16 - len(lines), sm.shape[2]), F32))
        small = jnp.concatenate(lines, axis=0)

        def finish():
            @pl.loop(0, batches)
            def _(b):
                @pl.when(sec == 0)
                def _():
                    for copy in relay(b):
                        copy.wait_send()

                @pl.when(sec == 1)
                def _():
                    relay_back(b).wait_send()

                for copy in halos(b):
                    copy.wait_send()

        if not z.scatter:
            small_out[...] = small
            table_out[...] = emb[...]
            finish()
            return

        def ring_copy(k):
            return remote(msend.at[k], mrecv.at[k], m_s.at[k], m_r.at[k], (sec, mate(1 << k)))

        def ring_start(k, value):
            msend[k] = value.astype(LOW)
            ring_copy(k).start()

        def ring_end(k):
            ring_copy(k).wait_recv()
            value = msend[k].astype(F32) + mrecv[k].astype(F32)
            if k + 1 < z.rings:
                ring_start(k + 1, value)
            else:
                tot[...] = value

        ring_start(0, small)
        begun = (1 - sec) * early

        @pl.loop(0, npiece + 2 * stages - 1)
        def _(p):
            @pl.when((p >= begun) & (p < npiece))
            def _():
                piece_start(p)

            for k in range(stages):
                lag = 2 * k + 1
                first = begun + lag if k == 0 else lag

                @pl.when((p >= first) & (p < npiece + lag))
                def _(k=k, lag=lag):
                    piece_step(p - lag, k)

            for k in range(z.rings):

                @pl.when(p == 2 + 2 * k)
                def _(k=k):
                    ring_end(k)

        count = batches * z.meshes
        table = emb[pl.ds(pl.multiple_of(me * own, own), own), :]
        grad = jnp.zeros((own, 4 * width), F32)
        for k in range(count):
            grad = grad + table[:, k : k + 1] * tot[k : k + 1, :]
        o_mod[0] = grad
        cols = 4 * width // shards
        mine = tot[:, pl.ds(pl.multiple_of(me * cols, cols), cols)]
        o_line[0:1, :] = jnp.sum(mine[0:count], axis=0, keepdims=True)
        o_line[1:2, :] = mine[count : count + 1]
        ratio = 128 // own
        line = tot[:, pl.ds(pl.multiple_of(me // ratio * 128, 128), 128)][count + 1 : count + 2]
        value = line
        for k in range(1, ratio):
            turned = jnp.concatenate([line[:, k * own :], line[:, : k * own]], axis=1)
            value = jnp.where(me % ratio == k, turned, value)
        o_line[2:3, :] = value
        finish()

        @pl.loop(0, npiece)
        def _(p):
            for k in range(stages):
                piece_copy(p, k).wait_send()

        for k in range(z.rings):
            ring_copy(k).wait_send()

    return kernel


def layout_of(z):
    own, groups = z.own, z.groups

    def kernel(
        lo, ig, piece, mod, line,
        o_lo, o_ig, o_qkv, o_out, o_up, o_upb, o_down, o_downb, o_mod, o_modb,
        v_lo, v_ig, v_piece, v_mod, into, back,
    ):
        moves = [(lo, v_lo, o_lo), (ig, v_ig, o_ig)]
        targets = [o_down.at[0, pl.ds(q * own, own), :] for q in range(groups)]
        targets += [o_up.at[0, :, pl.ds(q * TILE, TILE)] for q in range(groups)]
        targets += [o_out.at[0]] + [o_qkv.at[0, :, pl.ds(q * TILE, TILE)] for q in range(3)]
        moves += [(piece.at[k], v_piece.at[k], target) for k, target in enumerate(targets)]
        moves += [(mod, v_mod, o_mod)]
        firsts = [pltpu.make_async_copy(a, b, into.at[k]) for k, (a, b, _) in enumerate(moves)]
        lasts = [pltpu.make_async_copy(b, c, back.at[k]) for k, (_, b, c) in enumerate(moves)]
        for copy in firsts:
            copy.start()
        o_modb[...] = line[0:1, :]
        o_upb[...] = line[1:2, :]
        o_downb[...] = line[2:3, 0:own]
        for first, last in zip(firsts, lasts):
            first.wait()
            last.start()
        for copy in lasts:
            copy.wait()

    return kernel


def body(
    inputs,
    cotangent,
    neighbours,
    mesh_ids,
    noise_sigma,
    w_qkv,
    w_out,
    w_up,
    b_up,
    w_down,
    b_down,
    w_mod,
    b_mod,
):
    shards = lax.axis_size("nodes")
    z = Sizes(inputs, neighbours, noise_sigma, w_up, shards)
    batches, rows, width, hidden = z.batches, z.rows, z.width, z.hidden
    own, npiece = z.own, z.pieces
    shape = jax.ShapeDtypeStruct
    stack = shape((1, batches, rows, width), LOW)
    outs = [stack, stack]
    sides = [(z.lefts, TILE, batches * rows), (z.rights, batches * rows, TILE)]
    if z.scatter:
        outs += [shape((npiece, own, TILE), F32), shape((1, own, 4 * width), F32), shape((8, 128), F32)]
        scratch = [pltpu.VMEM(side, LOW) for side in sides]
    else:
        outs += [shape(side, LOW) for side in sides] + [shape((16, hidden), F32), shape((width, 128), F32)]
        scratch = []
    dma = pltpu.SemaphoreType.DMA
    scratch += [
        pltpu.VMEM((width, 3 * width), LOW),
        pltpu.VMEM((width, width), LOW),
        pltpu.VMEM((width, hidden), LOW),
        pltpu.VMEM((hidden, width), LOW),
        pltpu.VMEM((width, 4 * width), LOW),
        pltpu.VMEM((batches, z.ext, width), LOW),
        pltpu.VMEM((batches, rows, width), LOW),
        pltpu.VMEM((z.ext, 128), F32),
        pltpu.VMEM((16, rows), LOW),
        pltpu.VMEM((rows, z.window), F32),
        pltpu.VMEM((rows, z.window), LOW),
        pltpu.VMEM((rows, z.window), F32),
        pltpu.VMEM((batches, 8, 4 * width), F32),
        pltpu.VMEM((width, 128), F32),
        pltpu.VMEM((z.ext, width), LOW),
        pltpu.VMEM((batches, rows, width), LOW),
        pltpu.VMEM((batches, rows, width), F32),
        pltpu.VMEM((batches, rows, 128), F32),
        pltpu.VMEM((batches, rows, width), LOW),
        pltpu.VMEM((batches, z.window, 2 * width), LOW),
        pltpu.VMEM((HEADS, rows, z.window), F32),
        pltpu.VMEM((batches, HEADS, rows, z.window), F32),
        pltpu.VMEM((batches, HEADS, rows, z.window), LOW),
        pltpu.VMEM((batches, rows, width), LOW),
        pltpu.VMEM((batches, rows, width), LOW),
        pltpu.VMEM((batches, rows, width), F32),
        pltpu.VMEM((batches, rows, 128), F32),
        pltpu.VMEM((rows, width), F32),
        pltpu.VMEM((batches, rows, hidden), LOW),
        pltpu.VMEM((batches, rows, hidden), LOW),
        pltpu.VMEM((rows, width), LOW),
        pltpu.VMEM((rows, width), F32),
        pltpu.VMEM((HEADS, rows, z.window), LOW),
        pltpu.VMEM((batches, rows, width), F32),
        pltpu.VMEM((batches, rows, 2 * width), F32),
        pltpu.VMEM((batches, 2, REACH, 2 * width), LOW),
        pltpu.VMEM((batches, 2, REACH, 2 * width), LOW),
        pltpu.VMEM((batches, 8, hidden), F32),
        dma((7,)),
        dma((2,)),
        dma((2,)),
        dma((2,)),
        dma((2,)),
        dma((batches, 3)),
        dma((batches, 3)),
        dma((batches, 2)),
        dma((batches, 2)),
        dma((batches,)),
        dma((batches,)),
    ]
    if z.scatter:
        stages = len(z.bits)
        sizes = [TILE >> (k + 1) for k in range(stages)]
        scratch += [pltpu.VMEM((npiece, size, TILE), LOW) for size in sizes + sizes]
        scratch += [pltpu.VMEM((npiece, size, TILE), F32) for size in sizes[1:]]
        scratch += [
            pltpu.VMEM((sizes[0], TILE), F32),
            pltpu.VMEM((z.rings, 16, hidden), LOW),
            pltpu.VMEM((z.rings, 16, hidden), LOW),
            pltpu.VMEM((16, hidden), F32),
            dma((npiece, stages)),
            dma((npiece, stages)),
            dma((z.rings,)),
            dma((z.rings,)),
        ]
    hbm = pl.BlockSpec(memory_space=pl.ANY)
    vmem = pl.BlockSpec(memory_space=pltpu.VMEM)
    smem = pl.BlockSpec(memory_space=pltpu.SMEM)
    got = pl.pallas_call(
        kernel_of(z),
        out_shape=outs,
        in_specs=[hbm, hbm, vmem, vmem, smem, hbm, hbm, hbm, vmem, hbm, vmem, hbm, vmem],
        out_specs=[vmem] * len(outs),
        scratch_shapes=scratch,
        compiler_params=pltpu.CompilerParams(
            collective_id=0, has_side_effects=True, vmem_limit_bytes=62 * 2**20
        ),
    )(
        inputs,
        cotangent,
        neighbours.T,
        mesh_ids.reshape(1, rows),
        noise_sigma.T,
        w_qkv,
        w_out,
        w_up,
        b_up,
        w_down,
        b_down,
        w_mod,
        b_mod,
    )
    if z.scatter:
        lo, ig, piece, mod, line = got
        return tuple(
            pl.pallas_call(
                layout_of(z),
                out_shape=[
                    stack,
                    stack,
                    shape((1, own, 3 * width), F32),
                    shape((1, own, width), F32),
                    shape((1, own, hidden), F32),
                    shape((1, hidden // shards), F32),
                    shape((1, hidden // shards, width), F32),
                    shape((1, own), F32),
                    shape((1, own, 4 * width), F32),
                    shape((1, 4 * width // shards), F32),
                ],
                in_specs=[hbm, hbm, hbm, hbm, vmem],
                out_specs=[hbm, hbm, hbm, hbm, hbm, vmem, hbm, vmem, hbm, vmem],
                scratch_shapes=[
                    pltpu.VMEM(stack.shape, LOW),
                    pltpu.VMEM(stack.shape, LOW),
                    pltpu.VMEM((npiece, own, TILE), F32),
                    pltpu.VMEM((1, own, 4 * width), F32),
                    dma((npiece + 3,)),
                    dma((npiece + 3,)),
                ],
                compiler_params=pltpu.CompilerParams(vmem_limit_bytes=62 * 2**20),
            )(lo, ig, piece, mod, line)
        )
    lo, ig, left_t, right_t, small, table = got
    groups = z.groups

    def summed(value):
        return lax.psum_scatter(value, "nodes", scatter_dimension=0, tiled=True)

    def wide_sum(left, first, last):
        return summed(jnp.concatenate([dot(left_t[left], right_t[r]) for r in range(first, last)], axis=1))[None]

    down = [dot(left_t[q], right_t[0]).reshape(TILE // 32, 32, TILE) for q in range(groups)]
    down = jnp.stack(down, axis=1)
    count = batches * z.meshes
    small = lax.psum(small, "nodes")
    me = lax.axis_index("nodes")
    mod = jnp.dot(table[:, :count], small[:count], precision=lax.Precision.HIGHEST)

    def mine(value):
        size = value.shape[0] // shards
        return lax.dynamic_slice_in_dim(value, me * size, size, axis=0)[None]

    return (
        lo,
        ig,
        wide_sum(groups + 2, 2 + groups, 5 + groups),
        wide_sum(groups + 1, 1 + groups, 2 + groups),
        wide_sum(groups, 1, 1 + groups),
        mine(small[count]),
        summed(down.reshape(hidden, width))[None],
        mine(small[count + 1, :width]),
        mine(mod),
        mine(jnp.sum(small[:count], axis=0)),
    )


def solution(mesh):
    return jax.shard_map(
        body,
        mesh=mesh,
        in_specs=(
            P(None, "nodes", None),
            P(None, "nodes", None),
            P("nodes", None),
            P("nodes"),
            P(),
            P("section", None, None),
            P("section", None, None),
            P("section", None, None),
            P("section", None),
            P("section", None, None),
            P("section", None),
            P("section", None, None),
            P("section", None),
        ),
        out_specs=(
            P("section", None, "nodes", None),
            P("section", None, "nodes", None),
            P("section", "nodes", None),
            P("section", "nodes", None),
            P("section", "nodes", None),
            P("section", "nodes"),
            P("section", "nodes", None),
            P("section", "nodes"),
            P("section", "nodes", None),
            P("section", "nodes"),
        ),
        check_vma=False,
    )
```

```python
import jax
import jax.numpy as jnp
from jax import lax
from jax.experimental import pallas as pl
from jax.experimental.pallas import tpu as pltpu
from jax.sharding import PartitionSpec as P

HEADS = 4
REACH = 32
EPSILON = 1e-06
MASKED = -1e9
ABSENT = -2e38
TILE = 512
MESH = pl.DeviceIdType.MESH
F32, LOW = jnp.float32, jnp.bfloat16


def dot(a, b):
    return lax.dot_general(a, b, (((1,), (0,)), ((), ())), preferred_element_type=F32)


def dot_nt(a, b):
    return lax.dot_general(a, b, (((1,), (1,)), ((), ())), preferred_element_type=F32)


def dot_tn(a, b):
    return lax.dot_general(a, b, (((0,), (0,)), ((), ())), preferred_element_type=F32)


class Sizes:
    def __init__(self, inputs, neighbours, noise, w_up, shards):
        self.batches, self.rows, self.width = inputs.shape
        self.slots = neighbours.shape[1]
        self.meshes = noise.shape[1]
        self.hidden = w_up.shape[2]
        self.shards = shards
        self.ext = self.rows + 2 * REACH
        self.window = (self.ext // 128 + 1) * 128
        self.groups = self.hidden // TILE
        self.own = self.width // shards
        self.scatter = self.own % 16 == 0
        self.pieces = 2 * self.groups + 4
        self.lefts = 3 + self.groups
        self.rings = max(shards.bit_length() - 1, 1)

        self.bits = [1 << k for k in range(shards.bit_length() - 1)]

    def order(self, swapped):
        bits = list(self.bits)
        if swapped and len(bits) > 2:
            bits[1], bits[2] = bits[2], bits[1]
        return bits


def weave(*chains):
    chains = list(chains)
    while chains:
        for chain in list(chains):
            try:
                next(chain)
            except StopIteration:
                chains.remove(chain)


def kernel_of(z):
    batches, rows, width, ext, window = z.batches, z.rows, z.width, z.ext, z.window
    groups, shards, own = z.groups, z.shards, z.own
    head = width // HEADS
    score_scale = head ** (-0.5)
    log2e = 1.4426950408889634
    npiece = z.pieces
    half = TILE // 2
    stages = len(z.bits)

    def position(owner, first):
        if not z.scatter:
            return owner
        place = 0
        for bit in z.order(1 <= first < groups):
            place = 2 * place + owner // bit % 2
        return place

    def kernel(
        inputs, cotangent, neighbours, mesh_ids, sigma,
        w_qkv, w_out, w_up, b_up, w_down, b_down, w_mod, b_mod,
        lo, ig, *rest,
    ):
        if z.scatter:
            o_piece, o_mod, o_line, left_t, r_dr, r_dg, r_db, r_qkv = rest[:8]
            rest = rest[8:]
        else:
            left_t, r_dr, r_dg, r_db, r_qkv, small_out, table_out = rest[:7]
            rest = rest[7:]
        (
            wq, wo, wu, wd, wm, xext, dybuf, sel, pick, cnt, few, bias, mod, emb,
            n1, n1s, ua, ia, qb, kvext, sbuf, af, ca, obs, n2s, ub, ib, tb, gbuf, fp, hs,
            ob, dbuf, cds, dx1, dkv, hsend, hrecv, sm,
            lsem, hx_s, hx_r, hm_s, hm_r, fx_s, fx_r, bh_s, bh_r, bx_s, bx_r,
        ) = rest[:50]
        rest = rest[50:]
        if z.scatter:
            gives, gets, keeps = rest[:stages], rest[stages : 2 * stages], rest[2 * stages : 3 * stages - 1]
            mine, acc, msend, mrecv, tot, p_s, p_r, m_s, m_r = rest[3 * stages - 1 :]

        sec = lax.axis_index("section")
        me = lax.axis_index("nodes")
        up = lax.rem(me + 1, shards)
        down = lax.rem(me + shards - 1, shards)
        other = 1 - sec

        def local(src, dst, k):
            return pltpu.make_async_copy(src, dst, lsem.at[k])

        loads = [
            local(w_mod.at[0], wm, 0),
            local(w_qkv.at[0], wq, 1),
            local(w_out.at[0], wo, 2),
            local(w_up.at[0], wu, 3),
            local(w_down.at[0], wd, 4),
        ]
        own_rows = pl.ds(REACH, rows)
        first_load = local(inputs, xext.at[:, own_rows, :], 5)
        last_load = local(cotangent, dybuf, 6)
        loads[0].start()

        @pl.when(sec == 0)
        def _():
            first_load.start()

        for copy in loads[1:]:
            copy.start()

        @pl.when(sec == 1)
        def _():
            last_load.start()

        def side(bit):
            return lax.rem(lax.div(me, bit), 2)

        def mate(bit):
            return me + bit - 2 * bit * side(bit)

        barrier = pltpu.get_barrier_semaphore()
        mates = [(sec, up), (sec, down), (other, me), (other, up), (other, down)]
        if z.scatter:
            mates += [(sec, mate(bit)) for bit in z.bits[1:]]
        for peer in mates:
            pl.semaphore_signal(barrier, inc=1, device_id=peer, device_id_type=MESH)
        pl.semaphore_wait(barrier, len(mates))

        def remote(src, dst, s_sem, r_sem, peer):
            return pltpu.make_async_remote_copy(
                src_ref=src, dst_ref=dst, send_sem=s_sem, recv_sem=r_sem, device_id=peer, device_id_type=MESH
            )

        low_rows, top_rows = pl.ds(0, REACH), pl.ds(REACH + rows, REACH)
        head_rows, tail_rows = pl.ds(REACH, REACH), pl.ds(rows, REACH)
        x_down = remote(inputs.at[:, pl.ds(0, REACH), :], xext.at[:, top_rows, :], hx_s.at[0], hx_r.at[0], (sec, down))
        x_up = remote(inputs.at[:, pl.ds(rows - REACH, REACH), :], xext.at[:, low_rows, :], hx_s.at[1], hx_r.at[1], (sec, up))

        @pl.when(sec == 0)
        def _():
            x_down.start()
            x_up.start()

        ids = jnp.broadcast_to(mesh_ids[...].astype(F32), (128, rows))
        sel[own_rows, :] = ids.T
        m_down = remote(sel.at[head_rows, :], sel.at[top_rows, :], hm_s.at[0], hm_r.at[0], (sec, down))
        m_up = remote(sel.at[tail_rows, :], sel.at[low_rows, :], hm_s.at[1], hm_r.at[1], (sec, up))
        m_down.start()
        m_up.start()
        sample = lax.broadcasted_iota(jnp.int32, (16, rows), 0).astype(F32)
        pick[...] = jnp.where(ids[0:16] == sample, 1.0, 0.0).astype(LOW)

        row_no = lax.broadcasted_iota(jnp.int32, (16, width // 2), 0)
        level = jnp.ones((16, width // 2), F32)
        for b in range(batches):
            for m in range(z.meshes):
                level = jnp.where(row_no == b * z.meshes + m, sigma[m, b], level)
        place = lax.broadcasted_iota(jnp.int32, (16, width // 2), 1).astype(F32)
        frequency = 3.0 * jnp.exp(-jnp.log(100.0) * place / (width // 2))
        angles = jnp.log(level) * frequency
        embedded = jnp.concatenate([jnp.sin(angles), jnp.cos(angles)], axis=1).astype(LOW)
        padded = jnp.concatenate([embedded.astype(F32), jnp.zeros((112, width), F32)], axis=0)
        emb[...] = padded.T
        loads[0].wait()
        for g in range(4):
            cols = pl.ds(g * width, width)
            table = dot(embedded, wm[:, cols]) + b_mod[:, cols] + (1.0 - g % 2)
            for b in range(batches):
                mod[b, 0 : z.meshes, cols] = table[b * z.meshes : (b + 1) * z.meshes]

        slots = neighbours[...].astype(F32)
        slots = jnp.concatenate([slots, jnp.zeros((128 - z.slots, rows), F32)], axis=0).T
        slots = jnp.where(slots >= 0, slots - (me * rows - REACH).astype(F32), float(ext))
        column = lax.broadcasted_iota(jnp.int32, (rows, window), 1).astype(F32)
        counts = jnp.zeros((rows, window), F32)
        for n in range(z.slots):
            counts = counts + jnp.where(slots[:, n : n + 1] == column, 1.0, 0.0)
        cnt[...] = counts
        few[...] = counts.astype(LOW)
        bias[...] = jnp.where(counts > 0, jnp.where(column == ext, MASKED * log2e, 0.0), ABSENT)

        def mod_rows(b, part, ids_rows):
            cols = pl.ds(part * width, width)
            value = jnp.broadcast_to(mod[b, 0:1, cols], (ids_rows.shape[0], width))
            for m in range(1, z.meshes):
                value = jnp.where(ids_rows > m - 0.5, mod[b, m : m + 1, cols], value)
            return value

        def wide(ids_rows):
            return jnp.concatenate([ids_rows] * (width // 128), axis=1)

        def unit(x):
            centred = x - jnp.mean(x, axis=-1, keepdims=True)
            inv = lax.rsqrt(jnp.mean(centred * centred, axis=-1, keepdims=True) + EPSILON)
            return centred * inv, inv

        def batch_cols(b):
            return pl.ds(b * rows, rows) if isinstance(b, int) else pl.ds(pl.multiple_of(b * rows, rows), rows)

        span = own if z.scatter else 32

        def transposes(b, carry):
            for first, ref in ((groups, n2s), (groups + 1, obs), (groups + 2, n1s)):
                turned = ref[b].T
                for owner in range(TILE // span):
                    at = position(owner, first) * span
                    left_t[first, at : at + span, batch_cols(b)] = turned[owner * span : (owner + 1) * span]
            run = groups * span
            for g in range(groups):
                turned = hs[b, :, g * TILE : (g + 1) * TILE].T
                for k in range(TILE // span):
                    at = g * TILE + k * span
                    owner, part = at // run, at % run // span
                    to = position(owner, part) * span
                    left_t[part, to : to + span, batch_cols(b)] = turned[k * span : (k + 1) * span]
            return carry

        def slot(b):
            return b % 2 if isinstance(b, int) else lax.rem(b, 2)

        heads = [slice(h * head, (h + 1) * head) for h in range(HEADS)]
        heads_v = [slice(width + h * head, width + (h + 1) * head) for h in range(HEADS)]
        tiles = [slice(g * TILE, (g + 1) * TILE) for g in range(groups)]
        thirds = [slice(g * width, (g + 1) * width) for g in range(3)]

        def forward_first(b):
            ids_rows = wide(sel[0:ext, :])
            u, inv = unit(xext[b].astype(F32))
            normed = (u * mod_rows(b, 0, ids_rows) + mod_rows(b, 1, ids_rows)).astype(LOW)
            n1[...] = normed
            n1s[b] = normed[REACH : REACH + rows]
            ua[b] = u[REACH : REACH + rows]
            ia[b] = jnp.broadcast_to(inv[REACH : REACH + rows], (rows, 128))
            yield
            kvext[b, 0:ext, :] = dot(n1[...], wq[:, width : 3 * width]).astype(LOW)
            qb[b] = dot(n1s[b], wq[:, thirds[0]]).astype(LOW)
            yield
            for h in range(HEADS):
                sbuf[h] = dot_nt(qb[b, :, heads[h]], kvext[b, :, heads[h]]) * (score_scale * log2e) + bias[...]
            yield
            for h in range(HEADS):
                s = sbuf[h]
                e = jnp.exp2(s - jnp.max(s, axis=-1, keepdims=True))
                a = e * (1.0 / jnp.sum(e * cnt[...], axis=-1, keepdims=True))
                af[b, h] = a
                ca[b, h] = a.astype(LOW) * few[...]
                if h % 2 == 1:
                    yield
            for h in range(HEADS):
                obs[b, :, heads[h]] = dot(ca[b, h], kvext[b, :, heads_v[h]]).astype(LOW)
            yield

        def forward_second(b):
            x1 = xext[b, own_rows, :].astype(F32) + dot(obs[b], wo[...])
            u, inv = unit(x1)
            ub[b] = u
            ib[b] = jnp.broadcast_to(inv, (rows, 128))
            ids_rows = wide(sel[own_rows, :])
            n2s[b] = (u * mod_rows(b, 2, ids_rows) + mod_rows(b, 3, ids_rows)).astype(LOW)
            tb[...] = x1 + b_down[...]
            yield
            gbuf[...] = dot(n2s[b], wu[...])
            yield
            for gs in tiles:
                gate = gbuf[:, gs] + b_up[:, gs]
                s = 0.5 + 0.5 * jnp.tanh(0.5 * gate)
                hid = gate * s
                fp[b, :, gs] = (s + hid * (1.0 - s)).astype(LOW)
                hs[b, :, gs] = hid.astype(LOW)
                yield
            lo[0, b] = (tb[...] + dot(hs[b], wd[...])).astype(LOW)
            yield

        def relay(b):
            return [
                remote(lo.at[0, b], xext.at[b, own_rows, :], fx_s.at[b, 0], fx_r.at[b, 0], (other, me)),
                remote(lo.at[0, b, pl.ds(0, REACH), :], xext.at[b, top_rows, :], fx_s.at[b, 1], fx_r.at[b, 1], (other, down)),
                remote(lo.at[0, b, pl.ds(rows - REACH, REACH), :], xext.at[b, low_rows, :], fx_s.at[b, 2], fx_r.at[b, 2], (other, up)),
            ]

        def norm_back(d, u, inv, scale):
            scaled = d * scale
            return inv * (
                scaled
                - jnp.mean(scaled, axis=-1, keepdims=True)
                - u * jnp.mean(scaled * u, axis=-1, keepdims=True)
            )

        def mod_sums(b, part, d, u):
            for k, value in enumerate((d * u, d)):
                total = dot(pick[...], value.astype(LOW))
                sm[b, 0 : z.meshes, (part + k) * width : (part + k + 1) * width] = total[0 : z.meshes]

        def halos(b):
            return [
                remote(hsend.at[b, 0], hrecv.at[b, 1], bh_s.at[b, 0], bh_r.at[b, 0], (sec, down)),
                remote(hsend.at[b, 1], hrecv.at[b, 0], bh_s.at[b, 1], bh_r.at[b, 1], (sec, up)),
            ]

        def given(b):
            at = batch_cols(b)
            dr = dybuf[b]
            r_dr[at, :] = dr
            sm[b, 7:8, 0:width] = jnp.sum(dr.astype(F32), axis=0, keepdims=True)
            r_dg[at, :] = dot_nt(dr, wd[...]).astype(LOW)

        def back_ffn(b):
            at = batch_cols(b)
            for gs in tiles:
                dg = r_dg[at, gs].astype(F32) * fp[b, :, gs].astype(F32)
                sm[b, 6:7, gs] = jnp.sum(dg, axis=0, keepdims=True)
                r_dg[at, gs] = dg.astype(LOW)
                yield
            dbuf[...] = dot_nt(r_dg[at, :], wu[...])
            yield

        def back_middle(b):
            at = batch_cols(b)
            ids_rows = wide(sel[own_rows, :])
            d, u = dbuf[...], ub[b]
            grad = dybuf[b].astype(F32) + norm_back(d, u, ib[b][:, 0:1], mod_rows(b, 2, ids_rows))
            dx1[slot(b)] = grad
            r_db[at, :] = grad.astype(LOW)
            yield
            ob[...] = dot_nt(r_db[at, :], wo[...]).astype(LOW)
            mod_sums(b, 2, d, u)
            yield

        def back_attention(b):
            at = batch_cols(b)
            for h in range(HEADS):
                sbuf[h] = dot_nt(ob[:, heads[h]], kvext[b, :, heads_v[h]])
            for h in range(HEADS):
                dv = dot_tn(ca[b, h], ob[:, heads[h]])
                hsend[b, 0, :, heads_v[h]] = dv[0:REACH].astype(LOW)
                dkv[slot(b), :, heads_v[h]] = dv[REACH : REACH + rows]
                hsend[b, 1, :, heads_v[h]] = dv[REACH + rows : ext].astype(LOW)
            yield
            for h in range(HEADS):
                a, da = af[b, h], sbuf[h]
                ds = a * (da - jnp.sum(a * cnt[...] * da, axis=-1, keepdims=True))
                cds[h] = ds.astype(LOW) * few[...]
            yield
            for h in range(HEADS):
                dk = dot_tn(cds[h], qb[b, :, heads[h]]) * score_scale
                hsend[b, 0, :, heads[h]] = dk[0:REACH].astype(LOW)
                dkv[slot(b), :, heads[h]] = dk[REACH : REACH + rows]
                hsend[b, 1, :, heads[h]] = dk[REACH + rows : ext].astype(LOW)
            yield
            for h in range(HEADS):
                r_qkv[at, heads[h]] = (dot(cds[h], kvext[b, :, heads[h]]) * score_scale).astype(LOW)
            yield

        def back_second(b):
            at = batch_cols(b)
            edge = rows - REACH
            dkv[slot(b), 0:REACH, :] += hrecv[b, 0].astype(F32)
            dkv[slot(b), edge:rows, :] += hrecv[b, 1].astype(F32)
            r_qkv[at, width : 3 * width] = dkv[slot(b)].astype(LOW)
            yield
            tb[...] = dot_nt(r_qkv[at, :], wq[...])
            yield
            d, u = tb[...], ua[b]
            ids_rows = wide(sel[own_rows, :])
            grad = dx1[slot(b)] + norm_back(d, u, ia[b][:, 0:1], mod_rows(b, 0, ids_rows))
            ig[0, b] = grad.astype(LOW)
            mod_sums(b, 0, d, u)
            yield

        def relay_back(b):
            return remote(ig.at[0, b], dybuf.at[b], bx_s.at[b], bx_r.at[b], (other, me))

        def take(b):
            @pl.when(sec == 1)
            def _():
                for copy in relay(b):
                    copy.wait_recv()

        def hand(b):
            @pl.when(sec == 0)
            def _():
                for copy in relay(b):
                    copy.start()

        kvext[:, ext:window, :] = jnp.zeros((batches, window - ext, 2 * width), LOW)
        sm[...] = jnp.zeros(sm.shape, F32)
        for copy in loads[1:]:
            copy.wait()
        for copy in (m_down, m_up):
            copy.wait()

        @pl.when(sec == 0)
        def _():
            first_load.wait()
            x_down.wait()
            x_up.wait()

        @pl.when(sec == 1)
        def _():
            last_load.wait()

            @pl.loop(0, batches)
            def _(b):
                given(b)

        take(0)
        weave(forward_first(0))

        @pl.loop(0, batches - 1)
        def _(b):
            take(b + 1)
            weave(forward_second(b), forward_first(b + 1))
            hand(b)

        weave(forward_second(batches - 1))
        hand(batches - 1)

        @pl.when(sec == 0)
        def _():
            lax.fori_loop(0, batches, transposes, 0)

        def bit_of(p, k):
            plain, swapped = z.order(False)[k], z.order(True)[k]
            trades = jnp.minimum(p, 1) - jnp.minimum(lax.div(p, groups), 1)
            return plain + (swapped - plain) * trades

        def piece_copy(p, k):
            return remote(gives[k].at[p], gets[k].at[p], p_s.at[p, k], p_r.at[p, k], (sec, mate(bit_of(p, k))))

        def rows_of(c, size):
            return pl.ds(pl.multiple_of(c * size, size), size)

        def product(kind, c):
            at = rows_of(c, half)
            if kind == "down":
                value = dot(left_t[0:groups, at, :].reshape(groups * half, batches * rows), r_dr[...])
                return [(q, value[q * half : (q + 1) * half]) for q in range(groups)]
            left, right, first = {
                "up": (groups, r_dg, groups),
                "out": (groups + 1, r_db, 2 * groups),
                "qkv": (groups + 2, r_qkv, 2 * groups + 1),
            }[kind]
            value = dot(left_t[left, at, :], right[...])
            return [(first + q, value[:, q * TILE : (q + 1) * TILE]) for q in range(value.shape[1] // TILE)]

        def piece_send(kind):
            for p, value in product(kind, 1 - side(1)):
                gives[0][p] = value.astype(LOW)
                piece_copy(p, 0).start()

        def piece_sum(kind):
            firsts = product(kind, side(1))
            for q, (p, value) in enumerate(firsts):
                mine[q] = value
            for q, (p, _) in enumerate(firsts):
                piece_copy(p, 0).wait_recv()
                hand_on(p, 0, mine[q] + gets[0][p].astype(F32))

        def piece_step(p, k):
            piece_copy(p, k).wait_recv()
            hand_on(p, k, keeps[k - 1][p] + gets[k][p].astype(F32))

        def hand_on(p, k, value):
            size = half >> k
            if k == stages - 1:
                o_piece[p] = value
                return
            here = side(bit_of(p, k + 1))
            acc[0:size, :] = value
            gives[k + 1][p] = acc[rows_of(1 - here, size // 2), :].astype(LOW)
            piece_copy(p, k + 1).start()
            keeps[k][p] = acc[rows_of(here, size // 2), :]

        def arrive(b):
            relay_back(b).wait_recv()
            given(b)

        def send_halos(b):
            for copy in halos(b):
                copy.start()

        def get_halos(b):
            for copy in halos(b):
                copy.wait_recv()

        def send_back(b):
            @pl.when(sec == 1)
            def _():
                relay_back(b).start()

        @pl.when(sec == 0)
        def _():
            arrive(batches - 1)

        weave(back_ffn(batches - 1))
        weave(back_middle(batches - 1))
        weave(back_attention(batches - 1))
        send_halos(batches - 1)

        @pl.loop(0, batches - 2 + sec)
        def _(k):
            b = batches - 2 - k

            @pl.when(sec == 0)
            def _():
                arrive(b)

            get_halos(b + 1)
            weave(back_second(b + 1), back_ffn(b))
            send_back(b + 1)
            weave(back_middle(b))
            weave(back_attention(b))
            send_halos(b)

        @pl.when(sec == 0)
        def _():
            get_halos(1)
            weave(back_second(1))
            arrive(0)
            if z.scatter:
                piece_send("down")
            weave(back_ffn(0))
            if z.scatter:
                piece_sum("down")
                piece_send("up")
            weave(back_middle(0))
            if z.scatter:
                piece_send("out")
            weave(back_attention(0))
            send_halos(0)
            if z.scatter:
                piece_sum("up")
                piece_sum("out")

        get_halos(0)
        weave(back_second(0))
        send_back(0)

        @pl.when(sec == 1)
        def _():
            lax.fori_loop(0, batches, transposes, 0)

        lines = [sm[b, m : m + 1, :] for b in range(batches) for m in range(z.meshes)]
        for line in (6, 7):
            lines.append(sum(sm[b, line : line + 1, :] for b in range(batches)))
        lines.append(jnp.zeros((16 - len(lines), sm.shape[2]), F32))
        small = jnp.concatenate(lines, axis=0)

        def finish():
            @pl.loop(0, batches)
            def _(b):
                @pl.when(sec == 0)
                def _():
                    for copy in relay(b):
                        copy.wait_send()

                @pl.when(sec == 1)
                def _():
                    relay_back(b).wait_send()

                for copy in halos(b):
                    copy.wait_send()

        if not z.scatter:
            small_out[...] = small
            table_out[...] = emb[...]
            finish()
            return

        def ring_copy(k):
            return remote(msend.at[k], mrecv.at[k], m_s.at[k], m_r.at[k], (sec, mate(1 << k)))

        def ring_start(k, value):
            msend[k] = value.astype(LOW)
            ring_copy(k).start()

        def ring_end(k):
            ring_copy(k).wait_recv()
            value = msend[k].astype(F32) + mrecv[k].astype(F32)
            if k + 1 < z.rings:
                ring_start(k + 1, value)
            else:
                tot[...] = value

        ring_start(0, small)

        @pl.when(sec == 1)
        def _():
            piece_send("down")
            piece_send("up")
            piece_sum("down")
            piece_send("out")
            piece_sum("up")
            piece_sum("out")

        piece_send("qkv")
        ring_end(0)
        piece_sum("qkv")

        @pl.loop(0, npiece + 2 * stages - 4)
        def _(p):
            for k in range(1, stages):
                lag = 2 * (k - 1)

                @pl.when((p >= lag) & (p < npiece + lag))
                def _(k=k, lag=lag):
                    piece_step(p - lag, k)

            for k in range(1, z.rings):

                @pl.when(p == 2 * k)
                def _(k=k):
                    ring_end(k)

        count = batches * z.meshes
        table = emb[pl.ds(pl.multiple_of(me * own, own), own), :]
        grad = jnp.zeros((own, 4 * width), F32)
        for k in range(count):
            grad = grad + table[:, k : k + 1] * tot[k : k + 1, :]
        o_mod[0] = grad
        cols = 4 * width // shards
        owned = tot[:, pl.ds(pl.multiple_of(me * cols, cols), cols)]
        o_line[0:1, :] = jnp.sum(owned[0:count], axis=0, keepdims=True)
        o_line[1:2, :] = owned[count : count + 1]
        ratio = 128 // own
        line = tot[:, pl.ds(pl.multiple_of(me // ratio * 128, 128), 128)][count + 1 : count + 2]
        value = line
        for k in range(1, ratio):
            turned = jnp.concatenate([line[:, k * own :], line[:, : k * own]], axis=1)
            value = jnp.where(me % ratio == k, turned, value)
        o_line[2:3, :] = value
        finish()

        @pl.loop(0, npiece)
        def _(p):
            for k in range(stages):
                piece_copy(p, k).wait_send()

        for k in range(z.rings):
            ring_copy(k).wait_send()

    return kernel


def layout_of(z):
    own, groups = z.own, z.groups

    def kernel(
        lo, ig, piece, mod, line,
        o_lo, o_ig, o_qkv, o_out, o_up, o_upb, o_down, o_downb, o_mod, o_modb,
        v_lo, v_ig, v_piece, v_mod, into, back,
    ):
        moves = [(lo, v_lo, o_lo), (ig, v_ig, o_ig)]
        targets = [o_down.at[0, pl.ds(q * own, own), :] for q in range(groups)]
        targets += [o_up.at[0, :, pl.ds(q * TILE, TILE)] for q in range(groups)]
        targets += [o_out.at[0]] + [o_qkv.at[0, :, pl.ds(q * TILE, TILE)] for q in range(3)]
        moves += [(piece.at[k], v_piece.at[k], target) for k, target in enumerate(targets)]
        moves += [(mod, v_mod, o_mod)]
        firsts = [pltpu.make_async_copy(a, b, into.at[k]) for k, (a, b, _) in enumerate(moves)]
        lasts = [pltpu.make_async_copy(b, c, back.at[k]) for k, (_, b, c) in enumerate(moves)]
        for copy in firsts:
            copy.start()
        o_modb[...] = line[0:1, :]
        o_upb[...] = line[1:2, :]
        o_downb[...] = line[2:3, 0:own]
        for first, last in zip(firsts, lasts):
            first.wait()
            last.start()
        for copy in lasts:
            copy.wait()

    return kernel


def body(
    inputs,
    cotangent,
    neighbours,
    mesh_ids,
    noise_sigma,
    w_qkv,
    w_out,
    w_up,
    b_up,
    w_down,
    b_down,
    w_mod,
    b_mod,
):
    shards = lax.axis_size("nodes")
    z = Sizes(inputs, neighbours, noise_sigma, w_up, shards)
    batches, rows, width, hidden = z.batches, z.rows, z.width, z.hidden
    own, npiece = z.own, z.pieces
    shape = jax.ShapeDtypeStruct
    stack = shape((1, batches, rows, width), LOW)
    outs = [stack, stack]
    sides = [(z.lefts, TILE, batches * rows)]
    sides += [(batches * rows, columns) for columns in (width, hidden, width, 3 * width)]
    if z.scatter:
        outs += [shape((npiece, own, TILE), F32), shape((1, own, 4 * width), F32), shape((8, 128), F32)]
        scratch = [pltpu.VMEM(side, LOW) for side in sides]
    else:
        outs += [shape(side, LOW) for side in sides] + [shape((16, hidden), F32), shape((width, 128), F32)]
        scratch = []
    dma = pltpu.SemaphoreType.DMA
    scratch += [
        pltpu.VMEM((width, 3 * width), LOW),
        pltpu.VMEM((width, width), LOW),
        pltpu.VMEM((width, hidden), LOW),
        pltpu.VMEM((hidden, width), LOW),
        pltpu.VMEM((width, 4 * width), LOW),
        pltpu.VMEM((batches, z.ext, width), LOW),
        pltpu.VMEM((batches, rows, width), LOW),
        pltpu.VMEM((z.ext, 128), F32),
        pltpu.VMEM((16, rows), LOW),
        pltpu.VMEM((rows, z.window), F32),
        pltpu.VMEM((rows, z.window), LOW),
        pltpu.VMEM((rows, z.window), F32),
        pltpu.VMEM((batches, 8, 4 * width), F32),
        pltpu.VMEM((width, 128), F32),
        pltpu.VMEM((z.ext, width), LOW),
        pltpu.VMEM((batches, rows, width), LOW),
        pltpu.VMEM((batches, rows, width), F32),
        pltpu.VMEM((batches, rows, 128), F32),
        pltpu.VMEM((batches, rows, width), LOW),
        pltpu.VMEM((batches, z.window, 2 * width), LOW),
        pltpu.VMEM((HEADS, rows, z.window), F32),
        pltpu.VMEM((batches, HEADS, rows, z.window), F32),
        pltpu.VMEM((batches, HEADS, rows, z.window), LOW),
        pltpu.VMEM((batches, rows, width), LOW),
        pltpu.VMEM((batches, rows, width), LOW),
        pltpu.VMEM((batches, rows, width), F32),
        pltpu.VMEM((batches, rows, 128), F32),
        pltpu.VMEM((rows, width), F32),
        pltpu.VMEM((rows, hidden), F32),
        pltpu.VMEM((batches, rows, hidden), LOW),
        pltpu.VMEM((batches, rows, hidden), LOW),
        pltpu.VMEM((rows, width), LOW),
        pltpu.VMEM((rows, width), F32),
        pltpu.VMEM((HEADS, rows, z.window), LOW),
        pltpu.VMEM((2, rows, width), F32),
        pltpu.VMEM((2, rows, 2 * width), F32),
        pltpu.VMEM((batches, 2, REACH, 2 * width), LOW),
        pltpu.VMEM((batches, 2, REACH, 2 * width), LOW),
        pltpu.VMEM((batches, 8, hidden), F32),
        dma((7,)),
        dma((2,)),
        dma((2,)),
        dma((2,)),
        dma((2,)),
        dma((batches, 3)),
        dma((batches, 3)),
        dma((batches, 2)),
        dma((batches, 2)),
        dma((batches,)),
        dma((batches,)),
    ]
    if z.scatter:
        stages = len(z.bits)
        sizes = [TILE >> (k + 1) for k in range(stages)]
        scratch += [pltpu.VMEM((npiece, size, TILE), LOW) for size in sizes + sizes]
        scratch += [pltpu.VMEM((npiece, size, TILE), F32) for size in sizes[1:]]
        scratch += [
            pltpu.VMEM((z.groups, sizes[0], TILE), F32),
            pltpu.VMEM((sizes[0], TILE), F32),
            pltpu.VMEM((z.rings, 16, hidden), LOW),
            pltpu.VMEM((z.rings, 16, hidden), LOW),
            pltpu.VMEM((16, hidden), F32),
            dma((npiece, stages)),
            dma((npiece, stages)),
            dma((z.rings,)),
            dma((z.rings,)),
        ]
    hbm = pl.BlockSpec(memory_space=pl.ANY)
    vmem = pl.BlockSpec(memory_space=pltpu.VMEM)
    smem = pl.BlockSpec(memory_space=pltpu.SMEM)
    got = pl.pallas_call(
        kernel_of(z),
        out_shape=outs,
        in_specs=[hbm, hbm, vmem, vmem, smem, hbm, hbm, hbm, vmem, hbm, vmem, hbm, vmem],
        out_specs=[vmem] * len(outs),
        scratch_shapes=scratch,
        compiler_params=pltpu.CompilerParams(
            collective_id=0, has_side_effects=True, vmem_limit_bytes=63 * 2**20
        ),
    )(
        inputs,
        cotangent,
        neighbours.T,
        mesh_ids.reshape(1, rows),
        noise_sigma.T,
        w_qkv,
        w_out,
        w_up,
        b_up,
        w_down,
        b_down,
        w_mod,
        b_mod,
    )
    if z.scatter:
        lo, ig, piece, mod, line = got
        return tuple(
            pl.pallas_call(
                layout_of(z),
                out_shape=[
                    stack,
                    stack,
                    shape((1, own, 3 * width), F32),
                    shape((1, own, width), F32),
                    shape((1, own, hidden), F32),
                    shape((1, hidden // shards), F32),
                    shape((1, hidden // shards, width), F32),
                    shape((1, own), F32),
                    shape((1, own, 4 * width), F32),
                    shape((1, 4 * width // shards), F32),
                ],
                in_specs=[hbm, hbm, hbm, hbm, vmem],
                out_specs=[hbm, hbm, hbm, hbm, hbm, vmem, hbm, vmem, hbm, vmem],
                scratch_shapes=[
                    pltpu.VMEM(stack.shape, LOW),
                    pltpu.VMEM(stack.shape, LOW),
                    pltpu.VMEM((npiece, own, TILE), F32),
                    pltpu.VMEM((1, own, 4 * width), F32),
                    dma((npiece + 3,)),
                    dma((npiece + 3,)),
                ],
                compiler_params=pltpu.CompilerParams(vmem_limit_bytes=63 * 2**20),
            )(lo, ig, piece, mod, line)
        )
    lo, ig, left_t, r_dr, r_dg, r_db, r_qkv, small, table = got
    groups = z.groups

    def summed(value):
        return lax.psum_scatter(value, "nodes", scatter_dimension=0, tiled=True)

    def local_sum(left, right):
        return summed(dot(left_t[left], right))[None]

    down = [dot(left_t[q], r_dr).reshape(TILE // 32, 32, TILE) for q in range(groups)]
    down = jnp.stack(down, axis=1)
    count = batches * z.meshes
    small = lax.psum(small, "nodes")
    me = lax.axis_index("nodes")
    mod = jnp.dot(table[:, :count], small[:count], precision=lax.Precision.HIGHEST)

    def mine(value):
        size = value.shape[0] // shards
        return lax.dynamic_slice_in_dim(value, me * size, size, axis=0)[None]

    return (
        lo,
        ig,
        local_sum(groups + 2, r_qkv),
        local_sum(groups + 1, r_db),
        local_sum(groups, r_dg),
        mine(small[count]),
        summed(down.reshape(hidden, width))[None],
        mine(small[count + 1, :width]),
        mine(mod),
        mine(jnp.sum(small[:count], axis=0)),
    )


def solution(mesh):
    return jax.shard_map(
        body,
        mesh=mesh,
        in_specs=(
            P(None, "nodes", None),
            P(None, "nodes", None),
            P("nodes", None),
            P("nodes"),
            P(),
            P("section", None, None),
            P("section", None, None),
            P("section", None, None),
            P("section", None),
            P("section", None, None),
            P("section", None),
            P("section", None, None),
            P("section", None),
        ),
        out_specs=(
            P("section", None, "nodes", None),
            P("section", None, "nodes", None),
            P("section", "nodes", None),
            P("section", "nodes", None),
            P("section", "nodes", None),
            P("section", "nodes"),
            P("section", "nodes", None),
            P("section", "nodes"),
            P("section", "nodes", None),
            P("section", "nodes"),
        ),
        check_vma=False,
    )
```

```python
import jax
import jax.numpy as jnp
from jax import lax
from jax.experimental import pallas as pl
from jax.experimental.pallas import tpu as pltpu
from jax.sharding import PartitionSpec as P

HEADS = 4
REACH = 32
EPSILON = 1e-06
MASKED = -1e9
ABSENT = -2e38
TILE = 512
MESH = pl.DeviceIdType.MESH
F32, LOW = jnp.float32, jnp.bfloat16


def dot(a, b):
    return lax.dot_general(a, b, (((1,), (0,)), ((), ())), preferred_element_type=F32)


def dot_nt(a, b):
    return lax.dot_general(a, b, (((1,), (1,)), ((), ())), preferred_element_type=F32)


def dot_tn(a, b):
    return lax.dot_general(a, b, (((0,), (0,)), ((), ())), preferred_element_type=F32)


class Sizes:
    def __init__(self, inputs, neighbours, noise, w_up, shards):
        self.batches, self.rows, self.width = inputs.shape
        self.slots = neighbours.shape[1]
        self.meshes = noise.shape[1]
        self.hidden = w_up.shape[2]
        self.shards = shards
        self.ext = self.rows + 2 * REACH
        self.window = (self.ext // 128 + 1) * 128
        self.groups = self.hidden // TILE
        self.own = self.width // shards
        self.scatter = self.own % 16 == 0
        self.pieces = 2 * self.groups + 4
        self.lefts = 3 + self.groups
        self.rights = 2 + self.groups + 3
        self.rings = max(shards.bit_length() - 1, 1)

        self.bits = [1 << k for k in range(shards.bit_length() - 1)]

    def left(self, p):
        n = self.groups
        return jnp.minimum(p, n) + lax.div(p, 2 * n) + lax.div(p, 2 * n + 1)

    def order(self, swapped):
        bits = list(self.bits)
        if swapped and len(bits) > 2:
            bits[1], bits[2] = bits[2], bits[1]
        return bits

    def right(self, p):
        return jnp.maximum(p - (self.groups - 1), 0)


def weave(*chains):
    chains = list(chains)
    while chains:
        for chain in list(chains):
            try:
                next(chain)
            except StopIteration:
                chains.remove(chain)


def kernel_of(z):
    batches, rows, width, ext, window = z.batches, z.rows, z.width, z.ext, z.window
    groups, shards, own = z.groups, z.shards, z.own
    head = width // HEADS
    score_scale = head ** (-0.5)
    log2e = 1.4426950408889634
    npiece = z.pieces
    half = TILE // 2
    stages = len(z.bits)
    g_out, g_q, g_k = 1 + groups, 2 + groups, 3 + groups

    def position(owner, first):
        if not z.scatter:
            return owner
        place = 0
        for bit in z.order(1 <= first < groups):
            place = 2 * place + owner // bit % 2
        return place

    def kernel(
        inputs, cotangent, neighbours, mesh_ids, sigma,
        w_qkv, w_out, w_up, b_up, w_down, b_down, w_mod, b_mod,
        lo, ig, *rest,
    ):
        if z.scatter:
            o_piece, o_mod, o_line, left_t, right_t = rest[:5]
            rest = rest[5:]
        else:
            left_t, right_t, small_out, table_out = rest[:4]
            rest = rest[4:]
        (
            wq, wo, wu, wd, wm, xext, dybuf, sel, pick, cnt, few, bias, mod, emb,
            n1, n1s, ua, ia, qb, kvext, sbuf, af, ca, obs, n2s, ub, ib, tb, fp, hs,
            ob, dbuf, cds, dx1, dkv, hsend, hrecv, sm,
            lsem, hx_s, hx_r, hm_s, hm_r, fx_s, fx_r, bh_s, bh_r, bx_s, bx_r,
        ) = rest[:49]
        rest = rest[49:]
        if z.scatter:
            gives, gets, keeps = rest[:stages], rest[stages : 2 * stages], rest[2 * stages : 3 * stages - 1]
            acc, msend, mrecv, tot, p_s, p_r, m_s, m_r = rest[3 * stages - 1 :]

        sec = lax.axis_index("section")
        me = lax.axis_index("nodes")
        up = lax.rem(me + 1, shards)
        down = lax.rem(me + shards - 1, shards)
        other = 1 - sec

        def local(src, dst, k):
            return pltpu.make_async_copy(src, dst, lsem.at[k])

        loads = [
            local(w_mod.at[0], wm, 0),
            local(w_qkv.at[0], wq, 1),
            local(w_out.at[0], wo, 2),
            local(w_up.at[0], wu, 3),
            local(w_down.at[0], wd, 4),
        ]
        own_rows = pl.ds(REACH, rows)
        first_load = local(inputs, xext.at[:, own_rows, :], 5)
        last_load = local(cotangent, dybuf, 6)
        loads[0].start()

        @pl.when(sec == 0)
        def _():
            first_load.start()

        for copy in loads[1:]:
            copy.start()

        @pl.when(sec == 1)
        def _():
            last_load.start()

        def side(bit):
            return lax.rem(lax.div(me, bit), 2)

        def mate(bit):
            return me + bit - 2 * bit * side(bit)

        barrier = pltpu.get_barrier_semaphore()
        mates = [(sec, up), (sec, down), (other, me), (other, up), (other, down)]
        if z.scatter:
            mates += [(sec, mate(bit)) for bit in z.bits[1:]]
        for peer in mates:
            pl.semaphore_signal(barrier, inc=1, device_id=peer, device_id_type=MESH)
        pl.semaphore_wait(barrier, len(mates))

        def remote(src, dst, s_sem, r_sem, peer):
            return pltpu.make_async_remote_copy(
                src_ref=src, dst_ref=dst, send_sem=s_sem, recv_sem=r_sem, device_id=peer, device_id_type=MESH
            )

        low_rows, top_rows = pl.ds(0, REACH), pl.ds(REACH + rows, REACH)
        head_rows, tail_rows = pl.ds(REACH, REACH), pl.ds(rows, REACH)
        x_down = remote(inputs.at[:, pl.ds(0, REACH), :], xext.at[:, top_rows, :], hx_s.at[0], hx_r.at[0], (sec, down))
        x_up = remote(inputs.at[:, pl.ds(rows - REACH, REACH), :], xext.at[:, low_rows, :], hx_s.at[1], hx_r.at[1], (sec, up))

        @pl.when(sec == 0)
        def _():
            x_down.start()
            x_up.start()

        ids = jnp.broadcast_to(mesh_ids[...].astype(F32), (128, rows))
        sel[own_rows, :] = ids.T
        m_down = remote(sel.at[head_rows, :], sel.at[top_rows, :], hm_s.at[0], hm_r.at[0], (sec, down))
        m_up = remote(sel.at[tail_rows, :], sel.at[low_rows, :], hm_s.at[1], hm_r.at[1], (sec, up))
        m_down.start()
        m_up.start()
        sample = lax.broadcasted_iota(jnp.int32, (16, rows), 0).astype(F32)
        pick[...] = jnp.where(ids[0:16] == sample, 1.0, 0.0).astype(LOW)

        row_no = lax.broadcasted_iota(jnp.int32, (16, width // 2), 0)
        level = jnp.ones((16, width // 2), F32)
        for b in range(batches):
            for m in range(z.meshes):
                level = jnp.where(row_no == b * z.meshes + m, sigma[m, b], level)
        place = lax.broadcasted_iota(jnp.int32, (16, width // 2), 1).astype(F32)
        frequency = 3.0 * jnp.exp(-jnp.log(100.0) * place / (width // 2))
        angles = jnp.log(level) * frequency
        embedded = jnp.concatenate([jnp.sin(angles), jnp.cos(angles)], axis=1).astype(LOW)
        padded = jnp.concatenate([embedded.astype(F32), jnp.zeros((112, width), F32)], axis=0)
        emb[...] = padded.T
        loads[0].wait()
        for g in range(4):
            cols = pl.ds(g * width, width)
            table = dot(embedded, wm[:, cols]) + b_mod[:, cols] + (1.0 - g % 2)
            for b in range(batches):
                mod[b, 0 : z.meshes, cols] = table[b * z.meshes : (b + 1) * z.meshes]

        slots = neighbours[...].astype(F32)
        slots = jnp.concatenate([slots, jnp.zeros((128 - z.slots, rows), F32)], axis=0).T
        slots = jnp.where(slots >= 0, slots - (me * rows - REACH).astype(F32), float(ext))
        column = lax.broadcasted_iota(jnp.int32, (rows, window), 1).astype(F32)
        counts = jnp.zeros((rows, window), F32)
        for n in range(z.slots):
            counts = counts + jnp.where(slots[:, n : n + 1] == column, 1.0, 0.0)
        cnt[...] = counts
        few[...] = counts.astype(LOW)
        bias[...] = jnp.where(counts > 0, jnp.where(column == ext, MASKED * log2e, 0.0), ABSENT)

        def mod_rows(b, part, ids_rows):
            cols = pl.ds(part * width, width)
            value = jnp.broadcast_to(mod[b, 0:1, cols], (ids_rows.shape[0], width))
            for m in range(1, z.meshes):
                value = jnp.where(ids_rows > m - 0.5, mod[b, m : m + 1, cols], value)
            return value

        def wide(ids_rows):
            return jnp.concatenate([ids_rows] * (width // 128), axis=1)

        def unit(x):
            centred = x - jnp.mean(x, axis=-1, keepdims=True)
            inv = lax.rsqrt(jnp.mean(centred * centred, axis=-1, keepdims=True) + EPSILON)
            return centred * inv, inv

        def batch_cols(b):
            return pl.ds(b * rows, rows) if isinstance(b, int) else pl.ds(pl.multiple_of(b * rows, rows), rows)

        span = own if z.scatter else 32

        def transposes(b, carry):
            for first, ref in ((groups, n2s), (groups + 1, obs), (groups + 2, n1s)):
                turned = ref[b].T
                for owner in range(TILE // span):
                    at = position(owner, first) * span
                    left_t[first, at : at + span, batch_cols(b)] = turned[owner * span : (owner + 1) * span]
            run = groups * span
            for g in range(groups):
                turned = hs[b, :, g * TILE : (g + 1) * TILE].T
                for k in range(TILE // span):
                    at = g * TILE + k * span
                    owner, part = at // run, at % run // span
                    to = position(owner, part) * span
                    left_t[part, to : to + span, batch_cols(b)] = turned[k * span : (k + 1) * span]
            return carry

        heads = [slice(h * head, (h + 1) * head) for h in range(HEADS)]
        heads_v = [slice(width + h * head, width + (h + 1) * head) for h in range(HEADS)]
        tiles = [slice(g * TILE, (g + 1) * TILE) for g in range(groups)]
        thirds = [slice(g * width, (g + 1) * width) for g in range(3)]

        def forward_first(b):
            ids_rows = wide(sel[0:ext, :])
            u, inv = unit(xext[b].astype(F32))
            normed = (u * mod_rows(b, 0, ids_rows) + mod_rows(b, 1, ids_rows)).astype(LOW)
            n1[...] = normed
            n1s[b] = normed[REACH : REACH + rows]
            ua[b] = u[REACH : REACH + rows]
            ia[b] = jnp.broadcast_to(inv[REACH : REACH + rows], (rows, 128))
            yield
            kvext[b, 0:ext, thirds[0]] = dot(n1[...], wq[:, thirds[1]]).astype(LOW)
            qb[b] = dot(n1s[b], wq[:, thirds[0]]).astype(LOW)
            yield
            for h in range(HEADS):
                sbuf[h] = dot_nt(qb[b, :, heads[h]], kvext[b, :, heads[h]]) * (score_scale * log2e) + bias[...]
            kvext[b, 0:ext, thirds[1]] = dot(n1[...], wq[:, thirds[2]]).astype(LOW)
            yield
            for h in range(HEADS):
                s = sbuf[h]
                e = jnp.exp2(s - jnp.max(s, axis=-1, keepdims=True))
                a = e * (1.0 / jnp.sum(e * cnt[...], axis=-1, keepdims=True))
                af[b, h] = a
                ca[b, h] = a.astype(LOW) * few[...]
                if h % 2 == 1:
                    yield
            for h in range(HEADS):
                obs[b, :, heads[h]] = dot(ca[b, h], kvext[b, :, heads_v[h]]).astype(LOW)
            yield

        def forward_second(b):
            x1 = xext[b, own_rows, :].astype(F32) + dot(obs[b], wo[...])
            u, inv = unit(x1)
            ub[b] = u
            ib[b] = jnp.broadcast_to(inv, (rows, 128))
            ids_rows = wide(sel[own_rows, :])
            n2s[b] = (u * mod_rows(b, 2, ids_rows) + mod_rows(b, 3, ids_rows)).astype(LOW)
            tb[...] = x1 + b_down[...]
            yield
            for gs in tiles:
                gate = dot(n2s[b], wu[:, gs]) + b_up[:, gs]
                s = 0.5 + 0.5 * jnp.tanh(0.5 * gate)
                hid = gate * s
                fp[b, :, gs] = (s + hid * (1.0 - s)).astype(LOW)
                hid = hid.astype(LOW)
                hs[b, :, gs] = hid
                tb[...] += dot(hid, wd[gs, :])
                yield
            lo[0, b] = tb[...].astype(LOW)
            yield

        def relay(b):
            return [
                remote(lo.at[0, b], xext.at[b, own_rows, :], fx_s.at[b, 0], fx_r.at[b, 0], (other, me)),
                remote(lo.at[0, b, pl.ds(0, REACH), :], xext.at[b, top_rows, :], fx_s.at[b, 1], fx_r.at[b, 1], (other, down)),
                remote(lo.at[0, b, pl.ds(rows - REACH, REACH), :], xext.at[b, low_rows, :], fx_s.at[b, 2], fx_r.at[b, 2], (other, up)),
            ]

        def norm_back(d, u, inv, scale):
            scaled = d * scale
            return inv * (
                scaled
                - jnp.mean(scaled, axis=-1, keepdims=True)
                - u * jnp.mean(scaled * u, axis=-1, keepdims=True)
            )

        def mod_sums(b, part, d, u):
            for k, value in enumerate((d * u, d)):
                total = dot(pick[...], value.astype(LOW))
                sm[b, 0 : z.meshes, (part + k) * width : (part + k + 1) * width] = total[0 : z.meshes]

        def halos(b):
            return [
                remote(hsend.at[b, 0], hrecv.at[b, 1], bh_s.at[b, 0], bh_r.at[b, 0], (sec, down)),
                remote(hsend.at[b, 1], hrecv.at[b, 0], bh_s.at[b, 1], bh_r.at[b, 1], (sec, up)),
            ]

        def given(b):
            at = batch_cols(b)
            dr = dybuf[b]
            right_t[0, at, :] = dr
            sm[b, 7:8, 0:width] = jnp.sum(dr.astype(F32), axis=0, keepdims=True)
            for g in range(groups):
                right_t[1 + g, at, :] = dot_nt(dr, wd[tiles[g], :]).astype(LOW)

        def back_ffn(b):
            at = batch_cols(b)
            for g in range(groups):
                gs = tiles[g]
                dg = right_t[1 + g, at, :].astype(F32) * fp[b, :, gs].astype(F32)
                sm[b, 6:7, gs] = jnp.sum(dg, axis=0, keepdims=True)
                dg = dg.astype(LOW)
                right_t[1 + g, at, :] = dg
                part = dot_nt(dg, wu[:, gs])
                if g == 0:
                    dbuf[...] = part
                else:
                    dbuf[...] += part
                yield

        def back_middle(b):
            at = batch_cols(b)
            ids_rows = wide(sel[own_rows, :])
            d, u = dbuf[...], ub[b]
            grad = dybuf[b].astype(F32) + norm_back(d, u, ib[b][:, 0:1], mod_rows(b, 2, ids_rows))
            dx1[b] = grad
            right_t[g_out, at, :] = grad.astype(LOW)
            yield
            ob[...] = dot_nt(right_t[g_out, at, :], wo[...]).astype(LOW)
            mod_sums(b, 2, d, u)
            yield

        def back_attention(b):
            at = batch_cols(b)
            for h in range(HEADS):
                sbuf[h] = dot_nt(ob[:, heads[h]], kvext[b, :, heads_v[h]])
            for h in range(HEADS):
                dv = dot_tn(ca[b, h], ob[:, heads[h]])
                hsend[b, 0, :, heads_v[h]] = dv[0:REACH].astype(LOW)
                dkv[b, :, heads_v[h]] = dv[REACH : REACH + rows]
                hsend[b, 1, :, heads_v[h]] = dv[REACH + rows : ext].astype(LOW)
            yield
            for h in range(HEADS):
                a, da = af[b, h], sbuf[h]
                ds = a * (da - jnp.sum(a * cnt[...] * da, axis=-1, keepdims=True))
                cds[h] = ds.astype(LOW) * few[...]
            yield
            for h in range(HEADS):
                dk = dot_tn(cds[h], qb[b, :, heads[h]]) * score_scale
                hsend[b, 0, :, heads[h]] = dk[0:REACH].astype(LOW)
                dkv[b, :, heads[h]] = dk[REACH : REACH + rows]
                hsend[b, 1, :, heads[h]] = dk[REACH + rows : ext].astype(LOW)
            yield
            for h in range(HEADS):
                right_t[g_q, at, heads[h]] = (dot(cds[h], kvext[b, :, heads[h]]) * score_scale).astype(LOW)
            yield

        def back_second(b):
            at = batch_cols(b)
            edge = rows - REACH
            dkv[b, 0:REACH, :] += hrecv[b, 0].astype(F32)
            dkv[b, edge:rows, :] += hrecv[b, 1].astype(F32)
            for g in range(2):
                right_t[g_k + g, at, :] = dkv[b, :, thirds[g]].astype(LOW)
            yield
            d = dot_nt(right_t[g_q, at, :], wq[:, thirds[0]])
            for g in range(2):
                d = d + dot_nt(right_t[g_k + g, at, :], wq[:, thirds[g + 1]])
            tb[...] = d
            yield
            d, u = tb[...], ua[b]
            ids_rows = wide(sel[own_rows, :])
            grad = dx1[b] + norm_back(d, u, ia[b][:, 0:1], mod_rows(b, 0, ids_rows))
            ig[0, b] = grad.astype(LOW)
            mod_sums(b, 0, d, u)
            yield

        def relay_back(b):
            return remote(ig.at[0, b], dybuf.at[b], bx_s.at[b], bx_r.at[b], (other, me))

        def take(b):
            @pl.when(sec == 1)
            def _():
                for copy in relay(b):
                    copy.wait_recv()

        def hand(b):
            @pl.when(sec == 0)
            def _():
                for copy in relay(b):
                    copy.start()

        kvext[:, ext:window, :] = jnp.zeros((batches, window - ext, 2 * width), LOW)
        sm[...] = jnp.zeros(sm.shape, F32)
        for copy in loads[1:]:
            copy.wait()
        for copy in (m_down, m_up):
            copy.wait()

        @pl.when(sec == 0)
        def _():
            first_load.wait()
            x_down.wait()
            x_up.wait()

        @pl.when(sec == 1)
        def _():
            last_load.wait()

            @pl.loop(0, batches)
            def _(b):
                given(b)

        take(0)
        weave(forward_first(0))

        @pl.loop(0, batches - 1)
        def _(b):
            take(b + 1)
            weave(forward_second(b), forward_first(b + 1))
            hand(b)

        weave(forward_second(batches - 1))
        hand(batches - 1)

        @pl.when(sec == 0)
        def _():
            lax.fori_loop(0, batches, transposes, 0)

        def bit_of(p, k):
            plain, swapped = z.order(False)[k], z.order(True)[k]
            trades = jnp.minimum(p, 1) - jnp.minimum(lax.div(p, groups), 1)
            return plain + (swapped - plain) * trades

        parts = [4, 2] + [1] * stages

        def piece_copies(p, k):
            size = (half >> k) // parts[k]
            peer = (sec, mate(bit_of(p, k)))
            return [
                remote(
                    gives[k].at[p, pl.ds(j * size, size), :],
                    gets[k].at[p, pl.ds(j * size, size), :],
                    p_s.at[p, k, j],
                    p_r.at[p, k, j],
                    peer,
                )
                for j in range(parts[k])
            ]

        def piece_begin(p, k):
            for copy in piece_copies(p, k):
                copy.start()

        def rows_of(c, size):
            return pl.ds(pl.multiple_of(c * size, size), size)

        def piece_start(p):
            away = 1 - side(1)
            gives[0][p] = dot(left_t[z.left(p), rows_of(away, half), :], right_t[z.right(p)]).astype(LOW)
            piece_begin(p, 0)

        def piece_step(p, k):
            size = half >> k
            if k == 0:
                mine = dot(left_t[z.left(p), rows_of(side(1), half), :], right_t[z.right(p)])
            else:
                mine = keeps[k - 1][p]
            for copy in piece_copies(p, k):
                copy.wait_recv()
            value = mine + gets[k][p].astype(F32)
            if k == stages - 1:
                o_piece[p] = value
                return
            here = side(bit_of(p, k + 1))
            acc[0:size, :] = value
            gives[k + 1][p] = acc[rows_of(1 - here, size // 2), :].astype(LOW)
            piece_begin(p, k + 1)
            keeps[k][p] = acc[rows_of(here, size // 2), :]

        def pieces(first, last, step=None):
            @pl.loop(first, last)
            def _(p):
                if step is None:
                    piece_start(p)
                else:
                    piece_step(p, step)

        early = 2 * groups + 1

        def arrive(b):
            relay_back(b).wait_recv()
            given(b)

        def send_halos(b):
            for copy in halos(b):
                copy.start()

        def get_halos(b):
            for copy in halos(b):
                copy.wait_recv()

        def send_back(b):
            @pl.when(sec == 1)
            def _():
                relay_back(b).start()

        @pl.when(sec == 0)
        def _():
            arrive(batches - 1)

        weave(back_ffn(batches - 1))
        weave(back_middle(batches - 1))
        weave(back_attention(batches - 1))
        send_halos(batches - 1)

        @pl.loop(0, batches - 2 + sec)
        def _(k):
            b = batches - 2 - k

            @pl.when(sec == 0)
            def _():
                arrive(b)

            get_halos(b + 1)
            weave(back_second(b + 1), back_ffn(b))
            send_back(b + 1)
            weave(back_middle(b))
            weave(back_attention(b))
            send_halos(b)

        @pl.when(sec == 0)
        def _():
            get_halos(1)
            weave(back_second(1))
            arrive(0)
            if z.scatter:
                pieces(0, groups)
            weave(back_ffn(0))
            if z.scatter:
                pieces(0, groups, 0)
                pieces(groups, 2 * groups)
            weave(back_middle(0))
            if z.scatter:
                pieces(2 * groups, early)
            weave(back_attention(0))
            send_halos(0)
            if z.scatter:
                pieces(groups, early, 0)

        get_halos(0)
        weave(back_second(0))
        send_back(0)

        @pl.when(sec == 1)
        def _():
            lax.fori_loop(0, batches, transposes, 0)

        lines = [sm[b, m : m + 1, :] for b in range(batches) for m in range(z.meshes)]
        for line in (6, 7):
            lines.append(sum(sm[b, line : line + 1, :] for b in range(batches)))
        lines.append(jnp.zeros((16 - len(lines), sm.shape[2]), F32))
        small = jnp.concatenate(lines, axis=0)

        def finish():
            @pl.loop(0, batches)
            def _(b):
                @pl.when(sec == 0)
                def _():
                    for copy in relay(b):
                        copy.wait_send()

                @pl.when(sec == 1)
                def _():
                    relay_back(b).wait_send()

                for copy in halos(b):
                    copy.wait_send()

        if not z.scatter:
            small_out[...] = small
            table_out[...] = emb[...]
            finish()
            return

        def ring_copy(k):
            return remote(msend.at[k], mrecv.at[k], m_s.at[k], m_r.at[k], (sec, mate(1 << k)))

        def ring_start(k, value):
            msend[k] = value.astype(LOW)
            ring_copy(k).start()

        def ring_end(k):
            ring_copy(k).wait_recv()
            value = msend[k].astype(F32) + mrecv[k].astype(F32)
            if k + 1 < z.rings:
                ring_start(k + 1, value)
            else:
                tot[...] = value

        ring_start(0, small)
        begun = (1 - sec) * early

        @pl.loop(0, npiece + 2 * stages - 1)
        def _(p):
            @pl.when((p >= begun) & (p < npiece))
            def _():
                piece_start(p)

            for k in range(stages):
                lag = 2 * k + 1
                first = begun + lag if k == 0 else lag

                @pl.when((p >= first) & (p < npiece + lag))
                def _(k=k, lag=lag):
                    piece_step(p - lag, k)

            for k in range(z.rings):

                @pl.when(p == 2 + 2 * k)
                def _(k=k):
                    ring_end(k)

        count = batches * z.meshes
        table = emb[pl.ds(pl.multiple_of(me * own, own), own), :]
        grad = jnp.zeros((own, 4 * width), F32)
        for k in range(count):
            grad = grad + table[:, k : k + 1] * tot[k : k + 1, :]
        o_mod[0] = grad
        cols = 4 * width // shards
        mine = tot[:, pl.ds(pl.multiple_of(me * cols, cols), cols)]
        o_line[0:1, :] = jnp.sum(mine[0:count], axis=0, keepdims=True)
        o_line[1:2, :] = mine[count : count + 1]
        ratio = 128 // own
        line = tot[:, pl.ds(pl.multiple_of(me // ratio * 128, 128), 128)][count + 1 : count + 2]
        value = line
        for k in range(1, ratio):
            turned = jnp.concatenate([line[:, k * own :], line[:, : k * own]], axis=1)
            value = jnp.where(me % ratio == k, turned, value)
        o_line[2:3, :] = value
        finish()

        @pl.loop(0, npiece)
        def _(p):
            for k in range(stages):
                for copy in piece_copies(p, k):
                    copy.wait_send()

        for k in range(z.rings):
            ring_copy(k).wait_send()

    return kernel


def layout_of(z):
    own, groups = z.own, z.groups

    def kernel(
        lo, ig, piece, mod, line,
        o_lo, o_ig, o_qkv, o_out, o_up, o_upb, o_down, o_downb, o_mod, o_modb,
        v_lo, v_ig, v_piece, v_mod, into, back,
    ):
        moves = [(lo, v_lo, o_lo), (ig, v_ig, o_ig)]
        targets = [o_down.at[0, pl.ds(q * own, own), :] for q in range(groups)]
        targets += [o_up.at[0, :, pl.ds(q * TILE, TILE)] for q in range(groups)]
        targets += [o_out.at[0]] + [o_qkv.at[0, :, pl.ds(q * TILE, TILE)] for q in range(3)]
        moves += [(piece.at[k], v_piece.at[k], target) for k, target in enumerate(targets)]
        moves += [(mod, v_mod, o_mod)]
        firsts = [pltpu.make_async_copy(a, b, into.at[k]) for k, (a, b, _) in enumerate(moves)]
        lasts = [pltpu.make_async_copy(b, c, back.at[k]) for k, (_, b, c) in enumerate(moves)]
        for copy in firsts:
            copy.start()
        o_modb[...] = line[0:1, :]
        o_upb[...] = line[1:2, :]
        o_downb[...] = line[2:3, 0:own]
        for first, last in zip(firsts, lasts):
            first.wait()
            last.start()
        for copy in lasts:
            copy.wait()

    return kernel


def body(
    inputs,
    cotangent,
    neighbours,
    mesh_ids,
    noise_sigma,
    w_qkv,
    w_out,
    w_up,
    b_up,
    w_down,
    b_down,
    w_mod,
    b_mod,
):
    shards = lax.axis_size("nodes")
    z = Sizes(inputs, neighbours, noise_sigma, w_up, shards)
    batches, rows, width, hidden = z.batches, z.rows, z.width, z.hidden
    own, npiece = z.own, z.pieces
    shape = jax.ShapeDtypeStruct
    stack = shape((1, batches, rows, width), LOW)
    outs = [stack, stack]
    sides = [(z.lefts, TILE, batches * rows), (z.rights, batches * rows, TILE)]
    if z.scatter:
        outs += [shape((npiece, own, TILE), F32), shape((1, own, 4 * width), F32), shape((8, 128), F32)]
        scratch = [pltpu.VMEM(side, LOW) for side in sides]
    else:
        outs += [shape(side, LOW) for side in sides] + [shape((16, hidden), F32), shape((width, 128), F32)]
        scratch = []
    dma = pltpu.SemaphoreType.DMA
    scratch += [
        pltpu.VMEM((width, 3 * width), LOW),
        pltpu.VMEM((width, width), LOW),
        pltpu.VMEM((width, hidden), LOW),
        pltpu.VMEM((hidden, width), LOW),
        pltpu.VMEM((width, 4 * width), LOW),
        pltpu.VMEM((batches, z.ext, width), LOW),
        pltpu.VMEM((batches, rows, width), LOW),
        pltpu.VMEM((z.ext, 128), F32),
        pltpu.VMEM((16, rows), LOW),
        pltpu.VMEM((rows, z.window), F32),
        pltpu.VMEM((rows, z.window), LOW),
        pltpu.VMEM((rows, z.window), F32),
        pltpu.VMEM((batches, 8, 4 * width), F32),
        pltpu.VMEM((width, 128), F32),
        pltpu.VMEM((z.ext, width), LOW),
        pltpu.VMEM((batches, rows, width), LOW),
        pltpu.VMEM((batches, rows, width), F32),
        pltpu.VMEM((batches, rows, 128), F32),
        pltpu.VMEM((batches, rows, width), LOW),
        pltpu.VMEM((batches, z.window, 2 * width), LOW),
        pltpu.VMEM((HEADS, rows, z.window), F32),
        pltpu.VMEM((batches, HEADS, rows, z.window), F32),
        pltpu.VMEM((batches, HEADS, rows, z.window), LOW),
        pltpu.VMEM((batches, rows, width), LOW),
        pltpu.VMEM((batches, rows, width), LOW),
        pltpu.VMEM((batches, rows, width), F32),
        pltpu.VMEM((batches, rows, 128), F32),
        pltpu.VMEM((rows, width), F32),
        pltpu.VMEM((batches, rows, hidden), LOW),
        pltpu.VMEM((batches, rows, hidden), LOW),
        pltpu.VMEM((rows, width), LOW),
        pltpu.VMEM((rows, width), F32),
        pltpu.VMEM((HEADS, rows, z.window), LOW),
        pltpu.VMEM((batches, rows, width), F32),
        pltpu.VMEM((batches, rows, 2 * width), F32),
        pltpu.VMEM((batches, 2, REACH, 2 * width), LOW),
        pltpu.VMEM((batches, 2, REACH, 2 * width), LOW),
        pltpu.VMEM((batches, 8, hidden), F32),
        dma((7,)),
        dma((2,)),
        dma((2,)),
        dma((2,)),
        dma((2,)),
        dma((batches, 3)),
        dma((batches, 3)),
        dma((batches, 2)),
        dma((batches, 2)),
        dma((batches,)),
        dma((batches,)),
    ]
    if z.scatter:
        stages = len(z.bits)
        sizes = [TILE >> (k + 1) for k in range(stages)]
        scratch += [pltpu.VMEM((npiece, size, TILE), LOW) for size in sizes + sizes]
        scratch += [pltpu.VMEM((npiece, size, TILE), F32) for size in sizes[1:]]
        scratch += [
            pltpu.VMEM((sizes[0], TILE), F32),
            pltpu.VMEM((z.rings, 16, hidden), LOW),
            pltpu.VMEM((z.rings, 16, hidden), LOW),
            pltpu.VMEM((16, hidden), F32),
            dma((npiece, stages, 4)),
            dma((npiece, stages, 4)),
            dma((z.rings,)),
            dma((z.rings,)),
        ]
    hbm = pl.BlockSpec(memory_space=pl.ANY)
    vmem = pl.BlockSpec(memory_space=pltpu.VMEM)
    smem = pl.BlockSpec(memory_space=pltpu.SMEM)
    got = pl.pallas_call(
        kernel_of(z),
        out_shape=outs,
        in_specs=[hbm, hbm, vmem, vmem, smem, hbm, hbm, hbm, vmem, hbm, vmem, hbm, vmem],
        out_specs=[vmem] * len(outs),
        scratch_shapes=scratch,
        compiler_params=pltpu.CompilerParams(
            collective_id=0, has_side_effects=True, vmem_limit_bytes=62 * 2**20
        ),
    )(
        inputs,
        cotangent,
        neighbours.T,
        mesh_ids.reshape(1, rows),
        noise_sigma.T,
        w_qkv,
        w_out,
        w_up,
        b_up,
        w_down,
        b_down,
        w_mod,
        b_mod,
    )
    if z.scatter:
        lo, ig, piece, mod, line = got
        return tuple(
            pl.pallas_call(
                layout_of(z),
                out_shape=[
                    stack,
                    stack,
                    shape((1, own, 3 * width), F32),
                    shape((1, own, width), F32),
                    shape((1, own, hidden), F32),
                    shape((1, hidden // shards), F32),
                    shape((1, hidden // shards, width), F32),
                    shape((1, own), F32),
                    shape((1, own, 4 * width), F32),
                    shape((1, 4 * width // shards), F32),
                ],
                in_specs=[hbm, hbm, hbm, hbm, vmem],
                out_specs=[hbm, hbm, hbm, hbm, hbm, vmem, hbm, vmem, hbm, vmem],
                scratch_shapes=[
                    pltpu.VMEM(stack.shape, LOW),
                    pltpu.VMEM(stack.shape, LOW),
                    pltpu.VMEM((npiece, own, TILE), F32),
                    pltpu.VMEM((1, own, 4 * width), F32),
                    dma((npiece + 3,)),
                    dma((npiece + 3,)),
                ],
                compiler_params=pltpu.CompilerParams(vmem_limit_bytes=62 * 2**20),
            )(lo, ig, piece, mod, line)
        )
    lo, ig, left_t, right_t, small, table = got
    groups = z.groups

    def summed(value):
        return lax.psum_scatter(value, "nodes", scatter_dimension=0, tiled=True)

    def wide_sum(left, first, last):
        return summed(jnp.concatenate([dot(left_t[left], right_t[r]) for r in range(first, last)], axis=1))[None]

    down = [dot(left_t[q], right_t[0]).reshape(TILE // 32, 32, TILE) for q in range(groups)]
    down = jnp.stack(down, axis=1)
    count = batches * z.meshes
    small = lax.psum(small, "nodes")
    me = lax.axis_index("nodes")
    mod = jnp.dot(table[:, :count], small[:count], precision=lax.Precision.HIGHEST)

    def mine(value):
        size = value.shape[0] // shards
        return lax.dynamic_slice_in_dim(value, me * size, size, axis=0)[None]

    return (
        lo,
        ig,
        wide_sum(groups + 2, 2 + groups, 5 + groups),
        wide_sum(groups + 1, 1 + groups, 2 + groups),
        wide_sum(groups, 1, 1 + groups),
        mine(small[count]),
        summed(down.reshape(hidden, width))[None],
        mine(small[count + 1, :width]),
        mine(mod),
        mine(jnp.sum(small[:count], axis=0)),
    )


def solution(mesh):
    return jax.shard_map(
        body,
        mesh=mesh,
        in_specs=(
            P(None, "nodes", None),
            P(None, "nodes", None),
            P("nodes", None),
            P("nodes"),
            P(),
            P("section", None, None),
            P("section", None, None),
            P("section", None, None),
            P("section", None),
            P("section", None, None),
            P("section", None),
            P("section", None, None),
            P("section", None),
        ),
        out_specs=(
            P("section", None, "nodes", None),
            P("section", None, "nodes", None),
            P("section", "nodes", None),
            P("section", "nodes", None),
            P("section", "nodes", None),
            P("section", "nodes"),
            P("section", "nodes", None),
            P("section", "nodes"),
            P("section", "nodes", None),
            P("section", "nodes"),
        ),
        check_vma=False,
    )
```

```python
import jax
import jax.numpy as jnp
from jax import lax
from jax.experimental import pallas as pl
from jax.experimental.pallas import tpu as pltpu
from jax.sharding import PartitionSpec as P

HEADS = 4
REACH = 32
EPSILON = 1e-06
MASKED = -1e9
ABSENT = -2e38
TILE = 512
MESH = pl.DeviceIdType.MESH
F32, LOW = jnp.float32, jnp.bfloat16


def dot(a, b):
    return lax.dot_general(a, b, (((1,), (0,)), ((), ())), preferred_element_type=F32)


def dot_nt(a, b):
    return lax.dot_general(a, b, (((1,), (1,)), ((), ())), preferred_element_type=F32)


def dot_tn(a, b):
    return lax.dot_general(a, b, (((0,), (0,)), ((), ())), preferred_element_type=F32)


class Sizes:
    def __init__(self, inputs, neighbours, noise, w_up, shards):
        self.batches, self.rows, self.width = inputs.shape
        self.slots = neighbours.shape[1]
        self.meshes = noise.shape[1]
        self.hidden = w_up.shape[2]
        self.shards = shards
        self.ext = self.rows + 2 * REACH
        self.window = (self.ext // 128 + 1) * 128
        self.groups = self.hidden // TILE
        self.own = self.width // shards
        self.scatter = self.own % 16 == 0
        self.pieces = 2 * self.groups + 4
        self.lefts = 3 + self.groups
        self.rights = 2 + self.groups + 3
        self.rings = max(shards.bit_length() - 1, 1)

        self.bits = [1 << k for k in range(shards.bit_length() - 1)]

    def left(self, p):
        n = self.groups
        return jnp.minimum(p, n) + lax.div(p, 2 * n) + lax.div(p, 2 * n + 1)

    def order(self, swapped):
        bits = list(self.bits)
        if swapped and len(bits) > 2:
            bits[1], bits[2] = bits[2], bits[1]
        return bits

    def right(self, p):
        return jnp.maximum(p - (self.groups - 1), 0)


def weave(*chains):
    chains = list(chains)
    while chains:
        for chain in list(chains):
            try:
                next(chain)
            except StopIteration:
                chains.remove(chain)


def kernel_of(z):
    batches, rows, width, ext, window = z.batches, z.rows, z.width, z.ext, z.window
    groups, shards, own = z.groups, z.shards, z.own
    head = width // HEADS
    score_scale = head ** (-0.5)
    log2e = 1.4426950408889634
    npiece = z.pieces
    half = TILE // 2
    stages = len(z.bits)
    g_out, g_q, g_k = 1 + groups, 2 + groups, 3 + groups

    def position(owner, first):
        if not z.scatter:
            return owner
        place = 0
        for bit in z.order(1 <= first < groups):
            place = 2 * place + owner // bit % 2
        return place

    def kernel(
        inputs, cotangent, neighbours, mesh_ids, sigma,
        w_qkv, w_out, w_up, b_up, w_down, b_down, w_mod, b_mod,
        lo, ig, *rest,
    ):
        left_t, right_t, small_out, table_out = rest[:4]
        rest = rest[4:]
        (
            wq, wo, wu, wd, wm, xext, dybuf, sel, pick, cnt, few, bias, mod, emb,
            n1, n1s, ua, ia, qb, kvext, sbuf, af, ca, obs, n2s, ub, ib, tb, fp, hs,
            ob, dbuf, cds, dx1, dkv, hsend, hrecv, sm,
            lsem, hx_s, hx_r, hm_s, hm_r, fx_s, fx_r, bh_s, bh_r, bx_s, bx_r,
        ) = rest

        sec = lax.axis_index("section")
        me = lax.axis_index("nodes")
        up = lax.rem(me + 1, shards)
        down = lax.rem(me + shards - 1, shards)
        other = 1 - sec

        def local(src, dst, k):
            return pltpu.make_async_copy(src, dst, lsem.at[k])

        loads = [
            local(w_mod.at[0], wm, 0),
            local(w_qkv.at[0], wq, 1),
            local(w_out.at[0], wo, 2),
            local(w_up.at[0], wu, 3),
            local(w_down.at[0], wd, 4),
        ]
        own_rows = pl.ds(REACH, rows)
        first_load = local(inputs, xext.at[:, own_rows, :], 5)
        last_load = local(cotangent, dybuf, 6)
        loads[0].start()

        @pl.when(sec == 0)
        def _():
            first_load.start()

        for copy in loads[1:]:
            copy.start()

        @pl.when(sec == 1)
        def _():
            last_load.start()

        barrier = pltpu.get_barrier_semaphore()
        mates = [(sec, up), (sec, down), (other, me), (other, up), (other, down)]
        for peer in mates:
            pl.semaphore_signal(barrier, inc=1, device_id=peer, device_id_type=MESH)
        pl.semaphore_wait(barrier, len(mates))

        def remote(src, dst, s_sem, r_sem, peer):
            return pltpu.make_async_remote_copy(
                src_ref=src, dst_ref=dst, send_sem=s_sem, recv_sem=r_sem, device_id=peer, device_id_type=MESH
            )

        low_rows, top_rows = pl.ds(0, REACH), pl.ds(REACH + rows, REACH)
        head_rows, tail_rows = pl.ds(REACH, REACH), pl.ds(rows, REACH)
        x_down = remote(inputs.at[:, pl.ds(0, REACH), :], xext.at[:, top_rows, :], hx_s.at[0], hx_r.at[0], (sec, down))
        x_up = remote(inputs.at[:, pl.ds(rows - REACH, REACH), :], xext.at[:, low_rows, :], hx_s.at[1], hx_r.at[1], (sec, up))

        @pl.when(sec == 0)
        def _():
            x_down.start()
            x_up.start()

        ids = jnp.broadcast_to(mesh_ids[...].astype(F32), (128, rows))
        sel[own_rows, :] = ids.T
        m_down = remote(sel.at[head_rows, :], sel.at[top_rows, :], hm_s.at[0], hm_r.at[0], (sec, down))
        m_up = remote(sel.at[tail_rows, :], sel.at[low_rows, :], hm_s.at[1], hm_r.at[1], (sec, up))
        m_down.start()
        m_up.start()
        sample = lax.broadcasted_iota(jnp.int32, (16, rows), 0).astype(F32)
        pick[...] = jnp.where(ids[0:16] == sample, 1.0, 0.0).astype(LOW)

        row_no = lax.broadcasted_iota(jnp.int32, (16, width // 2), 0)
        level = jnp.ones((16, width // 2), F32)
        for b in range(batches):
            for m in range(z.meshes):
                level = jnp.where(row_no == b * z.meshes + m, sigma[m, b], level)
        place = lax.broadcasted_iota(jnp.int32, (16, width // 2), 1).astype(F32)
        frequency = 3.0 * jnp.exp(-jnp.log(100.0) * place / (width // 2))
        angles = jnp.log(level) * frequency
        embedded = jnp.concatenate([jnp.sin(angles), jnp.cos(angles)], axis=1).astype(LOW)
        padded = jnp.concatenate([embedded.astype(F32), jnp.zeros((112, width), F32)], axis=0)
        emb[...] = padded.T
        loads[0].wait()
        for g in range(4):
            cols = pl.ds(g * width, width)
            table = dot(embedded, wm[:, cols]) + b_mod[:, cols] + (1.0 - g % 2)
            for b in range(batches):
                mod[b, 0 : z.meshes, cols] = table[b * z.meshes : (b + 1) * z.meshes]

        slots = neighbours[...].astype(F32)
        slots = jnp.concatenate([slots, jnp.zeros((128 - z.slots, rows), F32)], axis=0).T
        slots = jnp.where(slots >= 0, slots - (me * rows - REACH).astype(F32), float(ext))
        column = lax.broadcasted_iota(jnp.int32, (rows, window), 1).astype(F32)
        counts = jnp.zeros((rows, window), F32)
        for n in range(z.slots):
            counts = counts + jnp.where(slots[:, n : n + 1] == column, 1.0, 0.0)
        cnt[...] = counts
        few[...] = counts.astype(LOW)
        bias[...] = jnp.where(counts > 0, jnp.where(column == ext, MASKED * log2e, 0.0), ABSENT)

        def mod_rows(b, part, ids_rows):
            cols = pl.ds(part * width, width)
            value = jnp.broadcast_to(mod[b, 0:1, cols], (ids_rows.shape[0], width))
            for m in range(1, z.meshes):
                value = jnp.where(ids_rows > m - 0.5, mod[b, m : m + 1, cols], value)
            return value

        def wide(ids_rows):
            return jnp.concatenate([ids_rows] * (width // 128), axis=1)

        def unit(x):
            centred = x - jnp.mean(x, axis=-1, keepdims=True)
            inv = lax.rsqrt(jnp.mean(centred * centred, axis=-1, keepdims=True) + EPSILON)
            return centred * inv, inv

        def batch_cols(b):
            return pl.ds(b * rows, rows) if isinstance(b, int) else pl.ds(pl.multiple_of(b * rows, rows), rows)

        span = own if z.scatter else 32

        def transposes(b, carry):
            for first, ref in ((groups, n2s), (groups + 1, obs), (groups + 2, n1s)):
                turned = ref[b].T
                for owner in range(TILE // span):
                    at = position(owner, first) * span
                    left_t[first, at : at + span, batch_cols(b)] = turned[owner * span : (owner + 1) * span]
            run = groups * span
            for g in range(groups):
                turned = hs[b, :, g * TILE : (g + 1) * TILE].T
                for k in range(TILE // span):
                    at = g * TILE + k * span
                    owner, part = at // run, at % run // span
                    to = position(owner, part) * span
                    left_t[part, to : to + span, batch_cols(b)] = turned[k * span : (k + 1) * span]
            return carry

        heads = [slice(h * head, (h + 1) * head) for h in range(HEADS)]
        heads_v = [slice(width + h * head, width + (h + 1) * head) for h in range(HEADS)]
        tiles = [slice(g * TILE, (g + 1) * TILE) for g in range(groups)]
        thirds = [slice(g * width, (g + 1) * width) for g in range(3)]

        def forward_first(b):
            ids_rows = wide(sel[0:ext, :])
            u, inv = unit(xext[b].astype(F32))
            normed = (u * mod_rows(b, 0, ids_rows) + mod_rows(b, 1, ids_rows)).astype(LOW)
            n1[...] = normed
            n1s[b] = normed[REACH : REACH + rows]
            ua[b] = u[REACH : REACH + rows]
            ia[b] = jnp.broadcast_to(inv[REACH : REACH + rows], (rows, 128))
            yield
            kvext[b, 0:ext, thirds[0]] = dot(n1[...], wq[:, thirds[1]]).astype(LOW)
            qb[b] = dot(n1s[b], wq[:, thirds[0]]).astype(LOW)
            yield
            for h in range(HEADS):
                sbuf[h] = dot_nt(qb[b, :, heads[h]], kvext[b, :, heads[h]]) * (score_scale * log2e) + bias[...]
            kvext[b, 0:ext, thirds[1]] = dot(n1[...], wq[:, thirds[2]]).astype(LOW)
            yield
            for h in range(HEADS):
                s = sbuf[h]
                e = jnp.exp2(s - jnp.max(s, axis=-1, keepdims=True))
                a = e * (1.0 / jnp.sum(e * cnt[...], axis=-1, keepdims=True))
                af[b, h] = a
                ca[b, h] = a.astype(LOW) * few[...]
                if h % 2 == 1:
                    yield
            for h in range(HEADS):
                obs[b, :, heads[h]] = dot(ca[b, h], kvext[b, :, heads_v[h]]).astype(LOW)
            yield

        def forward_second(b):
            x1 = xext[b, own_rows, :].astype(F32) + dot(obs[b], wo[...])
            u, inv = unit(x1)
            ub[b] = u
            ib[b] = jnp.broadcast_to(inv, (rows, 128))
            ids_rows = wide(sel[own_rows, :])
            n2s[b] = (u * mod_rows(b, 2, ids_rows) + mod_rows(b, 3, ids_rows)).astype(LOW)
            tb[...] = x1 + b_down[...]
            yield
            for gs in tiles:
                gate = dot(n2s[b], wu[:, gs]) + b_up[:, gs]
                s = 0.5 + 0.5 * jnp.tanh(0.5 * gate)
                hid = gate * s
                fp[b, :, gs] = (s + hid * (1.0 - s)).astype(LOW)
                hid = hid.astype(LOW)
                hs[b, :, gs] = hid
                tb[...] += dot(hid, wd[gs, :])
                yield
            lo[0, b] = tb[...].astype(LOW)
            yield

        def relay(b):
            return [
                remote(lo.at[0, b], xext.at[b, own_rows, :], fx_s.at[b, 0], fx_r.at[b, 0], (other, me)),
                remote(lo.at[0, b, pl.ds(0, REACH), :], xext.at[b, top_rows, :], fx_s.at[b, 1], fx_r.at[b, 1], (other, down)),
                remote(lo.at[0, b, pl.ds(rows - REACH, REACH), :], xext.at[b, low_rows, :], fx_s.at[b, 2], fx_r.at[b, 2], (other, up)),
            ]

        def norm_back(d, u, inv, scale):
            scaled = d * scale
            return inv * (
                scaled
                - jnp.mean(scaled, axis=-1, keepdims=True)
                - u * jnp.mean(scaled * u, axis=-1, keepdims=True)
            )

        def mod_sums(b, part, d, u):
            for k, value in enumerate((d * u, d)):
                total = dot(pick[...], value.astype(LOW))
                sm[b, 0 : z.meshes, (part + k) * width : (part + k + 1) * width] = total[0 : z.meshes]

        def halos(b):
            return [
                remote(hsend.at[b, 0], hrecv.at[b, 1], bh_s.at[b, 0], bh_r.at[b, 0], (sec, down)),
                remote(hsend.at[b, 1], hrecv.at[b, 0], bh_s.at[b, 1], bh_r.at[b, 1], (sec, up)),
            ]

        def given(b):
            at = batch_cols(b)
            dr = dybuf[b]
            right_t[0, at, :] = dr
            sm[b, 7:8, 0:width] = jnp.sum(dr.astype(F32), axis=0, keepdims=True)
            for g in range(groups):
                right_t[1 + g, at, :] = dot_nt(dr, wd[tiles[g], :]).astype(LOW)

        def back_ffn(b):
            at = batch_cols(b)
            for g in range(groups):
                gs = tiles[g]
                dg = right_t[1 + g, at, :].astype(F32) * fp[b, :, gs].astype(F32)
                sm[b, 6:7, gs] = jnp.sum(dg, axis=0, keepdims=True)
                dg = dg.astype(LOW)
                right_t[1 + g, at, :] = dg
                part = dot_nt(dg, wu[:, gs])
                if g == 0:
                    dbuf[...] = part
                else:
                    dbuf[...] += part
                yield

        def back_middle(b):
            at = batch_cols(b)
            ids_rows = wide(sel[own_rows, :])
            d, u = dbuf[...], ub[b]
            grad = dybuf[b].astype(F32) + norm_back(d, u, ib[b][:, 0:1], mod_rows(b, 2, ids_rows))
            dx1[b] = grad
            right_t[g_out, at, :] = grad.astype(LOW)
            yield
            ob[...] = dot_nt(right_t[g_out, at, :], wo[...]).astype(LOW)
            mod_sums(b, 2, d, u)
            yield

        def back_attention(b):
            at = batch_cols(b)
            for h in range(HEADS):
                sbuf[h] = dot_nt(ob[:, heads[h]], kvext[b, :, heads_v[h]])
            for h in range(HEADS):
                dv = dot_tn(ca[b, h], ob[:, heads[h]])
                hsend[b, 0, :, heads_v[h]] = dv[0:REACH].astype(LOW)
                dkv[b, :, heads_v[h]] = dv[REACH : REACH + rows]
                hsend[b, 1, :, heads_v[h]] = dv[REACH + rows : ext].astype(LOW)
            yield
            for h in range(HEADS):
                a, da = af[b, h], sbuf[h]
                ds = a * (da - jnp.sum(a * cnt[...] * da, axis=-1, keepdims=True))
                cds[h] = ds.astype(LOW) * few[...]
            yield
            for h in range(HEADS):
                dk = dot_tn(cds[h], qb[b, :, heads[h]]) * score_scale
                hsend[b, 0, :, heads[h]] = dk[0:REACH].astype(LOW)
                dkv[b, :, heads[h]] = dk[REACH : REACH + rows]
                hsend[b, 1, :, heads[h]] = dk[REACH + rows : ext].astype(LOW)
            yield
            for h in range(HEADS):
                right_t[g_q, at, heads[h]] = (dot(cds[h], kvext[b, :, heads[h]]) * score_scale).astype(LOW)
            yield

        def back_second(b):
            at = batch_cols(b)
            edge = rows - REACH
            dkv[b, 0:REACH, :] += hrecv[b, 0].astype(F32)
            dkv[b, edge:rows, :] += hrecv[b, 1].astype(F32)
            for g in range(2):
                right_t[g_k + g, at, :] = dkv[b, :, thirds[g]].astype(LOW)
            yield
            d = dot_nt(right_t[g_q, at, :], wq[:, thirds[0]])
            for g in range(2):
                d = d + dot_nt(right_t[g_k + g, at, :], wq[:, thirds[g + 1]])
            tb[...] = d
            yield
            d, u = tb[...], ua[b]
            ids_rows = wide(sel[own_rows, :])
            grad = dx1[b] + norm_back(d, u, ia[b][:, 0:1], mod_rows(b, 0, ids_rows))
            ig[0, b] = grad.astype(LOW)
            mod_sums(b, 0, d, u)
            yield

        def relay_back(b):
            return remote(ig.at[0, b], dybuf.at[b], bx_s.at[b], bx_r.at[b], (other, me))

        def take(b):
            @pl.when(sec == 1)
            def _():
                for copy in relay(b):
                    copy.wait_recv()

        def hand(b):
            @pl.when(sec == 0)
            def _():
                for copy in relay(b):
                    copy.start()

        kvext[:, ext:window, :] = jnp.zeros((batches, window - ext, 2 * width), LOW)
        sm[...] = jnp.zeros(sm.shape, F32)
        for copy in loads[1:]:
            copy.wait()
        for copy in (m_down, m_up):
            copy.wait()

        @pl.when(sec == 0)
        def _():
            first_load.wait()
            x_down.wait()
            x_up.wait()

        @pl.when(sec == 1)
        def _():
            last_load.wait()

            @pl.loop(0, batches)
            def _(b):
                given(b)

        take(0)
        weave(forward_first(0))

        @pl.loop(0, batches - 1)
        def _(b):
            take(b + 1)
            weave(forward_second(b), forward_first(b + 1))
            hand(b)

        weave(forward_second(batches - 1))
        hand(batches - 1)

        @pl.when(sec == 0)
        def _():
            lax.fori_loop(0, batches, transposes, 0)

        def arrive(b):
            relay_back(b).wait_recv()
            given(b)

        def send_halos(b):
            for copy in halos(b):
                copy.start()

        def get_halos(b):
            for copy in halos(b):
                copy.wait_recv()

        def send_back(b):
            @pl.when(sec == 1)
            def _():
                relay_back(b).start()

        @pl.when(sec == 0)
        def _():
            arrive(batches - 1)

        weave(back_ffn(batches - 1))
        weave(back_middle(batches - 1))
        weave(back_attention(batches - 1))
        send_halos(batches - 1)

        @pl.loop(0, batches - 2 + sec)
        def _(k):
            b = batches - 2 - k

            @pl.when(sec == 0)
            def _():
                arrive(b)

            get_halos(b + 1)
            weave(back_second(b + 1), back_ffn(b))
            send_back(b + 1)
            weave(back_middle(b))
            weave(back_attention(b))
            send_halos(b)

        @pl.when(sec == 0)
        def _():
            get_halos(1)
            weave(back_second(1))
            arrive(0)
            weave(back_ffn(0))
            weave(back_middle(0))
            weave(back_attention(0))
            send_halos(0)

        get_halos(0)
        weave(back_second(0))
        send_back(0)

        @pl.when(sec == 1)
        def _():
            lax.fori_loop(0, batches, transposes, 0)

        lines = [sm[b, m : m + 1, :] for b in range(batches) for m in range(z.meshes)]
        for line in (6, 7):
            lines.append(sum(sm[b, line : line + 1, :] for b in range(batches)))
        lines.append(jnp.zeros((16 - len(lines), sm.shape[2]), F32))
        small = jnp.concatenate(lines, axis=0)

        def finish():
            @pl.loop(0, batches)
            def _(b):
                @pl.when(sec == 0)
                def _():
                    for copy in relay(b):
                        copy.wait_send()

                @pl.when(sec == 1)
                def _():
                    relay_back(b).wait_send()

                for copy in halos(b):
                    copy.wait_send()

        small_out[...] = small
        table_out[...] = emb[...]
        finish()

    return kernel


def scatter_of(z):
    shards, own, groups, npiece, batches, width = z.shards, z.own, z.groups, z.pieces, z.batches, z.width
    half = TILE // 2
    stages = len(z.bits)

    def kernel(down, ups, out, qkv, small, emb, o_piece, o_mod, o_line, *rest):
        gives, gets, keeps = rest[: stages - 1], rest[stages - 1 : 2 * stages - 1], rest[2 * stages - 1 : 3 * stages - 2]
        first, acc, msend, mrecv, tot, p_l, p_s, p_r, m_s, m_r = rest[3 * stages - 2 :]
        sec = lax.axis_index("section")
        me = lax.axis_index("nodes")

        def bit_of(p, k):
            plain, swapped = z.order(False)[k], z.order(True)[k]
            trades = jnp.minimum(p, 1) - jnp.minimum(lax.div(p, groups), 1)
            return plain + (swapped - plain) * trades

        def side(bit):
            return lax.rem(lax.div(me, bit), 2)

        def mate(bit):
            return me + bit - 2 * bit * side(bit)

        def rows_of(c, size):
            return pl.ds(pl.multiple_of(c * size, size), size)

        def remote(src, dst, s_sem, r_sem, peer):
            return pltpu.make_async_remote_copy(
                src_ref=src, dst_ref=dst, send_sem=s_sem, recv_sem=r_sem, device_id=peer, device_id_type=MESH
            )

        sources = [ref.at[q] for ref, n in ((down, groups), (ups, groups), (out, 1), (qkv, 3)) for q in range(n)]

        def own_copy(p):
            return pltpu.make_async_copy(sources[p].at[rows_of(side(1), half), :], first.at[p], p_l.at[p])

        def first_copy(p):
            return remote(
                sources[p].at[rows_of(1 - side(1), half), :], gets[0].at[p], p_s.at[p, 0], p_r.at[p, 0], (sec, mate(1))
            )

        def piece_copy(p, k):
            if k == 0:
                return remote(gets[0].at[p], gets[0].at[p], p_s.at[p, 0], p_r.at[p, 0], (sec, mate(1)))
            return remote(gives[k - 1].at[p], gets[k].at[p], p_s.at[p, k], p_r.at[p, k], (sec, mate(bit_of(p, k))))

        def piece_step(p, k):
            size = half >> k
            if k == 0:
                pltpu.make_async_copy(first.at[p], first.at[p], p_l.at[p]).wait()
                mine = first[p].astype(F32)
            else:
                mine = keeps[k - 1][p]
            piece_copy(p, k).wait_recv()
            value = mine + gets[k][p].astype(F32)
            if k == stages - 1:
                o_piece[p] = value
                return
            here = side(bit_of(p, k + 1))
            acc[0:size, :] = value
            gives[k][p] = acc[rows_of(1 - here, size // 2), :].astype(LOW)
            piece_copy(p, k + 1).start()
            keeps[k][p] = acc[rows_of(here, size // 2), :]

        for p in range(npiece):
            own_copy(p).start()

        barrier = pltpu.get_barrier_semaphore()
        for bit in z.bits:
            pl.semaphore_signal(barrier, inc=1, device_id=(sec, mate(bit)), device_id_type=MESH)
        pl.semaphore_wait(barrier, stages)

        for p in range(npiece):
            first_copy(p).start()

        def ring_copy(k):
            return remote(msend.at[k], mrecv.at[k], m_s.at[k], m_r.at[k], (sec, mate(1 << k)))

        def ring_start(k, value):
            msend[k] = value.astype(LOW)
            ring_copy(k).start()

        def ring_end(k):
            ring_copy(k).wait_recv()
            value = msend[k].astype(F32) + mrecv[k].astype(F32)
            if k + 1 < z.rings:
                ring_start(k + 1, value)
            else:
                tot[...] = value

        ring_start(0, small[...])

        @pl.loop(0, npiece + 2 * stages - 2)
        def _(p):
            for k in range(stages):
                lag = 2 * k

                @pl.when((p >= lag) & (p < npiece + lag))
                def _(k=k, lag=lag):
                    piece_step(p - lag, k)

            for k in range(z.rings):

                @pl.when(p == 6 + 2 * k)
                def _(k=k):
                    ring_end(k)

        count = batches * z.meshes
        table = emb[pl.ds(pl.multiple_of(me * own, own), own), :]
        grad = jnp.zeros((own, 4 * width), F32)
        for k in range(count):
            grad = grad + table[:, k : k + 1] * tot[k : k + 1, :]
        o_mod[0] = grad
        cols = 4 * width // shards
        mine = tot[:, pl.ds(pl.multiple_of(me * cols, cols), cols)]
        o_line[0:1, :] = jnp.sum(mine[0:count], axis=0, keepdims=True)
        o_line[1:2, :] = mine[count : count + 1]
        ratio = 128 // own
        line = tot[:, pl.ds(pl.multiple_of(me // ratio * 128, 128), 128)][count + 1 : count + 2]
        value = line
        for k in range(1, ratio):
            turned = jnp.concatenate([line[:, k * own :], line[:, : k * own]], axis=1)
            value = jnp.where(me % ratio == k, turned, value)
        o_line[2:3, :] = value

        for p in range(npiece):
            first_copy(p).wait_send()

        @pl.loop(0, npiece)
        def _(p):
            for k in range(1, stages):
                piece_copy(p, k).wait_send()

        for k in range(z.rings):
            ring_copy(k).wait_send()

    return kernel


def layout_of(z):
    own, groups = z.own, z.groups

    def kernel(
        lo, ig, piece, mod, line,
        o_lo, o_ig, o_qkv, o_out, o_up, o_upb, o_down, o_downb, o_mod, o_modb,
        v_lo, v_ig, v_piece, v_mod, into, back,
    ):
        moves = [(lo, v_lo, o_lo), (ig, v_ig, o_ig)]
        targets = [o_down.at[0, pl.ds(q * own, own), :] for q in range(groups)]
        targets += [o_up.at[0, :, pl.ds(q * TILE, TILE)] for q in range(groups)]
        targets += [o_out.at[0]] + [o_qkv.at[0, :, pl.ds(q * TILE, TILE)] for q in range(3)]
        moves += [(piece.at[k], v_piece.at[k], target) for k, target in enumerate(targets)]
        moves += [(mod, v_mod, o_mod)]
        firsts = [pltpu.make_async_copy(a, b, into.at[k]) for k, (a, b, _) in enumerate(moves)]
        lasts = [pltpu.make_async_copy(b, c, back.at[k]) for k, (_, b, c) in enumerate(moves)]
        for copy in firsts:
            copy.start()
        o_modb[...] = line[0:1, :]
        o_upb[...] = line[1:2, :]
        o_downb[...] = line[2:3, 0:own]
        for first, last in zip(firsts, lasts):
            first.wait()
            last.start()
        for copy in lasts:
            copy.wait()

    return kernel


def body(
    inputs,
    cotangent,
    neighbours,
    mesh_ids,
    noise_sigma,
    w_qkv,
    w_out,
    w_up,
    b_up,
    w_down,
    b_down,
    w_mod,
    b_mod,
):
    shards = lax.axis_size("nodes")
    z = Sizes(inputs, neighbours, noise_sigma, w_up, shards)
    batches, rows, width, hidden = z.batches, z.rows, z.width, z.hidden
    own, npiece = z.own, z.pieces
    shape = jax.ShapeDtypeStruct
    stack = shape((1, batches, rows, width), LOW)
    outs = [stack, stack]
    sides = [(z.lefts, TILE, batches * rows), (z.rights, batches * rows, TILE)]
    outs += [shape(side, LOW) for side in sides] + [shape((16, hidden), F32), shape((width, 128), F32)]
    dma = pltpu.SemaphoreType.DMA
    scratch = [
        pltpu.VMEM((width, 3 * width), LOW),
        pltpu.VMEM((width, width), LOW),
        pltpu.VMEM((width, hidden), LOW),
        pltpu.VMEM((hidden, width), LOW),
        pltpu.VMEM((width, 4 * width), LOW),
        pltpu.VMEM((batches, z.ext, width), LOW),
        pltpu.VMEM((batches, rows, width), LOW),
        pltpu.VMEM((z.ext, 128), F32),
        pltpu.VMEM((16, rows), LOW),
        pltpu.VMEM((rows, z.window), F32),
        pltpu.VMEM((rows, z.window), LOW),
        pltpu.VMEM((rows, z.window), F32),
        pltpu.VMEM((batches, 8, 4 * width), F32),
        pltpu.VMEM((width, 128), F32),
        pltpu.VMEM((z.ext, width), LOW),
        pltpu.VMEM((batches, rows, width), LOW),
        pltpu.VMEM((batches, rows, width), F32),
        pltpu.VMEM((batches, rows, 128), F32),
        pltpu.VMEM((batches, rows, width), LOW),
        pltpu.VMEM((batches, z.window, 2 * width), LOW),
        pltpu.VMEM((HEADS, rows, z.window), F32),
        pltpu.VMEM((batches, HEADS, rows, z.window), F32),
        pltpu.VMEM((batches, HEADS, rows, z.window), LOW),
        pltpu.VMEM((batches, rows, width), LOW),
        pltpu.VMEM((batches, rows, width), LOW),
        pltpu.VMEM((batches, rows, width), F32),
        pltpu.VMEM((batches, rows, 128), F32),
        pltpu.VMEM((rows, width), F32),
        pltpu.VMEM((batches, rows, hidden), LOW),
        pltpu.VMEM((batches, rows, hidden), LOW),
        pltpu.VMEM((rows, width), LOW),
        pltpu.VMEM((rows, width), F32),
        pltpu.VMEM((HEADS, rows, z.window), LOW),
        pltpu.VMEM((batches, rows, width), F32),
        pltpu.VMEM((batches, rows, 2 * width), F32),
        pltpu.VMEM((batches, 2, REACH, 2 * width), LOW),
        pltpu.VMEM((batches, 2, REACH, 2 * width), LOW),
        pltpu.VMEM((batches, 8, hidden), F32),
        dma((7,)),
        dma((2,)),
        dma((2,)),
        dma((2,)),
        dma((2,)),
        dma((batches, 3)),
        dma((batches, 3)),
        dma((batches, 2)),
        dma((batches, 2)),
        dma((batches,)),
        dma((batches,)),
    ]
    hbm = pl.BlockSpec(memory_space=pl.ANY)
    vmem = pl.BlockSpec(memory_space=pltpu.VMEM)
    smem = pl.BlockSpec(memory_space=pltpu.SMEM)
    got = pl.pallas_call(
        kernel_of(z),
        out_shape=outs,
        in_specs=[hbm, hbm, vmem, vmem, smem, hbm, hbm, hbm, vmem, hbm, vmem, hbm, vmem],
        out_specs=[vmem] * len(outs),
        scratch_shapes=scratch,
        compiler_params=pltpu.CompilerParams(
            collective_id=0, has_side_effects=True, vmem_limit_bytes=62 * 2**20
        ),
    )(
        inputs,
        cotangent,
        neighbours.T,
        mesh_ids.reshape(1, rows),
        noise_sigma.T,
        w_qkv,
        w_out,
        w_up,
        b_up,
        w_down,
        b_down,
        w_mod,
        b_mod,
    )
    lo, ig, left_t, right_t, small, table = got
    groups = z.groups
    if z.scatter:
        stages = len(z.bits)
        sizes = [TILE >> (k + 1) for k in range(stages)]
        sums = [pltpu.VMEM((npiece, size, TILE), LOW) for size in sizes[1:] + sizes]
        sums += [pltpu.VMEM((npiece, size, TILE), F32) for size in sizes[1:]]
        sums += [
            pltpu.VMEM((npiece, sizes[0], TILE), LOW),
            pltpu.VMEM((sizes[0], TILE), F32),
            pltpu.VMEM((z.rings, 16, hidden), LOW),
            pltpu.VMEM((z.rings, 16, hidden), LOW),
            pltpu.VMEM((16, hidden), F32),
            dma((npiece,)),
            dma((npiece, stages)),
            dma((npiece, stages)),
            dma((z.rings,)),
            dma((z.rings,)),
        ]

        def products(form, left, right):
            return jnp.einsum(form, left, right, preferred_element_type=F32).astype(LOW)

        piece, mod, line = pl.pallas_call(
            scatter_of(z),
            out_shape=[shape((npiece, own, TILE), F32), shape((1, own, 4 * width), F32), shape((8, 128), F32)],
            in_specs=[hbm] * 4 + [vmem] * 2,
            out_specs=[vmem] * 3,
            scratch_shapes=sums,
            compiler_params=pltpu.CompilerParams(
                collective_id=1, has_side_effects=True, vmem_limit_bytes=62 * 2**20
            ),
        )(
            products("qmk,kn->qmn", left_t[0:groups], right_t[0]),
            products("mk,qkn->qmn", left_t[groups], right_t[1 : 1 + groups]),
            products("mk,qkn->qmn", left_t[groups + 1], right_t[1 + groups : 2 + groups]),
            products("mk,qkn->qmn", left_t[groups + 2], right_t[2 + groups :]),
            small,
            table,
        )
        return tuple(
            pl.pallas_call(
                layout_of(z),
                out_shape=[
                    stack,
                    stack,
                    shape((1, own, 3 * width), F32),
                    shape((1, own, width), F32),
                    shape((1, own, hidden), F32),
                    shape((1, hidden // shards), F32),
                    shape((1, hidden // shards, width), F32),
                    shape((1, own), F32),
                    shape((1, own, 4 * width), F32),
                    shape((1, 4 * width // shards), F32),
                ],
                in_specs=[hbm, hbm, hbm, hbm, vmem],
                out_specs=[hbm, hbm, hbm, hbm, hbm, vmem, hbm, vmem, hbm, vmem],
                scratch_shapes=[
                    pltpu.VMEM(stack.shape, LOW),
                    pltpu.VMEM(stack.shape, LOW),
                    pltpu.VMEM((npiece, own, TILE), F32),
                    pltpu.VMEM((1, own, 4 * width), F32),
                    dma((npiece + 3,)),
                    dma((npiece + 3,)),
                ],
                compiler_params=pltpu.CompilerParams(vmem_limit_bytes=62 * 2**20),
            )(lo, ig, piece, mod, line)
        )

    def summed(value):
        return lax.psum_scatter(value, "nodes", scatter_dimension=0, tiled=True)

    def wide_sum(left, first, last):
        return summed(jnp.concatenate([dot(left_t[left], right_t[r]) for r in range(first, last)], axis=1))[None]

    down = [dot(left_t[q], right_t[0]).reshape(TILE // 32, 32, TILE) for q in range(groups)]
    down = jnp.stack(down, axis=1)
    count = batches * z.meshes
    small = lax.psum(small, "nodes")
    me = lax.axis_index("nodes")
    mod = jnp.dot(table[:, :count], small[:count], precision=lax.Precision.HIGHEST)

    def mine(value):
        size = value.shape[0] // shards
        return lax.dynamic_slice_in_dim(value, me * size, size, axis=0)[None]

    return (
        lo,
        ig,
        wide_sum(groups + 2, 2 + groups, 5 + groups),
        wide_sum(groups + 1, 1 + groups, 2 + groups),
        wide_sum(groups, 1, 1 + groups),
        mine(small[count]),
        summed(down.reshape(hidden, width))[None],
        mine(small[count + 1, :width]),
        mine(mod),
        mine(jnp.sum(small[:count], axis=0)),
    )


def solution(mesh):
    return jax.shard_map(
        body,
        mesh=mesh,
        in_specs=(
            P(None, "nodes", None),
            P(None, "nodes", None),
            P("nodes", None),
            P("nodes"),
            P(),
            P("section", None, None),
            P("section", None, None),
            P("section", None, None),
            P("section", None),
            P("section", None, None),
            P("section", None),
            P("section", None, None),
            P("section", None),
        ),
        out_specs=(
            P("section", None, "nodes", None),
            P("section", None, "nodes", None),
            P("section", "nodes", None),
            P("section", "nodes", None),
            P("section", "nodes", None),
            P("section", "nodes"),
            P("section", "nodes", None),
            P("section", "nodes"),
            P("section", "nodes", None),
            P("section", "nodes"),
        ),
        check_vma=False,
    )
```

```python
import jax
import jax.numpy as jnp
from jax import lax
from jax.experimental import pallas as pl
from jax.experimental.pallas import tpu as pltpu
from jax.sharding import PartitionSpec as P

HEADS = 4
REACH = 32
EPSILON = 1e-06
MASKED = -1e9
ABSENT = -2e38
TILE = 512
TOGETHER = 2
MESH = pl.DeviceIdType.MESH
F32, LOW = jnp.float32, jnp.bfloat16


def dot(a, b):
    return lax.dot_general(a, b, (((1,), (0,)), ((), ())), preferred_element_type=F32)


def dot_nt(a, b):
    return lax.dot_general(a, b, (((1,), (1,)), ((), ())), preferred_element_type=F32)


def dot_tn(a, b):
    return lax.dot_general(a, b, (((0,), (0,)), ((), ())), preferred_element_type=F32)


class Sizes:
    def __init__(self, inputs, neighbours, noise, w_up, shards):
        self.batches, self.rows, self.width = inputs.shape
        self.together = TOGETHER if self.batches % TOGETHER == 0 else 1
        self.turns = self.batches // self.together
        self.slots = neighbours.shape[1]
        self.meshes = noise.shape[1]
        self.hidden = w_up.shape[2]
        self.shards = shards
        self.ext = self.rows + 2 * REACH
        self.window = (self.ext // 128 + 1) * 128
        self.groups = self.hidden // TILE
        self.own = self.width // shards
        self.scatter = self.own % 16 == 0
        self.pieces = 2 * self.groups + 4
        self.lefts = 3 + self.groups
        self.rights = 2 + self.groups + 3
        self.rings = max(shards.bit_length() - 1, 1)

        self.bits = [1 << k for k in range(shards.bit_length() - 1)]

    def left(self, p):
        n = self.groups
        return jnp.minimum(p, n) + lax.div(p, 2 * n) + lax.div(p, 2 * n + 1)

    def right(self, p):
        return jnp.maximum(p - (self.groups - 1), 0)


def kernel_of(z):
    batches, rows, width, ext, window = z.batches, z.rows, z.width, z.ext, z.window
    groups, shards, own, many = z.groups, z.shards, z.own, z.together
    head = width // HEADS
    score_scale = head ** (-0.5)
    log2e = 1.4426950408889634
    npiece = z.pieces
    half = TILE // 2
    stages = len(z.bits)
    g_out, g_q, g_k = 1 + groups, 2 + groups, 3 + groups

    def position(owner):
        if not z.scatter:
            return owner
        place = 0
        for bit in z.bits:
            place = 2 * place + owner // bit % 2
        return place

    def kernel(
        inputs, cotangent, neighbours, mesh_ids, sigma,
        w_qkv, w_out, w_up, b_up, w_down, b_down, w_mod, b_mod,
        lo, ig, *rest,
    ):
        if z.scatter:
            o_piece, o_mod, o_line, left_t, right_t = rest[:5]
            rest = rest[5:]
        else:
            left_t, right_t, small_out, table_out = rest[:4]
            rest = rest[4:]
        (
            wq, wo, wu, wd, wm, xext, dybuf, sel, pick, cnt, few, bias, mod, emb,
            n1, n1s, ua, ia, qb, kvext, sbuf, af, ca, obs, n2s, ub, ib, tb, fp, hs,
            ob, cds, dx1, dkv, hsend, hrecv, sm,
            lsem, hx_s, hx_r, hm_s, hm_r, fx_s, fx_r, bh_s, bh_r, bx_s, bx_r,
        ) = rest[:48]
        rest = rest[48:]
        if z.scatter:
            gives, gets, keeps = rest[:stages], rest[stages : 2 * stages], rest[2 * stages : 3 * stages - 1]
            acc, msend, mrecv, tot, p_s, p_r, m_s, m_r = rest[3 * stages - 1 :]

        sec = lax.axis_index("section")
        me = lax.axis_index("nodes")
        up = lax.rem(me + 1, shards)
        down = lax.rem(me + shards - 1, shards)
        other = 1 - sec
        def local(src, dst, k):
            return pltpu.make_async_copy(src, dst, lsem.at[k])

        loads = [
            local(w_mod.at[0], wm, 0),
            local(w_qkv.at[0], wq, 1),
            local(w_out.at[0], wo, 2),
            local(w_up.at[0], wu, 3),
            local(w_down.at[0], wd, 4),
        ]
        own_rows = pl.ds(REACH, rows)
        first_load = local(inputs, xext.at[:, own_rows, :], 5)
        last_load = local(cotangent, dybuf, 6)
        loads[0].start()

        @pl.when(sec == 0)
        def _():
            first_load.start()

        for copy in loads[1:]:
            copy.start()

        @pl.when(sec == 1)
        def _():
            last_load.start()

        def side(bit):
            return lax.rem(lax.div(me, bit), 2)

        def mate(bit):
            return me + bit - 2 * bit * side(bit)

        barrier = pltpu.get_barrier_semaphore()
        mates = [(sec, up), (sec, down), (other, me), (other, up), (other, down)]
        if z.scatter:
            mates += [(sec, mate(bit)) for bit in z.bits[1:]]
        for peer in mates:
            pl.semaphore_signal(barrier, inc=1, device_id=peer, device_id_type=MESH)
        pl.semaphore_wait(barrier, len(mates))

        def remote(src, dst, s_sem, r_sem, peer):
            return pltpu.make_async_remote_copy(
                src_ref=src, dst_ref=dst, send_sem=s_sem, recv_sem=r_sem, device_id=peer, device_id_type=MESH
            )

        low_rows, top_rows = pl.ds(0, REACH), pl.ds(REACH + rows, REACH)
        head_rows, tail_rows = pl.ds(REACH, REACH), pl.ds(rows, REACH)
        x_down = remote(inputs.at[:, pl.ds(0, REACH), :], xext.at[:, top_rows, :], hx_s.at[0], hx_r.at[0], (sec, down))
        x_up = remote(inputs.at[:, pl.ds(rows - REACH, REACH), :], xext.at[:, low_rows, :], hx_s.at[1], hx_r.at[1], (sec, up))

        @pl.when(sec == 0)
        def _():
            x_down.start()
            x_up.start()

        ids = jnp.broadcast_to(mesh_ids[...].astype(F32), (128, rows))
        sel[own_rows, :] = ids.T
        sample = lax.broadcasted_iota(jnp.int32, (16, rows), 0).astype(F32)
        pick[...] = jnp.where(ids[0:16] == sample, 1.0, 0.0).astype(LOW)
        m_down = remote(sel.at[head_rows, :], sel.at[top_rows, :], hm_s.at[0], hm_r.at[0], (sec, down))
        m_up = remote(sel.at[tail_rows, :], sel.at[low_rows, :], hm_s.at[1], hm_r.at[1], (sec, up))
        m_down.start()
        m_up.start()

        row_no = lax.broadcasted_iota(jnp.int32, (16, width // 2), 0)
        level = jnp.ones((16, width // 2), F32)
        for b in range(batches):
            for m in range(z.meshes):
                level = jnp.where(row_no == b * z.meshes + m, sigma[m, b], level)
        place = lax.broadcasted_iota(jnp.int32, (16, width // 2), 1).astype(F32)
        frequency = 3.0 * jnp.exp(-jnp.log(100.0) * place / (width // 2))
        angles = jnp.log(level) * frequency
        embedded = jnp.concatenate([jnp.sin(angles), jnp.cos(angles)], axis=1).astype(LOW)
        padded = jnp.concatenate([embedded.astype(F32), jnp.zeros((112, width), F32)], axis=0)
        emb[...] = padded.T
        loads[0].wait()
        for g in range(4):
            cols = pl.ds(g * width, width)
            table = dot(embedded, wm[:, cols]) + b_mod[:, cols] + (1.0 - g % 2)
            for b in range(batches):
                mod[b, 0 : z.meshes, cols] = table[b * z.meshes : (b + 1) * z.meshes]

        slots = neighbours[...].astype(F32)
        slots = jnp.concatenate([slots, jnp.zeros((128 - z.slots, rows), F32)], axis=0).T
        slots = jnp.where(slots >= 0, slots - (me * rows - REACH).astype(F32), float(ext))
        column = lax.broadcasted_iota(jnp.int32, (rows, window), 1).astype(F32)
        counts = jnp.zeros((rows, window), F32)
        for n in range(z.slots):
            counts = counts + jnp.where(slots[:, n : n + 1] == column, 1.0, 0.0)
        cnt[...] = counts
        few[...] = counts.astype(LOW)
        bias[...] = jnp.where(counts > 0, jnp.where(column == ext, MASKED * log2e, 0.0), ABSENT)

        def mod_rows(b, part, ids_rows):
            cols = pl.ds(part * width, width)
            value = jnp.broadcast_to(mod[b, 0:1, cols], (ids_rows.shape[0], width))
            for m in range(1, z.meshes):
                value = jnp.where(ids_rows > m - 0.5, mod[b, m : m + 1, cols], value)
            return value

        def wide(ids_rows):
            return jnp.concatenate([ids_rows] * (width // 128), axis=1)

        def unit(x):
            centred = x - jnp.mean(x, axis=-1, keepdims=True)
            inv = lax.rsqrt(jnp.mean(centred * centred, axis=-1, keepdims=True) + EPSILON)
            return centred * inv, inv

        def span_of(start, size):
            if isinstance(start, int):
                return pl.ds(start, size)
            return pl.ds(pl.multiple_of(start, size), size)

        def batch_cols(b):
            return span_of(b * rows, rows)

        def turn_cols(t):
            return span_of(t * many * rows, many * rows)

        def turn_of(ref, t):
            return ref[pl.ds(t * many, many)].reshape(many * rows, ref.shape[2])

        span = own if z.scatter else 32

        def transposes(b, carry):
            for first, ref in ((groups, n2s), (groups + 1, obs), (groups + 2, n1s)):
                turned = ref[b].T
                for owner in range(TILE // span):
                    at = position(owner) * span
                    left_t[first, at : at + span, batch_cols(b)] = turned[owner * span : (owner + 1) * span]
            run = groups * span
            for g in range(groups):
                turned = hs[b, :, g * TILE : (g + 1) * TILE].T
                for k in range(TILE // span):
                    at = g * TILE + k * span
                    owner, part = at // run, at % run // span
                    to = position(owner) * span
                    left_t[part, to : to + span, batch_cols(b)] = turned[k * span : (k + 1) * span]
            return carry

        def forward(t):
            for i in range(many):
                b = t * many + i
                ids_rows = wide(sel[0:ext, :])
                u, inv = unit(xext[b].astype(F32))
                normed = (u * mod_rows(b, 0, ids_rows) + mod_rows(b, 1, ids_rows)).astype(LOW)
                n1[i * ext : (i + 1) * ext, :] = normed
                n1s[b] = normed[REACH : REACH + rows]
                ua[b] = u[REACH : REACH + rows]
                ia[b] = jnp.broadcast_to(inv[REACH : REACH + rows], (rows, 128))
            part = dot(turn_of(n1s, t), wq[:, 0:width]).astype(LOW)
            qb[pl.ds(t * many, many)] = part.reshape(many, rows, width)
            for g in range(2):
                part = dot(n1[...], wq[:, (g + 1) * width : (g + 2) * width]).astype(LOW)
                for i in range(many):
                    kvext[t * many + i, 0:ext, g * width : (g + 1) * width] = part[i * ext : (i + 1) * ext]
            for i in range(many):
                b = t * many + i
                for h in range(HEADS):
                    hd = slice(h * head, (h + 1) * head)
                    sbuf[h] = dot_nt(qb[b, :, hd], kvext[b, :, hd]) * (score_scale * log2e) + bias[...]
                for h in range(HEADS):
                    s = sbuf[h]
                    e = jnp.exp2(s - jnp.max(s, axis=-1, keepdims=True))
                    a = e * (1.0 / jnp.sum(e * cnt[...], axis=-1, keepdims=True))
                    af[b, h] = a
                    ca[b, h] = a.astype(LOW) * few[...]
                for h in range(HEADS):
                    hd = slice(h * head, (h + 1) * head)
                    vd = slice(width + h * head, width + (h + 1) * head)
                    obs[b, :, hd] = dot(ca[b, h], kvext[b, :, vd]).astype(LOW)
            branch = dot(turn_of(obs, t), wo[...])
            for i in range(many):
                b = t * many + i
                x1 = xext[b, own_rows, :].astype(F32) + branch[i * rows : (i + 1) * rows]
                u, inv = unit(x1)
                ub[b] = u
                ib[b] = jnp.broadcast_to(inv, (rows, 128))
                ids_rows = wide(sel[own_rows, :])
                n2s[b] = (u * mod_rows(b, 2, ids_rows) + mod_rows(b, 3, ids_rows)).astype(LOW)
                tb[i * rows : (i + 1) * rows, :] = x1 + b_down[...]
            for g in range(groups):
                gs = slice(g * TILE, (g + 1) * TILE)
                gate = dot(turn_of(n2s, t), wu[:, gs]) + b_up[:, gs]
                s = 0.5 + 0.5 * jnp.tanh(0.5 * gate)
                hid = (gate * s).astype(LOW)
                slope = (s + gate * s * (1.0 - s)).astype(LOW)
                for i in range(many):
                    fp[t * many + i, :, gs] = slope[i * rows : (i + 1) * rows]
                    hs[t * many + i, :, gs] = hid[i * rows : (i + 1) * rows]
                tb[...] += dot(hid, wd[gs, :])
            for i in range(many):
                lo[0, t * many + i] = tb[i * rows : (i + 1) * rows, :].astype(LOW)

        def relay(b):
            return [
                remote(lo.at[0, b], xext.at[b, own_rows, :], fx_s.at[b, 0], fx_r.at[b, 0], (other, me)),
                remote(lo.at[0, b, pl.ds(0, REACH), :], xext.at[b, top_rows, :], fx_s.at[b, 1], fx_r.at[b, 1], (other, down)),
                remote(lo.at[0, b, pl.ds(rows - REACH, REACH), :], xext.at[b, low_rows, :], fx_s.at[b, 2], fx_r.at[b, 2], (other, up)),
            ]

        def norm_back(d, u, inv, scale):
            scaled = d * scale
            return inv * (
                scaled
                - jnp.mean(scaled, axis=-1, keepdims=True)
                - u * jnp.mean(scaled * u, axis=-1, keepdims=True)
            )

        def mod_sums(b, part, d, u):
            for k, value in enumerate((d * u, d)):
                total = dot(pick[...], value.astype(LOW))
                sm[b, 0 : z.meshes, (part + k) * width : (part + k + 1) * width] = total[0 : z.meshes]

        def halos(b):
            return [
                remote(hsend.at[b, 0], hrecv.at[b, 1], bh_s.at[b, 0], bh_r.at[b, 0], (sec, down)),
                remote(hsend.at[b, 1], hrecv.at[b, 0], bh_s.at[b, 1], bh_r.at[b, 1], (sec, up)),
            ]

        def given(t):
            at = turn_cols(t)
            dr = turn_of(dybuf, t)
            right_t[0, at, :] = dr
            for i in range(many):
                total = jnp.sum(dr[i * rows : (i + 1) * rows].astype(F32), axis=0, keepdims=True)
                sm[t * many + i, 7:8, 0:width] = total
            for g in range(groups):
                right_t[1 + g, at, :] = dot_nt(dr, wd[g * TILE : (g + 1) * TILE, :]).astype(LOW)

        def back_ffn(t):
            at = turn_cols(t)
            dn = jnp.zeros((many * rows, width), F32)
            for g in range(groups):
                gs = slice(g * TILE, (g + 1) * TILE)
                dg = right_t[1 + g, at, :].astype(F32) * turn_of(fp, t)[:, gs].astype(F32)
                sm[t * many, 6:7, gs] = jnp.sum(dg, axis=0, keepdims=True)
                dg = dg.astype(LOW)
                right_t[1 + g, at, :] = dg
                dn = dn + dot_nt(dg, wu[:, gs])
            ids_rows = wide(sel[own_rows, :])
            for i in range(many):
                b = t * many + i
                d = dn[i * rows : (i + 1) * rows]
                u = ub[b]
                grad = dybuf[b].astype(F32) + norm_back(d, u, ib[b][:, 0:1], mod_rows(b, 2, ids_rows))
                mod_sums(b, 2, d, u)
                dx1[i] = grad
                right_t[g_out, batch_cols(b), :] = grad.astype(LOW)
            ob[...] = dot_nt(right_t[g_out, at, :], wo[...]).astype(LOW)

        def back_attention(t):
            for i in range(many):
                b = t * many + i
                at = batch_cols(b)
                here = slice(i * rows, (i + 1) * rows)
                for h in range(HEADS):
                    hd = slice(h * head, (h + 1) * head)
                    vd = slice(width + h * head, width + (h + 1) * head)
                    sbuf[h] = dot_nt(ob[here, hd], kvext[b, :, vd])
                for h in range(HEADS):
                    a, da = af[b, h], sbuf[h]
                    ds = a * (da - jnp.sum(a * cnt[...] * da, axis=-1, keepdims=True))
                    cds[h] = ds.astype(LOW) * few[...]
                for h in range(HEADS):
                    hd = slice(h * head, (h + 1) * head)
                    vd = slice(width + h * head, width + (h + 1) * head)
                    dk = dot_tn(cds[h], qb[b, :, hd]) * score_scale
                    dv = dot_tn(ca[b, h], ob[here, hd])
                    for part, cols in ((dk, hd), (dv, vd)):
                        hsend[b, 0, :, cols] = part[0:REACH].astype(LOW)
                        dkv[i, :, cols] = part[REACH : REACH + rows]
                        hsend[b, 1, :, cols] = part[REACH + rows : ext].astype(LOW)
                for copy in halos(b):
                    copy.start()
                for h in range(HEADS):
                    hd = slice(h * head, (h + 1) * head)
                    right_t[g_q, at, hd] = (dot(cds[h], kvext[b, :, hd]) * score_scale).astype(LOW)

        def back_second(t):
            at = turn_cols(t)
            ids_rows = wide(sel[own_rows, :])
            edge = rows - REACH
            dn = dot_nt(right_t[g_q, at, :], wq[:, 0:width])
            for i in range(many):
                b = t * many + i
                for copy in halos(b):
                    copy.wait_recv()
                dkv[i, 0:REACH, :] += hrecv[b, 0].astype(F32)
                dkv[i, edge:rows, :] += hrecv[b, 1].astype(F32)
                for g in range(2):
                    right_t[g_k + g, batch_cols(b), :] = dkv[i, :, g * width : (g + 1) * width].astype(LOW)
            for g in range(2):
                dn = dn + dot_nt(right_t[g_k + g, at, :], wq[:, (g + 1) * width : (g + 2) * width])
            for i in range(many):
                b = t * many + i
                d = dn[i * rows : (i + 1) * rows]
                u = ua[b]
                grad = dx1[i] + norm_back(d, u, ia[b][:, 0:1], mod_rows(b, 0, ids_rows))
                ig[0, b] = grad.astype(LOW)

                @pl.when(sec == 1)
                def _(b=b):
                    relay_back(b).start()

                mod_sums(b, 0, d, u)

        def relay_back(b):
            return remote(ig.at[0, b], dybuf.at[b], bx_s.at[b], bx_r.at[b], (other, me))

        kvext[:, ext:window, :] = jnp.zeros((batches, window - ext, 2 * width), LOW)
        sm[...] = jnp.zeros(sm.shape, F32)
        for copy in loads[1:]:
            copy.wait()
        for copy in (m_down, m_up):
            copy.wait()

        @pl.when(sec == 0)
        def _():
            first_load.wait()
            x_down.wait()
            x_up.wait()

        @pl.when(sec == 1)
        def _():
            last_load.wait()

            @pl.loop(0, z.turns)
            def _(t):
                given(t)

        for t in range(z.turns):

            @pl.when(sec == 1)
            def _(t=t):
                for i in range(many):
                    for copy in relay(t * many + i):
                        copy.wait_recv()

            forward(t)

            @pl.when(sec == 0)
            def _(t=t):
                for i in range(many):
                    for copy in relay(t * many + i):
                        copy.start()

        @pl.when(sec == 0)
        def _():
            lax.fori_loop(0, batches, transposes, 0)

        early = 2 * groups + 1

        def rows_of(c, size):
            return pl.ds(pl.multiple_of(c * size, size), size)

        def turned(p):
            return lax.div(lax.rem(p, 4), 3) if stages > 2 else 0 * p

        def bit_of(p, k):
            bits = list(z.bits)
            if stages > 2:
                bits[1], bits[2] = bits[2], bits[1]
            return z.bits[k] + (bits[k] - z.bits[k]) * turned(p)

        def piece_copy(p, k):
            return remote(gives[k].at[p], gets[k].at[p], p_s.at[p, k], p_r.at[p, k], (sec, mate(bit_of(p, k))))

        def piece_start(p):
            away = 1 - side(1)
            gives[0][p] = dot(left_t[z.left(p), rows_of(away, half), :], right_t[z.right(p)]).astype(LOW)
            piece_copy(p, 0).start()

        def piece_first(p):
            own_half = dot(left_t[z.left(p), rows_of(side(1), half), :], right_t[z.right(p)])
            piece_copy(p, 0).wait_recv()
            acc[...] = own_half + gets[0][p].astype(F32)
            here = side(bit_of(p, 1))
            run = half // 4
            for j in range(2):
                at = [
                    (1 - turned(p)) * (2 * s + j) + turned(p) * (2 * j + s)
                    for s in (1 - here, here)
                ]
                part = slice(j * run, (j + 1) * run)
                gives[1][p, part, :] = acc[rows_of(at[0], run), :].astype(LOW)
                keeps[0][p, part, :] = acc[rows_of(at[1], run), :]
            piece_copy(p, 1).start()

        def piece_step(p, k):
            size = half >> k
            piece_copy(p, k).wait_recv()
            if k == stages - 1:
                o_piece[p] = keeps[k - 1][p] + gets[k][p].astype(F32)
                return
            here = side(bit_of(p, k + 1))
            for to, c in ((gives[k + 1], 1 - here), (keeps[k], here)):
                at = rows_of(c, size // 2)
                to[p] = (keeps[k - 1][p, at, :] + gets[k][p, at, :].astype(F32)).astype(to.dtype)
                if to is gives[k + 1]:
                    piece_copy(p, k + 1).start()

        def pieces(step, first, last):
            @pl.loop(first, last)
            def _(p):
                step(p)

        def only_first(body):
            if z.scatter:
                pl.when(sec == 0)(body)

        for t in reversed(range(z.turns)):

            @pl.when(sec == 0)
            def _(t=t):
                for i in range(many):
                    relay_back(t * many + i).wait_recv()
                given(t)

            if t == 0:

                @only_first
                def _():
                    pieces(piece_start, 0, groups)
                    pieces(piece_first, 0, groups)

            back_ffn(t)
            back_attention(t)
            if t == 0:

                @only_first
                def _():
                    pieces(lambda p: piece_step(p, 1), 0, groups)
                    pieces(piece_start, groups, early)
                    pieces(piece_first, groups, early)

            back_second(t)

        @pl.when(sec == 1)
        def _():
            lax.fori_loop(0, batches, transposes, 0)

        lines = [sm[b, m : m + 1, :] for b in range(batches) for m in range(z.meshes)]
        for line in (6, 7):
            lines.append(sum(sm[b, line : line + 1, :] for b in range(batches)))
        lines.append(jnp.zeros((16 - len(lines), sm.shape[2]), F32))
        small = jnp.concatenate(lines, axis=0)

        def finish():
            @pl.loop(0, batches)
            def _(b):
                @pl.when(sec == 0)
                def _():
                    for copy in relay(b):
                        copy.wait_send()

                @pl.when(sec == 1)
                def _():
                    relay_back(b).wait_send()

                for copy in halos(b):
                    copy.wait_send()

        if not z.scatter:
            small_out[...] = small
            table_out[...] = emb[...]
            finish()
            return

        def ring_copy(k):
            return remote(msend.at[k], mrecv.at[k], m_s.at[k], m_r.at[k], (sec, mate(1 << k)))

        def ring_start(k, value):
            msend[k] = value.astype(LOW)
            ring_copy(k).start()

        def ring_end(k):
            ring_copy(k).wait_recv()
            value = msend[k].astype(F32) + mrecv[k].astype(F32)
            if k + 1 < z.rings:
                ring_start(k + 1, value)
            else:
                tot[...] = value

        ring_start(0, small)

        @pl.when(sec == 0)
        def _():
            pieces(piece_start, early, npiece)
            pieces(piece_first, early, npiece)

        lags = [0, 1] + [4 + 2 * k for k in range(stages - 1)]
        fresh, stepped = (1 - sec) * npiece, (1 - sec) * groups

        @pl.loop((1 - sec) * (lags[2] + 1), npiece + lags[-1])
        def _(p):
            @pl.when((p >= fresh) & (p < npiece))
            def _():
                piece_start(p)

            @pl.when((p >= fresh + 1) & (p < npiece + 1))
            def _():
                piece_first(p - 1)

            for k in range(1, stages):
                lag = lags[k + 1]
                begin = stepped + lag if k == 1 else lag

                @pl.when((p >= begin) & (p < npiece + lag))
                def _(k=k, lag=lag):
                    piece_step(p - lag, k)

            for k in range(z.rings):

                @pl.when(p == groups + lags[2] + 1 + k)
                def _(k=k):
                    ring_end(k)

        count = batches * z.meshes
        table = emb[pl.ds(pl.multiple_of(me * own, own), own), :]
        grad = jnp.zeros((own, 4 * width), F32)
        for k in range(count):
            grad = grad + table[:, k : k + 1] * tot[k : k + 1, :]
        o_mod[0] = grad
        cols = 4 * width // shards
        mine = tot[:, pl.ds(pl.multiple_of(me * cols, cols), cols)]
        o_line[0:1, :] = jnp.sum(mine[0:count], axis=0, keepdims=True)
        o_line[1:2, :] = mine[count : count + 1]
        ratio = 128 // own
        line = tot[:, pl.ds(pl.multiple_of(me // ratio * 128, 128), 128)][count + 1 : count + 2]
        value = line
        for k in range(1, ratio):
            rolled = jnp.concatenate([line[:, k * own :], line[:, : k * own]], axis=1)
            value = jnp.where(me % ratio == k, rolled, value)
        o_line[2:3, :] = value
        finish()

        @pl.loop(0, npiece)
        def _(p):
            for k in range(stages):
                piece_copy(p, k).wait_send()

        for k in range(z.rings):
            ring_copy(k).wait_send()

    return kernel


def layout_of(z):
    own, groups = z.own, z.groups

    def kernel(
        lo, ig, piece, mod, line,
        o_lo, o_ig, o_qkv, o_out, o_up, o_upb, o_down, o_downb, o_mod, o_modb,
        v_lo, v_ig, v_piece, v_mod, into, back,
    ):
        moves = [(lo, v_lo, o_lo), (ig, v_ig, o_ig)]
        targets = [o_down.at[0, pl.ds(q * own, own), :] for q in range(groups)]
        targets += [o_up.at[0, :, pl.ds(q * TILE, TILE)] for q in range(groups)]
        targets += [o_out.at[0]] + [o_qkv.at[0, :, pl.ds(q * TILE, TILE)] for q in range(3)]
        moves += [(piece.at[k], v_piece.at[k], target) for k, target in enumerate(targets)]
        moves += [(mod, v_mod, o_mod)]
        firsts = [pltpu.make_async_copy(a, b, into.at[k]) for k, (a, b, _) in enumerate(moves)]
        lasts = [pltpu.make_async_copy(b, c, back.at[k]) for k, (_, b, c) in enumerate(moves)]
        for copy in firsts:
            copy.start()
        o_modb[...] = line[0:1, :]
        o_upb[...] = line[1:2, :]
        o_downb[...] = line[2:3, 0:own]
        for first, last in zip(firsts, lasts):
            first.wait()
            last.start()
        for copy in lasts:
            copy.wait()

    return kernel


def body(
    inputs,
    cotangent,
    neighbours,
    mesh_ids,
    noise_sigma,
    w_qkv,
    w_out,
    w_up,
    b_up,
    w_down,
    b_down,
    w_mod,
    b_mod,
):
    shards = lax.axis_size("nodes")
    z = Sizes(inputs, neighbours, noise_sigma, w_up, shards)
    batches, rows, width, hidden, many = z.batches, z.rows, z.width, z.hidden, z.together
    own, npiece = z.own, z.pieces
    shape = jax.ShapeDtypeStruct
    stack = shape((1, batches, rows, width), LOW)
    outs = [stack, stack]
    sides = [(z.lefts, TILE, batches * rows), (z.rights, batches * rows, TILE)]
    if z.scatter:
        outs += [shape((npiece, own, TILE), F32), shape((1, own, 4 * width), F32), shape((8, 128), F32)]
        scratch = [pltpu.VMEM(side, LOW) for side in sides]
    else:
        outs += [shape(side, LOW) for side in sides] + [shape((16, hidden), F32), shape((width, 128), F32)]
        scratch = []
    dma = pltpu.SemaphoreType.DMA
    scratch += [
        pltpu.VMEM((width, 3 * width), LOW),
        pltpu.VMEM((width, width), LOW),
        pltpu.VMEM((width, hidden), LOW),
        pltpu.VMEM((hidden, width), LOW),
        pltpu.VMEM((width, 4 * width), LOW),
        pltpu.VMEM((batches, z.ext, width), LOW),
        pltpu.VMEM((batches, rows, width), LOW),
        pltpu.VMEM((z.ext, 128), F32),
        pltpu.VMEM((16, rows), LOW),
        pltpu.VMEM((rows, z.window), F32),
        pltpu.VMEM((rows, z.window), LOW),
        pltpu.VMEM((rows, z.window), F32),
        pltpu.VMEM((batches, 8, 4 * width), F32),
        pltpu.VMEM((width, 128), F32),
        pltpu.VMEM((many * z.ext, width), LOW),
        pltpu.VMEM((batches, rows, width), LOW),
        pltpu.VMEM((batches, rows, width), F32),
        pltpu.VMEM((batches, rows, 128), F32),
        pltpu.VMEM((batches, rows, width), LOW),
        pltpu.VMEM((batches, z.window, 2 * width), LOW),
        pltpu.VMEM((HEADS, rows, z.window), F32),
        pltpu.VMEM((batches, HEADS, rows, z.window), F32),
        pltpu.VMEM((batches, HEADS, rows, z.window), LOW),
        pltpu.VMEM((batches, rows, width), LOW),
        pltpu.VMEM((batches, rows, width), LOW),
        pltpu.VMEM((batches, rows, width), F32),
        pltpu.VMEM((batches, rows, 128), F32),
        pltpu.VMEM((many * rows, width), F32),
        pltpu.VMEM((batches, rows, hidden), LOW),
        pltpu.VMEM((batches, rows, hidden), LOW),
        pltpu.VMEM((many * rows, width), LOW),
        pltpu.VMEM((HEADS, rows, z.window), LOW),
        pltpu.VMEM((many, rows, width), F32),
        pltpu.VMEM((many, rows, 2 * width), F32),
        pltpu.VMEM((batches, 2, REACH, 2 * width), LOW),
        pltpu.VMEM((batches, 2, REACH, 2 * width), LOW),
        pltpu.VMEM((batches, 8, hidden), F32),
        dma((7,)),
        dma((2,)),
        dma((2,)),
        dma((2,)),
        dma((2,)),
        dma((batches, 3)),
        dma((batches, 3)),
        dma((batches, 2)),
        dma((batches, 2)),
        dma((batches,)),
        dma((batches,)),
    ]
    if z.scatter:
        stages = len(z.bits)
        sizes = [TILE >> (k + 1) for k in range(stages)]
        scratch += [pltpu.VMEM((npiece, size, TILE), LOW) for size in sizes + sizes]
        scratch += [pltpu.VMEM((npiece, size, TILE), F32) for size in sizes[1:]]
        scratch += [
            pltpu.VMEM((sizes[0], TILE), F32),
            pltpu.VMEM((z.rings, 16, hidden), LOW),
            pltpu.VMEM((z.rings, 16, hidden), LOW),
            pltpu.VMEM((16, hidden), F32),
            dma((npiece, stages)),
            dma((npiece, stages)),
            dma((z.rings,)),
            dma((z.rings,)),
        ]
    hbm = pl.BlockSpec(memory_space=pl.ANY)
    vmem = pl.BlockSpec(memory_space=pltpu.VMEM)
    smem = pl.BlockSpec(memory_space=pltpu.SMEM)
    got = pl.pallas_call(
        kernel_of(z),
        out_shape=outs,
        in_specs=[hbm, hbm, vmem, vmem, smem, hbm, hbm, hbm, vmem, hbm, vmem, hbm, vmem],
        out_specs=[vmem] * len(outs),
        scratch_shapes=scratch,
        compiler_params=pltpu.CompilerParams(
            collective_id=0, has_side_effects=True, vmem_limit_bytes=63 * 2**20
        ),
    )(
        inputs,
        cotangent,
        neighbours.T,
        mesh_ids.reshape(1, rows),
        noise_sigma.T,
        w_qkv,
        w_out,
        w_up,
        b_up,
        w_down,
        b_down,
        w_mod,
        b_mod,
    )
    if z.scatter:
        lo, ig, piece, mod, line = got
        return tuple(
            pl.pallas_call(
                layout_of(z),
                out_shape=[
                    stack,
                    stack,
                    shape((1, own, 3 * width), F32),
                    shape((1, own, width), F32),
                    shape((1, own, hidden), F32),
                    shape((1, hidden // shards), F32),
                    shape((1, hidden // shards, width), F32),
                    shape((1, own), F32),
                    shape((1, own, 4 * width), F32),
                    shape((1, 4 * width // shards), F32),
                ],
                in_specs=[hbm, hbm, hbm, hbm, vmem],
                out_specs=[hbm, hbm, hbm, hbm, hbm, vmem, hbm, vmem, hbm, vmem],
                scratch_shapes=[
                    pltpu.VMEM(stack.shape, LOW),
                    pltpu.VMEM(stack.shape, LOW),
                    pltpu.VMEM((npiece, own, TILE), F32),
                    pltpu.VMEM((1, own, 4 * width), F32),
                    dma((npiece + 3,)),
                    dma((npiece + 3,)),
                ],
                compiler_params=pltpu.CompilerParams(vmem_limit_bytes=63 * 2**20),
            )(lo, ig, piece, mod, line)
        )
    lo, ig, left_t, right_t, small, table = got
    groups = z.groups

    def summed(value):
        return lax.psum_scatter(value, "nodes", scatter_dimension=0, tiled=True)

    def wide_sum(left, first, last):
        return summed(jnp.concatenate([dot(left_t[left], right_t[r]) for r in range(first, last)], axis=1))[None]

    down = [dot(left_t[q], right_t[0]).reshape(TILE // 32, 32, TILE) for q in range(groups)]
    down = jnp.stack(down, axis=1)
    count = batches * z.meshes
    small = lax.psum(small, "nodes")
    me = lax.axis_index("nodes")
    mod = jnp.dot(table[:, :count], small[:count], precision=lax.Precision.HIGHEST)

    def mine(value):
        size = value.shape[0] // shards
        return lax.dynamic_slice_in_dim(value, me * size, size, axis=0)[None]

    return (
        lo,
        ig,
        wide_sum(groups + 2, 2 + groups, 5 + groups),
        wide_sum(groups + 1, 1 + groups, 2 + groups),
        wide_sum(groups, 1, 1 + groups),
        mine(small[count]),
        summed(down.reshape(hidden, width))[None],
        mine(small[count + 1, :width]),
        mine(mod),
        mine(jnp.sum(small[:count], axis=0)),
    )


def solution(mesh):
    return jax.shard_map(
        body,
        mesh=mesh,
        in_specs=(
            P(None, "nodes", None),
            P(None, "nodes", None),
            P("nodes", None),
            P("nodes"),
            P(),
            P("section", None, None),
            P("section", None, None),
            P("section", None, None),
            P("section", None),
            P("section", None, None),
            P("section", None),
            P("section", None, None),
            P("section", None),
        ),
        out_specs=(
            P("section", None, "nodes", None),
            P("section", None, "nodes", None),
            P("section", "nodes", None),
            P("section", "nodes", None),
            P("section", "nodes", None),
            P("section", "nodes"),
            P("section", "nodes", None),
            P("section", "nodes"),
            P("section", "nodes", None),
            P("section", "nodes"),
        ),
        check_vma=False,
    )
```

```python
import jax
import jax.numpy as jnp
from jax import lax
from jax.experimental import pallas as pl
from jax.experimental.pallas import tpu as pltpu
from jax.sharding import PartitionSpec as P

HEADS = 4
REACH = 32
EPSILON = 1e-06
MASKED = -1e9
ABSENT = -2e38
TILE = 512
TOGETHER = 2
MESH = pl.DeviceIdType.MESH
F32, LOW = jnp.float32, jnp.bfloat16


def dot(a, b):
    return lax.dot_general(a, b, (((1,), (0,)), ((), ())), preferred_element_type=F32)


def dot_nt(a, b):
    return lax.dot_general(a, b, (((1,), (1,)), ((), ())), preferred_element_type=F32)


def dot_tn(a, b):
    return lax.dot_general(a, b, (((0,), (0,)), ((), ())), preferred_element_type=F32)


class Sizes:
    def __init__(self, inputs, neighbours, noise, w_up, shards):
        self.batches, self.rows, self.width = inputs.shape
        self.together = TOGETHER if self.batches % TOGETHER == 0 else 1
        self.turns = self.batches // self.together
        self.slots = neighbours.shape[1]
        self.meshes = noise.shape[1]
        self.hidden = w_up.shape[2]
        self.shards = shards
        self.ext = self.rows + 2 * REACH
        self.window = (self.ext // 128 + 1) * 128
        self.groups = self.hidden // TILE
        self.own = self.width // shards
        self.scatter = self.own % 16 == 0
        self.pieces = 2 * self.groups + 4
        self.lefts = 3 + self.groups
        self.rights = 2 + self.groups + 3
        self.rings = max(shards.bit_length() - 1, 1)

        self.bits = [1 << k for k in range(shards.bit_length() - 1)]

    def left(self, p):
        n = self.groups
        return jnp.minimum(p, n) + lax.div(p, 2 * n) + lax.div(p, 2 * n + 1)

    def right(self, p):
        return jnp.maximum(p - (self.groups - 1), 0)


def kernel_of(z):
    batches, rows, width, ext, window = z.batches, z.rows, z.width, z.ext, z.window
    groups, shards, own, many = z.groups, z.shards, z.own, z.together
    head = width // HEADS
    score_scale = head ** (-0.5)
    log2e = 1.4426950408889634
    npiece = z.pieces
    half = TILE // 2
    stages = len(z.bits)
    g_out, g_q, g_k = 1 + groups, 2 + groups, 3 + groups

    def position(owner):
        if not z.scatter:
            return owner
        place = 0
        for bit in z.bits:
            place = 2 * place + owner // bit % 2
        return place

    def kernel(
        inputs, cotangent, neighbours, mesh_ids, sigma,
        w_qkv, w_out, w_up, b_up, w_down, b_down, w_mod, b_mod,
        lo, ig, *rest,
    ):
        if z.scatter:
            o_piece, o_mod, o_line, left_t, right_t = rest[:5]
            rest = rest[5:]
        else:
            left_t, right_t, small_out, table_out = rest[:4]
            rest = rest[4:]
        (
            wq, wo, wu, wd, wm, xext, dybuf, sel, pick, cnt, few, bias, mod, emb,
            n1, n1s, ua, ia, qb, kvext, sbuf, af, ca, obs, n2s, ub, ib, tb, fp, hs,
            ob, cds, dx1, dkv, hsend, hrecv, sm,
            lsem, hx_s, hx_r, hm_s, hm_r, fx_s, fx_r, bh_s, bh_r, bx_s, bx_r,
        ) = rest[:48]
        rest = rest[48:]
        if z.scatter:
            gives, gets, keeps = rest[:stages], rest[stages : 2 * stages], rest[2 * stages : 3 * stages - 1]
            acc, msend, mrecv, tot, p_s, p_r, m_s, m_r = rest[3 * stages - 1 :]

        sec = lax.axis_index("section")
        me = lax.axis_index("nodes")
        up = lax.rem(me + 1, shards)
        down = lax.rem(me + shards - 1, shards)
        other = 1 - sec
        def local(src, dst, k):
            return pltpu.make_async_copy(src, dst, lsem.at[k])

        loads = [
            local(w_mod.at[0], wm, 0),
            local(w_qkv.at[0], wq, 1),
            local(w_out.at[0], wo, 2),
            local(w_up.at[0], wu, 3),
            local(w_down.at[0], wd, 4),
        ]
        own_rows = pl.ds(REACH, rows)
        first_load = local(inputs, xext.at[:, own_rows, :], 5)
        last_load = local(cotangent, dybuf, 6)
        loads[0].start()

        @pl.when(sec == 0)
        def _():
            first_load.start()

        for copy in loads[1:]:
            copy.start()

        @pl.when(sec == 1)
        def _():
            last_load.start()

        def side(bit):
            return lax.rem(lax.div(me, bit), 2)

        def mate(bit):
            return me + bit - 2 * bit * side(bit)

        barrier = pltpu.get_barrier_semaphore()
        mates = [(sec, up), (sec, down), (other, me), (other, up), (other, down)]
        if z.scatter:
            mates += [(sec, mate(bit)) for bit in z.bits[1:]]
        for peer in mates:
            pl.semaphore_signal(barrier, inc=1, device_id=peer, device_id_type=MESH)
        pl.semaphore_wait(barrier, len(mates))

        def remote(src, dst, s_sem, r_sem, peer):
            return pltpu.make_async_remote_copy(
                src_ref=src, dst_ref=dst, send_sem=s_sem, recv_sem=r_sem, device_id=peer, device_id_type=MESH
            )

        low_rows, top_rows = pl.ds(0, REACH), pl.ds(REACH + rows, REACH)
        head_rows, tail_rows = pl.ds(REACH, REACH), pl.ds(rows, REACH)
        x_down = remote(inputs.at[:, pl.ds(0, REACH), :], xext.at[:, top_rows, :], hx_s.at[0], hx_r.at[0], (sec, down))
        x_up = remote(inputs.at[:, pl.ds(rows - REACH, REACH), :], xext.at[:, low_rows, :], hx_s.at[1], hx_r.at[1], (sec, up))

        @pl.when(sec == 0)
        def _():
            x_down.start()
            x_up.start()

        ids = jnp.broadcast_to(mesh_ids[...].astype(F32), (128, rows))
        sel[own_rows, :] = ids.T
        sample = lax.broadcasted_iota(jnp.int32, (16, rows), 0).astype(F32)
        pick[...] = jnp.where(ids[0:16] == sample, 1.0, 0.0).astype(LOW)
        m_down = remote(sel.at[head_rows, :], sel.at[top_rows, :], hm_s.at[0], hm_r.at[0], (sec, down))
        m_up = remote(sel.at[tail_rows, :], sel.at[low_rows, :], hm_s.at[1], hm_r.at[1], (sec, up))
        m_down.start()
        m_up.start()

        row_no = lax.broadcasted_iota(jnp.int32, (16, width // 2), 0)
        level = jnp.ones((16, width // 2), F32)
        for b in range(batches):
            for m in range(z.meshes):
                level = jnp.where(row_no == b * z.meshes + m, sigma[m, b], level)
        place = lax.broadcasted_iota(jnp.int32, (16, width // 2), 1).astype(F32)
        frequency = 3.0 * jnp.exp(-jnp.log(100.0) * place / (width // 2))
        angles = jnp.log(level) * frequency
        embedded = jnp.concatenate([jnp.sin(angles), jnp.cos(angles)], axis=1).astype(LOW)
        padded = jnp.concatenate([embedded.astype(F32), jnp.zeros((112, width), F32)], axis=0)
        emb[...] = padded.T
        loads[0].wait()
        for g in range(4):
            cols = pl.ds(g * width, width)
            table = dot(embedded, wm[:, cols]) + b_mod[:, cols] + (1.0 - g % 2)
            for b in range(batches):
                mod[b, 0 : z.meshes, cols] = table[b * z.meshes : (b + 1) * z.meshes]

        slots = neighbours[...].astype(F32)
        slots = jnp.concatenate([slots, jnp.zeros((128 - z.slots, rows), F32)], axis=0).T
        slots = jnp.where(slots >= 0, slots - (me * rows - REACH).astype(F32), float(ext))
        column = lax.broadcasted_iota(jnp.int32, (rows, window), 1).astype(F32)
        counts = jnp.zeros((rows, window), F32)
        for n in range(z.slots):
            counts = counts + jnp.where(slots[:, n : n + 1] == column, 1.0, 0.0)
        cnt[...] = counts
        few[...] = counts.astype(LOW)
        bias[...] = jnp.where(counts > 0, jnp.where(column == ext, MASKED * log2e, 0.0), ABSENT)

        def mod_rows(b, part, ids_rows):
            cols = pl.ds(part * width, width)
            value = jnp.broadcast_to(mod[b, 0:1, cols], (ids_rows.shape[0], width))
            for m in range(1, z.meshes):
                value = jnp.where(ids_rows > m - 0.5, mod[b, m : m + 1, cols], value)
            return value

        def wide(ids_rows):
            return jnp.concatenate([ids_rows] * (width // 128), axis=1)

        def unit(x):
            centred = x - jnp.mean(x, axis=-1, keepdims=True)
            inv = lax.rsqrt(jnp.mean(centred * centred, axis=-1, keepdims=True) + EPSILON)
            return centred * inv, inv

        def span_of(start, size):
            if isinstance(start, int):
                return pl.ds(start, size)
            return pl.ds(pl.multiple_of(start, size), size)

        def batch_cols(b):
            return span_of(b * rows, rows)

        def turn_cols(t):
            return span_of(t * many * rows, many * rows)

        def turn_of(ref, t):
            return ref[pl.ds(t * many, many)].reshape(many * rows, ref.shape[2])

        span = own if z.scatter else 32

        def transposes(b, carry):
            for first, ref in ((groups, n2s), (groups + 1, obs), (groups + 2, n1s)):
                turned = ref[b].T
                for owner in range(TILE // span):
                    at = position(owner) * span
                    left_t[first, at : at + span, batch_cols(b)] = turned[owner * span : (owner + 1) * span]
            run = groups * span
            for g in range(groups):
                turned = hs[b, :, g * TILE : (g + 1) * TILE].T
                for k in range(TILE // span):
                    at = g * TILE + k * span
                    owner, part = at // run, at % run // span
                    to = position(owner) * span
                    left_t[part, to : to + span, batch_cols(b)] = turned[k * span : (k + 1) * span]
            return carry

        heads = [slice(h * head, (h + 1) * head) for h in range(HEADS)]
        heads_v = [slice(width + h * head, width + (h + 1) * head) for h in range(HEADS)]
        tiles = [slice(g * TILE, (g + 1) * TILE) for g in range(groups)]
        thirds = [slice(g * width, (g + 1) * width) for g in range(3)]

        def forward(b):
            ids_rows = wide(sel[0:ext, :])
            u, inv = unit(xext[b].astype(F32))
            normed = (u * mod_rows(b, 0, ids_rows) + mod_rows(b, 1, ids_rows)).astype(LOW)
            n1[...] = normed
            n1s[b] = normed[REACH : REACH + rows]
            ua[b] = u[REACH : REACH + rows]
            ia[b] = jnp.broadcast_to(inv[REACH : REACH + rows], (rows, 128))
            kvext[b, 0:ext, thirds[0]] = dot(n1[...], wq[:, thirds[1]]).astype(LOW)
            qb[b] = dot(n1s[b], wq[:, thirds[0]]).astype(LOW)
            for h in range(HEADS):
                sbuf[h] = dot_nt(qb[b, :, heads[h]], kvext[b, :, heads[h]]) * (score_scale * log2e) + bias[...]
            kvext[b, 0:ext, thirds[1]] = dot(n1[...], wq[:, thirds[2]]).astype(LOW)
            for h in range(HEADS):
                s = sbuf[h]
                e = jnp.exp2(s - jnp.max(s, axis=-1, keepdims=True))
                a = e * (1.0 / jnp.sum(e * cnt[...], axis=-1, keepdims=True))
                af[b, h] = a
                ca[b, h] = a.astype(LOW) * few[...]
            for h in range(HEADS):
                obs[b, :, heads[h]] = dot(ca[b, h], kvext[b, :, heads_v[h]]).astype(LOW)

            x1 = xext[b, own_rows, :].astype(F32) + dot(obs[b], wo[...])
            u, inv = unit(x1)
            ub[b] = u
            ib[b] = jnp.broadcast_to(inv, (rows, 128))
            ids_rows = wide(sel[own_rows, :])
            n2s[b] = (u * mod_rows(b, 2, ids_rows) + mod_rows(b, 3, ids_rows)).astype(LOW)
            tb[...] = x1 + b_down[...]
            for gs in tiles:
                gate = dot(n2s[b], wu[:, gs]) + b_up[:, gs]
                s = 0.5 + 0.5 * jnp.tanh(0.5 * gate)
                hid = gate * s
                fp[b, :, gs] = (s + hid * (1.0 - s)).astype(LOW)
                hid = hid.astype(LOW)
                hs[b, :, gs] = hid
                tb[...] += dot(hid, wd[gs, :])
            lo[0, b] = tb[...].astype(LOW)

        def relay(b):
            return [
                remote(lo.at[0, b], xext.at[b, own_rows, :], fx_s.at[b, 0], fx_r.at[b, 0], (other, me)),
                remote(lo.at[0, b, pl.ds(0, REACH), :], xext.at[b, top_rows, :], fx_s.at[b, 1], fx_r.at[b, 1], (other, down)),
                remote(lo.at[0, b, pl.ds(rows - REACH, REACH), :], xext.at[b, low_rows, :], fx_s.at[b, 2], fx_r.at[b, 2], (other, up)),
            ]

        def norm_back(d, u, inv, scale):
            scaled = d * scale
            return inv * (
                scaled
                - jnp.mean(scaled, axis=-1, keepdims=True)
                - u * jnp.mean(scaled * u, axis=-1, keepdims=True)
            )

        def mod_sums(b, part, d, u):
            for k, value in enumerate((d * u, d)):
                total = dot(pick[...], value.astype(LOW))
                sm[b, 0 : z.meshes, (part + k) * width : (part + k + 1) * width] = total[0 : z.meshes]

        def halos(b):
            return [
                remote(hsend.at[b, 0], hrecv.at[b, 1], bh_s.at[b, 0], bh_r.at[b, 0], (sec, down)),
                remote(hsend.at[b, 1], hrecv.at[b, 0], bh_s.at[b, 1], bh_r.at[b, 1], (sec, up)),
            ]

        def given(t):
            at = turn_cols(t)
            dr = turn_of(dybuf, t)
            right_t[0, at, :] = dr
            for i in range(many):
                total = jnp.sum(dr[i * rows : (i + 1) * rows].astype(F32), axis=0, keepdims=True)
                sm[t * many + i, 7:8, 0:width] = total
            for g in range(groups):
                right_t[1 + g, at, :] = dot_nt(dr, wd[g * TILE : (g + 1) * TILE, :]).astype(LOW)

        def back_ffn(t):
            at = turn_cols(t)
            dn = jnp.zeros((many * rows, width), F32)
            for g in range(groups):
                gs = slice(g * TILE, (g + 1) * TILE)
                dg = right_t[1 + g, at, :].astype(F32) * turn_of(fp, t)[:, gs].astype(F32)
                sm[t * many, 6:7, gs] = jnp.sum(dg, axis=0, keepdims=True)
                dg = dg.astype(LOW)
                right_t[1 + g, at, :] = dg
                dn = dn + dot_nt(dg, wu[:, gs])
            ids_rows = wide(sel[own_rows, :])
            for i in range(many):
                b = t * many + i
                d = dn[i * rows : (i + 1) * rows]
                u = ub[b]
                grad = dybuf[b].astype(F32) + norm_back(d, u, ib[b][:, 0:1], mod_rows(b, 2, ids_rows))
                mod_sums(b, 2, d, u)
                dx1[i] = grad
                right_t[g_out, batch_cols(b), :] = grad.astype(LOW)
            ob[...] = dot_nt(right_t[g_out, at, :], wo[...]).astype(LOW)

        def back_attention(t):
            for i in range(many):
                b = t * many + i
                at = batch_cols(b)
                here = slice(i * rows, (i + 1) * rows)
                for h in range(HEADS):
                    hd = slice(h * head, (h + 1) * head)
                    vd = slice(width + h * head, width + (h + 1) * head)
                    sbuf[h] = dot_nt(ob[here, hd], kvext[b, :, vd])
                for h in range(HEADS):
                    a, da = af[b, h], sbuf[h]
                    ds = a * (da - jnp.sum(a * cnt[...] * da, axis=-1, keepdims=True))
                    cds[h] = ds.astype(LOW) * few[...]
                for h in range(HEADS):
                    hd = slice(h * head, (h + 1) * head)
                    vd = slice(width + h * head, width + (h + 1) * head)
                    dk = dot_tn(cds[h], qb[b, :, hd]) * score_scale
                    dv = dot_tn(ca[b, h], ob[here, hd])
                    for part, cols in ((dk, hd), (dv, vd)):
                        hsend[b, 0, :, cols] = part[0:REACH].astype(LOW)
                        dkv[i, :, cols] = part[REACH : REACH + rows]
                        hsend[b, 1, :, cols] = part[REACH + rows : ext].astype(LOW)
                for copy in halos(b):
                    copy.start()
                for h in range(HEADS):
                    hd = slice(h * head, (h + 1) * head)
                    right_t[g_q, at, hd] = (dot(cds[h], kvext[b, :, hd]) * score_scale).astype(LOW)

        def back_second(t):
            at = turn_cols(t)
            ids_rows = wide(sel[own_rows, :])
            edge = rows - REACH
            dn = dot_nt(right_t[g_q, at, :], wq[:, 0:width])
            for i in range(many):
                b = t * many + i
                for copy in halos(b):
                    copy.wait_recv()
                dkv[i, 0:REACH, :] += hrecv[b, 0].astype(F32)
                dkv[i, edge:rows, :] += hrecv[b, 1].astype(F32)
                for g in range(2):
                    right_t[g_k + g, batch_cols(b), :] = dkv[i, :, g * width : (g + 1) * width].astype(LOW)
            for g in range(2):
                dn = dn + dot_nt(right_t[g_k + g, at, :], wq[:, (g + 1) * width : (g + 2) * width])
            for i in range(many):
                b = t * many + i
                d = dn[i * rows : (i + 1) * rows]
                u = ua[b]
                grad = dx1[i] + norm_back(d, u, ia[b][:, 0:1], mod_rows(b, 0, ids_rows))
                ig[0, b] = grad.astype(LOW)

                @pl.when(sec == 1)
                def _(b=b):
                    relay_back(b).start()

                mod_sums(b, 0, d, u)

        def relay_back(b):
            return remote(ig.at[0, b], dybuf.at[b], bx_s.at[b], bx_r.at[b], (other, me))

        kvext[:, ext:window, :] = jnp.zeros((batches, window - ext, 2 * width), LOW)
        sm[...] = jnp.zeros(sm.shape, F32)
        for copy in loads[1:]:
            copy.wait()
        for copy in (m_down, m_up):
            copy.wait()

        @pl.when(sec == 0)
        def _():
            first_load.wait()
            x_down.wait()
            x_up.wait()

        @pl.when(sec == 1)
        def _():
            last_load.wait()

            @pl.loop(0, z.turns)
            def _(t):
                given(t)

        @pl.loop(0, batches)
        def _(b):
            @pl.when(sec == 1)
            def _():
                for copy in relay(b):
                    copy.wait_recv()

            forward(b)

            @pl.when(sec == 0)
            def _():
                for copy in relay(b):
                    copy.start()

        @pl.when(sec == 0)
        def _():
            lax.fori_loop(0, batches, transposes, 0)

        def rows_of(c, size):
            return pl.ds(pl.multiple_of(c * size, size), size)

        def turned(p):
            return lax.div(lax.rem(p, 4), 3) if stages > 2 else 0 * p

        def bit_of(p, k):
            bits = list(z.bits)
            if stages > 2:
                bits[1], bits[2] = bits[2], bits[1]
            return z.bits[k] + (bits[k] - z.bits[k]) * turned(p)

        def piece_copy(p, k):
            return remote(gives[k].at[p], gets[k].at[p], p_s.at[p, k], p_r.at[p, k], (sec, mate(bit_of(p, k))))

        def piece_start(p):
            away = 1 - side(1)
            gives[0][p] = dot(left_t[z.left(p), rows_of(away, half), :], right_t[z.right(p)]).astype(LOW)
            piece_copy(p, 0).start()

        def piece_first(p):
            own_half = dot(left_t[z.left(p), rows_of(side(1), half), :], right_t[z.right(p)])
            piece_copy(p, 0).wait_recv()
            acc[...] = own_half + gets[0][p].astype(F32)
            here = side(bit_of(p, 1))
            run = half // 4
            for j in range(2):
                at = [
                    (1 - turned(p)) * (2 * s + j) + turned(p) * (2 * j + s)
                    for s in (1 - here, here)
                ]
                part = slice(j * run, (j + 1) * run)
                gives[1][p, part, :] = acc[rows_of(at[0], run), :].astype(LOW)
                keeps[0][p, part, :] = acc[rows_of(at[1], run), :]
            piece_copy(p, 1).start()

        def piece_step(p, k):
            size = half >> k
            piece_copy(p, k).wait_recv()
            if k == stages - 1:
                o_piece[p] = keeps[k - 1][p] + gets[k][p].astype(F32)
                return
            here = side(bit_of(p, k + 1))
            for to, c in ((gives[k + 1], 1 - here), (keeps[k], here)):
                at = rows_of(c, size // 2)
                to[p] = (keeps[k - 1][p, at, :] + gets[k][p, at, :].astype(F32)).astype(to.dtype)
                if to is gives[k + 1]:
                    piece_copy(p, k + 1).start()

        def pieces(step, first, last):
            @pl.loop(first, last)
            def _(p):
                step(p)

        def only_first(body):
            if z.scatter:
                pl.when(sec == 0)(body)

        for t in reversed(range(z.turns)):

            @pl.when(sec == 0)
            def _(t=t):
                for i in range(many):
                    relay_back(t * many + i).wait_recv()
                given(t)

            back_ffn(t)
            back_attention(t)
            if t == 0:

                @only_first
                def _():
                    pieces(piece_start, 0, groups)

            back_second(t)

        @pl.when(sec == 1)
        def _():
            lax.fori_loop(0, batches, transposes, 0)

        lines = [sm[b, m : m + 1, :] for b in range(batches) for m in range(z.meshes)]
        for line in (6, 7):
            lines.append(sum(sm[b, line : line + 1, :] for b in range(batches)))
        lines.append(jnp.zeros((16 - len(lines), sm.shape[2]), F32))
        small = jnp.concatenate(lines, axis=0)

        def finish():
            @pl.loop(0, batches)
            def _(b):
                @pl.when(sec == 0)
                def _():
                    for copy in relay(b):
                        copy.wait_send()

                @pl.when(sec == 1)
                def _():
                    relay_back(b).wait_send()

                for copy in halos(b):
                    copy.wait_send()

        if not z.scatter:
            small_out[...] = small
            table_out[...] = emb[...]
            finish()
            return

        def ring_copy(k):
            return remote(msend.at[k], mrecv.at[k], m_s.at[k], m_r.at[k], (sec, mate(1 << k)))

        def ring_start(k, value):
            msend[k] = value.astype(LOW)
            ring_copy(k).start()

        def ring_end(k):
            ring_copy(k).wait_recv()
            value = msend[k].astype(F32) + mrecv[k].astype(F32)
            if k + 1 < z.rings:
                ring_start(k + 1, value)
            else:
                tot[...] = value

        ring_start(0, small)

        lags = [0, 1] + [4 + 2 * k for k in range(stages - 1)]
        begun = (1 - sec) * groups

        @pl.loop(0, npiece + lags[-1])
        def _(p):
            @pl.when((p >= begun) & (p < npiece))
            def _():
                piece_start(p)

            @pl.when((p >= 1) & (p < npiece + 1))
            def _():
                piece_first(p - 1)

            for k in range(1, stages):
                lag = lags[k + 1]

                @pl.when((p >= lag) & (p < npiece + lag))
                def _(k=k, lag=lag):
                    piece_step(p - lag, k)

            for k in range(z.rings):

                @pl.when(p == 3 + 2 * k)
                def _(k=k):
                    ring_end(k)

        count = batches * z.meshes
        table = emb[pl.ds(pl.multiple_of(me * own, own), own), :]
        grad = jnp.zeros((own, 4 * width), F32)
        for k in range(count):
            grad = grad + table[:, k : k + 1] * tot[k : k + 1, :]
        o_mod[0] = grad
        cols = 4 * width // shards
        mine = tot[:, pl.ds(pl.multiple_of(me * cols, cols), cols)]
        o_line[0:1, :] = jnp.sum(mine[0:count], axis=0, keepdims=True)
        o_line[1:2, :] = mine[count : count + 1]
        ratio = 128 // own
        line = tot[:, pl.ds(pl.multiple_of(me // ratio * 128, 128), 128)][count + 1 : count + 2]
        value = line
        for k in range(1, ratio):
            rolled = jnp.concatenate([line[:, k * own :], line[:, : k * own]], axis=1)
            value = jnp.where(me % ratio == k, rolled, value)
        o_line[2:3, :] = value
        finish()

        @pl.loop(0, npiece)
        def _(p):
            for k in range(stages):
                piece_copy(p, k).wait_send()

        for k in range(z.rings):
            ring_copy(k).wait_send()

    return kernel


def layout_of(z):
    own, groups = z.own, z.groups

    def kernel(
        lo, ig, piece, mod, line,
        o_lo, o_ig, o_qkv, o_out, o_up, o_upb, o_down, o_downb, o_mod, o_modb,
        v_lo, v_ig, v_piece, v_mod, into, back,
    ):
        moves = [(lo, v_lo, o_lo), (ig, v_ig, o_ig)]
        targets = [o_down.at[0, pl.ds(q * own, own), :] for q in range(groups)]
        targets += [o_up.at[0, :, pl.ds(q * TILE, TILE)] for q in range(groups)]
        targets += [o_out.at[0]] + [o_qkv.at[0, :, pl.ds(q * TILE, TILE)] for q in range(3)]
        moves += [(piece.at[k], v_piece.at[k], target) for k, target in enumerate(targets)]
        moves += [(mod, v_mod, o_mod)]
        firsts = [pltpu.make_async_copy(a, b, into.at[k]) for k, (a, b, _) in enumerate(moves)]
        lasts = [pltpu.make_async_copy(b, c, back.at[k]) for k, (_, b, c) in enumerate(moves)]
        for copy in firsts:
            copy.start()
        o_modb[...] = line[0:1, :]
        o_upb[...] = line[1:2, :]
        o_downb[...] = line[2:3, 0:own]
        for first, last in zip(firsts, lasts):
            first.wait()
            last.start()
        for copy in lasts:
            copy.wait()

    return kernel


def body(
    inputs,
    cotangent,
    neighbours,
    mesh_ids,
    noise_sigma,
    w_qkv,
    w_out,
    w_up,
    b_up,
    w_down,
    b_down,
    w_mod,
    b_mod,
):
    shards = lax.axis_size("nodes")
    z = Sizes(inputs, neighbours, noise_sigma, w_up, shards)
    batches, rows, width, hidden, many = z.batches, z.rows, z.width, z.hidden, z.together
    own, npiece = z.own, z.pieces
    shape = jax.ShapeDtypeStruct
    stack = shape((1, batches, rows, width), LOW)
    outs = [stack, stack]
    sides = [(z.lefts, TILE, batches * rows), (z.rights, batches * rows, TILE)]
    if z.scatter:
        outs += [shape((npiece, own, TILE), F32), shape((1, own, 4 * width), F32), shape((8, 128), F32)]
        scratch = [pltpu.VMEM(side, LOW) for side in sides]
    else:
        outs += [shape(side, LOW) for side in sides] + [shape((16, hidden), F32), shape((width, 128), F32)]
        scratch = []
    dma = pltpu.SemaphoreType.DMA
    scratch += [
        pltpu.VMEM((width, 3 * width), LOW),
        pltpu.VMEM((width, width), LOW),
        pltpu.VMEM((width, hidden), LOW),
        pltpu.VMEM((hidden, width), LOW),
        pltpu.VMEM((width, 4 * width), LOW),
        pltpu.VMEM((batches, z.ext, width), LOW),
        pltpu.VMEM((batches, rows, width), LOW),
        pltpu.VMEM((z.ext, 128), F32),
        pltpu.VMEM((16, rows), LOW),
        pltpu.VMEM((rows, z.window), F32),
        pltpu.VMEM((rows, z.window), LOW),
        pltpu.VMEM((rows, z.window), F32),
        pltpu.VMEM((batches, 8, 4 * width), F32),
        pltpu.VMEM((width, 128), F32),
        pltpu.VMEM((z.ext, width), LOW),
        pltpu.VMEM((batches, rows, width), LOW),
        pltpu.VMEM((batches, rows, width), F32),
        pltpu.VMEM((batches, rows, 128), F32),
        pltpu.VMEM((batches, rows, width), LOW),
        pltpu.VMEM((batches, z.window, 2 * width), LOW),
        pltpu.VMEM((HEADS, rows, z.window), F32),
        pltpu.VMEM((batches, HEADS, rows, z.window), F32),
        pltpu.VMEM((batches, HEADS, rows, z.window), LOW),
        pltpu.VMEM((batches, rows, width), LOW),
        pltpu.VMEM((batches, rows, width), LOW),
        pltpu.VMEM((batches, rows, width), F32),
        pltpu.VMEM((batches, rows, 128), F32),
        pltpu.VMEM((rows, width), F32),
        pltpu.VMEM((batches, rows, hidden), LOW),
        pltpu.VMEM((batches, rows, hidden), LOW),
        pltpu.VMEM((many * rows, width), LOW),
        pltpu.VMEM((HEADS, rows, z.window), LOW),
        pltpu.VMEM((many, rows, width), F32),
        pltpu.VMEM((many, rows, 2 * width), F32),
        pltpu.VMEM((batches, 2, REACH, 2 * width), LOW),
        pltpu.VMEM((batches, 2, REACH, 2 * width), LOW),
        pltpu.VMEM((batches, 8, hidden), F32),
        dma((7,)),
        dma((2,)),
        dma((2,)),
        dma((2,)),
        dma((2,)),
        dma((batches, 3)),
        dma((batches, 3)),
        dma((batches, 2)),
        dma((batches, 2)),
        dma((batches,)),
        dma((batches,)),
    ]
    if z.scatter:
        stages = len(z.bits)
        sizes = [TILE >> (k + 1) for k in range(stages)]
        scratch += [pltpu.VMEM((npiece, size, TILE), LOW) for size in sizes + sizes]
        scratch += [pltpu.VMEM((npiece, size, TILE), F32) for size in sizes[1:]]
        scratch += [
            pltpu.VMEM((sizes[0], TILE), F32),
            pltpu.VMEM((z.rings, 16, hidden), LOW),
            pltpu.VMEM((z.rings, 16, hidden), LOW),
            pltpu.VMEM((16, hidden), F32),
            dma((npiece, stages)),
            dma((npiece, stages)),
            dma((z.rings,)),
            dma((z.rings,)),
        ]
    hbm = pl.BlockSpec(memory_space=pl.ANY)
    vmem = pl.BlockSpec(memory_space=pltpu.VMEM)
    smem = pl.BlockSpec(memory_space=pltpu.SMEM)
    got = pl.pallas_call(
        kernel_of(z),
        out_shape=outs,
        in_specs=[hbm, hbm, vmem, vmem, smem, hbm, hbm, hbm, vmem, hbm, vmem, hbm, vmem],
        out_specs=[vmem] * len(outs),
        scratch_shapes=scratch,
        compiler_params=pltpu.CompilerParams(
            collective_id=0, has_side_effects=True, vmem_limit_bytes=63 * 2**20
        ),
    )(
        inputs,
        cotangent,
        neighbours.T,
        mesh_ids.reshape(1, rows),
        noise_sigma.T,
        w_qkv,
        w_out,
        w_up,
        b_up,
        w_down,
        b_down,
        w_mod,
        b_mod,
    )
    if z.scatter:
        lo, ig, piece, mod, line = got
        return tuple(
            pl.pallas_call(
                layout_of(z),
                out_shape=[
                    stack,
                    stack,
                    shape((1, own, 3 * width), F32),
                    shape((1, own, width), F32),
                    shape((1, own, hidden), F32),
                    shape((1, hidden // shards), F32),
                    shape((1, hidden // shards, width), F32),
                    shape((1, own), F32),
                    shape((1, own, 4 * width), F32),
                    shape((1, 4 * width // shards), F32),
                ],
                in_specs=[hbm, hbm, hbm, hbm, vmem],
                out_specs=[hbm, hbm, hbm, hbm, hbm, vmem, hbm, vmem, hbm, vmem],
                scratch_shapes=[
                    pltpu.VMEM(stack.shape, LOW),
                    pltpu.VMEM(stack.shape, LOW),
                    pltpu.VMEM((npiece, own, TILE), F32),
                    pltpu.VMEM((1, own, 4 * width), F32),
                    dma((npiece + 3,)),
                    dma((npiece + 3,)),
                ],
                compiler_params=pltpu.CompilerParams(vmem_limit_bytes=63 * 2**20),
            )(lo, ig, piece, mod, line)
        )
    lo, ig, left_t, right_t, small, table = got
    groups = z.groups

    def summed(value):
        return lax.psum_scatter(value, "nodes", scatter_dimension=0, tiled=True)

    def wide_sum(left, first, last):
        return summed(jnp.concatenate([dot(left_t[left], right_t[r]) for r in range(first, last)], axis=1))[None]

    down = [dot(left_t[q], right_t[0]).reshape(TILE // 32, 32, TILE) for q in range(groups)]
    down = jnp.stack(down, axis=1)
    count = batches * z.meshes
    small = lax.psum(small, "nodes")
    me = lax.axis_index("nodes")
    mod = jnp.dot(table[:, :count], small[:count], precision=lax.Precision.HIGHEST)

    def mine(value):
        size = value.shape[0] // shards
        return lax.dynamic_slice_in_dim(value, me * size, size, axis=0)[None]

    return (
        lo,
        ig,
        wide_sum(groups + 2, 2 + groups, 5 + groups),
        wide_sum(groups + 1, 1 + groups, 2 + groups),
        wide_sum(groups, 1, 1 + groups),
        mine(small[count]),
        summed(down.reshape(hidden, width))[None],
        mine(small[count + 1, :width]),
        mine(mod),
        mine(jnp.sum(small[:count], axis=0)),
    )


def solution(mesh):
    return jax.shard_map(
        body,
        mesh=mesh,
        in_specs=(
            P(None, "nodes", None),
            P(None, "nodes", None),
            P("nodes", None),
            P("nodes"),
            P(),
            P("section", None, None),
            P("section", None, None),
            P("section", None, None),
            P("section", None),
            P("section", None, None),
            P("section", None),
            P("section", None, None),
            P("section", None),
        ),
        out_specs=(
            P("section", None, "nodes", None),
            P("section", None, "nodes", None),
            P("section", "nodes", None),
            P("section", "nodes", None),
            P("section", "nodes", None),
            P("section", "nodes"),
            P("section", "nodes", None),
            P("section", "nodes"),
            P("section", "nodes", None),
            P("section", "nodes"),
        ),
        check_vma=False,
    )
```

```python
import jax
import jax.numpy as jnp
from jax import lax
from jax.experimental import pallas as pl
from jax.experimental.pallas import tpu as pltpu
from jax.sharding import PartitionSpec as P

HEADS = 4
REACH = 32
EPSILON = 1e-06
MASKED = -1e9
ABSENT = -2e38
TILE = 512
TOGETHER = 2
MESH = pl.DeviceIdType.MESH
F32, LOW = jnp.float32, jnp.bfloat16


def dot(a, b):
    return lax.dot_general(a, b, (((1,), (0,)), ((), ())), preferred_element_type=F32)


def dot_nt(a, b):
    return lax.dot_general(a, b, (((1,), (1,)), ((), ())), preferred_element_type=F32)


def dot_tn(a, b):
    return lax.dot_general(a, b, (((0,), (0,)), ((), ())), preferred_element_type=F32)


class Sizes:
    def __init__(self, inputs, neighbours, noise, w_up, shards):
        self.batches, self.rows, self.width = inputs.shape
        self.together = TOGETHER if self.batches % TOGETHER == 0 else 1
        self.turns = self.batches // self.together
        self.slots = neighbours.shape[1]
        self.meshes = noise.shape[1]
        self.hidden = w_up.shape[2]
        self.shards = shards
        self.ext = self.rows + 2 * REACH
        self.window = (self.ext // 128 + 1) * 128
        self.groups = self.hidden // TILE
        self.own = self.width // shards
        self.scatter = self.own % 16 == 0
        self.pieces = 2 * self.groups + 4
        self.lefts = 3 + self.groups
        self.rights = 2 + self.groups + 3
        self.rings = max(shards.bit_length() - 1, 1)

        self.bits = [1 << k for k in range(shards.bit_length() - 1)]

    def left(self, p):
        n = self.groups
        return jnp.minimum(p, n) + lax.div(p, 2 * n) + lax.div(p, 2 * n + 1)

    def right(self, p):
        return jnp.maximum(p - (self.groups - 1), 0)


def kernel_of(z):
    batches, rows, width, ext, window = z.batches, z.rows, z.width, z.ext, z.window
    groups, shards, own, many = z.groups, z.shards, z.own, z.together
    head = width // HEADS
    score_scale = head ** (-0.5)
    log2e = 1.4426950408889634
    npiece = z.pieces
    half = TILE // 2
    stages = len(z.bits)
    g_out, g_q, g_k = 1 + groups, 2 + groups, 3 + groups

    def position(owner):
        if not z.scatter:
            return owner
        place = 0
        for bit in z.bits:
            place = 2 * place + owner // bit % 2
        return place

    def kernel(
        inputs, cotangent, neighbours, mesh_ids, sigma,
        w_qkv, w_out, w_up, b_up, w_down, b_down, w_mod, b_mod,
        lo, ig, *rest,
    ):
        if z.scatter:
            o_piece, o_mod, o_line, left_t, right_t = rest[:5]
            rest = rest[5:]
        else:
            left_t, right_t, small_out, table_out = rest[:4]
            rest = rest[4:]
        (
            wq, wo, wu, wd, wm, xext, dybuf, sel, pick, cnt, few, bias, mod, emb,
            n1, n1s, ua, ia, qb, kvext, sbuf, af, ca, obs, n2s, ub, ib, tb, fp, hs,
            ob, cds, dx1, dkv, hsend, hrecv, sm,
            lsem, hx_s, hx_r, hm_s, hm_r, fx_s, fx_r, bh_s, bh_r, bx_s, bx_r,
        ) = rest[:48]
        rest = rest[48:]
        if z.scatter:
            gives, gets, keeps = rest[:stages], rest[stages : 2 * stages], rest[2 * stages : 3 * stages - 1]
            acc, msend, mrecv, tot, p_s, p_r, m_s, m_r = rest[3 * stages - 1 :]

        sec = lax.axis_index("section")
        me = lax.axis_index("nodes")
        up = lax.rem(me + 1, shards)
        down = lax.rem(me + shards - 1, shards)
        other = 1 - sec
        def local(src, dst, k):
            return pltpu.make_async_copy(src, dst, lsem.at[k])

        loads = [
            local(w_mod.at[0], wm, 0),
            local(w_qkv.at[0], wq, 1),
            local(w_out.at[0], wo, 2),
            local(w_up.at[0], wu, 3),
            local(w_down.at[0], wd, 4),
        ]
        own_rows = pl.ds(REACH, rows)
        first_load = local(inputs, xext.at[:, own_rows, :], 5)
        last_load = local(cotangent, dybuf, 6)
        loads[0].start()

        @pl.when(sec == 0)
        def _():
            first_load.start()

        for copy in loads[1:]:
            copy.start()

        @pl.when(sec == 1)
        def _():
            last_load.start()

        def side(bit):
            return lax.rem(lax.div(me, bit), 2)

        def mate(bit):
            return me + bit - 2 * bit * side(bit)

        barrier = pltpu.get_barrier_semaphore()
        mates = [(sec, up), (sec, down), (other, me), (other, up), (other, down)]
        if z.scatter:
            mates += [(sec, mate(bit)) for bit in z.bits[1:]]
        for peer in mates:
            pl.semaphore_signal(barrier, inc=1, device_id=peer, device_id_type=MESH)
        pl.semaphore_wait(barrier, len(mates))

        def remote(src, dst, s_sem, r_sem, peer):
            return pltpu.make_async_remote_copy(
                src_ref=src, dst_ref=dst, send_sem=s_sem, recv_sem=r_sem, device_id=peer, device_id_type=MESH
            )

        low_rows, top_rows = pl.ds(0, REACH), pl.ds(REACH + rows, REACH)
        head_rows, tail_rows = pl.ds(REACH, REACH), pl.ds(rows, REACH)
        x_down = remote(inputs.at[:, pl.ds(0, REACH), :], xext.at[:, top_rows, :], hx_s.at[0], hx_r.at[0], (sec, down))
        x_up = remote(inputs.at[:, pl.ds(rows - REACH, REACH), :], xext.at[:, low_rows, :], hx_s.at[1], hx_r.at[1], (sec, up))

        @pl.when(sec == 0)
        def _():
            x_down.start()
            x_up.start()

        ids = jnp.broadcast_to(mesh_ids[...].astype(F32), (128, rows))
        sel[own_rows, :] = ids.T
        sample = lax.broadcasted_iota(jnp.int32, (16, rows), 0).astype(F32)
        pick[...] = jnp.where(ids[0:16] == sample, 1.0, 0.0).astype(LOW)
        m_down = remote(sel.at[head_rows, :], sel.at[top_rows, :], hm_s.at[0], hm_r.at[0], (sec, down))
        m_up = remote(sel.at[tail_rows, :], sel.at[low_rows, :], hm_s.at[1], hm_r.at[1], (sec, up))
        m_down.start()
        m_up.start()

        kvext[:, ext:window, :] = jnp.zeros((batches, window - ext, 2 * width), LOW)
        sm[...] = jnp.zeros(sm.shape, F32)

        slots = neighbours[...].astype(F32)
        slots = jnp.concatenate([slots, jnp.zeros((128 - z.slots, rows), F32)], axis=0).T
        slots = jnp.where(slots >= 0, slots - (me * rows - REACH).astype(F32), float(ext))
        column = lax.broadcasted_iota(jnp.int32, (rows, window), 1).astype(F32)
        counts = jnp.zeros((rows, window), F32)
        for n in range(z.slots):
            counts = counts + jnp.where(slots[:, n : n + 1] == column, 1.0, 0.0)
        cnt[...] = counts
        few[...] = counts.astype(LOW)
        bias[...] = jnp.where(counts > 0, jnp.where(column == ext, MASKED * log2e, 0.0), ABSENT)

        row_no = lax.broadcasted_iota(jnp.int32, (16, width // 2), 0)
        level = jnp.ones((16, width // 2), F32)
        for b in range(batches):
            for m in range(z.meshes):
                level = jnp.where(row_no == b * z.meshes + m, sigma[m, b], level)
        place = lax.broadcasted_iota(jnp.int32, (16, width // 2), 1).astype(F32)
        frequency = 3.0 * jnp.exp(-jnp.log(100.0) * place / (width // 2))
        angles = jnp.log(level) * frequency
        embedded = jnp.concatenate([jnp.sin(angles), jnp.cos(angles)], axis=1).astype(LOW)
        padded = jnp.concatenate([embedded.astype(F32), jnp.zeros((112, width), F32)], axis=0)
        emb[...] = padded.T
        loads[0].wait()
        for g in range(4):
            cols = pl.ds(g * width, width)
            table = dot(embedded, wm[:, cols]) + b_mod[:, cols] + (1.0 - g % 2)
            for b in range(batches):
                mod[b, 0 : z.meshes, cols] = table[b * z.meshes : (b + 1) * z.meshes]

        def mod_rows(b, part, ids_rows):
            cols = pl.ds(part * width, width)
            value = jnp.broadcast_to(mod[b, 0:1, cols], (ids_rows.shape[0], width))
            for m in range(1, z.meshes):
                value = jnp.where(ids_rows > m - 0.5, mod[b, m : m + 1, cols], value)
            return value

        def wide(ids_rows):
            return jnp.concatenate([ids_rows] * (width // 128), axis=1)

        def unit(x):
            centred = x - jnp.mean(x, axis=-1, keepdims=True)
            inv = lax.rsqrt(jnp.mean(centred * centred, axis=-1, keepdims=True) + EPSILON)
            return centred * inv, inv

        def span_of(start, size):
            if isinstance(start, int):
                return pl.ds(start, size)
            return pl.ds(pl.multiple_of(start, size), size)

        def batch_cols(b):
            return span_of(b * rows, rows)

        def turn_cols(t):
            return span_of(t * many * rows, many * rows)

        def turn_of(ref, t):
            return ref[pl.ds(t * many, many)].reshape(many * rows, ref.shape[2])

        span = own if z.scatter else 32

        def transposes(b, carry):
            for first, ref in ((groups, n2s), (groups + 1, obs), (groups + 2, n1s)):
                turned = ref[b].T
                for owner in range(TILE // span):
                    at = position(owner) * span
                    left_t[first, at : at + span, batch_cols(b)] = turned[owner * span : (owner + 1) * span]
            run = groups * span
            for g in range(groups):
                turned = hs[b, :, g * TILE : (g + 1) * TILE].T
                for k in range(TILE // span):
                    at = g * TILE + k * span
                    owner, part = at // run, at % run // span
                    to = position(owner) * span
                    left_t[part, to : to + span, batch_cols(b)] = turned[k * span : (k + 1) * span]
            return carry

        heads = [slice(h * head, (h + 1) * head) for h in range(HEADS)]
        heads_v = [slice(width + h * head, width + (h + 1) * head) for h in range(HEADS)]
        tiles = [slice(g * TILE, (g + 1) * TILE) for g in range(groups)]
        thirds = [slice(g * width, (g + 1) * width) for g in range(3)]

        def forward(b):
            ids_rows = wide(sel[0:ext, :])
            u, inv = unit(xext[b].astype(F32))
            normed = (u * mod_rows(b, 0, ids_rows) + mod_rows(b, 1, ids_rows)).astype(LOW)
            n1[...] = normed
            n1s[b] = normed[REACH : REACH + rows]
            ua[b] = u[REACH : REACH + rows]
            ia[b] = jnp.broadcast_to(inv[REACH : REACH + rows], (rows, 128))
            kvext[b, 0:ext, thirds[0]] = dot(n1[...], wq[:, thirds[1]]).astype(LOW)
            qb[b] = dot(n1s[b], wq[:, thirds[0]]).astype(LOW)
            for h in range(HEADS):
                sbuf[h] = dot_nt(qb[b, :, heads[h]], kvext[b, :, heads[h]]) * (score_scale * log2e) + bias[...]
            kvext[b, 0:ext, thirds[1]] = dot(n1[...], wq[:, thirds[2]]).astype(LOW)
            for h in range(HEADS):
                s = sbuf[h]
                e = jnp.exp2(s - jnp.max(s, axis=-1, keepdims=True))
                a = e * (1.0 / jnp.sum(e * cnt[...], axis=-1, keepdims=True))
                af[b, h] = a
                ca[b, h] = a.astype(LOW) * few[...]
            for h in range(HEADS):
                obs[b, :, heads[h]] = dot(ca[b, h], kvext[b, :, heads_v[h]]).astype(LOW)

            x1 = xext[b, own_rows, :].astype(F32) + dot(obs[b], wo[...])
            u, inv = unit(x1)
            ub[b] = u
            ib[b] = jnp.broadcast_to(inv, (rows, 128))
            ids_rows = wide(sel[own_rows, :])
            n2s[b] = (u * mod_rows(b, 2, ids_rows) + mod_rows(b, 3, ids_rows)).astype(LOW)
            tb[...] = x1 + b_down[...]
            for gs in tiles:
                gate = dot(n2s[b], wu[:, gs]) + b_up[:, gs]
                s = 0.5 + 0.5 * jnp.tanh(0.5 * gate)
                hid = gate * s
                fp[b, :, gs] = (s + hid * (1.0 - s)).astype(LOW)
                hid = hid.astype(LOW)
                hs[b, :, gs] = hid
                tb[...] += dot(hid, wd[gs, :])
            lo[0, b] = tb[...].astype(LOW)

        def relay(b):
            return [
                remote(lo.at[0, b], xext.at[b, own_rows, :], fx_s.at[b, 0], fx_r.at[b, 0], (other, me)),
                remote(lo.at[0, b, pl.ds(0, REACH), :], xext.at[b, top_rows, :], fx_s.at[b, 1], fx_r.at[b, 1], (other, down)),
                remote(lo.at[0, b, pl.ds(rows - REACH, REACH), :], xext.at[b, low_rows, :], fx_s.at[b, 2], fx_r.at[b, 2], (other, up)),
            ]

        def norm_back(d, u, inv, scale):
            scaled = d * scale
            return inv * (
                scaled
                - jnp.mean(scaled, axis=-1, keepdims=True)
                - u * jnp.mean(scaled * u, axis=-1, keepdims=True)
            )

        def mod_sums(b, part, d, u):
            for k, value in enumerate((d * u, d)):
                total = dot(pick[...], value.astype(LOW))
                sm[b, 0 : z.meshes, (part + k) * width : (part + k + 1) * width] = total[0 : z.meshes]

        def halos(b):
            return [
                remote(hsend.at[b, 0], hrecv.at[b, 1], bh_s.at[b, 0], bh_r.at[b, 0], (sec, down)),
                remote(hsend.at[b, 1], hrecv.at[b, 0], bh_s.at[b, 1], bh_r.at[b, 1], (sec, up)),
            ]

        def given(b):
            at = batch_cols(b)
            dr = dybuf[b]
            right_t[0, at, :] = dr
            sm[b, 7:8, 0:width] = jnp.sum(dr.astype(F32), axis=0, keepdims=True)
            for g in range(groups):
                right_t[1 + g, at, :] = dot_nt(dr, wd[g * TILE : (g + 1) * TILE, :]).astype(LOW)

        def back_ffn(t):
            at = turn_cols(t)
            dn = jnp.zeros((many * rows, width), F32)
            for g in range(groups):
                gs = slice(g * TILE, (g + 1) * TILE)
                dg = right_t[1 + g, at, :].astype(F32) * turn_of(fp, t)[:, gs].astype(F32)
                sm[t * many, 6:7, gs] = jnp.sum(dg, axis=0, keepdims=True)
                dg = dg.astype(LOW)
                right_t[1 + g, at, :] = dg
                dn = dn + dot_nt(dg, wu[:, gs])
            ids_rows = wide(sel[own_rows, :])
            for i in range(many):
                b = t * many + i
                d = dn[i * rows : (i + 1) * rows]
                u = ub[b]
                grad = dybuf[b].astype(F32) + norm_back(d, u, ib[b][:, 0:1], mod_rows(b, 2, ids_rows))
                mod_sums(b, 2, d, u)
                dx1[i] = grad
                right_t[g_out, batch_cols(b), :] = grad.astype(LOW)
            ob[...] = dot_nt(right_t[g_out, at, :], wo[...]).astype(LOW)

        def back_attention(t):
            units = [(i, h) for i in range(many) for h in range(HEADS)]
            here = [slice(i * rows, (i + 1) * rows) for i in range(many)]
            for i, h in units:
                sbuf[i * HEADS + h] = dot_nt(ob[here[i], heads[h]], kvext[t * many + i, :, heads_v[h]])
            for i, h in units:
                b, k = t * many + i, i * HEADS + h
                a, da = af[b, h], sbuf[k]
                ds = a * (da - jnp.sum(a * cnt[...] * da, axis=-1, keepdims=True))
                cds[k] = ds.astype(LOW) * few[...]
            for i in range(many):
                b = t * many + i
                for h in range(HEADS):
                    dk = dot_tn(cds[i * HEADS + h], qb[b, :, heads[h]]) * score_scale
                    dv = dot_tn(ca[b, h], ob[here[i], heads[h]])
                    for part, cols in ((dk, heads[h]), (dv, heads_v[h])):
                        hsend[b, 0, :, cols] = part[0:REACH].astype(LOW)
                        dkv[i, :, cols] = part[REACH : REACH + rows]
                        hsend[b, 1, :, cols] = part[REACH + rows : ext].astype(LOW)
                for copy in halos(b):
                    copy.start()
            for i, h in units:
                b = t * many + i
                value = dot(cds[i * HEADS + h], kvext[b, :, heads[h]]) * score_scale
                right_t[g_q, batch_cols(b), heads[h]] = value.astype(LOW)

        def back_second(t):
            at = turn_cols(t)
            ids_rows = wide(sel[own_rows, :])
            edge = rows - REACH
            dn = dot_nt(right_t[g_q, at, :], wq[:, 0:width])
            for i in range(many):
                b = t * many + i
                for copy in halos(b):
                    copy.wait_recv()
                dkv[i, 0:REACH, :] += hrecv[b, 0].astype(F32)
                dkv[i, edge:rows, :] += hrecv[b, 1].astype(F32)
                for g in range(2):
                    right_t[g_k + g, batch_cols(b), :] = dkv[i, :, g * width : (g + 1) * width].astype(LOW)
            for g in range(2):
                dn = dn + dot_nt(right_t[g_k + g, at, :], wq[:, (g + 1) * width : (g + 2) * width])
            for i in range(many):
                b = t * many + i
                d = dn[i * rows : (i + 1) * rows]
                u = ua[b]
                grad = dx1[i] + norm_back(d, u, ia[b][:, 0:1], mod_rows(b, 0, ids_rows))
                ig[0, b] = grad.astype(LOW)

                @pl.when(sec == 1)
                def _(b=b):
                    relay_back(b).start()

                mod_sums(b, 0, d, u)

        def relay_back(b):
            return remote(ig.at[0, b], dybuf.at[b], bx_s.at[b], bx_r.at[b], (other, me))

        for copy in loads[1:]:
            copy.wait()
        for copy in (m_down, m_up):
            copy.wait()

        @pl.when(sec == 0)
        def _():
            first_load.wait()
            x_down.wait()
            x_up.wait()

        @pl.when(sec == 1)
        def _():
            last_load.wait()

            @pl.loop(0, batches)
            def _(b):
                given(b)

        @pl.loop(0, batches)
        def _(b):
            @pl.when(sec == 1)
            def _():
                for copy in relay(b):
                    copy.wait_recv()

            forward(b)

            @pl.when(sec == 0)
            def _():
                for copy in relay(b):
                    copy.start()

        @pl.when(sec == 0)
        def _():
            lax.fori_loop(0, batches, transposes, 0)

        def rows_of(c, size):
            return pl.ds(pl.multiple_of(c * size, size), size)

        def turned(p):
            return lax.div(lax.rem(p, 4), 3) if stages > 2 else 0 * p

        def bit_of(p, k):
            bits = list(z.bits)
            if stages > 2:
                bits[1], bits[2] = bits[2], bits[1]
            return z.bits[k] + (bits[k] - z.bits[k]) * turned(p)

        def piece_copy(p, k):
            return remote(gives[k].at[p], gets[k].at[p], p_s.at[p, k], p_r.at[p, k], (sec, mate(bit_of(p, k))))

        def piece_start(p):
            away = 1 - side(1)
            gives[0][p] = dot(left_t[z.left(p), rows_of(away, half), :], right_t[z.right(p)]).astype(LOW)
            piece_copy(p, 0).start()

        def piece_first(p):
            own_half = dot(left_t[z.left(p), rows_of(side(1), half), :], right_t[z.right(p)])
            piece_copy(p, 0).wait_recv()
            acc[...] = own_half + gets[0][p].astype(F32)
            here = side(bit_of(p, 1))
            run = half // 4
            for j in range(2):
                at = [
                    (1 - turned(p)) * (2 * s + j) + turned(p) * (2 * j + s)
                    for s in (1 - here, here)
                ]
                part = slice(j * run, (j + 1) * run)
                gives[1][p, part, :] = acc[rows_of(at[0], run), :].astype(LOW)
                keeps[0][p, part, :] = acc[rows_of(at[1], run), :]
            piece_copy(p, 1).start()

        def piece_step(p, k):
            size = half >> k
            piece_copy(p, k).wait_recv()
            if k == stages - 1:
                o_piece[p] = keeps[k - 1][p] + gets[k][p].astype(F32)
                return
            here = side(bit_of(p, k + 1))
            for to, c in ((gives[k + 1], 1 - here), (keeps[k], here)):
                at = rows_of(c, size // 2)
                to[p] = (keeps[k - 1][p, at, :] + gets[k][p, at, :].astype(F32)).astype(to.dtype)
                if to is gives[k + 1]:
                    piece_copy(p, k + 1).start()

        def pieces(step, first, last):
            @pl.loop(first, last)
            def _(p):
                step(p)

        def only_first(body):
            if z.scatter:
                pl.when(sec == 0)(body)

        for t in reversed(range(z.turns)):

            @pl.when(sec == 0)
            def _(t=t):
                for i in range(many):
                    relay_back(t * many + i).wait_recv()
                    given(t * many + i)

            back_ffn(t)
            back_attention(t)
            if t == 0:

                @only_first
                def _():
                    pieces(piece_start, 0, groups)
                    pieces(piece_first, 0, groups)

            back_second(t)

        @pl.when(sec == 1)
        def _():
            lax.fori_loop(0, batches, transposes, 0)

        lines = [sm[b, m : m + 1, :] for b in range(batches) for m in range(z.meshes)]
        for line in (6, 7):
            lines.append(sum(sm[b, line : line + 1, :] for b in range(batches)))
        lines.append(jnp.zeros((16 - len(lines), sm.shape[2]), F32))
        small = jnp.concatenate(lines, axis=0)

        def finish():
            @pl.loop(0, batches)
            def _(b):
                @pl.when(sec == 0)
                def _():
                    for copy in relay(b):
                        copy.wait_send()

                @pl.when(sec == 1)
                def _():
                    relay_back(b).wait_send()

                for copy in halos(b):
                    copy.wait_send()

        if not z.scatter:
            small_out[...] = small
            table_out[...] = emb[...]
            finish()
            return

        def ring_copy(k):
            return remote(msend.at[k], mrecv.at[k], m_s.at[k], m_r.at[k], (sec, mate(1 << k)))

        def ring_start(k, value):
            msend[k] = value.astype(LOW)
            ring_copy(k).start()

        def ring_end(k):
            ring_copy(k).wait_recv()
            value = msend[k].astype(F32) + mrecv[k].astype(F32)
            if k + 1 < z.rings:
                ring_start(k + 1, value)
            else:
                tot[...] = value

        ring_start(0, small)

        lags = [0, 1] + [4 + 2 * k for k in range(stages - 1)]
        begun = (1 - sec) * groups

        @pl.loop(0, npiece + lags[-1])
        def _(p):
            @pl.when((p >= begun) & (p < npiece))
            def _():
                piece_start(p)

            @pl.when((p >= begun + 1) & (p < npiece + 1))
            def _():
                piece_first(p - 1)

            for k in range(1, stages):
                lag = lags[k + 1]

                @pl.when((p >= lag) & (p < npiece + lag))
                def _(k=k, lag=lag):
                    piece_step(p - lag, k)

            for k in range(z.rings):

                @pl.when(p == 3 + 2 * k)
                def _(k=k):
                    ring_end(k)

            @pl.when(p == 3 + 2 * z.rings)
            def _():
                count = batches * z.meshes
                table = emb[pl.ds(pl.multiple_of(me * own, own), own), :]
                grad = jnp.zeros((own, 4 * width), F32)
                for k in range(count):
                    grad = grad + table[:, k : k + 1] * tot[k : k + 1, :]
                o_mod[0] = grad
                cols = 4 * width // shards
                mine = tot[:, pl.ds(pl.multiple_of(me * cols, cols), cols)]
                o_line[0:1, :] = jnp.sum(mine[0:count], axis=0, keepdims=True)
                o_line[1:2, :] = mine[count : count + 1]
                ratio = 128 // own
                line = tot[:, pl.ds(pl.multiple_of(me // ratio * 128, 128), 128)][count + 1 : count + 2]
                value = line
                for k in range(1, ratio):
                    rolled = jnp.concatenate([line[:, k * own :], line[:, : k * own]], axis=1)
                    value = jnp.where(me % ratio == k, rolled, value)
                o_line[2:3, :] = value

        finish()

        @pl.loop(0, npiece)
        def _(p):
            for k in range(stages):
                piece_copy(p, k).wait_send()

        for k in range(z.rings):
            ring_copy(k).wait_send()

    return kernel


def layout_of(z):
    own, groups = z.own, z.groups

    def kernel(
        lo, ig, piece, mod, line,
        o_lo, o_ig, o_qkv, o_out, o_up, o_upb, o_down, o_downb, o_mod, o_modb,
        v_lo, v_ig, v_piece, v_mod, into, back,
    ):
        moves = [(lo, v_lo, o_lo), (ig, v_ig, o_ig)]
        targets = [o_down.at[0, pl.ds(q * own, own), :] for q in range(groups)]
        targets += [o_up.at[0, :, pl.ds(q * TILE, TILE)] for q in range(groups)]
        targets += [o_out.at[0]] + [o_qkv.at[0, :, pl.ds(q * TILE, TILE)] for q in range(3)]
        moves += [(piece.at[k], v_piece.at[k], target) for k, target in enumerate(targets)]
        moves += [(mod, v_mod, o_mod)]
        firsts = [pltpu.make_async_copy(a, b, into.at[k]) for k, (a, b, _) in enumerate(moves)]
        lasts = [pltpu.make_async_copy(b, c, back.at[k]) for k, (_, b, c) in enumerate(moves)]
        for copy in firsts:
            copy.start()
        o_modb[...] = line[0:1, :]
        o_upb[...] = line[1:2, :]
        o_downb[...] = line[2:3, 0:own]
        for first, last in zip(firsts, lasts):
            first.wait()
            last.start()
        for copy in lasts:
            copy.wait()

    return kernel


def body(
    inputs,
    cotangent,
    neighbours,
    mesh_ids,
    noise_sigma,
    w_qkv,
    w_out,
    w_up,
    b_up,
    w_down,
    b_down,
    w_mod,
    b_mod,
):
    shards = lax.axis_size("nodes")
    z = Sizes(inputs, neighbours, noise_sigma, w_up, shards)
    batches, rows, width, hidden, many = z.batches, z.rows, z.width, z.hidden, z.together
    own, npiece = z.own, z.pieces
    shape = jax.ShapeDtypeStruct
    stack = shape((1, batches, rows, width), LOW)
    outs = [stack, stack]
    sides = [(z.lefts, TILE, batches * rows), (z.rights, batches * rows, TILE)]
    if z.scatter:
        outs += [shape((npiece, own, TILE), F32), shape((1, own, 4 * width), F32), shape((8, 128), F32)]
        scratch = [pltpu.VMEM(side, LOW) for side in sides]
    else:
        outs += [shape(side, LOW) for side in sides] + [shape((16, hidden), F32), shape((width, 128), F32)]
        scratch = []
    dma = pltpu.SemaphoreType.DMA
    scratch += [
        pltpu.VMEM((width, 3 * width), LOW),
        pltpu.VMEM((width, width), LOW),
        pltpu.VMEM((width, hidden), LOW),
        pltpu.VMEM((hidden, width), LOW),
        pltpu.VMEM((width, 4 * width), LOW),
        pltpu.VMEM((batches, z.ext, width), LOW),
        pltpu.VMEM((batches, rows, width), LOW),
        pltpu.VMEM((z.ext, 128), F32),
        pltpu.VMEM((16, rows), LOW),
        pltpu.VMEM((rows, z.window), F32),
        pltpu.VMEM((rows, z.window), LOW),
        pltpu.VMEM((rows, z.window), F32),
        pltpu.VMEM((batches, 8, 4 * width), F32),
        pltpu.VMEM((width, 128), F32),
        pltpu.VMEM((z.ext, width), LOW),
        pltpu.VMEM((batches, rows, width), LOW),
        pltpu.VMEM((batches, rows, width), F32),
        pltpu.VMEM((batches, rows, 128), F32),
        pltpu.VMEM((batches, rows, width), LOW),
        pltpu.VMEM((batches, z.window, 2 * width), LOW),
        pltpu.VMEM((many * HEADS, rows, z.window), F32),
        pltpu.VMEM((batches, HEADS, rows, z.window), F32),
        pltpu.VMEM((batches, HEADS, rows, z.window), LOW),
        pltpu.VMEM((batches, rows, width), LOW),
        pltpu.VMEM((batches, rows, width), LOW),
        pltpu.VMEM((batches, rows, width), F32),
        pltpu.VMEM((batches, rows, 128), F32),
        pltpu.VMEM((rows, width), F32),
        pltpu.VMEM((batches, rows, hidden), LOW),
        pltpu.VMEM((batches, rows, hidden), LOW),
        pltpu.VMEM((many * rows, width), LOW),
        pltpu.VMEM((many * HEADS, rows, z.window), LOW),
        pltpu.VMEM((many, rows, width), F32),
        pltpu.VMEM((many, rows, 2 * width), F32),
        pltpu.VMEM((batches, 2, REACH, 2 * width), LOW),
        pltpu.VMEM((batches, 2, REACH, 2 * width), LOW),
        pltpu.VMEM((batches, 8, hidden), F32),
        dma((7,)),
        dma((2,)),
        dma((2,)),
        dma((2,)),
        dma((2,)),
        dma((batches, 3)),
        dma((batches, 3)),
        dma((batches, 2)),
        dma((batches, 2)),
        dma((batches,)),
        dma((batches,)),
    ]
    if z.scatter:
        stages = len(z.bits)
        sizes = [TILE >> (k + 1) for k in range(stages)]
        scratch += [pltpu.VMEM((npiece, size, TILE), LOW) for size in sizes + sizes]
        scratch += [pltpu.VMEM((npiece, size, TILE), F32) for size in sizes[1:]]
        scratch += [
            pltpu.VMEM((sizes[0], TILE), F32),
            pltpu.VMEM((z.rings, 16, hidden), LOW),
            pltpu.VMEM((z.rings, 16, hidden), LOW),
            pltpu.VMEM((16, hidden), F32),
            dma((npiece, stages)),
            dma((npiece, stages)),
            dma((z.rings,)),
            dma((z.rings,)),
        ]
    hbm = pl.BlockSpec(memory_space=pl.ANY)
    vmem = pl.BlockSpec(memory_space=pltpu.VMEM)
    smem = pl.BlockSpec(memory_space=pltpu.SMEM)
    got = pl.pallas_call(
        kernel_of(z),
        out_shape=outs,
        in_specs=[hbm, hbm, vmem, vmem, smem, hbm, hbm, hbm, vmem, hbm, vmem, hbm, vmem],
        out_specs=[vmem] * len(outs),
        scratch_shapes=scratch,
        compiler_params=pltpu.CompilerParams(
            collective_id=0, has_side_effects=True, vmem_limit_bytes=63 * 2**20
        ),
    )(
        inputs,
        cotangent,
        neighbours.T,
        mesh_ids.reshape(1, rows),
        noise_sigma.T,
        w_qkv,
        w_out,
        w_up,
        b_up,
        w_down,
        b_down,
        w_mod,
        b_mod,
    )
    if z.scatter:
        lo, ig, piece, mod, line = got
        return tuple(
            pl.pallas_call(
                layout_of(z),
                out_shape=[
                    stack,
                    stack,
                    shape((1, own, 3 * width), F32),
                    shape((1, own, width), F32),
                    shape((1, own, hidden), F32),
                    shape((1, hidden // shards), F32),
                    shape((1, hidden // shards, width), F32),
                    shape((1, own), F32),
                    shape((1, own, 4 * width), F32),
                    shape((1, 4 * width // shards), F32),
                ],
                in_specs=[hbm, hbm, hbm, hbm, vmem],
                out_specs=[hbm, hbm, hbm, hbm, hbm, vmem, hbm, vmem, hbm, vmem],
                scratch_shapes=[
                    pltpu.VMEM(stack.shape, LOW),
                    pltpu.VMEM(stack.shape, LOW),
                    pltpu.VMEM((npiece, own, TILE), F32),
                    pltpu.VMEM((1, own, 4 * width), F32),
                    dma((npiece + 3,)),
                    dma((npiece + 3,)),
                ],
                compiler_params=pltpu.CompilerParams(vmem_limit_bytes=63 * 2**20),
            )(lo, ig, piece, mod, line)
        )
    lo, ig, left_t, right_t, small, table = got
    groups = z.groups

    def summed(value):
        return lax.psum_scatter(value, "nodes", scatter_dimension=0, tiled=True)

    def wide_sum(left, first, last):
        return summed(jnp.concatenate([dot(left_t[left], right_t[r]) for r in range(first, last)], axis=1))[None]

    down = [dot(left_t[q], right_t[0]).reshape(TILE // 32, 32, TILE) for q in range(groups)]
    down = jnp.stack(down, axis=1)
    count = batches * z.meshes
    small = lax.psum(small, "nodes")
    me = lax.axis_index("nodes")
    mod = jnp.dot(table[:, :count], small[:count], precision=lax.Precision.HIGHEST)

    def mine(value):
        size = value.shape[0] // shards
        return lax.dynamic_slice_in_dim(value, me * size, size, axis=0)[None]

    return (
        lo,
        ig,
        wide_sum(groups + 2, 2 + groups, 5 + groups),
        wide_sum(groups + 1, 1 + groups, 2 + groups),
        wide_sum(groups, 1, 1 + groups),
        mine(small[count]),
        summed(down.reshape(hidden, width))[None],
        mine(small[count + 1, :width]),
        mine(mod),
        mine(jnp.sum(small[:count], axis=0)),
    )


def solution(mesh):
    return jax.shard_map(
        body,
        mesh=mesh,
        in_specs=(
            P(None, "nodes", None),
            P(None, "nodes", None),
            P("nodes", None),
            P("nodes"),
            P(),
            P("section", None, None),
            P("section", None, None),
            P("section", None, None),
            P("section", None),
            P("section", None, None),
            P("section", None),
            P("section", None, None),
            P("section", None),
        ),
        out_specs=(
            P("section", None, "nodes", None),
            P("section", None, "nodes", None),
            P("section", "nodes", None),
            P("section", "nodes", None),
            P("section", "nodes", None),
            P("section", "nodes"),
            P("section", "nodes", None),
            P("section", "nodes"),
            P("section", "nodes", None),
            P("section", "nodes"),
        ),
        check_vma=False,
    )
```

```python
import jax
import jax.numpy as jnp
from jax import lax
from jax.experimental import pallas as pl
from jax.experimental.pallas import tpu as pltpu
from jax.sharding import PartitionSpec as P

HEADS = 4
REACH = 32
EPSILON = 1e-06
MASKED = -1e9
ABSENT = -2e38
TILE = 512
TOGETHER = 2
MESH = pl.DeviceIdType.MESH
F32, LOW = jnp.float32, jnp.bfloat16


def dot(a, b):
    return lax.dot_general(a, b, (((1,), (0,)), ((), ())), preferred_element_type=F32)


def dot_nt(a, b):
    return lax.dot_general(a, b, (((1,), (1,)), ((), ())), preferred_element_type=F32)


def dot_tn(a, b):
    return lax.dot_general(a, b, (((0,), (0,)), ((), ())), preferred_element_type=F32)


class Sizes:
    def __init__(self, inputs, neighbours, noise, w_up, shards):
        self.batches, self.rows, self.width = inputs.shape
        self.together = TOGETHER if self.batches % TOGETHER == 0 else 1
        self.turns = self.batches // self.together
        self.slots = neighbours.shape[1]
        self.meshes = noise.shape[1]
        self.hidden = w_up.shape[2]
        self.shards = shards
        self.ext = self.rows + 2 * REACH
        self.window = (self.ext // 128 + 1) * 128
        self.groups = self.hidden // TILE
        self.own = self.width // shards
        self.scatter = self.own % 16 == 0
        self.pieces = 2 * self.groups + 4
        self.lefts = 3 + self.groups
        self.rights = 2 + self.groups + 3
        self.rings = max(shards.bit_length() - 1, 1)

        self.bits = [1 << k for k in range(shards.bit_length() - 1)]

    def left(self, p):
        n = self.groups
        return jnp.minimum(p, n) + lax.div(p, 2 * n) + lax.div(p, 2 * n + 1)

    def right(self, p):
        return jnp.maximum(p - (self.groups - 1), 0)


def kernel_of(z):
    batches, rows, width, ext, window = z.batches, z.rows, z.width, z.ext, z.window
    groups, shards, own, many = z.groups, z.shards, z.own, z.together
    head = width // HEADS
    score_scale = head ** (-0.5)
    log2e = 1.4426950408889634
    npiece = z.pieces
    half = TILE // 2
    stages = len(z.bits)
    g_out, g_q, g_k = 1 + groups, 2 + groups, 3 + groups

    def position(owner):
        if not z.scatter:
            return owner
        place = 0
        for bit in z.bits:
            place = 2 * place + owner // bit % 2
        return place

    def kernel(
        inputs, cotangent, neighbours, mesh_ids, sigma,
        w_qkv, w_out, w_up, b_up, w_down, b_down, w_mod, b_mod,
        lo, ig, *rest,
    ):
        if z.scatter:
            o_piece, o_mod, o_line, left_t, right_t = rest[:5]
            rest = rest[5:]
        else:
            left_t, right_t, small_out, table_out = rest[:4]
            rest = rest[4:]
        (
            wq, wo, wu, wd, wm, xext, dybuf, sel, pick, cnt, few, bias, mod, emb,
            n1, n1s, ua, ia, qb, kvext, sbuf, af, ca, obs, n2s, ub, ib, tb, fp, hs,
            ob, dbuf, cds, dx1, dkv, hsend, hrecv, sm,
            lsem, hx_s, hx_r, hm_s, hm_r, fx_s, fx_r, bh_s, bh_r, bx_s, bx_r,
        ) = rest[:49]
        rest = rest[49:]
        if z.scatter:
            gives, gets, keeps = rest[:stages], rest[stages : 2 * stages], rest[2 * stages : 3 * stages - 1]
            acc, msend, mrecv, tot, p_s, p_r, m_s, m_r = rest[3 * stages - 1 :]

        sec = lax.axis_index("section")
        me = lax.axis_index("nodes")
        up = lax.rem(me + 1, shards)
        down = lax.rem(me + shards - 1, shards)
        other = 1 - sec
        def local(src, dst, k):
            return pltpu.make_async_copy(src, dst, lsem.at[k])

        loads = [
            local(w_mod.at[0], wm, 0),
            local(w_qkv.at[0], wq, 1),
            local(w_out.at[0], wo, 2),
            local(w_up.at[0], wu, 3),
            local(w_down.at[0], wd, 4),
        ]
        own_rows = pl.ds(REACH, rows)
        first_load = local(inputs, xext.at[:, own_rows, :], 5)
        last_load = local(cotangent, dybuf, 6)
        loads[0].start()

        @pl.when(sec == 0)
        def _():
            first_load.start()

        for copy in loads[1:]:
            copy.start()

        @pl.when(sec == 1)
        def _():
            last_load.start()

        def side(bit):
            return lax.rem(lax.div(me, bit), 2)

        def mate(bit):
            return me + bit - 2 * bit * side(bit)

        barrier = pltpu.get_barrier_semaphore()
        mates = [(sec, up), (sec, down), (other, me), (other, up), (other, down)]
        if z.scatter:
            mates += [(sec, mate(bit)) for bit in z.bits[1:]]
        for peer in mates:
            pl.semaphore_signal(barrier, inc=1, device_id=peer, device_id_type=MESH)
        pl.semaphore_wait(barrier, len(mates))

        def remote(src, dst, s_sem, r_sem, peer):
            return pltpu.make_async_remote_copy(
                src_ref=src, dst_ref=dst, send_sem=s_sem, recv_sem=r_sem, device_id=peer, device_id_type=MESH
            )

        low_rows, top_rows = pl.ds(0, REACH), pl.ds(REACH + rows, REACH)
        head_rows, tail_rows = pl.ds(REACH, REACH), pl.ds(rows, REACH)
        x_down = remote(inputs.at[:, pl.ds(0, REACH), :], xext.at[:, top_rows, :], hx_s.at[0], hx_r.at[0], (sec, down))
        x_up = remote(inputs.at[:, pl.ds(rows - REACH, REACH), :], xext.at[:, low_rows, :], hx_s.at[1], hx_r.at[1], (sec, up))

        @pl.when(sec == 0)
        def _():
            x_down.start()
            x_up.start()

        ids = jnp.broadcast_to(mesh_ids[...].astype(F32), (128, rows))
        sel[own_rows, :] = ids.T
        sample = lax.broadcasted_iota(jnp.int32, (16, rows), 0).astype(F32)
        pick[...] = jnp.where(ids[0:16] == sample, 1.0, 0.0).astype(LOW)
        m_down = remote(sel.at[head_rows, :], sel.at[top_rows, :], hm_s.at[0], hm_r.at[0], (sec, down))
        m_up = remote(sel.at[tail_rows, :], sel.at[low_rows, :], hm_s.at[1], hm_r.at[1], (sec, up))
        m_down.start()
        m_up.start()

        kvext[:, ext:window, :] = jnp.zeros((batches, window - ext, 2 * width), LOW)
        sm[...] = jnp.zeros(sm.shape, F32)

        slots = neighbours[...].astype(F32)
        slots = jnp.concatenate([slots, jnp.zeros((128 - z.slots, rows), F32)], axis=0).T
        slots = jnp.where(slots >= 0, slots - (me * rows - REACH).astype(F32), float(ext))
        column = lax.broadcasted_iota(jnp.int32, (rows, window), 1).astype(F32)
        counts = jnp.zeros((rows, window), F32)
        for n in range(z.slots):
            counts = counts + jnp.where(slots[:, n : n + 1] == column, 1.0, 0.0)
        cnt[...] = counts
        few[...] = counts.astype(LOW)
        bias[...] = jnp.where(counts > 0, jnp.where(column == ext, MASKED * log2e, 0.0), ABSENT)

        row_no = lax.broadcasted_iota(jnp.int32, (16, width // 2), 0)
        level = jnp.ones((16, width // 2), F32)
        for b in range(batches):
            for m in range(z.meshes):
                level = jnp.where(row_no == b * z.meshes + m, sigma[m, b], level)
        place = lax.broadcasted_iota(jnp.int32, (16, width // 2), 1).astype(F32)
        frequency = 3.0 * jnp.exp(-jnp.log(100.0) * place / (width // 2))
        angles = jnp.log(level) * frequency
        embedded = jnp.concatenate([jnp.sin(angles), jnp.cos(angles)], axis=1).astype(LOW)
        padded = jnp.concatenate([embedded.astype(F32), jnp.zeros((112, width), F32)], axis=0)
        emb[...] = padded.T
        loads[0].wait()
        for g in range(4):
            cols = pl.ds(g * width, width)
            table = dot(embedded, wm[:, cols]) + b_mod[:, cols] + (1.0 - g % 2)
            for b in range(batches):
                mod[b, 0 : z.meshes, cols] = table[b * z.meshes : (b + 1) * z.meshes]

        def mod_rows(b, part, ids_rows):
            cols = pl.ds(part * width, width)
            value = jnp.broadcast_to(mod[b, 0:1, cols], (ids_rows.shape[0], width))
            for m in range(1, z.meshes):
                value = jnp.where(ids_rows > m - 0.5, mod[b, m : m + 1, cols], value)
            return value

        def wide(ids_rows):
            return jnp.concatenate([ids_rows] * (width // 128), axis=1)

        def unit(x):
            centred = x - jnp.mean(x, axis=-1, keepdims=True)
            inv = lax.rsqrt(jnp.mean(centred * centred, axis=-1, keepdims=True) + EPSILON)
            return centred * inv, inv

        def span_of(start, size):
            if isinstance(start, int):
                return pl.ds(start, size)
            return pl.ds(pl.multiple_of(start, size), size)

        def batch_cols(b):
            return span_of(b * rows, rows)

        def turn_cols(t):
            return span_of(t * many * rows, many * rows)

        def turn_of(ref, t):
            return ref[pl.ds(t * many, many)].reshape(many * rows, ref.shape[2])

        span = own if z.scatter else 32

        def transposes(b, carry):
            for first, ref in ((groups, n2s), (groups + 1, obs), (groups + 2, n1s)):
                turned = ref[b].T
                for owner in range(TILE // span):
                    at = position(owner) * span
                    left_t[first, at : at + span, batch_cols(b)] = turned[owner * span : (owner + 1) * span]
            run = groups * span
            for g in range(groups):
                turned = hs[b, :, g * TILE : (g + 1) * TILE].T
                for k in range(TILE // span):
                    at = g * TILE + k * span
                    owner, part = at // run, at % run // span
                    to = position(owner) * span
                    left_t[part, to : to + span, batch_cols(b)] = turned[k * span : (k + 1) * span]
            return carry

        heads = [slice(h * head, (h + 1) * head) for h in range(HEADS)]
        heads_v = [slice(width + h * head, width + (h + 1) * head) for h in range(HEADS)]
        tiles = [slice(g * TILE, (g + 1) * TILE) for g in range(groups)]
        thirds = [slice(g * width, (g + 1) * width) for g in range(3)]

        def forward(b):
            ids_rows = wide(sel[0:ext, :])
            u, inv = unit(xext[b].astype(F32))
            normed = (u * mod_rows(b, 0, ids_rows) + mod_rows(b, 1, ids_rows)).astype(LOW)
            n1[...] = normed
            n1s[b] = normed[REACH : REACH + rows]
            ua[b] = u[REACH : REACH + rows]
            ia[b] = jnp.broadcast_to(inv[REACH : REACH + rows], (rows, 128))
            kvext[b, 0:ext, thirds[0]] = dot(n1[...], wq[:, thirds[1]]).astype(LOW)
            qb[b] = dot(n1s[b], wq[:, thirds[0]]).astype(LOW)
            for h in range(HEADS):
                sbuf[h] = dot_nt(qb[b, :, heads[h]], kvext[b, :, heads[h]]) * (score_scale * log2e) + bias[...]
            kvext[b, 0:ext, thirds[1]] = dot(n1[...], wq[:, thirds[2]]).astype(LOW)
            for h in range(HEADS):
                s = sbuf[h]
                e = jnp.exp2(s - jnp.max(s, axis=-1, keepdims=True))
                a = e * (1.0 / jnp.sum(e * cnt[...], axis=-1, keepdims=True))
                af[b, h] = a
                ca[b, h] = a.astype(LOW) * few[...]
            for h in range(HEADS):
                obs[b, :, heads[h]] = dot(ca[b, h], kvext[b, :, heads_v[h]]).astype(LOW)

            x1 = xext[b, own_rows, :].astype(F32) + dot(obs[b], wo[...])
            u, inv = unit(x1)
            ub[b] = u
            ib[b] = jnp.broadcast_to(inv, (rows, 128))
            ids_rows = wide(sel[own_rows, :])
            n2s[b] = (u * mod_rows(b, 2, ids_rows) + mod_rows(b, 3, ids_rows)).astype(LOW)
            tb[...] = x1 + b_down[...]
            for gs in tiles:
                gate = dot(n2s[b], wu[:, gs]) + b_up[:, gs]
                s = 0.5 + 0.5 * jnp.tanh(0.5 * gate)
                hid = gate * s
                fp[b, :, gs] = (s + hid * (1.0 - s)).astype(LOW)
                hid = hid.astype(LOW)
                hs[b, :, gs] = hid
                tb[...] += dot(hid, wd[gs, :])
            lo[0, b] = tb[...].astype(LOW)

        def relay(b):
            return [
                remote(lo.at[0, b], xext.at[b, own_rows, :], fx_s.at[b, 0], fx_r.at[b, 0], (other, me)),
                remote(lo.at[0, b, pl.ds(0, REACH), :], xext.at[b, top_rows, :], fx_s.at[b, 1], fx_r.at[b, 1], (other, down)),
                remote(lo.at[0, b, pl.ds(rows - REACH, REACH), :], xext.at[b, low_rows, :], fx_s.at[b, 2], fx_r.at[b, 2], (other, up)),
            ]

        def norm_back(d, u, inv, scale):
            scaled = d * scale
            return inv * (
                scaled
                - jnp.mean(scaled, axis=-1, keepdims=True)
                - u * jnp.mean(scaled * u, axis=-1, keepdims=True)
            )

        def mod_sums(b, part, d, u):
            for k, value in enumerate((d * u, d)):
                total = dot(pick[...], value.astype(LOW))
                sm[b, 0 : z.meshes, (part + k) * width : (part + k + 1) * width] = total[0 : z.meshes]

        def halos(b):
            return [
                remote(hsend.at[b, 0], hrecv.at[b, 1], bh_s.at[b, 0], bh_r.at[b, 0], (sec, down)),
                remote(hsend.at[b, 1], hrecv.at[b, 0], bh_s.at[b, 1], bh_r.at[b, 1], (sec, up)),
            ]

        def given(b):
            at = batch_cols(b)
            dr = dybuf[b]
            right_t[0, at, :] = dr
            sm[b, 7:8, 0:width] = jnp.sum(dr.astype(F32), axis=0, keepdims=True)
            for g in range(groups):
                right_t[1 + g, at, :] = dot_nt(dr, wd[g * TILE : (g + 1) * TILE, :]).astype(LOW)

        def back_ffn(t):
            at = turn_cols(t)
            dn = jnp.zeros((many * rows, width), F32)
            for g in range(groups):
                gs = slice(g * TILE, (g + 1) * TILE)
                dg = right_t[1 + g, at, :].astype(F32) * turn_of(fp, t)[:, gs].astype(F32)
                sm[t * many, 6:7, gs] = jnp.sum(dg, axis=0, keepdims=True)
                dg = dg.astype(LOW)
                right_t[1 + g, at, :] = dg
                dn = dn + dot_nt(dg, wu[:, gs])
            ids_rows = wide(sel[own_rows, :])
            for i in range(many):
                b = t * many + i
                d = dn[i * rows : (i + 1) * rows]
                u = ub[b]
                grad = dybuf[b].astype(F32) + norm_back(d, u, ib[b][:, 0:1], mod_rows(b, 2, ids_rows))
                mod_sums(b, 2, d, u)
                dx1[i] = grad
                right_t[g_out, batch_cols(b), :] = grad.astype(LOW)
            ob[...] = dot_nt(right_t[g_out, at, :], wo[...]).astype(LOW)

        def back_attention(t):
            units = [(i, h) for i in range(many) for h in range(HEADS)]
            here = [slice(i * rows, (i + 1) * rows) for i in range(many)]
            for i, h in units:
                sbuf[i * HEADS + h] = dot_nt(ob[here[i], heads[h]], kvext[t * many + i, :, heads_v[h]])
            for i, h in units:
                b, k = t * many + i, i * HEADS + h
                a, da = af[b, h], sbuf[k]
                ds = a * (da - jnp.sum(a * cnt[...] * da, axis=-1, keepdims=True))
                cds[k] = ds.astype(LOW) * few[...]
            for i in range(many):
                b = t * many + i
                for h in range(HEADS):
                    dk = dot_tn(cds[i * HEADS + h], qb[b, :, heads[h]]) * score_scale
                    dv = dot_tn(ca[b, h], ob[here[i], heads[h]])
                    for part, cols in ((dk, heads[h]), (dv, heads_v[h])):
                        hsend[b, 0, :, cols] = part[0:REACH].astype(LOW)
                        dkv[i, :, cols] = part[REACH : REACH + rows]
                        hsend[b, 1, :, cols] = part[REACH + rows : ext].astype(LOW)
                for copy in halos(b):
                    copy.start()
            for i, h in units:
                b = t * many + i
                value = dot(cds[i * HEADS + h], kvext[b, :, heads[h]]) * score_scale
                right_t[g_q, batch_cols(b), heads[h]] = value.astype(LOW)

        def back_second(t):
            at = turn_cols(t)
            ids_rows = wide(sel[own_rows, :])
            edge = rows - REACH
            dbuf[...] = dot_nt(right_t[g_q, at, :], wq[:, 0:width])
            for i in range(many):
                b = t * many + i
                for copy in halos(b):
                    copy.wait_recv()
                dkv[i, 0:REACH, :] += hrecv[b, 0].astype(F32)
                dkv[i, edge:rows, :] += hrecv[b, 1].astype(F32)
                d = dbuf[i * rows : (i + 1) * rows]
                for g in range(2):
                    part = dkv[i, :, g * width : (g + 1) * width].astype(LOW)
                    right_t[g_k + g, batch_cols(b), :] = part
                    d = d + dot_nt(part, wq[:, (g + 1) * width : (g + 2) * width])
                u = ua[b]
                grad = dx1[i] + norm_back(d, u, ia[b][:, 0:1], mod_rows(b, 0, ids_rows))
                ig[0, b] = grad.astype(LOW)

                @pl.when(sec == 1)
                def _(b=b):
                    relay_back(b).start()

                mod_sums(b, 0, d, u)

        def relay_back(b):
            return remote(ig.at[0, b], dybuf.at[b], bx_s.at[b], bx_r.at[b], (other, me))

        for copy in loads[1:]:
            copy.wait()
        for copy in (m_down, m_up):
            copy.wait()

        @pl.when(sec == 0)
        def _():
            first_load.wait()
            x_down.wait()
            x_up.wait()

        @pl.when(sec == 1)
        def _():
            last_load.wait()

            @pl.loop(0, batches)
            def _(b):
                given(b)

        @pl.loop(0, batches)
        def _(b):
            @pl.when(sec == 1)
            def _():
                for copy in relay(b):
                    copy.wait_recv()

            forward(b)

            @pl.when(sec == 0)
            def _():
                for copy in relay(b):
                    copy.start()

        @pl.when(sec == 0)
        def _():
            lax.fori_loop(0, batches, transposes, 0)

        def rows_of(c, size):
            return pl.ds(pl.multiple_of(c * size, size), size)

        def turned(p):
            return lax.div(lax.rem(p, 4), 3) if stages > 2 else 0 * p

        def bit_of(p, k):
            bits = list(z.bits)
            if stages > 2:
                bits[1], bits[2] = bits[2], bits[1]
            return z.bits[k] + (bits[k] - z.bits[k]) * turned(p)

        def piece_copy(p, k):
            return remote(gives[k].at[p], gets[k].at[p], p_s.at[p, k], p_r.at[p, k], (sec, mate(bit_of(p, k))))

        def piece_start(p):
            away = 1 - side(1)
            gives[0][p] = dot(left_t[z.left(p), rows_of(away, half), :], right_t[z.right(p)]).astype(LOW)
            piece_copy(p, 0).start()

        def piece_first(p):
            own_half = dot(left_t[z.left(p), rows_of(side(1), half), :], right_t[z.right(p)])
            piece_copy(p, 0).wait_recv()
            acc[...] = own_half + gets[0][p].astype(F32)
            here = side(bit_of(p, 1))
            run = half // 4
            for j in range(2):
                at = [
                    (1 - turned(p)) * (2 * s + j) + turned(p) * (2 * j + s)
                    for s in (1 - here, here)
                ]
                part = slice(j * run, (j + 1) * run)
                gives[1][p, part, :] = acc[rows_of(at[0], run), :].astype(LOW)
                keeps[0][p, part, :] = acc[rows_of(at[1], run), :]
            piece_copy(p, 1).start()

        def piece_step(p, k):
            size = half >> k
            piece_copy(p, k).wait_recv()
            if k == stages - 1:
                o_piece[p] = keeps[k - 1][p] + gets[k][p].astype(F32)
                return
            here = side(bit_of(p, k + 1))
            for to, c in ((gives[k + 1], 1 - here), (keeps[k], here)):
                at = rows_of(c, size // 2)
                to[p] = (keeps[k - 1][p, at, :] + gets[k][p, at, :].astype(F32)).astype(to.dtype)
                if to is gives[k + 1]:
                    piece_copy(p, k + 1).start()

        def pieces(step, first, last):
            @pl.loop(first, last)
            def _(p):
                step(p)

        def only_first(body):
            if z.scatter:
                pl.when(sec == 0)(body)

        for t in reversed(range(z.turns)):

            @pl.when(sec == 0)
            def _(t=t):
                for i in range(many):
                    relay_back(t * many + i).wait_recv()
                    given(t * many + i)

            back_ffn(t)
            back_attention(t)
            if t == 0:

                @only_first
                def _():
                    pieces(piece_start, 0, groups)
                    pieces(piece_first, 0, groups)

            back_second(t)

        @pl.when(sec == 1)
        def _():
            lax.fori_loop(0, batches, transposes, 0)

        lines = [sm[b, m : m + 1, :] for b in range(batches) for m in range(z.meshes)]
        for line in (6, 7):
            lines.append(sum(sm[b, line : line + 1, :] for b in range(batches)))
        lines.append(jnp.zeros((16 - len(lines), sm.shape[2]), F32))
        small = jnp.concatenate(lines, axis=0)

        def finish():
            @pl.loop(0, batches)
            def _(b):
                @pl.when(sec == 0)
                def _():
                    for copy in relay(b):
                        copy.wait_send()

                @pl.when(sec == 1)
                def _():
                    relay_back(b).wait_send()

                for copy in halos(b):
                    copy.wait_send()

        if not z.scatter:
            small_out[...] = small
            table_out[...] = emb[...]
            finish()
            return

        def ring_copy(k):
            return remote(msend.at[k], mrecv.at[k], m_s.at[k], m_r.at[k], (sec, mate(1 << k)))

        def ring_start(k, value):
            msend[k] = value.astype(LOW)
            ring_copy(k).start()

        def ring_end(k):
            ring_copy(k).wait_recv()
            value = msend[k].astype(F32) + mrecv[k].astype(F32)
            if k + 1 < z.rings:
                ring_start(k + 1, value)
            else:
                tot[...] = value

        ring_start(0, small)

        lags = [0, 1] + [4 + 2 * k for k in range(stages - 1)]
        begun = (1 - sec) * groups

        @pl.loop(0, npiece + lags[-1])
        def _(p):
            @pl.when((p >= begun) & (p < npiece))
            def _():
                piece_start(p)

            @pl.when((p >= begun + 1) & (p < npiece + 1))
            def _():
                piece_first(p - 1)

            for k in range(1, stages):
                lag = lags[k + 1]

                @pl.when((p >= lag) & (p < npiece + lag))
                def _(k=k, lag=lag):
                    piece_step(p - lag, k)

            for k in range(z.rings):

                @pl.when(p == 6 + 3 * k)
                def _(k=k):
                    ring_end(k)

            @pl.when(p == 4 + 3 * z.rings)
            def _():
                count = batches * z.meshes
                table = emb[pl.ds(pl.multiple_of(me * own, own), own), :]
                grad = jnp.zeros((own, 4 * width), F32)
                for k in range(count):
                    grad = grad + table[:, k : k + 1] * tot[k : k + 1, :]
                o_mod[0] = grad
                cols = 4 * width // shards
                mine = tot[:, pl.ds(pl.multiple_of(me * cols, cols), cols)]
                o_line[0:1, :] = jnp.sum(mine[0:count], axis=0, keepdims=True)
                o_line[1:2, :] = mine[count : count + 1]
                ratio = 128 // own
                line = tot[:, pl.ds(pl.multiple_of(me // ratio * 128, 128), 128)][count + 1 : count + 2]
                value = line
                for k in range(1, ratio):
                    rolled = jnp.concatenate([line[:, k * own :], line[:, : k * own]], axis=1)
                    value = jnp.where(me % ratio == k, rolled, value)
                o_line[2:3, :] = value

        finish()

        @pl.loop(0, npiece)
        def _(p):
            for k in range(stages):
                piece_copy(p, k).wait_send()

        for k in range(z.rings):
            ring_copy(k).wait_send()

    return kernel


def layout_of(z):
    own, groups = z.own, z.groups

    def kernel(
        lo, ig, piece, mod, line,
        o_lo, o_ig, o_qkv, o_out, o_up, o_upb, o_down, o_downb, o_mod, o_modb,
        sems,
    ):
        targets = [o_down.at[0, pl.ds(q * own, own), :] for q in range(groups)]
        targets += [o_up.at[0, :, pl.ds(q * TILE, TILE)] for q in range(groups)]
        targets += [o_out.at[0]] + [o_qkv.at[0, :, pl.ds(q * TILE, TILE)] for q in range(3)]
        moves = [(lo, o_lo), (ig, o_ig), (mod, o_mod)]
        moves += [(piece.at[k], target) for k, target in enumerate(targets)]
        copies = [pltpu.make_async_copy(a, b, sems.at[k]) for k, (a, b) in enumerate(moves)]
        for copy in copies:
            copy.start()
        o_modb[...] = line[0:1, :]
        o_upb[...] = line[1:2, :]
        o_downb[...] = line[2:3, 0:own]
        for copy in copies:
            copy.wait()

    return kernel


def body(
    inputs,
    cotangent,
    neighbours,
    mesh_ids,
    noise_sigma,
    w_qkv,
    w_out,
    w_up,
    b_up,
    w_down,
    b_down,
    w_mod,
    b_mod,
):
    shards = lax.axis_size("nodes")
    z = Sizes(inputs, neighbours, noise_sigma, w_up, shards)
    batches, rows, width, hidden, many = z.batches, z.rows, z.width, z.hidden, z.together
    own, npiece = z.own, z.pieces
    shape = jax.ShapeDtypeStruct
    stack = shape((1, batches, rows, width), LOW)
    outs = [stack, stack]
    sides = [(z.lefts, TILE, batches * rows), (z.rights, batches * rows, TILE)]
    if z.scatter:
        outs = [pltpu.VMEM(stack.shape, LOW)] * 2
        outs += [pltpu.VMEM((npiece, own, TILE), F32), pltpu.VMEM((1, own, 4 * width), F32), pltpu.VMEM((8, 128), F32)]
        scratch = [pltpu.VMEM(side, LOW) for side in sides]
    else:
        outs += [shape(side, LOW) for side in sides] + [shape((16, hidden), F32), shape((width, 128), F32)]
        scratch = []
    dma = pltpu.SemaphoreType.DMA
    scratch += [
        pltpu.VMEM((width, 3 * width), LOW),
        pltpu.VMEM((width, width), LOW),
        pltpu.VMEM((width, hidden), LOW),
        pltpu.VMEM((hidden, width), LOW),
        pltpu.VMEM((width, 4 * width), LOW),
        pltpu.VMEM((batches, z.ext, width), LOW),
        pltpu.VMEM((batches, rows, width), LOW),
        pltpu.VMEM((z.ext, 128), F32),
        pltpu.VMEM((16, rows), LOW),
        pltpu.VMEM((rows, z.window), F32),
        pltpu.VMEM((rows, z.window), LOW),
        pltpu.VMEM((rows, z.window), F32),
        pltpu.VMEM((batches, 8, 4 * width), F32),
        pltpu.VMEM((width, 128), F32),
        pltpu.VMEM((z.ext, width), LOW),
        pltpu.VMEM((batches, rows, width), LOW),
        pltpu.VMEM((batches, rows, width), F32),
        pltpu.VMEM((batches, rows, 128), F32),
        pltpu.VMEM((batches, rows, width), LOW),
        pltpu.VMEM((batches, z.window, 2 * width), LOW),
        pltpu.VMEM((many * HEADS, rows, z.window), F32),
        pltpu.VMEM((batches, HEADS, rows, z.window), F32),
        pltpu.VMEM((batches, HEADS, rows, z.window), LOW),
        pltpu.VMEM((batches, rows, width), LOW),
        pltpu.VMEM((batches, rows, width), LOW),
        pltpu.VMEM((batches, rows, width), F32),
        pltpu.VMEM((batches, rows, 128), F32),
        pltpu.VMEM((rows, width), F32),
        pltpu.VMEM((batches, rows, hidden), LOW),
        pltpu.VMEM((batches, rows, hidden), LOW),
        pltpu.VMEM((many * rows, width), LOW),
        pltpu.VMEM((many * rows, width), F32),
        pltpu.VMEM((many * HEADS, rows, z.window), LOW),
        pltpu.VMEM((many, rows, width), F32),
        pltpu.VMEM((many, rows, 2 * width), F32),
        pltpu.VMEM((batches, 2, REACH, 2 * width), LOW),
        pltpu.VMEM((batches, 2, REACH, 2 * width), LOW),
        pltpu.VMEM((batches, 8, hidden), F32),
        dma((7,)),
        dma((2,)),
        dma((2,)),
        dma((2,)),
        dma((2,)),
        dma((batches, 3)),
        dma((batches, 3)),
        dma((batches, 2)),
        dma((batches, 2)),
        dma((batches,)),
        dma((batches,)),
    ]
    if z.scatter:
        stages = len(z.bits)
        sizes = [TILE >> (k + 1) for k in range(stages)]
        scratch += [pltpu.VMEM((npiece, size, TILE), LOW) for size in sizes + sizes]
        scratch += [pltpu.VMEM((npiece, size, TILE), F32) for size in sizes[1:]]
        scratch += [
            pltpu.VMEM((sizes[0], TILE), F32),
            pltpu.VMEM((z.rings, 16, hidden), LOW),
            pltpu.VMEM((z.rings, 16, hidden), LOW),
            pltpu.VMEM((16, hidden), F32),
            dma((npiece, stages)),
            dma((npiece, stages)),
            dma((z.rings,)),
            dma((z.rings,)),
        ]
    hbm = pl.BlockSpec(memory_space=pl.ANY)
    vmem = pl.BlockSpec(memory_space=pltpu.VMEM)
    smem = pl.BlockSpec(memory_space=pltpu.SMEM)
    got = pl.pallas_call(
        kernel_of(z),
        out_shape=outs,
        in_specs=[hbm, hbm, vmem, vmem, smem, hbm, hbm, hbm, vmem, hbm, vmem, hbm, vmem],
        out_specs=[vmem] * len(outs),
        scratch_shapes=scratch,
        compiler_params=pltpu.CompilerParams(
            collective_id=0, has_side_effects=True, vmem_limit_bytes=60 * 2**20
        ),
    )(
        inputs,
        cotangent,
        neighbours.T,
        mesh_ids.reshape(1, rows),
        noise_sigma.T,
        w_qkv,
        w_out,
        w_up,
        b_up,
        w_down,
        b_down,
        w_mod,
        b_mod,
    )
    if z.scatter:
        lo, ig, piece, mod, line = got
        return tuple(
            pl.pallas_call(
                layout_of(z),
                out_shape=[
                    stack,
                    stack,
                    shape((1, own, 3 * width), F32),
                    shape((1, own, width), F32),
                    shape((1, own, hidden), F32),
                    shape((1, hidden // shards), F32),
                    shape((1, hidden // shards, width), F32),
                    shape((1, own), F32),
                    shape((1, own, 4 * width), F32),
                    shape((1, 4 * width // shards), F32),
                ],
                in_specs=[vmem] * 5,
                out_specs=[hbm, hbm, hbm, hbm, hbm, vmem, hbm, vmem, hbm, vmem],
                scratch_shapes=[dma((npiece + 3,))],
            )(lo, ig, piece, mod, line)
        )
    lo, ig, left_t, right_t, small, table = got
    groups = z.groups

    def summed(value):
        return lax.psum_scatter(value, "nodes", scatter_dimension=0, tiled=True)

    def wide_sum(left, first, last):
        return summed(jnp.concatenate([dot(left_t[left], right_t[r]) for r in range(first, last)], axis=1))[None]

    down = [dot(left_t[q], right_t[0]).reshape(TILE // 32, 32, TILE) for q in range(groups)]
    down = jnp.stack(down, axis=1)
    count = batches * z.meshes
    small = lax.psum(small, "nodes")
    me = lax.axis_index("nodes")
    mod = jnp.dot(table[:, :count], small[:count], precision=lax.Precision.HIGHEST)

    def mine(value):
        size = value.shape[0] // shards
        return lax.dynamic_slice_in_dim(value, me * size, size, axis=0)[None]

    return (
        lo,
        ig,
        wide_sum(groups + 2, 2 + groups, 5 + groups),
        wide_sum(groups + 1, 1 + groups, 2 + groups),
        wide_sum(groups, 1, 1 + groups),
        mine(small[count]),
        summed(down.reshape(hidden, width))[None],
        mine(small[count + 1, :width]),
        mine(mod),
        mine(jnp.sum(small[:count], axis=0)),
    )


def solution(mesh):
    return jax.shard_map(
        body,
        mesh=mesh,
        in_specs=(
            P(None, "nodes", None),
            P(None, "nodes", None),
            P("nodes", None),
            P("nodes"),
            P(),
            P("section", None, None),
            P("section", None, None),
            P("section", None, None),
            P("section", None),
            P("section", None, None),
            P("section", None),
            P("section", None, None),
            P("section", None),
        ),
        out_specs=(
            P("section", None, "nodes", None),
            P("section", None, "nodes", None),
            P("section", "nodes", None),
            P("section", "nodes", None),
            P("section", "nodes", None),
            P("section", "nodes"),
            P("section", "nodes", None),
            P("section", "nodes"),
            P("section", "nodes", None),
            P("section", "nodes"),
        ),
        check_vma=False,
    )
```

```python
import jax
import jax.numpy as jnp
from jax import lax
from jax.experimental import pallas as pl
from jax.experimental.pallas import tpu as pltpu
from jax.sharding import PartitionSpec as P

HEADS = 4
REACH = 32
EPSILON = 1e-06
MASKED = -1e9
ABSENT = -2e38
TILE = 512
TOGETHER = 2
MESH = pl.DeviceIdType.MESH
F32, LOW = jnp.float32, jnp.bfloat16


def dot(a, b):
    return lax.dot_general(a, b, (((1,), (0,)), ((), ())), preferred_element_type=F32)


def dot_nt(a, b):
    return lax.dot_general(a, b, (((1,), (1,)), ((), ())), preferred_element_type=F32)


def dot_tn(a, b):
    return lax.dot_general(a, b, (((0,), (0,)), ((), ())), preferred_element_type=F32)


class Sizes:
    def __init__(self, inputs, neighbours, noise, w_up, shards):
        self.batches, self.rows, self.width = inputs.shape
        self.together = TOGETHER if self.batches % TOGETHER == 0 else 1
        self.turns = self.batches // self.together
        self.slots = neighbours.shape[1]
        self.meshes = noise.shape[1]
        self.hidden = w_up.shape[2]
        self.shards = shards
        self.ext = self.rows + 2 * REACH
        self.window = (self.ext // 128 + 1) * 128
        self.groups = self.hidden // TILE
        self.own = self.width // shards
        self.scatter = self.own % 16 == 0
        self.pieces = 2 * self.groups + 4
        self.lefts = 3 + self.groups
        self.rights = 2 + self.groups + 3
        self.rings = max(shards.bit_length() - 1, 1)

        self.bits = [1 << k for k in range(shards.bit_length() - 1)]

    def left(self, p):
        n = self.groups
        return jnp.minimum(p, n) + lax.div(p, 2 * n) + lax.div(p, 2 * n + 1)

    def right(self, p):
        return jnp.maximum(p - (self.groups - 1), 0)


def kernel_of(z):
    batches, rows, width, ext, window = z.batches, z.rows, z.width, z.ext, z.window
    groups, shards, own, many = z.groups, z.shards, z.own, z.together
    head = width // HEADS
    score_scale = head ** (-0.5)
    log2e = 1.4426950408889634
    npiece = z.pieces
    half = TILE // 2
    stages = len(z.bits)
    g_out, g_q, g_k = 1 + groups, 2 + groups, 3 + groups

    def position(owner):
        if not z.scatter:
            return owner
        place = 0
        for bit in z.bits:
            place = 2 * place + owner // bit % 2
        return place

    def kernel(
        inputs, cotangent, neighbours, mesh_ids, sigma,
        w_qkv, w_out, w_up, b_up, w_down, b_down, w_mod, b_mod,
        lo, ig, *rest,
    ):
        if z.scatter:
            o_piece, o_mod, o_line, left_t, right_t = rest[:5]
            rest = rest[5:]
        else:
            left_t, right_t, small_out, table_out = rest[:4]
            rest = rest[4:]
        (
            wq, wo, wu, wd, wm, xext, dybuf, sel, pick, cnt, few, bias, mod, emb,
            n1, n1s, ua, ia, qb, kvext, sbuf, af, ca, obs, n2s, ub, ib, tb, fp, hs,
            ob, dbuf, cds, dx1, dkv, hsend, hrecv, sm,
            lsem, hx_s, hx_r, hm_s, hm_r, fx_s, fx_r, bh_s, bh_r, bx_s, bx_r,
        ) = rest[:49]
        rest = rest[49:]
        if z.scatter:
            gives, gets, keeps = rest[:stages], rest[stages : 2 * stages], rest[2 * stages : 3 * stages - 1]
            acc, msend, mrecv, tot, p_s, p_r, m_s, m_r = rest[3 * stages - 1 :]

        sec = lax.axis_index("section")
        me = lax.axis_index("nodes")
        up = lax.rem(me + 1, shards)
        down = lax.rem(me + shards - 1, shards)
        other = 1 - sec
        def local(src, dst, k):
            return pltpu.make_async_copy(src, dst, lsem.at[k])

        loads = [
            local(w_mod.at[0], wm, 0),
            local(w_qkv.at[0], wq, 1),
            local(w_out.at[0], wo, 2),
            local(w_up.at[0], wu, 3),
            local(w_down.at[0], wd, 4),
        ]
        own_rows = pl.ds(REACH, rows)
        first_load = local(inputs, xext.at[:, own_rows, :], 5)
        last_load = local(cotangent, dybuf, 6)
        loads[0].start()

        @pl.when(sec == 0)
        def _():
            first_load.start()

        for copy in loads[1:]:
            copy.start()

        @pl.when(sec == 1)
        def _():
            last_load.start()

        def side(bit):
            return lax.rem(lax.div(me, bit), 2)

        def mate(bit):
            return me + bit - 2 * bit * side(bit)

        barrier = pltpu.get_barrier_semaphore()
        mates = [(sec, up), (sec, down), (other, me), (other, up), (other, down)]
        if z.scatter:
            mates += [(sec, mate(bit)) for bit in z.bits[1:]]
        for peer in mates:
            pl.semaphore_signal(barrier, inc=1, device_id=peer, device_id_type=MESH)
        pl.semaphore_wait(barrier, len(mates))

        def remote(src, dst, s_sem, r_sem, peer):
            return pltpu.make_async_remote_copy(
                src_ref=src, dst_ref=dst, send_sem=s_sem, recv_sem=r_sem, device_id=peer, device_id_type=MESH
            )

        low_rows, top_rows = pl.ds(0, REACH), pl.ds(REACH + rows, REACH)
        head_rows, tail_rows = pl.ds(REACH, REACH), pl.ds(rows, REACH)
        x_down = remote(inputs.at[:, pl.ds(0, REACH), :], xext.at[:, top_rows, :], hx_s.at[0], hx_r.at[0], (sec, down))
        x_up = remote(inputs.at[:, pl.ds(rows - REACH, REACH), :], xext.at[:, low_rows, :], hx_s.at[1], hx_r.at[1], (sec, up))

        @pl.when(sec == 0)
        def _():
            x_down.start()
            x_up.start()

        ids = jnp.broadcast_to(mesh_ids[...].astype(F32), (128, rows))
        sel[own_rows, :] = ids.T
        sample = lax.broadcasted_iota(jnp.int32, (16, rows), 0).astype(F32)
        pick[...] = jnp.where(ids[0:16] == sample, 1.0, 0.0).astype(LOW)
        m_down = remote(sel.at[head_rows, :], sel.at[top_rows, :], hm_s.at[0], hm_r.at[0], (sec, down))
        m_up = remote(sel.at[tail_rows, :], sel.at[low_rows, :], hm_s.at[1], hm_r.at[1], (sec, up))
        m_down.start()
        m_up.start()

        kvext[:, ext:window, :] = jnp.zeros((batches, window - ext, 2 * width), LOW)
        sm[...] = jnp.zeros(sm.shape, F32)

        slots = neighbours[...].astype(F32)
        slots = jnp.concatenate([slots, jnp.zeros((128 - z.slots, rows), F32)], axis=0).T
        slots = jnp.where(slots >= 0, slots - (me * rows - REACH).astype(F32), float(ext))
        column = lax.broadcasted_iota(jnp.int32, (rows, window), 1).astype(F32)
        counts = jnp.zeros((rows, window), F32)
        for n in range(z.slots):
            counts = counts + jnp.where(slots[:, n : n + 1] == column, 1.0, 0.0)
        cnt[...] = counts
        few[...] = counts.astype(LOW)
        bias[...] = jnp.where(counts > 0, jnp.where(column == ext, MASKED * log2e, 0.0), ABSENT)

        row_no = lax.broadcasted_iota(jnp.int32, (16, width // 2), 0)
        level = jnp.ones((16, width // 2), F32)
        for b in range(batches):
            for m in range(z.meshes):
                level = jnp.where(row_no == b * z.meshes + m, sigma[m, b], level)
        place = lax.broadcasted_iota(jnp.int32, (16, width // 2), 1).astype(F32)
        frequency = 3.0 * jnp.exp(-jnp.log(100.0) * place / (width // 2))
        angles = jnp.log(level) * frequency
        embedded = jnp.concatenate([jnp.sin(angles), jnp.cos(angles)], axis=1).astype(LOW)
        padded = jnp.concatenate([embedded.astype(F32), jnp.zeros((112, width), F32)], axis=0)
        emb[...] = padded.T
        loads[0].wait()
        for g in range(4):
            cols = pl.ds(g * width, width)
            table = dot(embedded, wm[:, cols]) + b_mod[:, cols] + (1.0 - g % 2)
            for b in range(batches):
                mod[b, 0 : z.meshes, cols] = table[b * z.meshes : (b + 1) * z.meshes]

        def mod_rows(b, part, ids_rows):
            cols = pl.ds(part * width, width)
            value = jnp.broadcast_to(mod[b, 0:1, cols], (ids_rows.shape[0], width))
            for m in range(1, z.meshes):
                value = jnp.where(ids_rows > m - 0.5, mod[b, m : m + 1, cols], value)
            return value

        def wide(ids_rows):
            return jnp.concatenate([ids_rows] * (width // 128), axis=1)

        def unit(x):
            centred = x - jnp.mean(x, axis=-1, keepdims=True)
            inv = lax.rsqrt(jnp.mean(centred * centred, axis=-1, keepdims=True) + EPSILON)
            return centred * inv, inv

        def span_of(start, size):
            if isinstance(start, int):
                return pl.ds(start, size)
            return pl.ds(pl.multiple_of(start, size), size)

        def batch_cols(b):
            return span_of(b * rows, rows)

        def turn_cols(t):
            return span_of(t * many * rows, many * rows)

        def turn_of(ref, t):
            return ref[pl.ds(t * many, many)].reshape(many * rows, ref.shape[2])

        span = own if z.scatter else 32

        def transposes(b, carry):
            for first, ref in ((groups, n2s), (groups + 1, obs), (groups + 2, n1s)):
                turned = ref[b].T
                for owner in range(TILE // span):
                    at = position(owner) * span
                    left_t[first, at : at + span, batch_cols(b)] = turned[owner * span : (owner + 1) * span]
            run = groups * span
            for g in range(groups):
                turned = hs[b, :, g * TILE : (g + 1) * TILE].T
                for k in range(TILE // span):
                    at = g * TILE + k * span
                    owner, part = at // run, at % run // span
                    to = position(owner) * span
                    left_t[part, to : to + span, batch_cols(b)] = turned[k * span : (k + 1) * span]
            return carry

        heads = [slice(h * head, (h + 1) * head) for h in range(HEADS)]
        heads_v = [slice(width + h * head, width + (h + 1) * head) for h in range(HEADS)]
        tiles = [slice(g * TILE, (g + 1) * TILE) for g in range(groups)]
        thirds = [slice(g * width, (g + 1) * width) for g in range(3)]

        def forward(b):
            ids_rows = wide(sel[0:ext, :])
            u, inv = unit(xext[b].astype(F32))
            normed = (u * mod_rows(b, 0, ids_rows) + mod_rows(b, 1, ids_rows)).astype(LOW)
            n1[...] = normed
            n1s[b] = normed[REACH : REACH + rows]
            ua[b] = u[REACH : REACH + rows]
            ia[b] = jnp.broadcast_to(inv[REACH : REACH + rows], (rows, 128))
            kvext[b, 0:ext, thirds[0]] = dot(n1[...], wq[:, thirds[1]]).astype(LOW)
            qb[b] = dot(n1s[b], wq[:, thirds[0]]).astype(LOW)
            for h in range(HEADS):
                sbuf[h] = dot_nt(qb[b, :, heads[h]], kvext[b, :, heads[h]]) * (score_scale * log2e) + bias[...]
            kvext[b, 0:ext, thirds[1]] = dot(n1[...], wq[:, thirds[2]]).astype(LOW)
            for h in range(HEADS):
                s = sbuf[h]
                e = jnp.exp2(s - jnp.max(s, axis=-1, keepdims=True))
                a = e * (1.0 / jnp.sum(e * cnt[...], axis=-1, keepdims=True))
                af[b, h] = a
                ca[b, h] = a.astype(LOW) * few[...]
            for h in range(HEADS):
                obs[b, :, heads[h]] = dot(ca[b, h], kvext[b, :, heads_v[h]]).astype(LOW)

            x1 = xext[b, own_rows, :].astype(F32) + dot(obs[b], wo[...])
            u, inv = unit(x1)
            ub[b] = u
            ib[b] = jnp.broadcast_to(inv, (rows, 128))
            ids_rows = wide(sel[own_rows, :])
            n2s[b] = (u * mod_rows(b, 2, ids_rows) + mod_rows(b, 3, ids_rows)).astype(LOW)
            tb[...] = x1 + b_down[...]
            for gs in tiles:
                gate = dot(n2s[b], wu[:, gs]) + b_up[:, gs]
                s = 0.5 + 0.5 * jnp.tanh(0.5 * gate)
                hid = gate * s
                fp[b, :, gs] = (s + hid * (1.0 - s)).astype(LOW)
                hid = hid.astype(LOW)
                hs[b, :, gs] = hid
                tb[...] += dot(hid, wd[gs, :])
            lo[0, b] = tb[...].astype(LOW)

        def relay(b):
            return [
                remote(lo.at[0, b], xext.at[b, own_rows, :], fx_s.at[b, 0], fx_r.at[b, 0], (other, me)),
                remote(lo.at[0, b, pl.ds(0, REACH), :], xext.at[b, top_rows, :], fx_s.at[b, 1], fx_r.at[b, 1], (other, down)),
                remote(lo.at[0, b, pl.ds(rows - REACH, REACH), :], xext.at[b, low_rows, :], fx_s.at[b, 2], fx_r.at[b, 2], (other, up)),
            ]

        def norm_back(d, u, inv, scale):
            scaled = d * scale
            return inv * (
                scaled
                - jnp.mean(scaled, axis=-1, keepdims=True)
                - u * jnp.mean(scaled * u, axis=-1, keepdims=True)
            )

        def mod_sums(b, part, d, u):
            for k, value in enumerate((d * u, d)):
                total = dot(pick[...], value.astype(LOW))
                sm[b, 0 : z.meshes, (part + k) * width : (part + k + 1) * width] = total[0 : z.meshes]

        def halos(b):
            return [
                remote(hsend.at[b, 0], hrecv.at[b, 1], bh_s.at[b, 0], bh_r.at[b, 0], (sec, down)),
                remote(hsend.at[b, 1], hrecv.at[b, 0], bh_s.at[b, 1], bh_r.at[b, 1], (sec, up)),
            ]

        def given(b):
            at = batch_cols(b)
            dr = dybuf[b]
            right_t[0, at, :] = dr
            sm[b, 7:8, 0:width] = jnp.sum(dr.astype(F32), axis=0, keepdims=True)
            for g in range(groups):
                right_t[1 + g, at, :] = dot_nt(dr, wd[g * TILE : (g + 1) * TILE, :]).astype(LOW)

        def back_ffn(t):
            at = turn_cols(t)
            dn = jnp.zeros((many * rows, width), F32)
            for g in range(groups):
                gs = slice(g * TILE, (g + 1) * TILE)
                dg = right_t[1 + g, at, :].astype(F32) * turn_of(fp, t)[:, gs].astype(F32)
                sm[t * many, 6:7, gs] = jnp.sum(dg, axis=0, keepdims=True)
                dg = dg.astype(LOW)
                right_t[1 + g, at, :] = dg
                dn = dn + dot_nt(dg, wu[:, gs])
            dbuf[...] = dn

        def back_middle(t):
            at = turn_cols(t)
            ids_rows = wide(sel[own_rows, :])
            for i in range(many):
                b = t * many + i
                d = dbuf[i * rows : (i + 1) * rows]
                u = ub[b]
                grad = dybuf[b].astype(F32) + norm_back(d, u, ib[b][:, 0:1], mod_rows(b, 2, ids_rows))
                mod_sums(b, 2, d, u)
                dx1[i] = grad
                right_t[g_out, batch_cols(b), :] = grad.astype(LOW)
            ob[...] = dot_nt(right_t[g_out, at, :], wo[...]).astype(LOW)

        def back_attention(t):
            units = [(i, h) for i in range(many) for h in range(HEADS)]
            here = [slice(i * rows, (i + 1) * rows) for i in range(many)]
            for i, h in units:
                sbuf[i * HEADS + h] = dot_nt(ob[here[i], heads[h]], kvext[t * many + i, :, heads_v[h]])
            for i, h in units:
                b, k = t * many + i, i * HEADS + h
                a, da = af[b, h], sbuf[k]
                ds = a * (da - jnp.sum(a * cnt[...] * da, axis=-1, keepdims=True))
                cds[k] = ds.astype(LOW) * few[...]
            for i in range(many):
                b = t * many + i
                for h in range(HEADS):
                    dk = dot_tn(cds[i * HEADS + h], qb[b, :, heads[h]]) * score_scale
                    dv = dot_tn(ca[b, h], ob[here[i], heads[h]])
                    for part, cols in ((dk, heads[h]), (dv, heads_v[h])):
                        hsend[b, 0, :, cols] = part[0:REACH].astype(LOW)
                        dkv[i, :, cols] = part[REACH : REACH + rows]
                        hsend[b, 1, :, cols] = part[REACH + rows : ext].astype(LOW)
                for copy in halos(b):
                    copy.start()
            for i, h in units:
                b = t * many + i
                value = dot(cds[i * HEADS + h], kvext[b, :, heads[h]]) * score_scale
                right_t[g_q, batch_cols(b), heads[h]] = value.astype(LOW)

        def back_second(t):
            at = turn_cols(t)
            ids_rows = wide(sel[own_rows, :])
            edge = rows - REACH
            dbuf[...] = dot_nt(right_t[g_q, at, :], wq[:, 0:width])
            for i in range(many):
                b = t * many + i
                for copy in halos(b):
                    copy.wait_recv()
                dkv[i, 0:REACH, :] += hrecv[b, 0].astype(F32)
                dkv[i, edge:rows, :] += hrecv[b, 1].astype(F32)
                d = dbuf[i * rows : (i + 1) * rows]
                for g in range(2):
                    part = dkv[i, :, g * width : (g + 1) * width].astype(LOW)
                    right_t[g_k + g, batch_cols(b), :] = part
                    d = d + dot_nt(part, wq[:, (g + 1) * width : (g + 2) * width])
                u = ua[b]
                grad = dx1[i] + norm_back(d, u, ia[b][:, 0:1], mod_rows(b, 0, ids_rows))
                ig[0, b] = grad.astype(LOW)

                @pl.when(sec == 1)
                def _(b=b):
                    relay_back(b).start()

                mod_sums(b, 0, d, u)

        def relay_back(b):
            return remote(ig.at[0, b], dybuf.at[b], bx_s.at[b], bx_r.at[b], (other, me))

        for copy in loads[1:]:
            copy.wait()
        for copy in (m_down, m_up):
            copy.wait()

        @pl.when(sec == 0)
        def _():
            first_load.wait()
            x_down.wait()
            x_up.wait()

        @pl.when(sec == 1)
        def _():
            last_load.wait()

            @pl.loop(0, batches)
            def _(b):
                given(b)

        @pl.loop(0, batches)
        def _(b):
            @pl.when(sec == 1)
            def _():
                for copy in relay(b):
                    copy.wait_recv()

            forward(b)

            @pl.when(sec == 0)
            def _():
                for copy in relay(b):
                    copy.start()

        @pl.when(sec == 0)
        def _():
            lax.fori_loop(0, batches, transposes, 0)

        early = 2 * groups + 1

        def rows_of(c, size):
            return pl.ds(pl.multiple_of(c * size, size), size)

        def turned(p):
            return lax.div(lax.rem(p, 4), 3) if stages > 2 else 0 * p

        def bit_of(p, k):
            bits = list(z.bits)
            if stages > 2:
                bits[1], bits[2] = bits[2], bits[1]
            return z.bits[k] + (bits[k] - z.bits[k]) * turned(p)

        def piece_copy(p, k):
            return remote(gives[k].at[p], gets[k].at[p], p_s.at[p, k], p_r.at[p, k], (sec, mate(bit_of(p, k))))

        def piece_start(p):
            away = 1 - side(1)
            gives[0][p] = dot(left_t[z.left(p), rows_of(away, half), :], right_t[z.right(p)]).astype(LOW)
            piece_copy(p, 0).start()

        def piece_first(p):
            own_half = dot(left_t[z.left(p), rows_of(side(1), half), :], right_t[z.right(p)])
            piece_copy(p, 0).wait_recv()
            acc[...] = own_half + gets[0][p].astype(F32)
            here = side(bit_of(p, 1))
            run = half // 4
            for j in range(2):
                at = [
                    (1 - turned(p)) * (2 * s + j) + turned(p) * (2 * j + s)
                    for s in (1 - here, here)
                ]
                part = slice(j * run, (j + 1) * run)
                gives[1][p, part, :] = acc[rows_of(at[0], run), :].astype(LOW)
                keeps[0][p, part, :] = acc[rows_of(at[1], run), :]
            piece_copy(p, 1).start()

        def piece_step(p, k):
            size = half >> k
            piece_copy(p, k).wait_recv()
            if k == stages - 1:
                o_piece[p] = keeps[k - 1][p] + gets[k][p].astype(F32)
                return
            here = side(bit_of(p, k + 1))
            for to, c in ((gives[k + 1], 1 - here), (keeps[k], here)):
                at = rows_of(c, size // 2)
                to[p] = (keeps[k - 1][p, at, :] + gets[k][p, at, :].astype(F32)).astype(to.dtype)
                if to is gives[k + 1]:
                    piece_copy(p, k + 1).start()

        def pieces(step, first, last):
            @pl.loop(first, last)
            def _(p):
                step(p)

        def only_first(body):
            if z.scatter:
                pl.when(sec == 0)(body)

        for t in reversed(range(z.turns)):

            @pl.when(sec == 0)
            def _(t=t):
                for i in range(many):
                    relay_back(t * many + i).wait_recv()
                    given(t * many + i)

            if t == 0:

                @only_first
                def _():
                    pieces(piece_start, 0, groups)
                    pieces(piece_first, 0, groups)

            back_ffn(t)
            if t == 0:

                @only_first
                def _():
                    pieces(piece_start, groups, 2 * groups)
                    pieces(piece_first, groups, groups + 1)

            back_middle(t)
            back_attention(t)
            if t == 0:

                @only_first
                def _():
                    piece_start(2 * groups)
                    pieces(piece_first, groups + 1, early)

            back_second(t)

        @pl.when(sec == 1)
        def _():
            lax.fori_loop(0, batches, transposes, 0)

        lines = [sm[b, m : m + 1, :] for b in range(batches) for m in range(z.meshes)]
        for line in (6, 7):
            lines.append(sum(sm[b, line : line + 1, :] for b in range(batches)))
        lines.append(jnp.zeros((16 - len(lines), sm.shape[2]), F32))
        small = jnp.concatenate(lines, axis=0)

        def finish():
            @pl.loop(0, batches)
            def _(b):
                @pl.when(sec == 0)
                def _():
                    for copy in relay(b):
                        copy.wait_send()

                @pl.when(sec == 1)
                def _():
                    relay_back(b).wait_send()

                for copy in halos(b):
                    copy.wait_send()

        if not z.scatter:
            small_out[...] = small
            table_out[...] = emb[...]
            finish()
            return

        def ring_copy(k):
            return remote(msend.at[k], mrecv.at[k], m_s.at[k], m_r.at[k], (sec, mate(1 << k)))

        def ring_start(k, value):
            msend[k] = value.astype(LOW)
            ring_copy(k).start()

        def ring_end(k):
            ring_copy(k).wait_recv()
            value = msend[k].astype(F32) + mrecv[k].astype(F32)
            if k + 1 < z.rings:
                ring_start(k + 1, value)
            else:
                tot[...] = value

        ring_start(0, small)

        lags = [0, 1] + [4 + 2 * k for k in range(stages - 1)]
        begun = (1 - sec) * early

        @pl.loop(0, npiece + lags[-1])
        def _(p):
            @pl.when((p >= begun) & (p < npiece))
            def _():
                piece_start(p)

            @pl.when((p >= begun + 1) & (p < npiece + 1))
            def _():
                piece_first(p - 1)

            for k in range(1, stages):
                lag = lags[k + 1]

                @pl.when((p >= lag) & (p < npiece + lag))
                def _(k=k, lag=lag):
                    piece_step(p - lag, k)

            for k in range(z.rings):

                @pl.when(p == 6 + 3 * k)
                def _(k=k):
                    ring_end(k)

            @pl.when(p == 4 + 3 * z.rings)
            def _():
                count = batches * z.meshes
                table = emb[pl.ds(pl.multiple_of(me * own, own), own), :]
                grad = jnp.zeros((own, 4 * width), F32)
                for k in range(count):
                    grad = grad + table[:, k : k + 1] * tot[k : k + 1, :]
                o_mod[0] = grad
                cols = 4 * width // shards
                mine = tot[:, pl.ds(pl.multiple_of(me * cols, cols), cols)]
                o_line[0:1, :] = jnp.sum(mine[0:count], axis=0, keepdims=True)
                o_line[1:2, :] = mine[count : count + 1]
                ratio = 128 // own
                line = tot[:, pl.ds(pl.multiple_of(me // ratio * 128, 128), 128)][count + 1 : count + 2]
                value = line
                for k in range(1, ratio):
                    rolled = jnp.concatenate([line[:, k * own :], line[:, : k * own]], axis=1)
                    value = jnp.where(me % ratio == k, rolled, value)
                o_line[2:3, :] = value

        finish()

        @pl.loop(0, npiece)
        def _(p):
            for k in range(stages):
                piece_copy(p, k).wait_send()

        for k in range(z.rings):
            ring_copy(k).wait_send()

    return kernel


def layout_of(z):
    own, groups = z.own, z.groups

    def kernel(
        lo, ig, piece, mod, line,
        o_lo, o_ig, o_qkv, o_out, o_up, o_upb, o_down, o_downb, o_mod, o_modb,
        sems,
    ):
        targets = [o_down.at[0, pl.ds(q * own, own), :] for q in range(groups)]
        targets += [o_up.at[0, :, pl.ds(q * TILE, TILE)] for q in range(groups)]
        targets += [o_out.at[0]] + [o_qkv.at[0, :, pl.ds(q * TILE, TILE)] for q in range(3)]
        moves = [(lo, o_lo), (ig, o_ig), (mod, o_mod)]
        moves += [(piece.at[k], target) for k, target in enumerate(targets)]
        copies = [pltpu.make_async_copy(a, b, sems.at[k]) for k, (a, b) in enumerate(moves)]
        for copy in copies:
            copy.start()
        o_modb[...] = line[0:1, :]
        o_upb[...] = line[1:2, :]
        o_downb[...] = line[2:3, 0:own]
        for copy in copies:
            copy.wait()

    return kernel


def body(
    inputs,
    cotangent,
    neighbours,
    mesh_ids,
    noise_sigma,
    w_qkv,
    w_out,
    w_up,
    b_up,
    w_down,
    b_down,
    w_mod,
    b_mod,
):
    shards = lax.axis_size("nodes")
    z = Sizes(inputs, neighbours, noise_sigma, w_up, shards)
    batches, rows, width, hidden, many = z.batches, z.rows, z.width, z.hidden, z.together
    own, npiece = z.own, z.pieces
    shape = jax.ShapeDtypeStruct
    stack = shape((1, batches, rows, width), LOW)
    outs = [stack, stack]
    sides = [(z.lefts, TILE, batches * rows), (z.rights, batches * rows, TILE)]
    if z.scatter:
        outs = [pltpu.VMEM(stack.shape, LOW)] * 2
        outs += [pltpu.VMEM((npiece, own, TILE), F32), pltpu.VMEM((1, own, 4 * width), F32), pltpu.VMEM((8, 128), F32)]
        scratch = [pltpu.VMEM(side, LOW) for side in sides]
    else:
        outs += [shape(side, LOW) for side in sides] + [shape((16, hidden), F32), shape((width, 128), F32)]
        scratch = []
    dma = pltpu.SemaphoreType.DMA
    scratch += [
        pltpu.VMEM((width, 3 * width), LOW),
        pltpu.VMEM((width, width), LOW),
        pltpu.VMEM((width, hidden), LOW),
        pltpu.VMEM((hidden, width), LOW),
        pltpu.VMEM((width, 4 * width), LOW),
        pltpu.VMEM((batches, z.ext, width), LOW),
        pltpu.VMEM((batches, rows, width), LOW),
        pltpu.VMEM((z.ext, 128), F32),
        pltpu.VMEM((16, rows), LOW),
        pltpu.VMEM((rows, z.window), F32),
        pltpu.VMEM((rows, z.window), LOW),
        pltpu.VMEM((rows, z.window), F32),
        pltpu.VMEM((batches, 8, 4 * width), F32),
        pltpu.VMEM((width, 128), F32),
        pltpu.VMEM((z.ext, width), LOW),
        pltpu.VMEM((batches, rows, width), LOW),
        pltpu.VMEM((batches, rows, width), F32),
        pltpu.VMEM((batches, rows, 128), F32),
        pltpu.VMEM((batches, rows, width), LOW),
        pltpu.VMEM((batches, z.window, 2 * width), LOW),
        pltpu.VMEM((many * HEADS, rows, z.window), F32),
        pltpu.VMEM((batches, HEADS, rows, z.window), F32),
        pltpu.VMEM((batches, HEADS, rows, z.window), LOW),
        pltpu.VMEM((batches, rows, width), LOW),
        pltpu.VMEM((batches, rows, width), LOW),
        pltpu.VMEM((batches, rows, width), F32),
        pltpu.VMEM((batches, rows, 128), F32),
        pltpu.VMEM((rows, width), F32),
        pltpu.VMEM((batches, rows, hidden), LOW),
        pltpu.VMEM((batches, rows, hidden), LOW),
        pltpu.VMEM((many * rows, width), LOW),
        pltpu.VMEM((many * rows, width), F32),
        pltpu.VMEM((many * HEADS, rows, z.window), LOW),
        pltpu.VMEM((many, rows, width), F32),
        pltpu.VMEM((many, rows, 2 * width), F32),
        pltpu.VMEM((batches, 2, REACH, 2 * width), LOW),
        pltpu.VMEM((batches, 2, REACH, 2 * width), LOW),
        pltpu.VMEM((batches, 8, hidden), F32),
        dma((7,)),
        dma((2,)),
        dma((2,)),
        dma((2,)),
        dma((2,)),
        dma((batches, 3)),
        dma((batches, 3)),
        dma((batches, 2)),
        dma((batches, 2)),
        dma((batches,)),
        dma((batches,)),
    ]
    if z.scatter:
        stages = len(z.bits)
        sizes = [TILE >> (k + 1) for k in range(stages)]
        scratch += [pltpu.VMEM((npiece, size, TILE), LOW) for size in sizes + sizes]
        scratch += [pltpu.VMEM((npiece, size, TILE), F32) for size in sizes[1:]]
        scratch += [
            pltpu.VMEM((sizes[0], TILE), F32),
            pltpu.VMEM((z.rings, 16, hidden), LOW),
            pltpu.VMEM((z.rings, 16, hidden), LOW),
            pltpu.VMEM((16, hidden), F32),
            dma((npiece, stages)),
            dma((npiece, stages)),
            dma((z.rings,)),
            dma((z.rings,)),
        ]
    hbm = pl.BlockSpec(memory_space=pl.ANY)
    vmem = pl.BlockSpec(memory_space=pltpu.VMEM)
    smem = pl.BlockSpec(memory_space=pltpu.SMEM)
    got = pl.pallas_call(
        kernel_of(z),
        out_shape=outs,
        in_specs=[hbm, hbm, vmem, vmem, smem, hbm, hbm, hbm, vmem, hbm, vmem, hbm, vmem],
        out_specs=[vmem] * len(outs),
        scratch_shapes=scratch,
        compiler_params=pltpu.CompilerParams(
            collective_id=0, has_side_effects=True, vmem_limit_bytes=60 * 2**20
        ),
    )(
        inputs,
        cotangent,
        neighbours.T,
        mesh_ids.reshape(1, rows),
        noise_sigma.T,
        w_qkv,
        w_out,
        w_up,
        b_up,
        w_down,
        b_down,
        w_mod,
        b_mod,
    )
    if z.scatter:
        lo, ig, piece, mod, line = got
        return tuple(
            pl.pallas_call(
                layout_of(z),
                out_shape=[
                    stack,
                    stack,
                    shape((1, own, 3 * width), F32),
                    shape((1, own, width), F32),
                    shape((1, own, hidden), F32),
                    shape((1, hidden // shards), F32),
                    shape((1, hidden // shards, width), F32),
                    shape((1, own), F32),
                    shape((1, own, 4 * width), F32),
                    shape((1, 4 * width // shards), F32),
                ],
                in_specs=[vmem] * 5,
                out_specs=[hbm, hbm, hbm, hbm, hbm, vmem, hbm, vmem, hbm, vmem],
                scratch_shapes=[dma((npiece + 3,))],
                compiler_params=pltpu.CompilerParams(vmem_limit_bytes=2 * 2**20),
            )(lo, ig, piece, mod, line)
        )
    lo, ig, left_t, right_t, small, table = got
    groups = z.groups

    def summed(value):
        return lax.psum_scatter(value, "nodes", scatter_dimension=0, tiled=True)

    def wide_sum(left, first, last):
        return summed(jnp.concatenate([dot(left_t[left], right_t[r]) for r in range(first, last)], axis=1))[None]

    down = [dot(left_t[q], right_t[0]).reshape(TILE // 32, 32, TILE) for q in range(groups)]
    down = jnp.stack(down, axis=1)
    count = batches * z.meshes
    small = lax.psum(small, "nodes")
    me = lax.axis_index("nodes")
    mod = jnp.dot(table[:, :count], small[:count], precision=lax.Precision.HIGHEST)

    def mine(value):
        size = value.shape[0] // shards
        return lax.dynamic_slice_in_dim(value, me * size, size, axis=0)[None]

    return (
        lo,
        ig,
        wide_sum(groups + 2, 2 + groups, 5 + groups),
        wide_sum(groups + 1, 1 + groups, 2 + groups),
        wide_sum(groups, 1, 1 + groups),
        mine(small[count]),
        summed(down.reshape(hidden, width))[None],
        mine(small[count + 1, :width]),
        mine(mod),
        mine(jnp.sum(small[:count], axis=0)),
    )


def solution(mesh):
    return jax.shard_map(
        body,
        mesh=mesh,
        in_specs=(
            P(None, "nodes", None),
            P(None, "nodes", None),
            P("nodes", None),
            P("nodes"),
            P(),
            P("section", None, None),
            P("section", None, None),
            P("section", None, None),
            P("section", None),
            P("section", None, None),
            P("section", None),
            P("section", None, None),
            P("section", None),
        ),
        out_specs=(
            P("section", None, "nodes", None),
            P("section", None, "nodes", None),
            P("section", "nodes", None),
            P("section", "nodes", None),
            P("section", "nodes", None),
            P("section", "nodes"),
            P("section", "nodes", None),
            P("section", "nodes"),
            P("section", "nodes", None),
            P("section", "nodes"),
        ),
        check_vma=False,
    )
```

```python
import jax
import jax.numpy as jnp
from jax import lax
from jax.experimental import pallas as pl
from jax.experimental.pallas import tpu as pltpu
from jax.sharding import PartitionSpec as P

HEADS = 4
REACH = 32
EPSILON = 1e-06
MASKED = -1e9
ABSENT = -2e38
TILE = 512
TOGETHER = 2
MESH = pl.DeviceIdType.MESH
F32, LOW = jnp.float32, jnp.bfloat16


def dot(a, b):
    return lax.dot_general(a, b, (((1,), (0,)), ((), ())), preferred_element_type=F32)


def dot_nt(a, b):
    return lax.dot_general(a, b, (((1,), (1,)), ((), ())), preferred_element_type=F32)


def dot_tn(a, b):
    return lax.dot_general(a, b, (((0,), (0,)), ((), ())), preferred_element_type=F32)


class Sizes:
    def __init__(self, inputs, neighbours, noise, w_up, shards):
        self.batches, self.rows, self.width = inputs.shape
        self.together = TOGETHER if self.batches % TOGETHER == 0 else 1
        self.turns = self.batches // self.together
        self.slots = neighbours.shape[1]
        self.meshes = noise.shape[1]
        self.hidden = w_up.shape[2]
        self.shards = shards
        self.ext = self.rows + 2 * REACH
        self.window = (self.ext // 128 + 1) * 128
        self.groups = self.hidden // TILE
        self.own = self.width // shards
        self.scatter = self.own % 16 == 0
        self.pieces = 2 * self.groups + 4
        self.lefts = 3 + self.groups
        self.rights = 2 + self.groups + 3
        self.rings = max(shards.bit_length() - 1, 1)

        self.bits = [1 << k for k in range(shards.bit_length() - 1)]

    def left(self, p):
        n = self.groups
        return jnp.minimum(p, n) + lax.div(p, 2 * n) + lax.div(p, 2 * n + 1)

    def right(self, p):
        return jnp.maximum(p - (self.groups - 1), 0)


def kernel_of(z):
    batches, rows, width, ext, window = z.batches, z.rows, z.width, z.ext, z.window
    groups, shards, own, many = z.groups, z.shards, z.own, z.together
    head = width // HEADS
    score_scale = head ** (-0.5)
    log2e = 1.4426950408889634
    npiece = z.pieces
    half = TILE // 2
    stages = len(z.bits)
    g_out, g_q, g_k = 1 + groups, 2 + groups, 3 + groups

    def position(owner):
        if not z.scatter:
            return owner
        place = 0
        for bit in z.bits:
            place = 2 * place + owner // bit % 2
        return place

    def kernel(
        inputs, cotangent, neighbours, mesh_ids, sigma,
        w_qkv, w_out, w_up, b_up, w_down, b_down, w_mod, b_mod,
        lo, ig, *rest,
    ):
        if z.scatter:
            o_piece, o_mod, o_line, left_t, right_t = rest[:5]
            rest = rest[5:]
        else:
            left_t, right_t, small_out, table_out = rest[:4]
            rest = rest[4:]
        (
            wq, wo, wu, wd, wm, xext, dybuf, sel, pick, cnt, few, bias, mod, emb,
            n1, n1s, ua, ia, qb, kvext, sbuf, af, ca, obs, n2s, ub, ib, tb, fp, hs,
            ob, dbuf, cds, dx1, dkv, hsend, hrecv, sm,
            lsem, hx_s, hx_r, hm_s, hm_r, fx_s, fx_r, bh_s, bh_r, bx_s, bx_r,
        ) = rest[:49]
        rest = rest[49:]
        if z.scatter:
            gives, gets, keeps = rest[:stages], rest[stages : 2 * stages], rest[2 * stages : 3 * stages - 1]
            acc, msend, mrecv, tot, p_s, p_r, m_s, m_r = rest[3 * stages - 1 :]

        sec = lax.axis_index("section")
        me = lax.axis_index("nodes")
        up = lax.rem(me + 1, shards)
        down = lax.rem(me + shards - 1, shards)
        other = 1 - sec
        def local(src, dst, k):
            return pltpu.make_async_copy(src, dst, lsem.at[k])

        loads = [
            local(w_mod.at[0], wm, 0),
            local(w_qkv.at[0], wq, 1),
            local(w_out.at[0], wo, 2),
            local(w_up.at[0], wu, 3),
            local(w_down.at[0], wd, 4),
        ]
        own_rows = pl.ds(REACH, rows)
        first_load = local(inputs, xext.at[:, own_rows, :], 5)
        last_load = local(cotangent, dybuf, 6)
        loads[0].start()

        @pl.when(sec == 0)
        def _():
            first_load.start()

        for copy in loads[1:]:
            copy.start()

        @pl.when(sec == 1)
        def _():
            last_load.start()

        def side(bit):
            return lax.rem(lax.div(me, bit), 2)

        def mate(bit):
            return me + bit - 2 * bit * side(bit)

        barrier = pltpu.get_barrier_semaphore()
        mates = [(sec, up), (sec, down), (other, me), (other, up), (other, down)]
        if z.scatter:
            mates += [(sec, mate(bit)) for bit in z.bits[1:]]
        for peer in mates:
            pl.semaphore_signal(barrier, inc=1, device_id=peer, device_id_type=MESH)
        pl.semaphore_wait(barrier, len(mates))

        def remote(src, dst, s_sem, r_sem, peer):
            return pltpu.make_async_remote_copy(
                src_ref=src, dst_ref=dst, send_sem=s_sem, recv_sem=r_sem, device_id=peer, device_id_type=MESH
            )

        low_rows, top_rows = pl.ds(0, REACH), pl.ds(REACH + rows, REACH)
        head_rows, tail_rows = pl.ds(REACH, REACH), pl.ds(rows, REACH)
        x_down = remote(inputs.at[:, pl.ds(0, REACH), :], xext.at[:, top_rows, :], hx_s.at[0], hx_r.at[0], (sec, down))
        x_up = remote(inputs.at[:, pl.ds(rows - REACH, REACH), :], xext.at[:, low_rows, :], hx_s.at[1], hx_r.at[1], (sec, up))

        @pl.when(sec == 0)
        def _():
            x_down.start()
            x_up.start()

        ids = jnp.broadcast_to(mesh_ids[...].astype(F32), (128, rows))
        sel[own_rows, :] = ids.T
        sample = lax.broadcasted_iota(jnp.int32, (16, rows), 0).astype(F32)
        pick[...] = jnp.where(ids[0:16] == sample, 1.0, 0.0).astype(LOW)
        m_down = remote(sel.at[head_rows, :], sel.at[top_rows, :], hm_s.at[0], hm_r.at[0], (sec, down))
        m_up = remote(sel.at[tail_rows, :], sel.at[low_rows, :], hm_s.at[1], hm_r.at[1], (sec, up))
        m_down.start()
        m_up.start()

        kvext[:, ext:window, :] = jnp.zeros((batches, window - ext, 2 * width), LOW)
        sm[...] = jnp.zeros(sm.shape, F32)

        slots = neighbours[...].astype(F32)
        slots = jnp.concatenate([slots, jnp.zeros((128 - z.slots, rows), F32)], axis=0).T
        slots = jnp.where(slots >= 0, slots - (me * rows - REACH).astype(F32), float(ext))
        column = lax.broadcasted_iota(jnp.int32, (rows, window), 1).astype(F32)
        counts = jnp.zeros((rows, window), F32)
        for n in range(z.slots):
            counts = counts + jnp.where(slots[:, n : n + 1] == column, 1.0, 0.0)
        cnt[...] = counts
        few[...] = counts.astype(LOW)
        bias[...] = jnp.where(counts > 0, jnp.where(column == ext, MASKED * log2e, 0.0), ABSENT)

        row_no = lax.broadcasted_iota(jnp.int32, (16, width // 2), 0)
        level = jnp.ones((16, width // 2), F32)
        for b in range(batches):
            for m in range(z.meshes):
                level = jnp.where(row_no == b * z.meshes + m, sigma[m, b], level)
        place = lax.broadcasted_iota(jnp.int32, (16, width // 2), 1).astype(F32)
        frequency = 3.0 * jnp.exp(-jnp.log(100.0) * place / (width // 2))
        angles = jnp.log(level) * frequency
        embedded = jnp.concatenate([jnp.sin(angles), jnp.cos(angles)], axis=1).astype(LOW)
        padded = jnp.concatenate([embedded.astype(F32), jnp.zeros((112, width), F32)], axis=0)
        emb[...] = padded.T
        loads[0].wait()
        for g in range(4):
            cols = pl.ds(g * width, width)
            table = dot(embedded, wm[:, cols]) + b_mod[:, cols] + (1.0 - g % 2)
            for b in range(batches):
                mod[b, 0 : z.meshes, cols] = table[b * z.meshes : (b + 1) * z.meshes]

        def mod_rows(b, part, ids_rows):
            cols = pl.ds(part * width, width)
            value = jnp.broadcast_to(mod[b, 0:1, cols], (ids_rows.shape[0], width))
            for m in range(1, z.meshes):
                value = jnp.where(ids_rows > m - 0.5, mod[b, m : m + 1, cols], value)
            return value

        def wide(ids_rows):
            return jnp.concatenate([ids_rows] * (width // 128), axis=1)

        def unit(x):
            centred = x - jnp.mean(x, axis=-1, keepdims=True)
            inv = lax.rsqrt(jnp.mean(centred * centred, axis=-1, keepdims=True) + EPSILON)
            return centred * inv, inv

        def span_of(start, size):
            if isinstance(start, int):
                return pl.ds(start, size)
            return pl.ds(pl.multiple_of(start, size), size)

        def batch_cols(b):
            return span_of(b * rows, rows)

        def turn_cols(t):
            return span_of(t * many * rows, many * rows)

        def turn_of(ref, t):
            return ref[pl.ds(t * many, many)].reshape(many * rows, ref.shape[2])

        span = own if z.scatter else 32

        def transposes(b, carry):
            for first, ref in ((groups, n2s), (groups + 1, obs), (groups + 2, n1s)):
                turned = ref[b].T
                for owner in range(TILE // span):
                    at = position(owner) * span
                    left_t[first, at : at + span, batch_cols(b)] = turned[owner * span : (owner + 1) * span]
            run = groups * span
            for g in range(groups):
                turned = hs[b, :, g * TILE : (g + 1) * TILE].T
                for k in range(TILE // span):
                    at = g * TILE + k * span
                    owner, part = at // run, at % run // span
                    to = position(owner) * span
                    left_t[part, to : to + span, batch_cols(b)] = turned[k * span : (k + 1) * span]
            return carry

        heads = [slice(h * head, (h + 1) * head) for h in range(HEADS)]
        heads_v = [slice(width + h * head, width + (h + 1) * head) for h in range(HEADS)]
        tiles = [slice(g * TILE, (g + 1) * TILE) for g in range(groups)]
        thirds = [slice(g * width, (g + 1) * width) for g in range(3)]

        def forward(b):
            ids_rows = wide(sel[0:ext, :])
            u, inv = unit(xext[b].astype(F32))
            normed = (u * mod_rows(b, 0, ids_rows) + mod_rows(b, 1, ids_rows)).astype(LOW)
            n1[...] = normed
            n1s[b] = normed[REACH : REACH + rows]
            ua[b] = u[REACH : REACH + rows]
            ia[b] = jnp.broadcast_to(inv[REACH : REACH + rows], (rows, 128))
            kvext[b, 0:ext, thirds[0]] = dot(n1[...], wq[:, thirds[1]]).astype(LOW)
            qb[b] = dot(n1s[b], wq[:, thirds[0]]).astype(LOW)
            for h in range(HEADS):
                sbuf[h] = dot_nt(qb[b, :, heads[h]], kvext[b, :, heads[h]]) * (score_scale * log2e) + bias[...]
            kvext[b, 0:ext, thirds[1]] = dot(n1[...], wq[:, thirds[2]]).astype(LOW)
            for h in range(HEADS):
                s = sbuf[h]
                e = jnp.exp2(s - jnp.max(s, axis=-1, keepdims=True))
                a = e * (1.0 / jnp.sum(e * cnt[...], axis=-1, keepdims=True))
                af[b, h] = a
                ca[b, h] = a.astype(LOW) * few[...]
            for h in range(HEADS):
                obs[b, :, heads[h]] = dot(ca[b, h], kvext[b, :, heads_v[h]]).astype(LOW)

            x1 = xext[b, own_rows, :].astype(F32) + dot(obs[b], wo[...])
            u, inv = unit(x1)
            ub[b] = u
            ib[b] = jnp.broadcast_to(inv, (rows, 128))
            ids_rows = wide(sel[own_rows, :])
            n2s[b] = (u * mod_rows(b, 2, ids_rows) + mod_rows(b, 3, ids_rows)).astype(LOW)
            tb[...] = x1 + b_down[...]
            for gs in tiles:
                gate = dot(n2s[b], wu[:, gs]) + b_up[:, gs]
                s = 0.5 + 0.5 * jnp.tanh(0.5 * gate)
                hid = gate * s
                fp[b, :, gs] = (s + hid * (1.0 - s)).astype(LOW)
                hid = hid.astype(LOW)
                hs[b, :, gs] = hid
                tb[...] += dot(hid, wd[gs, :])
            lo[0, b] = tb[...].astype(LOW)

        def relay(b):
            return [
                remote(lo.at[0, b], xext.at[b, own_rows, :], fx_s.at[b, 0], fx_r.at[b, 0], (other, me)),
                remote(lo.at[0, b, pl.ds(0, REACH), :], xext.at[b, top_rows, :], fx_s.at[b, 1], fx_r.at[b, 1], (other, down)),
                remote(lo.at[0, b, pl.ds(rows - REACH, REACH), :], xext.at[b, low_rows, :], fx_s.at[b, 2], fx_r.at[b, 2], (other, up)),
            ]

        def norm_back(d, u, inv, scale):
            scaled = d * scale
            return inv * (
                scaled
                - jnp.mean(scaled, axis=-1, keepdims=True)
                - u * jnp.mean(scaled * u, axis=-1, keepdims=True)
            )

        def mod_sums(b, part, d, u):
            for k, value in enumerate((d * u, d)):
                total = dot(pick[...], value.astype(LOW))
                sm[b, 0 : z.meshes, (part + k) * width : (part + k + 1) * width] = total[0 : z.meshes]

        def halos(b):
            return [
                remote(hsend.at[b, 0], hrecv.at[b, 1], bh_s.at[b, 0], bh_r.at[b, 0], (sec, down)),
                remote(hsend.at[b, 1], hrecv.at[b, 0], bh_s.at[b, 1], bh_r.at[b, 1], (sec, up)),
            ]

        def given(b):
            at = batch_cols(b)
            dr = dybuf[b]
            right_t[0, at, :] = dr
            sm[b, 7:8, 0:width] = jnp.sum(dr.astype(F32), axis=0, keepdims=True)
            for g in range(groups):
                right_t[1 + g, at, :] = dot_nt(dr, wd[g * TILE : (g + 1) * TILE, :]).astype(LOW)

        def back_ffn(t):
            at = turn_cols(t)
            dn = jnp.zeros((many * rows, width), F32)
            for g in range(groups):
                gs = slice(g * TILE, (g + 1) * TILE)
                dg = right_t[1 + g, at, :].astype(F32) * turn_of(fp, t)[:, gs].astype(F32)
                sm[t * many, 6:7, gs] = jnp.sum(dg, axis=0, keepdims=True)
                dg = dg.astype(LOW)
                right_t[1 + g, at, :] = dg
                dn = dn + dot_nt(dg, wu[:, gs])
            dbuf[...] = dn

        def back_middle(t):
            at = turn_cols(t)
            ids_rows = wide(sel[own_rows, :])
            for i in range(many):
                b = t * many + i
                d = dbuf[i * rows : (i + 1) * rows]
                u = ub[b]
                grad = dybuf[b].astype(F32) + norm_back(d, u, ib[b][:, 0:1], mod_rows(b, 2, ids_rows))
                mod_sums(b, 2, d, u)
                dx1[i] = grad
                right_t[g_out, batch_cols(b), :] = grad.astype(LOW)
            ob[...] = dot_nt(right_t[g_out, at, :], wo[...]).astype(LOW)

        def back_attention(t):
            units = [(i, h) for i in range(many) for h in range(HEADS)]
            here = [slice(i * rows, (i + 1) * rows) for i in range(many)]
            for i, h in units:
                sbuf[i * HEADS + h] = dot_nt(ob[here[i], heads[h]], kvext[t * many + i, :, heads_v[h]])
            for i, h in units:
                b, k = t * many + i, i * HEADS + h
                a, da = af[b, h], sbuf[k]
                ds = a * (da - jnp.sum(a * cnt[...] * da, axis=-1, keepdims=True))
                cds[k] = ds.astype(LOW) * few[...]
            for i in range(many):
                b = t * many + i
                for h in range(HEADS):
                    dk = dot_tn(cds[i * HEADS + h], qb[b, :, heads[h]]) * score_scale
                    dv = dot_tn(ca[b, h], ob[here[i], heads[h]])
                    for part, cols in ((dk, heads[h]), (dv, heads_v[h])):
                        hsend[b, 0, :, cols] = part[0:REACH].astype(LOW)
                        dkv[i, :, cols] = part[REACH : REACH + rows]
                        hsend[b, 1, :, cols] = part[REACH + rows : ext].astype(LOW)
                for copy in halos(b):
                    copy.start()
            for i, h in units:
                b = t * many + i
                value = dot(cds[i * HEADS + h], kvext[b, :, heads[h]]) * score_scale
                right_t[g_q, batch_cols(b), heads[h]] = value.astype(LOW)

        def back_second(t):
            at = turn_cols(t)
            ids_rows = wide(sel[own_rows, :])
            edge = rows - REACH
            dbuf[...] = dot_nt(right_t[g_q, at, :], wq[:, 0:width])
            for i in range(many):
                b = t * many + i
                for copy in halos(b):
                    copy.wait_recv()
                dkv[i, 0:REACH, :] += hrecv[b, 0].astype(F32)
                dkv[i, edge:rows, :] += hrecv[b, 1].astype(F32)
                d = dbuf[i * rows : (i + 1) * rows]
                for g in range(2):
                    part = dkv[i, :, g * width : (g + 1) * width].astype(LOW)
                    right_t[g_k + g, batch_cols(b), :] = part
                    d = d + dot_nt(part, wq[:, (g + 1) * width : (g + 2) * width])
                u = ua[b]
                grad = dx1[i] + norm_back(d, u, ia[b][:, 0:1], mod_rows(b, 0, ids_rows))
                ig[0, b] = grad.astype(LOW)

                @pl.when(sec == 1)
                def _(b=b):
                    relay_back(b).start()

                mod_sums(b, 0, d, u)

        def relay_back(b):
            return remote(ig.at[0, b], dybuf.at[b], bx_s.at[b], bx_r.at[b], (other, me))

        for copy in loads[1:]:
            copy.wait()
        for copy in (m_down, m_up):
            copy.wait()

        @pl.when(sec == 0)
        def _():
            first_load.wait()
            x_down.wait()
            x_up.wait()

        @pl.when(sec == 1)
        def _():
            last_load.wait()

            @pl.loop(0, batches)
            def _(b):
                given(b)

        @pl.loop(0, batches)
        def _(b):
            @pl.when(sec == 1)
            def _():
                for copy in relay(b):
                    copy.wait_recv()

            forward(b)

            @pl.when(sec == 0)
            def _():
                for copy in relay(b):
                    copy.start()

        @pl.when(sec == 0)
        def _():
            lax.fori_loop(0, batches, transposes, 0)

        def rows_of(c, size):
            return pl.ds(pl.multiple_of(c * size, size), size)

        def turned(p):
            return lax.div(lax.rem(p, 4), 3) if stages > 2 else 0 * p

        def bit_of(p, k):
            bits = list(z.bits)
            if stages > 2:
                bits[1], bits[2] = bits[2], bits[1]
            return z.bits[k] + (bits[k] - z.bits[k]) * turned(p)

        def piece_copy(p, k):
            return remote(gives[k].at[p], gets[k].at[p], p_s.at[p, k], p_r.at[p, k], (sec, mate(bit_of(p, k))))

        def piece_start(p):
            left = z.left(p)
            sides = [left_t[left, rows_of(c, half), :] for c in (1 - side(1), side(1))]
            value = dot(jnp.concatenate(sides, axis=0), right_t[z.right(p)])
            gives[0][p] = value[0:half].astype(LOW)
            piece_copy(p, 0).start()
            acc[lax.rem(p, 2)] = value[half : 2 * half]

        def piece_first(p):
            piece_copy(p, 0).wait_recv()
            here = side(bit_of(p, 1))
            run = half // 4
            for s, to in ((1 - here, gives[1]), (here, keeps[0])):
                for j in range(2):
                    at = rows_of((1 - turned(p)) * (2 * s + j) + turned(p) * (2 * j + s), run)
                    value = acc[lax.rem(p, 2), at, :] + gets[0][p, at, :].astype(F32)
                    to[p, j * run : (j + 1) * run, :] = value.astype(to.dtype)
                if to is gives[1]:
                    piece_copy(p, 1).start()

        def piece_step(p, k):
            size = half >> k
            piece_copy(p, k).wait_recv()
            if k == stages - 1:
                o_piece[p] = keeps[k - 1][p] + gets[k][p].astype(F32)
                return
            here = side(bit_of(p, k + 1))
            for to, c in ((gives[k + 1], 1 - here), (keeps[k], here)):
                at = rows_of(c, size // 2)
                to[p] = (keeps[k - 1][p, at, :] + gets[k][p, at, :].astype(F32)).astype(to.dtype)
                if to is gives[k + 1]:
                    piece_copy(p, k + 1).start()

        def only_first(body):
            if z.scatter:
                pl.when(sec == 0)(body)

        for t in reversed(range(z.turns)):

            @pl.when(sec == 0)
            def _(t=t):
                for i in range(many):
                    relay_back(t * many + i).wait_recv()
                    given(t * many + i)

            back_ffn(t)
            back_middle(t)
            back_attention(t)
            if t == 0:

                @only_first
                def _():
                    @pl.loop(0, groups)
                    def _(p):
                        piece_start(p)

                        @pl.when(p > 0)
                        def _():
                            piece_first(p - 1)

            back_second(t)

        @pl.when(sec == 1)
        def _():
            lax.fori_loop(0, batches, transposes, 0)

        lines = [sm[b, m : m + 1, :] for b in range(batches) for m in range(z.meshes)]
        for line in (6, 7):
            lines.append(sum(sm[b, line : line + 1, :] for b in range(batches)))
        lines.append(jnp.zeros((16 - len(lines), sm.shape[2]), F32))
        small = jnp.concatenate(lines, axis=0)

        def finish():
            @pl.loop(0, batches)
            def _(b):
                @pl.when(sec == 0)
                def _():
                    for copy in relay(b):
                        copy.wait_send()

                @pl.when(sec == 1)
                def _():
                    relay_back(b).wait_send()

                for copy in halos(b):
                    copy.wait_send()

        if not z.scatter:
            small_out[...] = small
            table_out[...] = emb[...]
            finish()
            return

        def ring_copy(k):
            return remote(msend.at[k], mrecv.at[k], m_s.at[k], m_r.at[k], (sec, mate(1 << k)))

        def ring_start(k, value):
            msend[k] = value.astype(LOW)
            ring_copy(k).start()

        def ring_end(k):
            ring_copy(k).wait_recv()
            value = msend[k].astype(F32) + mrecv[k].astype(F32)
            if k + 1 < z.rings:
                ring_start(k + 1, value)
            else:
                tot[...] = value

        ring_start(0, small)

        lags = [0, 1] + [4 + 2 * k for k in range(stages - 1)]
        begun = (1 - sec) * groups

        @pl.loop(0, npiece + lags[-1])
        def _(p):
            @pl.when((p >= begun) & (p < npiece))
            def _():
                piece_start(p)

            @pl.when((p >= begun + sec) & (p >= 1) & (p < npiece + 1))
            def _():
                piece_first(p - 1)

            for k in range(1, stages):
                lag = lags[k + 1]

                @pl.when((p >= lag) & (p < npiece + lag))
                def _(k=k, lag=lag):
                    piece_step(p - lag, k)

            for k in range(z.rings):

                @pl.when(p == 6 + 3 * k)
                def _(k=k):
                    ring_end(k)

            @pl.when(p == 4 + 3 * z.rings)
            def _():
                count = batches * z.meshes
                table = emb[pl.ds(pl.multiple_of(me * own, own), own), :]
                grad = jnp.zeros((own, 4 * width), F32)
                for k in range(count):
                    grad = grad + table[:, k : k + 1] * tot[k : k + 1, :]
                o_mod[0] = grad
                cols = 4 * width // shards
                mine = tot[:, pl.ds(pl.multiple_of(me * cols, cols), cols)]
                o_line[0:1, :] = jnp.sum(mine[0:count], axis=0, keepdims=True)
                o_line[1:2, :] = mine[count : count + 1]
                ratio = 128 // own
                line = tot[:, pl.ds(pl.multiple_of(me // ratio * 128, 128), 128)][count + 1 : count + 2]
                value = line
                for k in range(1, ratio):
                    rolled = jnp.concatenate([line[:, k * own :], line[:, : k * own]], axis=1)
                    value = jnp.where(me % ratio == k, rolled, value)
                o_line[2:3, :] = value

        finish()

        @pl.loop(0, npiece)
        def _(p):
            for k in range(stages):
                piece_copy(p, k).wait_send()

        for k in range(z.rings):
            ring_copy(k).wait_send()

    return kernel


def layout_of(z):
    own, groups = z.own, z.groups

    def kernel(
        lo, ig, piece, mod, line,
        o_lo, o_ig, o_qkv, o_out, o_up, o_upb, o_down, o_downb, o_mod, o_modb,
        sems,
    ):
        targets = [o_down.at[0, pl.ds(q * own, own), :] for q in range(groups)]
        targets += [o_up.at[0, :, pl.ds(q * TILE, TILE)] for q in range(groups)]
        targets += [o_out.at[0]] + [o_qkv.at[0, :, pl.ds(q * TILE, TILE)] for q in range(3)]
        moves = [(lo, o_lo), (ig, o_ig), (mod, o_mod)]
        moves += [(piece.at[k], target) for k, target in enumerate(targets)]
        copies = [pltpu.make_async_copy(a, b, sems.at[k]) for k, (a, b) in enumerate(moves)]
        for copy in copies:
            copy.start()
        o_modb[...] = line[0:1, :]
        o_upb[...] = line[1:2, :]
        o_downb[...] = line[2:3, 0:own]
        for copy in copies:
            copy.wait()

    return kernel


def body(
    inputs,
    cotangent,
    neighbours,
    mesh_ids,
    noise_sigma,
    w_qkv,
    w_out,
    w_up,
    b_up,
    w_down,
    b_down,
    w_mod,
    b_mod,
):
    shards = lax.axis_size("nodes")
    z = Sizes(inputs, neighbours, noise_sigma, w_up, shards)
    batches, rows, width, hidden, many = z.batches, z.rows, z.width, z.hidden, z.together
    own, npiece = z.own, z.pieces
    shape = jax.ShapeDtypeStruct
    stack = shape((1, batches, rows, width), LOW)
    outs = [stack, stack]
    sides = [(z.lefts, TILE, batches * rows), (z.rights, batches * rows, TILE)]
    if z.scatter:
        outs = [pltpu.VMEM(stack.shape, LOW)] * 2
        outs += [pltpu.VMEM((npiece, own, TILE), F32), pltpu.VMEM((1, own, 4 * width), F32), pltpu.VMEM((8, 128), F32)]
        scratch = [pltpu.VMEM(side, LOW) for side in sides]
    else:
        outs += [shape(side, LOW) for side in sides] + [shape((16, hidden), F32), shape((width, 128), F32)]
        scratch = []
    dma = pltpu.SemaphoreType.DMA
    scratch += [
        pltpu.VMEM((width, 3 * width), LOW),
        pltpu.VMEM((width, width), LOW),
        pltpu.VMEM((width, hidden), LOW),
        pltpu.VMEM((hidden, width), LOW),
        pltpu.VMEM((width, 4 * width), LOW),
        pltpu.VMEM((batches, z.ext, width), LOW),
        pltpu.VMEM((batches, rows, width), LOW),
        pltpu.VMEM((z.ext, 128), F32),
        pltpu.VMEM((16, rows), LOW),
        pltpu.VMEM((rows, z.window), F32),
        pltpu.VMEM((rows, z.window), LOW),
        pltpu.VMEM((rows, z.window), F32),
        pltpu.VMEM((batches, 8, 4 * width), F32),
        pltpu.VMEM((width, 128), F32),
        pltpu.VMEM((z.ext, width), LOW),
        pltpu.VMEM((batches, rows, width), LOW),
        pltpu.VMEM((batches, rows, width), F32),
        pltpu.VMEM((batches, rows, 128), F32),
        pltpu.VMEM((batches, rows, width), LOW),
        pltpu.VMEM((batches, z.window, 2 * width), LOW),
        pltpu.VMEM((many * HEADS, rows, z.window), F32),
        pltpu.VMEM((batches, HEADS, rows, z.window), F32),
        pltpu.VMEM((batches, HEADS, rows, z.window), LOW),
        pltpu.VMEM((batches, rows, width), LOW),
        pltpu.VMEM((batches, rows, width), LOW),
        pltpu.VMEM((batches, rows, width), F32),
        pltpu.VMEM((batches, rows, 128), F32),
        pltpu.VMEM((rows, width), F32),
        pltpu.VMEM((batches, rows, hidden), LOW),
        pltpu.VMEM((batches, rows, hidden), LOW),
        pltpu.VMEM((many * rows, width), LOW),
        pltpu.VMEM((many * rows, width), F32),
        pltpu.VMEM((many * HEADS, rows, z.window), LOW),
        pltpu.VMEM((many, rows, width), F32),
        pltpu.VMEM((many, rows, 2 * width), F32),
        pltpu.VMEM((batches, 2, REACH, 2 * width), LOW),
        pltpu.VMEM((batches, 2, REACH, 2 * width), LOW),
        pltpu.VMEM((batches, 8, hidden), F32),
        dma((7,)),
        dma((2,)),
        dma((2,)),
        dma((2,)),
        dma((2,)),
        dma((batches, 3)),
        dma((batches, 3)),
        dma((batches, 2)),
        dma((batches, 2)),
        dma((batches,)),
        dma((batches,)),
    ]
    if z.scatter:
        stages = len(z.bits)
        sizes = [TILE >> (k + 1) for k in range(stages)]
        scratch += [pltpu.VMEM((npiece, size, TILE), LOW) for size in sizes + sizes]
        scratch += [pltpu.VMEM((npiece, size, TILE), F32) for size in sizes[1:]]
        scratch += [
            pltpu.VMEM((2, sizes[0], TILE), F32),
            pltpu.VMEM((z.rings, 16, hidden), LOW),
            pltpu.VMEM((z.rings, 16, hidden), LOW),
            pltpu.VMEM((16, hidden), F32),
            dma((npiece, stages)),
            dma((npiece, stages)),
            dma((z.rings,)),
            dma((z.rings,)),
        ]
    hbm = pl.BlockSpec(memory_space=pl.ANY)
    vmem = pl.BlockSpec(memory_space=pltpu.VMEM)
    smem = pl.BlockSpec(memory_space=pltpu.SMEM)
    got = pl.pallas_call(
        kernel_of(z),
        out_shape=outs,
        in_specs=[hbm, hbm, vmem, vmem, smem, hbm, hbm, hbm, vmem, hbm, vmem, hbm, vmem],
        out_specs=[vmem] * len(outs),
        scratch_shapes=scratch,
        compiler_params=pltpu.CompilerParams(
            collective_id=0, has_side_effects=True, vmem_limit_bytes=61 * 2**20
        ),
    )(
        inputs,
        cotangent,
        neighbours.T,
        mesh_ids.reshape(1, rows),
        noise_sigma.T,
        w_qkv,
        w_out,
        w_up,
        b_up,
        w_down,
        b_down,
        w_mod,
        b_mod,
    )
    if z.scatter:
        lo, ig, piece, mod, line = got
        return tuple(
            pl.pallas_call(
                layout_of(z),
                out_shape=[
                    stack,
                    stack,
                    shape((1, own, 3 * width), F32),
                    shape((1, own, width), F32),
                    shape((1, own, hidden), F32),
                    shape((1, hidden // shards), F32),
                    shape((1, hidden // shards, width), F32),
                    shape((1, own), F32),
                    shape((1, own, 4 * width), F32),
                    shape((1, 4 * width // shards), F32),
                ],
                in_specs=[vmem] * 5,
                out_specs=[hbm, hbm, hbm, hbm, hbm, vmem, hbm, vmem, hbm, vmem],
                scratch_shapes=[dma((npiece + 3,))],
                compiler_params=pltpu.CompilerParams(vmem_limit_bytes=2 * 2**20),
            )(lo, ig, piece, mod, line)
        )
    lo, ig, left_t, right_t, small, table = got
    groups = z.groups

    def summed(value):
        return lax.psum_scatter(value, "nodes", scatter_dimension=0, tiled=True)

    def wide_sum(left, first, last):
        return summed(jnp.concatenate([dot(left_t[left], right_t[r]) for r in range(first, last)], axis=1))[None]

    down = [dot(left_t[q], right_t[0]).reshape(TILE // 32, 32, TILE) for q in range(groups)]
    down = jnp.stack(down, axis=1)
    count = batches * z.meshes
    small = lax.psum(small, "nodes")
    me = lax.axis_index("nodes")
    mod = jnp.dot(table[:, :count], small[:count], precision=lax.Precision.HIGHEST)

    def mine(value):
        size = value.shape[0] // shards
        return lax.dynamic_slice_in_dim(value, me * size, size, axis=0)[None]

    return (
        lo,
        ig,
        wide_sum(groups + 2, 2 + groups, 5 + groups),
        wide_sum(groups + 1, 1 + groups, 2 + groups),
        wide_sum(groups, 1, 1 + groups),
        mine(small[count]),
        summed(down.reshape(hidden, width))[None],
        mine(small[count + 1, :width]),
        mine(mod),
        mine(jnp.sum(small[:count], axis=0)),
    )


def solution(mesh):
    return jax.shard_map(
        body,
        mesh=mesh,
        in_specs=(
            P(None, "nodes", None),
            P(None, "nodes", None),
            P("nodes", None),
            P("nodes"),
            P(),
            P("section", None, None),
            P("section", None, None),
            P("section", None, None),
            P("section", None),
            P("section", None, None),
            P("section", None),
            P("section", None, None),
            P("section", None),
        ),
        out_specs=(
            P("section", None, "nodes", None),
            P("section", None, "nodes", None),
            P("section", "nodes", None),
            P("section", "nodes", None),
            P("section", "nodes", None),
            P("section", "nodes"),
            P("section", "nodes", None),
            P("section", "nodes"),
            P("section", "nodes", None),
            P("section", "nodes"),
        ),
        check_vma=False,
    )
```

```python
import jax
import jax.numpy as jnp
from jax import lax
from jax.experimental import pallas as pl
from jax.experimental.pallas import tpu as pltpu
from jax.sharding import PartitionSpec as P

HEADS = 4
REACH = 32
EPSILON = 1e-06
MASKED = -1e9
ABSENT = -2e38
TILE = 512
TOGETHER = 2
MESH = pl.DeviceIdType.MESH
F32, LOW = jnp.float32, jnp.bfloat16


def dot(a, b):
    return lax.dot_general(a, b, (((1,), (0,)), ((), ())), preferred_element_type=F32)


def dot_nt(a, b):
    return lax.dot_general(a, b, (((1,), (1,)), ((), ())), preferred_element_type=F32)


def dot_tn(a, b):
    return lax.dot_general(a, b, (((0,), (0,)), ((), ())), preferred_element_type=F32)


class Sizes:
    def __init__(self, inputs, neighbours, noise, w_up, shards):
        self.batches, self.rows, self.width = inputs.shape
        self.together = TOGETHER if self.batches % TOGETHER == 0 else 1
        self.turns = self.batches // self.together
        self.slots = neighbours.shape[1]
        self.meshes = noise.shape[1]
        self.hidden = w_up.shape[2]
        self.shards = shards
        self.ext = self.rows + 2 * REACH
        self.window = (self.ext // 128 + 1) * 128
        self.groups = self.hidden // TILE
        self.own = self.width // shards
        self.scatter = self.own % 16 == 0
        self.pieces = 2 * self.groups + 4
        self.lefts = 3 + self.groups
        self.rights = 2 + self.groups + 3
        self.rings = max(shards.bit_length() - 1, 1)

        self.bits = [1 << k for k in range(shards.bit_length() - 1)]

    def left(self, p):
        n = self.groups
        return jnp.minimum(p, n) + lax.div(p, 2 * n) + lax.div(p, 2 * n + 1)

    def right(self, p):
        return jnp.maximum(p - (self.groups - 1), 0)


def kernel_of(z):
    batches, rows, width, ext, window = z.batches, z.rows, z.width, z.ext, z.window
    groups, shards, own, many = z.groups, z.shards, z.own, z.together
    head = width // HEADS
    score_scale = head ** (-0.5)
    log2e = 1.4426950408889634
    npiece = z.pieces
    half = TILE // 2
    stages = len(z.bits)
    g_out, g_q, g_k = 1 + groups, 2 + groups, 3 + groups

    def position(owner):
        if not z.scatter:
            return owner
        place = 0
        for bit in z.bits:
            place = 2 * place + owner // bit % 2
        return place

    def kernel(
        inputs, cotangent, neighbours, mesh_ids, sigma,
        w_qkv, w_out, w_up, b_up, w_down, b_down, w_mod, b_mod,
        lo, ig, *rest,
    ):
        if z.scatter:
            o_piece, o_mod, o_line, left_t, right_t = rest[:5]
            rest = rest[5:]
        else:
            left_t, right_t, small_out, table_out = rest[:4]
            rest = rest[4:]
        (
            wq, wo, wu, wd, wm, xext, dybuf, sel, pick, cnt, few, bias, mod, emb,
            n1, n1s, ua, ia, qb, kvext, sbuf, af, ca, obs, n2s, ub, ib, tb, fp, hs,
            ob, dbuf, cds, dx1, dkv, hsend, hrecv, sm,
            lsem, hx_s, hx_r, hm_s, hm_r, fx_s, fx_r, bh_s, bh_r, bx_s, bx_r,
        ) = rest[:49]
        rest = rest[49:]
        if z.scatter:
            gives, gets, keeps = rest[:stages], rest[stages : 2 * stages], rest[2 * stages : 3 * stages - 1]
            acc, msend, mrecv, tot, p_s, p_r, m_s, m_r = rest[3 * stages - 1 :]

        sec = lax.axis_index("section")
        me = lax.axis_index("nodes")
        up = lax.rem(me + 1, shards)
        down = lax.rem(me + shards - 1, shards)
        other = 1 - sec
        def local(src, dst, k):
            return pltpu.make_async_copy(src, dst, lsem.at[k])

        loads = [
            local(w_mod.at[0], wm, 0),
            local(w_qkv.at[0], wq, 1),
            local(w_out.at[0], wo, 2),
            local(w_up.at[0], wu, 3),
            local(w_down.at[0], wd, 4),
        ]
        own_rows = pl.ds(REACH, rows)
        first_load = local(inputs, xext.at[:, own_rows, :], 5)
        last_load = local(cotangent, dybuf, 6)
        loads[0].start()

        @pl.when(sec == 0)
        def _():
            first_load.start()

        for copy in loads[1:]:
            copy.start()

        @pl.when(sec == 1)
        def _():
            last_load.start()

        def side(bit):
            return lax.rem(lax.div(me, bit), 2)

        def mate(bit):
            return me + bit - 2 * bit * side(bit)

        barrier = pltpu.get_barrier_semaphore()
        mates = [(sec, up), (sec, down), (other, me), (other, up), (other, down)]
        if z.scatter:
            mates += [(sec, mate(bit)) for bit in z.bits[1:]]
        for peer in mates:
            pl.semaphore_signal(barrier, inc=1, device_id=peer, device_id_type=MESH)
        pl.semaphore_wait(barrier, len(mates))

        def remote(src, dst, s_sem, r_sem, peer):
            return pltpu.make_async_remote_copy(
                src_ref=src, dst_ref=dst, send_sem=s_sem, recv_sem=r_sem, device_id=peer, device_id_type=MESH
            )

        low_rows, top_rows = pl.ds(0, REACH), pl.ds(REACH + rows, REACH)
        head_rows, tail_rows = pl.ds(REACH, REACH), pl.ds(rows, REACH)
        x_down = remote(inputs.at[:, pl.ds(0, REACH), :], xext.at[:, top_rows, :], hx_s.at[0], hx_r.at[0], (sec, down))
        x_up = remote(inputs.at[:, pl.ds(rows - REACH, REACH), :], xext.at[:, low_rows, :], hx_s.at[1], hx_r.at[1], (sec, up))

        @pl.when(sec == 0)
        def _():
            x_down.start()
            x_up.start()

        ids = jnp.broadcast_to(mesh_ids[...].astype(F32), (128, rows))
        sel[own_rows, :] = ids.T
        sample = lax.broadcasted_iota(jnp.int32, (16, rows), 0).astype(F32)
        pick[...] = jnp.where(ids[0:16] == sample, 1.0, 0.0).astype(LOW)
        m_down = remote(sel.at[head_rows, :], sel.at[top_rows, :], hm_s.at[0], hm_r.at[0], (sec, down))
        m_up = remote(sel.at[tail_rows, :], sel.at[low_rows, :], hm_s.at[1], hm_r.at[1], (sec, up))
        m_down.start()
        m_up.start()

        kvext[:, ext:window, :] = jnp.zeros((batches, window - ext, 2 * width), LOW)
        sm[...] = jnp.zeros(sm.shape, F32)

        slots = neighbours[...].astype(F32)
        slots = jnp.concatenate([slots, jnp.zeros((128 - z.slots, rows), F32)], axis=0).T
        slots = jnp.where(slots >= 0, slots - (me * rows - REACH).astype(F32), float(ext))
        column = lax.broadcasted_iota(jnp.int32, (rows, window), 1).astype(F32)
        counts = jnp.zeros((rows, window), F32)
        for n in range(z.slots):
            counts = counts + jnp.where(slots[:, n : n + 1] == column, 1.0, 0.0)
        cnt[...] = counts
        few[...] = counts.astype(LOW)
        bias[...] = jnp.where(counts > 0, jnp.where(column == ext, MASKED * log2e, 0.0), ABSENT)

        row_no = lax.broadcasted_iota(jnp.int32, (16, width // 2), 0)
        level = jnp.ones((16, width // 2), F32)
        for b in range(batches):
            for m in range(z.meshes):
                level = jnp.where(row_no == b * z.meshes + m, sigma[m, b], level)
        place = lax.broadcasted_iota(jnp.int32, (16, width // 2), 1).astype(F32)
        frequency = 3.0 * jnp.exp(-jnp.log(100.0) * place / (width // 2))
        angles = jnp.log(level) * frequency
        embedded = jnp.concatenate([jnp.sin(angles), jnp.cos(angles)], axis=1).astype(LOW)
        padded = jnp.concatenate([embedded.astype(F32), jnp.zeros((112, width), F32)], axis=0)
        emb[...] = padded.T
        loads[0].wait()
        for g in range(4):
            cols = pl.ds(g * width, width)
            table = dot(embedded, wm[:, cols]) + b_mod[:, cols] + (1.0 - g % 2)
            for b in range(batches):
                mod[b, 0 : z.meshes, cols] = table[b * z.meshes : (b + 1) * z.meshes]

        def mod_rows(b, part, ids_rows):
            cols = pl.ds(part * width, width)
            value = jnp.broadcast_to(mod[b, 0:1, cols], (ids_rows.shape[0], width))
            for m in range(1, z.meshes):
                value = jnp.where(ids_rows > m - 0.5, mod[b, m : m + 1, cols], value)
            return value

        def wide(ids_rows):
            return jnp.concatenate([ids_rows] * (width // 128), axis=1)

        def unit(x):
            centred = x - jnp.mean(x, axis=-1, keepdims=True)
            inv = lax.rsqrt(jnp.mean(centred * centred, axis=-1, keepdims=True) + EPSILON)
            return centred * inv, inv

        def span_of(start, size):
            if isinstance(start, int):
                return pl.ds(start, size)
            return pl.ds(pl.multiple_of(start, size), size)

        def batch_cols(b):
            return span_of(b * rows, rows)

        def turn_cols(t):
            return span_of(t * many * rows, many * rows)

        def turn_of(ref, t):
            return ref[pl.ds(t * many, many)].reshape(many * rows, ref.shape[2])

        span = own if z.scatter else 32

        def transposes(b, carry):
            for first, ref in ((groups, n2s), (groups + 1, obs), (groups + 2, n1s)):
                turned = ref[b].T
                for owner in range(TILE // span):
                    at = position(owner) * span
                    left_t[first, at : at + span, batch_cols(b)] = turned[owner * span : (owner + 1) * span]
            run = groups * span
            for g in range(groups):
                turned = hs[b, :, g * TILE : (g + 1) * TILE].T
                for k in range(TILE // span):
                    at = g * TILE + k * span
                    owner, part = at // run, at % run // span
                    to = position(owner) * span
                    left_t[part, to : to + span, batch_cols(b)] = turned[k * span : (k + 1) * span]
            return carry

        heads = [slice(h * head, (h + 1) * head) for h in range(HEADS)]
        heads_v = [slice(width + h * head, width + (h + 1) * head) for h in range(HEADS)]
        tiles = [slice(g * TILE, (g + 1) * TILE) for g in range(groups)]
        thirds = [slice(g * width, (g + 1) * width) for g in range(3)]

        def forward(b):
            ids_rows = wide(sel[0:ext, :])
            u, inv = unit(xext[b].astype(F32))
            normed = (u * mod_rows(b, 0, ids_rows) + mod_rows(b, 1, ids_rows)).astype(LOW)
            n1[...] = normed
            n1s[b] = normed[REACH : REACH + rows]
            ua[b] = u[REACH : REACH + rows]
            ia[b] = jnp.broadcast_to(inv[REACH : REACH + rows], (rows, 128))
            kvext[b, 0:ext, thirds[0]] = dot(n1[...], wq[:, thirds[1]]).astype(LOW)
            qb[b] = dot(n1s[b], wq[:, thirds[0]]).astype(LOW)
            for h in range(HEADS):
                sbuf[h] = dot_nt(qb[b, :, heads[h]], kvext[b, :, heads[h]]) * (score_scale * log2e) + bias[...]
            kvext[b, 0:ext, thirds[1]] = dot(n1[...], wq[:, thirds[2]]).astype(LOW)
            for h in range(HEADS):
                s = sbuf[h]
                e = jnp.exp2(s - jnp.max(s, axis=-1, keepdims=True))
                a = e * (1.0 / jnp.sum(e * cnt[...], axis=-1, keepdims=True))
                af[b, h] = a
                ca[b, h] = a.astype(LOW) * few[...]
            for h in range(HEADS):
                obs[b, :, heads[h]] = dot(ca[b, h], kvext[b, :, heads_v[h]]).astype(LOW)

            x1 = xext[b, own_rows, :].astype(F32) + dot(obs[b], wo[...])
            u, inv = unit(x1)
            ub[b] = u
            ib[b] = jnp.broadcast_to(inv, (rows, 128))
            ids_rows = wide(sel[own_rows, :])
            n2s[b] = (u * mod_rows(b, 2, ids_rows) + mod_rows(b, 3, ids_rows)).astype(LOW)
            tb[...] = x1 + b_down[...]
            for gs in tiles:
                gate = dot(n2s[b], wu[:, gs]) + b_up[:, gs]
                s = 0.5 + 0.5 * jnp.tanh(0.5 * gate)
                hid = gate * s
                fp[b, :, gs] = (s + hid * (1.0 - s)).astype(LOW)
                hid = hid.astype(LOW)
                hs[b, :, gs] = hid
                tb[...] += dot(hid, wd[gs, :])
            lo[0, b] = tb[...].astype(LOW)

        def relay(b):
            return [
                remote(lo.at[0, b], xext.at[b, own_rows, :], fx_s.at[b, 0], fx_r.at[b, 0], (other, me)),
                remote(lo.at[0, b, pl.ds(0, REACH), :], xext.at[b, top_rows, :], fx_s.at[b, 1], fx_r.at[b, 1], (other, down)),
                remote(lo.at[0, b, pl.ds(rows - REACH, REACH), :], xext.at[b, low_rows, :], fx_s.at[b, 2], fx_r.at[b, 2], (other, up)),
            ]

        def norm_back(d, u, inv, scale):
            scaled = d * scale
            return inv * (
                scaled
                - jnp.mean(scaled, axis=-1, keepdims=True)
                - u * jnp.mean(scaled * u, axis=-1, keepdims=True)
            )

        def mod_sums(b, part, d, u):
            for k, value in enumerate((d * u, d)):
                total = dot(pick[...], value.astype(LOW))
                sm[b, 0 : z.meshes, (part + k) * width : (part + k + 1) * width] = total[0 : z.meshes]

        def halos(b):
            return [
                remote(hsend.at[b, 0], hrecv.at[b, 1], bh_s.at[b, 0], bh_r.at[b, 0], (sec, down)),
                remote(hsend.at[b, 1], hrecv.at[b, 0], bh_s.at[b, 1], bh_r.at[b, 1], (sec, up)),
            ]

        def given(b):
            at = batch_cols(b)
            dr = dybuf[b]
            right_t[0, at, :] = dr
            sm[b, 7:8, 0:width] = jnp.sum(dr.astype(F32), axis=0, keepdims=True)
            for g in range(groups):
                right_t[1 + g, at, :] = dot_nt(dr, wd[g * TILE : (g + 1) * TILE, :]).astype(LOW)

        def back_ffn(t):
            at = turn_cols(t)
            dn = jnp.zeros((many * rows, width), F32)
            for g in range(groups):
                gs = slice(g * TILE, (g + 1) * TILE)
                dg = right_t[1 + g, at, :].astype(F32) * turn_of(fp, t)[:, gs].astype(F32)
                sm[t * many, 6:7, gs] = jnp.sum(dg, axis=0, keepdims=True)
                dg = dg.astype(LOW)
                right_t[1 + g, at, :] = dg
                dn = dn + dot_nt(dg, wu[:, gs])
            dbuf[...] = dn

        def back_middle(t):
            at = turn_cols(t)
            ids_rows = wide(sel[own_rows, :])
            for i in range(many):
                b = t * many + i
                d = dbuf[i * rows : (i + 1) * rows]
                u = ub[b]
                grad = dybuf[b].astype(F32) + norm_back(d, u, ib[b][:, 0:1], mod_rows(b, 2, ids_rows))
                mod_sums(b, 2, d, u)
                dx1[i] = grad
                right_t[g_out, batch_cols(b), :] = grad.astype(LOW)
            ob[...] = dot_nt(right_t[g_out, at, :], wo[...]).astype(LOW)

        def back_attention(t):
            units = [(i, h) for i in range(many) for h in range(HEADS)]
            here = [slice(i * rows, (i + 1) * rows) for i in range(many)]
            for i, h in units:
                sbuf[i * HEADS + h] = dot_nt(ob[here[i], heads[h]], kvext[t * many + i, :, heads_v[h]])
            for i, h in units:
                b, k = t * many + i, i * HEADS + h
                a, da = af[b, h], sbuf[k]
                ds = a * (da - jnp.sum(a * cnt[...] * da, axis=-1, keepdims=True))
                cds[k] = ds.astype(LOW) * few[...]
            for i in range(many):
                b = t * many + i
                for h in range(HEADS):
                    dk = dot_tn(cds[i * HEADS + h], qb[b, :, heads[h]]) * score_scale
                    dv = dot_tn(ca[b, h], ob[here[i], heads[h]])
                    for part, cols in ((dk, heads[h]), (dv, heads_v[h])):
                        hsend[b, 0, :, cols] = part[0:REACH].astype(LOW)
                        dkv[i, :, cols] = part[REACH : REACH + rows]
                        hsend[b, 1, :, cols] = part[REACH + rows : ext].astype(LOW)
                for copy in halos(b):
                    copy.start()
            for i, h in units:
                b = t * many + i
                value = dot(cds[i * HEADS + h], kvext[b, :, heads[h]]) * score_scale
                right_t[g_q, batch_cols(b), heads[h]] = value.astype(LOW)

        def back_second(t):
            at = turn_cols(t)
            ids_rows = wide(sel[own_rows, :])
            edge = rows - REACH
            dbuf[...] = dot_nt(right_t[g_q, at, :], wq[:, 0:width])
            for i in range(many):
                b = t * many + i
                for copy in halos(b):
                    copy.wait_recv()
                dkv[i, 0:REACH, :] += hrecv[b, 0].astype(F32)
                dkv[i, edge:rows, :] += hrecv[b, 1].astype(F32)
                d = dbuf[i * rows : (i + 1) * rows]
                for g in range(2):
                    part = dkv[i, :, g * width : (g + 1) * width].astype(LOW)
                    right_t[g_k + g, batch_cols(b), :] = part
                    d = d + dot_nt(part, wq[:, (g + 1) * width : (g + 2) * width])
                u = ua[b]
                grad = dx1[i] + norm_back(d, u, ia[b][:, 0:1], mod_rows(b, 0, ids_rows))
                ig[0, b] = grad.astype(LOW)

                @pl.when(sec == 1)
                def _(b=b):
                    relay_back(b).start()

                mod_sums(b, 0, d, u)

        def relay_back(b):
            return remote(ig.at[0, b], dybuf.at[b], bx_s.at[b], bx_r.at[b], (other, me))

        for copy in loads[1:]:
            copy.wait()
        for copy in (m_down, m_up):
            copy.wait()

        @pl.when(sec == 0)
        def _():
            first_load.wait()
            x_down.wait()
            x_up.wait()

        @pl.when(sec == 1)
        def _():
            last_load.wait()

            @pl.loop(0, batches)
            def _(b):
                given(b)

        @pl.loop(0, batches)
        def _(b):
            @pl.when(sec == 1)
            def _():
                for copy in relay(b):
                    copy.wait_recv()

            forward(b)

            @pl.when(sec == 0)
            def _():
                for copy in relay(b):
                    copy.start()

        @pl.when(sec == 0)
        def _():
            lax.fori_loop(0, batches, transposes, 0)

        def rows_of(c, size):
            return pl.ds(pl.multiple_of(c * size, size), size)

        def turned(p):
            return lax.rem(p, 2) * side(1) if stages > 2 else 0 * p

        def bit_of(p, k):
            bits = list(z.bits)
            if stages > 2:
                bits[1], bits[2] = bits[2], bits[1]
            return z.bits[k] + (bits[k] - z.bits[k]) * turned(p)

        def piece_copy(p, k):
            return remote(gives[k].at[p], gets[k].at[p], p_s.at[p, k], p_r.at[p, k], (sec, mate(bit_of(p, k))))

        def piece_start(p):
            left = z.left(p)
            sides = [left_t[left, rows_of(c, half), :] for c in (1 - side(1), side(1))]
            value = dot(jnp.concatenate(sides, axis=0), right_t[z.right(p)])
            gives[0][p] = value[0:half].astype(LOW)
            piece_copy(p, 0).start()
            acc[lax.rem(p, 2)] = value[half : 2 * half]

        def piece_first(p):
            piece_copy(p, 0).wait_recv()
            here = side(bit_of(p, 1))
            run = half // 4
            for s, to in ((1 - here, gives[1]), (here, keeps[0])):
                for j in range(2):
                    at = rows_of((1 - turned(p)) * (2 * s + j) + turned(p) * (2 * j + s), run)
                    value = acc[lax.rem(p, 2), at, :] + gets[0][p, at, :].astype(F32)
                    to[p, j * run : (j + 1) * run, :] = value.astype(to.dtype)
                if to is gives[1]:
                    piece_copy(p, 1).start()

        def piece_step(p, k):
            size = half >> k
            piece_copy(p, k).wait_recv()
            if k == stages - 1:
                o_piece[p] = keeps[k - 1][p] + gets[k][p].astype(F32)
                return
            here = side(bit_of(p, k + 1))
            for to, c in ((gives[k + 1], 1 - here), (keeps[k], here)):
                at = rows_of(c, size // 2)
                to[p] = (keeps[k - 1][p, at, :] + gets[k][p, at, :].astype(F32)).astype(to.dtype)
                if to is gives[k + 1]:
                    piece_copy(p, k + 1).start()

        def only_first(body):
            if z.scatter:
                pl.when(sec == 0)(body)

        for t in reversed(range(z.turns)):

            @pl.when(sec == 0)
            def _(t=t):
                for i in range(many):
                    relay_back(t * many + i).wait_recv()
                    given(t * many + i)

            back_ffn(t)
            back_middle(t)
            back_attention(t)
            if t == 0:

                @only_first
                def _():
                    @pl.loop(0, groups)
                    def _(p):
                        piece_start(p)

                        @pl.when(p > 0)
                        def _():
                            piece_first(p - 1)

            back_second(t)

        @pl.when(sec == 1)
        def _():
            lax.fori_loop(0, batches, transposes, 0)

        lines = [sm[b, m : m + 1, :] for b in range(batches) for m in range(z.meshes)]
        for line in (6, 7):
            lines.append(sum(sm[b, line : line + 1, :] for b in range(batches)))
        lines.append(jnp.zeros((16 - len(lines), sm.shape[2]), F32))
        small = jnp.concatenate(lines, axis=0)

        def finish():
            @pl.loop(0, batches)
            def _(b):
                @pl.when(sec == 0)
                def _():
                    for copy in relay(b):
                        copy.wait_send()

                @pl.when(sec == 1)
                def _():
                    relay_back(b).wait_send()

                for copy in halos(b):
                    copy.wait_send()

        if not z.scatter:
            small_out[...] = small
            table_out[...] = emb[...]
            finish()
            return

        def ring_copy(k):
            return remote(msend.at[k], mrecv.at[k], m_s.at[k], m_r.at[k], (sec, mate(1 << k)))

        def ring_start(k, value):
            msend[k] = value.astype(LOW)
            ring_copy(k).start()

        def ring_end(k):
            ring_copy(k).wait_recv()
            value = msend[k].astype(F32) + mrecv[k].astype(F32)
            if k + 1 < z.rings:
                ring_start(k + 1, value)
            else:
                tot[...] = value

        ring_start(0, small)

        lags = [0, 1] + [4 + 4 * k for k in range(stages - 1)]
        begun = (1 - sec) * groups

        @pl.loop(0, npiece + lags[-1])
        def _(p):
            @pl.when((p >= begun) & (p < npiece))
            def _():
                piece_start(p)

            @pl.when((p >= begun + sec) & (p >= 1) & (p < npiece + 1))
            def _():
                piece_first(p - 1)

            for k in range(1, stages):
                lag = lags[k + 1]

                @pl.when((p >= lag) & (p < npiece + lag))
                def _(k=k, lag=lag):
                    piece_step(p - lag, k)

            for k in range(z.rings):

                @pl.when(p == 6 + 3 * k)
                def _(k=k):
                    ring_end(k)

            @pl.when(p == 4 + 3 * z.rings)
            def _():
                count = batches * z.meshes
                table = emb[pl.ds(pl.multiple_of(me * own, own), own), :]
                grad = jnp.zeros((own, 4 * width), F32)
                for k in range(count):
                    grad = grad + table[:, k : k + 1] * tot[k : k + 1, :]
                o_mod[0] = grad
                cols = 4 * width // shards
                mine = tot[:, pl.ds(pl.multiple_of(me * cols, cols), cols)]
                o_line[0:1, :] = jnp.sum(mine[0:count], axis=0, keepdims=True)
                o_line[1:2, :] = mine[count : count + 1]
                ratio = 128 // own
                line = tot[:, pl.ds(pl.multiple_of(me // ratio * 128, 128), 128)][count + 1 : count + 2]
                value = line
                for k in range(1, ratio):
                    rolled = jnp.concatenate([line[:, k * own :], line[:, : k * own]], axis=1)
                    value = jnp.where(me % ratio == k, rolled, value)
                o_line[2:3, :] = value

        finish()

        @pl.loop(0, npiece)
        def _(p):
            for k in range(stages):
                piece_copy(p, k).wait_send()

        for k in range(z.rings):
            ring_copy(k).wait_send()

    return kernel


def layout_of(z):
    own, groups = z.own, z.groups

    def kernel(
        lo, ig, piece, mod, line,
        o_lo, o_ig, o_qkv, o_out, o_up, o_upb, o_down, o_downb, o_mod, o_modb,
        sems,
    ):
        targets = [o_down.at[0, pl.ds(q * own, own), :] for q in range(groups)]
        targets += [o_up.at[0, :, pl.ds(q * TILE, TILE)] for q in range(groups)]
        targets += [o_out.at[0]] + [o_qkv.at[0, :, pl.ds(q * TILE, TILE)] for q in range(3)]
        moves = [(lo, o_lo), (ig, o_ig), (mod, o_mod)]
        moves += [(piece.at[k], target) for k, target in enumerate(targets)]
        copies = [pltpu.make_async_copy(a, b, sems.at[k]) for k, (a, b) in enumerate(moves)]
        for copy in copies:
            copy.start()
        o_modb[...] = line[0:1, :]
        o_upb[...] = line[1:2, :]
        o_downb[...] = line[2:3, 0:own]
        for copy in copies:
            copy.wait()

    return kernel


def body(
    inputs,
    cotangent,
    neighbours,
    mesh_ids,
    noise_sigma,
    w_qkv,
    w_out,
    w_up,
    b_up,
    w_down,
    b_down,
    w_mod,
    b_mod,
):
    shards = lax.axis_size("nodes")
    z = Sizes(inputs, neighbours, noise_sigma, w_up, shards)
    batches, rows, width, hidden, many = z.batches, z.rows, z.width, z.hidden, z.together
    own, npiece = z.own, z.pieces
    shape = jax.ShapeDtypeStruct
    stack = shape((1, batches, rows, width), LOW)
    outs = [stack, stack]
    sides = [(z.lefts, TILE, batches * rows), (z.rights, batches * rows, TILE)]
    if z.scatter:
        outs = [pltpu.VMEM(stack.shape, LOW)] * 2
        outs += [pltpu.VMEM((npiece, own, TILE), F32), pltpu.VMEM((1, own, 4 * width), F32), pltpu.VMEM((8, 128), F32)]
        scratch = [pltpu.VMEM(side, LOW) for side in sides]
    else:
        outs += [shape(side, LOW) for side in sides] + [shape((16, hidden), F32), shape((width, 128), F32)]
        scratch = []
    dma = pltpu.SemaphoreType.DMA
    scratch += [
        pltpu.VMEM((width, 3 * width), LOW),
        pltpu.VMEM((width, width), LOW),
        pltpu.VMEM((width, hidden), LOW),
        pltpu.VMEM((hidden, width), LOW),
        pltpu.VMEM((width, 4 * width), LOW),
        pltpu.VMEM((batches, z.ext, width), LOW),
        pltpu.VMEM((batches, rows, width), LOW),
        pltpu.VMEM((z.ext, 128), F32),
        pltpu.VMEM((16, rows), LOW),
        pltpu.VMEM((rows, z.window), F32),
        pltpu.VMEM((rows, z.window), LOW),
        pltpu.VMEM((rows, z.window), F32),
        pltpu.VMEM((batches, 8, 4 * width), F32),
        pltpu.VMEM((width, 128), F32),
        pltpu.VMEM((z.ext, width), LOW),
        pltpu.VMEM((batches, rows, width), LOW),
        pltpu.VMEM((batches, rows, width), F32),
        pltpu.VMEM((batches, rows, 128), F32),
        pltpu.VMEM((batches, rows, width), LOW),
        pltpu.VMEM((batches, z.window, 2 * width), LOW),
        pltpu.VMEM((many * HEADS, rows, z.window), F32),
        pltpu.VMEM((batches, HEADS, rows, z.window), F32),
        pltpu.VMEM((batches, HEADS, rows, z.window), LOW),
        pltpu.VMEM((batches, rows, width), LOW),
        pltpu.VMEM((batches, rows, width), LOW),
        pltpu.VMEM((batches, rows, width), F32),
        pltpu.VMEM((batches, rows, 128), F32),
        pltpu.VMEM((rows, width), F32),
        pltpu.VMEM((batches, rows, hidden), LOW),
        pltpu.VMEM((batches, rows, hidden), LOW),
        pltpu.VMEM((many * rows, width), LOW),
        pltpu.VMEM((many * rows, width), F32),
        pltpu.VMEM((many * HEADS, rows, z.window), LOW),
        pltpu.VMEM((many, rows, width), F32),
        pltpu.VMEM((many, rows, 2 * width), F32),
        pltpu.VMEM((batches, 2, REACH, 2 * width), LOW),
        pltpu.VMEM((batches, 2, REACH, 2 * width), LOW),
        pltpu.VMEM((batches, 8, hidden), F32),
        dma((7,)),
        dma((2,)),
        dma((2,)),
        dma((2,)),
        dma((2,)),
        dma((batches, 3)),
        dma((batches, 3)),
        dma((batches, 2)),
        dma((batches, 2)),
        dma((batches,)),
        dma((batches,)),
    ]
    if z.scatter:
        stages = len(z.bits)
        sizes = [TILE >> (k + 1) for k in range(stages)]
        scratch += [pltpu.VMEM((npiece, size, TILE), LOW) for size in sizes + sizes]
        scratch += [pltpu.VMEM((npiece, size, TILE), F32) for size in sizes[1:]]
        scratch += [
            pltpu.VMEM((2, sizes[0], TILE), F32),
            pltpu.VMEM((z.rings, 16, hidden), LOW),
            pltpu.VMEM((z.rings, 16, hidden), LOW),
            pltpu.VMEM((16, hidden), F32),
            dma((npiece, stages)),
            dma((npiece, stages)),
            dma((z.rings,)),
            dma((z.rings,)),
        ]
    hbm = pl.BlockSpec(memory_space=pl.ANY)
    vmem = pl.BlockSpec(memory_space=pltpu.VMEM)
    smem = pl.BlockSpec(memory_space=pltpu.SMEM)
    got = pl.pallas_call(
        kernel_of(z),
        out_shape=outs,
        in_specs=[hbm, hbm, vmem, vmem, smem, hbm, hbm, hbm, vmem, hbm, vmem, hbm, vmem],
        out_specs=[vmem] * len(outs),
        scratch_shapes=scratch,
        compiler_params=pltpu.CompilerParams(
            collective_id=0, has_side_effects=True, vmem_limit_bytes=61 * 2**20
        ),
    )(
        inputs,
        cotangent,
        neighbours.T,
        mesh_ids.reshape(1, rows),
        noise_sigma.T,
        w_qkv,
        w_out,
        w_up,
        b_up,
        w_down,
        b_down,
        w_mod,
        b_mod,
    )
    if z.scatter:
        lo, ig, piece, mod, line = got
        return tuple(
            pl.pallas_call(
                layout_of(z),
                out_shape=[
                    stack,
                    stack,
                    shape((1, own, 3 * width), F32),
                    shape((1, own, width), F32),
                    shape((1, own, hidden), F32),
                    shape((1, hidden // shards), F32),
                    shape((1, hidden // shards, width), F32),
                    shape((1, own), F32),
                    shape((1, own, 4 * width), F32),
                    shape((1, 4 * width // shards), F32),
                ],
                in_specs=[vmem] * 5,
                out_specs=[hbm, hbm, hbm, hbm, hbm, vmem, hbm, vmem, hbm, vmem],
                scratch_shapes=[dma((npiece + 3,))],
                compiler_params=pltpu.CompilerParams(vmem_limit_bytes=2 * 2**20),
            )(lo, ig, piece, mod, line)
        )
    lo, ig, left_t, right_t, small, table = got
    groups = z.groups

    def summed(value):
        return lax.psum_scatter(value, "nodes", scatter_dimension=0, tiled=True)

    def wide_sum(left, first, last):
        return summed(jnp.concatenate([dot(left_t[left], right_t[r]) for r in range(first, last)], axis=1))[None]

    down = [dot(left_t[q], right_t[0]).reshape(TILE // 32, 32, TILE) for q in range(groups)]
    down = jnp.stack(down, axis=1)
    count = batches * z.meshes
    small = lax.psum(small, "nodes")
    me = lax.axis_index("nodes")
    mod = jnp.dot(table[:, :count], small[:count], precision=lax.Precision.HIGHEST)

    def mine(value):
        size = value.shape[0] // shards
        return lax.dynamic_slice_in_dim(value, me * size, size, axis=0)[None]

    return (
        lo,
        ig,
        wide_sum(groups + 2, 2 + groups, 5 + groups),
        wide_sum(groups + 1, 1 + groups, 2 + groups),
        wide_sum(groups, 1, 1 + groups),
        mine(small[count]),
        summed(down.reshape(hidden, width))[None],
        mine(small[count + 1, :width]),
        mine(mod),
        mine(jnp.sum(small[:count], axis=0)),
    )


def solution(mesh):
    return jax.shard_map(
        body,
        mesh=mesh,
        in_specs=(
            P(None, "nodes", None),
            P(None, "nodes", None),
            P("nodes", None),
            P("nodes"),
            P(),
            P("section", None, None),
            P("section", None, None),
            P("section", None, None),
            P("section", None),
            P("section", None, None),
            P("section", None),
            P("section", None, None),
            P("section", None),
        ),
        out_specs=(
            P("section", None, "nodes", None),
            P("section", None, "nodes", None),
            P("section", "nodes", None),
            P("section", "nodes", None),
            P("section", "nodes", None),
            P("section", "nodes"),
            P("section", "nodes", None),
            P("section", "nodes"),
            P("section", "nodes", None),
            P("section", "nodes"),
        ),
        check_vma=False,
    )
```

```python
import jax
import jax.numpy as jnp
from jax import lax
from jax.experimental import pallas as pl
from jax.experimental.pallas import tpu as pltpu
from jax.sharding import PartitionSpec as P

HEADS = 4
REACH = 32
EPSILON = 1e-06
MASKED = -1e9
ABSENT = -2e38
TILE = 512
TOGETHER = 2
MESH = pl.DeviceIdType.MESH
F32, LOW = jnp.float32, jnp.bfloat16


def dot(a, b):
    return lax.dot_general(a, b, (((1,), (0,)), ((), ())), preferred_element_type=F32)


def dot_nt(a, b):
    return lax.dot_general(a, b, (((1,), (1,)), ((), ())), preferred_element_type=F32)


def dot_tn(a, b):
    return lax.dot_general(a, b, (((0,), (0,)), ((), ())), preferred_element_type=F32)


class Sizes:
    def __init__(self, inputs, neighbours, noise, w_up, shards):
        self.batches, self.rows, self.width = inputs.shape
        self.together = TOGETHER if self.batches % TOGETHER == 0 else 1
        self.turns = self.batches // self.together
        self.slots = neighbours.shape[1]
        self.meshes = noise.shape[1]
        self.hidden = w_up.shape[2]
        self.shards = shards
        self.ext = self.rows + 2 * REACH
        self.window = (self.ext // 128 + 1) * 128
        self.groups = self.hidden // TILE
        self.own = self.width // shards
        self.scatter = self.own % 16 == 0
        self.pieces = 2 * self.groups + 4
        self.lefts = 3 + self.groups
        self.rights = 2 + self.groups + 3
        self.rings = max(shards.bit_length() - 1, 1)

        self.bits = [1 << k for k in range(shards.bit_length() - 1)]

    def left(self, p):
        n = self.groups
        return jnp.minimum(p, n) + lax.div(p, 2 * n) + lax.div(p, 2 * n + 1)

    def right(self, p):
        return jnp.maximum(p - (self.groups - 1), 0)


def kernel_of(z):
    batches, rows, width, ext, window = z.batches, z.rows, z.width, z.ext, z.window
    groups, shards, own, many = z.groups, z.shards, z.own, z.together
    head = width // HEADS
    score_scale = head ** (-0.5)
    log2e = 1.4426950408889634
    npiece = z.pieces
    half = TILE // 2
    stages = len(z.bits)
    g_out, g_q, g_k = 1 + groups, 2 + groups, 3 + groups

    def position(owner):
        if not z.scatter:
            return owner
        place = 0
        for bit in z.bits:
            place = 2 * place + owner // bit % 2
        return place

    def kernel(
        inputs, cotangent, neighbours, mesh_ids, sigma,
        w_qkv, w_out, w_up, b_up, w_down, b_down, w_mod, b_mod,
        lo, ig, *rest,
    ):
        if z.scatter:
            o_piece, o_mod, o_line, left_t, right_t = rest[:5]
            rest = rest[5:]
        else:
            left_t, right_t, small_out, table_out = rest[:4]
            rest = rest[4:]
        (
            wq, wo, wu, wd, wm, xext, dybuf, sel, pick, cnt, few, bias, mod, emb,
            n1, n1s, ua, ia, qb, kvext, sbuf, af, ca, obs, n2s, ub, ib, tb, fp, hs,
            ob, dbuf, cds, dx1, dkv, hsend, hrecv, sm,
            lsem, hx_s, hx_r, hm_s, hm_r, fx_s, fx_r, bh_s, bh_r, bx_s, bx_r,
        ) = rest[:49]
        rest = rest[49:]
        if z.scatter:
            gives, gets, keeps = rest[:stages], rest[stages : 2 * stages], rest[2 * stages : 3 * stages - 1]
            acc, msend, mrecv, tot, p_s, p_r, m_s, m_r = rest[3 * stages - 1 :]

        sec = lax.axis_index("section")
        me = lax.axis_index("nodes")
        up = lax.rem(me + 1, shards)
        down = lax.rem(me + shards - 1, shards)
        other = 1 - sec
        def local(src, dst, k):
            return pltpu.make_async_copy(src, dst, lsem.at[k])

        loads = [
            local(w_mod.at[0], wm, 0),
            local(w_qkv.at[0], wq, 1),
            local(w_out.at[0], wo, 2),
            local(w_up.at[0], wu, 3),
            local(w_down.at[0], wd, 4),
        ]
        own_rows = pl.ds(REACH, rows)
        first_load = local(inputs, xext.at[:, own_rows, :], 5)
        last_load = local(cotangent, dybuf, 6)
        loads[0].start()

        @pl.when(sec == 0)
        def _():
            first_load.start()

        for copy in loads[1:]:
            copy.start()

        @pl.when(sec == 1)
        def _():
            last_load.start()

        def side(bit):
            return lax.rem(lax.div(me, bit), 2)

        def mate(bit):
            return me + bit - 2 * bit * side(bit)

        barrier = pltpu.get_barrier_semaphore()
        mates = [(sec, up), (sec, down), (other, me), (other, up), (other, down)]
        if z.scatter:
            mates += [(sec, mate(bit)) for bit in z.bits[1:]]
        for peer in mates:
            pl.semaphore_signal(barrier, inc=1, device_id=peer, device_id_type=MESH)
        pl.semaphore_wait(barrier, len(mates))

        def remote(src, dst, s_sem, r_sem, peer):
            return pltpu.make_async_remote_copy(
                src_ref=src, dst_ref=dst, send_sem=s_sem, recv_sem=r_sem, device_id=peer, device_id_type=MESH
            )

        low_rows, top_rows = pl.ds(0, REACH), pl.ds(REACH + rows, REACH)
        head_rows, tail_rows = pl.ds(REACH, REACH), pl.ds(rows, REACH)
        x_down = remote(inputs.at[:, pl.ds(0, REACH), :], xext.at[:, top_rows, :], hx_s.at[0], hx_r.at[0], (sec, down))
        x_up = remote(inputs.at[:, pl.ds(rows - REACH, REACH), :], xext.at[:, low_rows, :], hx_s.at[1], hx_r.at[1], (sec, up))

        @pl.when(sec == 0)
        def _():
            x_down.start()
            x_up.start()

        ids = jnp.broadcast_to(mesh_ids[...].astype(F32), (128, rows))
        sel[own_rows, :] = ids.T
        sample = lax.broadcasted_iota(jnp.int32, (16, rows), 0).astype(F32)
        pick[...] = jnp.where(ids[0:16] == sample, 1.0, 0.0).astype(LOW)
        m_down = remote(sel.at[head_rows, :], sel.at[top_rows, :], hm_s.at[0], hm_r.at[0], (sec, down))
        m_up = remote(sel.at[tail_rows, :], sel.at[low_rows, :], hm_s.at[1], hm_r.at[1], (sec, up))
        m_down.start()
        m_up.start()

        kvext[:, ext:window, :] = jnp.zeros((batches, window - ext, 2 * width), LOW)
        sm[...] = jnp.zeros(sm.shape, F32)

        slots = neighbours[...].astype(F32)
        slots = jnp.concatenate([slots, jnp.zeros((128 - z.slots, rows), F32)], axis=0).T
        slots = jnp.where(slots >= 0, slots - (me * rows - REACH).astype(F32), float(ext))
        column = lax.broadcasted_iota(jnp.int32, (rows, window), 1).astype(F32)
        counts = jnp.zeros((rows, window), F32)
        for n in range(z.slots):
            counts = counts + jnp.where(slots[:, n : n + 1] == column, 1.0, 0.0)
        cnt[...] = counts
        few[...] = counts.astype(LOW)
        bias[...] = jnp.where(counts > 0, jnp.where(column == ext, MASKED * log2e, 0.0), ABSENT)

        row_no = lax.broadcasted_iota(jnp.int32, (16, width // 2), 0)
        level = jnp.ones((16, width // 2), F32)
        for b in range(batches):
            for m in range(z.meshes):
                level = jnp.where(row_no == b * z.meshes + m, sigma[m, b], level)
        place = lax.broadcasted_iota(jnp.int32, (16, width // 2), 1).astype(F32)
        frequency = 3.0 * jnp.exp(-jnp.log(100.0) * place / (width // 2))
        angles = jnp.log(level) * frequency
        embedded = jnp.concatenate([jnp.sin(angles), jnp.cos(angles)], axis=1).astype(LOW)
        padded = jnp.concatenate([embedded.astype(F32), jnp.zeros((112, width), F32)], axis=0)
        emb[...] = padded.T
        loads[0].wait()
        for g in range(4):
            cols = pl.ds(g * width, width)
            table = dot(embedded, wm[:, cols]) + b_mod[:, cols] + (1.0 - g % 2)
            for b in range(batches):
                mod[b, 0 : z.meshes, cols] = table[b * z.meshes : (b + 1) * z.meshes]

        def mod_rows(b, part, ids_rows):
            cols = pl.ds(part * width, width)
            value = jnp.broadcast_to(mod[b, 0:1, cols], (ids_rows.shape[0], width))
            for m in range(1, z.meshes):
                value = jnp.where(ids_rows > m - 0.5, mod[b, m : m + 1, cols], value)
            return value

        def wide(ids_rows):
            return jnp.concatenate([ids_rows] * (width // 128), axis=1)

        def unit(x):
            centred = x - jnp.mean(x, axis=-1, keepdims=True)
            inv = lax.rsqrt(jnp.mean(centred * centred, axis=-1, keepdims=True) + EPSILON)
            return centred * inv, inv

        def span_of(start, size):
            if isinstance(start, int):
                return pl.ds(start, size)
            return pl.ds(pl.multiple_of(start, size), size)

        def batch_cols(b):
            return span_of(b * rows, rows)

        def turn_cols(t):
            return span_of(t * many * rows, many * rows)

        def turn_of(ref, t):
            return ref[pl.ds(t * many, many)].reshape(many * rows, ref.shape[2])

        span = own if z.scatter else 32

        def transposes(b, carry):
            for first, ref in ((groups, n2s), (groups + 1, obs), (groups + 2, n1s)):
                turned = ref[b].T
                for owner in range(TILE // span):
                    at = position(owner) * span
                    left_t[first, at : at + span, batch_cols(b)] = turned[owner * span : (owner + 1) * span]
            run = groups * span
            for g in range(groups):
                turned = hs[b, :, g * TILE : (g + 1) * TILE].T
                for k in range(TILE // span):
                    at = g * TILE + k * span
                    owner, part = at // run, at % run // span
                    to = position(owner) * span
                    left_t[part, to : to + span, batch_cols(b)] = turned[k * span : (k + 1) * span]
            return carry

        heads = [slice(h * head, (h + 1) * head) for h in range(HEADS)]
        heads_v = [slice(width + h * head, width + (h + 1) * head) for h in range(HEADS)]
        tiles = [slice(g * TILE, (g + 1) * TILE) for g in range(groups)]
        thirds = [slice(g * width, (g + 1) * width) for g in range(3)]

        def forward(b):
            ids_rows = wide(sel[0:ext, :])
            u, inv = unit(xext[b].astype(F32))
            normed = (u * mod_rows(b, 0, ids_rows) + mod_rows(b, 1, ids_rows)).astype(LOW)
            n1[...] = normed
            n1s[b] = normed[REACH : REACH + rows]
            ua[b] = u[REACH : REACH + rows]
            ia[b] = jnp.broadcast_to(inv[REACH : REACH + rows], (rows, 128))
            kvext[b, 0:ext, thirds[0]] = dot(n1[...], wq[:, thirds[1]]).astype(LOW)
            qb[b] = dot(n1s[b], wq[:, thirds[0]]).astype(LOW)
            for h in range(HEADS):
                sbuf[h] = dot_nt(qb[b, :, heads[h]], kvext[b, :, heads[h]]) * (score_scale * log2e) + bias[...]
            kvext[b, 0:ext, thirds[1]] = dot(n1[...], wq[:, thirds[2]]).astype(LOW)
            for h in range(HEADS):
                s = sbuf[h]
                e = jnp.exp2(s - jnp.max(s, axis=-1, keepdims=True))
                a = e * (1.0 / jnp.sum(e * cnt[...], axis=-1, keepdims=True))
                af[b, h] = a
                ca[b, h] = a.astype(LOW) * few[...]
            for h in range(HEADS):
                obs[b, :, heads[h]] = dot(ca[b, h], kvext[b, :, heads_v[h]]).astype(LOW)

            x1 = xext[b, own_rows, :].astype(F32) + dot(obs[b], wo[...])
            u, inv = unit(x1)
            ub[b] = u
            ib[b] = jnp.broadcast_to(inv, (rows, 128))
            ids_rows = wide(sel[own_rows, :])
            n2s[b] = (u * mod_rows(b, 2, ids_rows) + mod_rows(b, 3, ids_rows)).astype(LOW)
            tb[...] = x1 + b_down[...]
            for gs in tiles:
                gate = dot(n2s[b], wu[:, gs]) + b_up[:, gs]
                s = 0.5 + 0.5 * jnp.tanh(0.5 * gate)
                hid = gate * s
                fp[b, :, gs] = (s + hid * (1.0 - s)).astype(LOW)
                hid = hid.astype(LOW)
                hs[b, :, gs] = hid
                tb[...] += dot(hid, wd[gs, :])
            lo[0, b] = tb[...].astype(LOW)

        def relay(b):
            return [
                remote(lo.at[0, b], xext.at[b, own_rows, :], fx_s.at[b, 0], fx_r.at[b, 0], (other, me)),
                remote(lo.at[0, b, pl.ds(0, REACH), :], xext.at[b, top_rows, :], fx_s.at[b, 1], fx_r.at[b, 1], (other, down)),
                remote(lo.at[0, b, pl.ds(rows - REACH, REACH), :], xext.at[b, low_rows, :], fx_s.at[b, 2], fx_r.at[b, 2], (other, up)),
            ]

        def norm_back(d, u, inv, scale):
            scaled = d * scale
            return inv * (
                scaled
                - jnp.mean(scaled, axis=-1, keepdims=True)
                - u * jnp.mean(scaled * u, axis=-1, keepdims=True)
            )

        def mod_sums(b, part, d, u):
            for k, value in enumerate((d * u, d)):
                total = dot(pick[...], value.astype(LOW))
                sm[b, 0 : z.meshes, (part + k) * width : (part + k + 1) * width] = total[0 : z.meshes]

        def halos(b):
            return [
                remote(hsend.at[b, 0], hrecv.at[b, 1], bh_s.at[b, 0], bh_r.at[b, 0], (sec, down)),
                remote(hsend.at[b, 1], hrecv.at[b, 0], bh_s.at[b, 1], bh_r.at[b, 1], (sec, up)),
            ]

        def given(b):
            at = batch_cols(b)
            dr = dybuf[b]
            right_t[0, at, :] = dr
            sm[b, 7:8, 0:width] = jnp.sum(dr.astype(F32), axis=0, keepdims=True)
            for g in range(groups):
                right_t[1 + g, at, :] = dot_nt(dr, wd[g * TILE : (g + 1) * TILE, :]).astype(LOW)

        def back_ffn(t):
            at = turn_cols(t)
            dn = jnp.zeros((many * rows, width), F32)
            for g in range(groups):
                gs = slice(g * TILE, (g + 1) * TILE)
                dg = right_t[1 + g, at, :].astype(F32) * turn_of(fp, t)[:, gs].astype(F32)
                sm[t * many, 6:7, gs] = jnp.sum(dg, axis=0, keepdims=True)
                dg = dg.astype(LOW)
                right_t[1 + g, at, :] = dg
                dn = dn + dot_nt(dg, wu[:, gs])
            dbuf[...] = dn

        def back_middle(t):
            at = turn_cols(t)
            ids_rows = wide(sel[own_rows, :])
            for i in range(many):
                b = t * many + i
                d = dbuf[i * rows : (i + 1) * rows]
                u = ub[b]
                grad = dybuf[b].astype(F32) + norm_back(d, u, ib[b][:, 0:1], mod_rows(b, 2, ids_rows))
                mod_sums(b, 2, d, u)
                dx1[i] = grad
                right_t[g_out, batch_cols(b), :] = grad.astype(LOW)
            ob[...] = dot_nt(right_t[g_out, at, :], wo[...]).astype(LOW)

        def back_attention(t):
            units = [(i, h) for i in range(many) for h in range(HEADS)]
            here = [slice(i * rows, (i + 1) * rows) for i in range(many)]
            for i, h in units:
                sbuf[i * HEADS + h] = dot_nt(ob[here[i], heads[h]], kvext[t * many + i, :, heads_v[h]])
            for i, h in units:
                b, k = t * many + i, i * HEADS + h
                a, da = af[b, h], sbuf[k]
                ds = a * (da - jnp.sum(a * cnt[...] * da, axis=-1, keepdims=True))
                cds[k] = ds.astype(LOW) * few[...]
            for i in range(many):
                b = t * many + i
                for h in range(HEADS):
                    dk = dot_tn(cds[i * HEADS + h], qb[b, :, heads[h]]) * score_scale
                    dv = dot_tn(ca[b, h], ob[here[i], heads[h]])
                    for part, cols in ((dk, heads[h]), (dv, heads_v[h])):
                        hsend[b, 0, :, cols] = part[0:REACH].astype(LOW)
                        dkv[i, :, cols] = part[REACH : REACH + rows]
                        hsend[b, 1, :, cols] = part[REACH + rows : ext].astype(LOW)
                for copy in halos(b):
                    copy.start()
            for i, h in units:
                b = t * many + i
                value = dot(cds[i * HEADS + h], kvext[b, :, heads[h]]) * score_scale
                right_t[g_q, batch_cols(b), heads[h]] = value.astype(LOW)

        def back_second(t):
            at = turn_cols(t)
            ids_rows = wide(sel[own_rows, :])
            edge = rows - REACH
            dbuf[...] = dot_nt(right_t[g_q, at, :], wq[:, 0:width])
            for i in range(many):
                b = t * many + i
                for copy in halos(b):
                    copy.wait_recv()
                dkv[i, 0:REACH, :] += hrecv[b, 0].astype(F32)
                dkv[i, edge:rows, :] += hrecv[b, 1].astype(F32)
                d = dbuf[i * rows : (i + 1) * rows]
                for g in range(2):
                    part = dkv[i, :, g * width : (g + 1) * width].astype(LOW)
                    right_t[g_k + g, batch_cols(b), :] = part
                    d = d + dot_nt(part, wq[:, (g + 1) * width : (g + 2) * width])
                u = ua[b]
                grad = dx1[i] + norm_back(d, u, ia[b][:, 0:1], mod_rows(b, 0, ids_rows))
                ig[0, b] = grad.astype(LOW)

                @pl.when(sec == 1)
                def _(b=b):
                    relay_back(b).start()

                mod_sums(b, 0, d, u)

        def relay_back(b):
            return remote(ig.at[0, b], dybuf.at[b], bx_s.at[b], bx_r.at[b], (other, me))

        for copy in loads[1:]:
            copy.wait()
        for copy in (m_down, m_up):
            copy.wait()

        @pl.when(sec == 0)
        def _():
            first_load.wait()
            x_down.wait()
            x_up.wait()

        @pl.when(sec == 1)
        def _():
            last_load.wait()

            @pl.loop(0, batches)
            def _(b):
                given(b)

        @pl.loop(0, batches)
        def _(b):
            @pl.when(sec == 1)
            def _():
                for copy in relay(b):
                    copy.wait_recv()

            forward(b)

            @pl.when(sec == 0)
            def _():
                for copy in relay(b):
                    copy.start()

        @pl.when(sec == 0)
        def _():
            lax.fori_loop(0, batches, transposes, 0)

        def rows_of(c, size):
            return pl.ds(pl.multiple_of(c * size, size), size)

        def turned(p):
            return lax.rem(p, 2) * side(1) if stages > 2 else 0 * p

        def bit_of(p, k):
            bits = list(z.bits)
            if stages > 2:
                bits[1], bits[2] = bits[2], bits[1]
            return z.bits[k] + (bits[k] - z.bits[k]) * turned(p)

        def piece_copy(p, k):
            return remote(gives[k].at[p], gets[k].at[p], p_s.at[p, k], p_r.at[p, k], (sec, mate(bit_of(p, k))))

        slots_held, ahead = 4, 2

        def piece_start(p):
            left = z.left(p)
            sides = [left_t[left, rows_of(c, half), :] for c in (1 - side(1), side(1))]
            value = dot(jnp.concatenate(sides, axis=0), right_t[z.right(p)])
            gives[0][p] = value[0:half].astype(LOW)
            piece_copy(p, 0).start()
            acc[lax.rem(p, slots_held)] = value[half : 2 * half].astype(LOW)

        def piece_first(p):
            piece_copy(p, 0).wait()
            here = side(bit_of(p, 1))
            run = half // 4
            for s, to in ((1 - here, gives[1]), (here, keeps[0])):
                for j in range(2):
                    at = rows_of((1 - turned(p)) * (2 * s + j) + turned(p) * (2 * j + s), run)
                    value = acc[lax.rem(p, slots_held), at, :].astype(F32) + gets[0][p, at, :].astype(F32)
                    to[p, j * run : (j + 1) * run, :] = value.astype(to.dtype)
                if to is gives[1]:
                    piece_copy(p, 1).start()

        def piece_step(p, k):
            size = half >> k
            piece_copy(p, k).wait()
            if k == stages - 1:
                o_piece[p] = keeps[k - 1][p] + gets[k][p].astype(F32)
                return
            here = side(bit_of(p, k + 1))
            for to, c in ((gives[k + 1], 1 - here), (keeps[k], here)):
                at = rows_of(c, size // 2)
                to[p] = (keeps[k - 1][p, at, :] + gets[k][p, at, :].astype(F32)).astype(to.dtype)
                if to is gives[k + 1]:
                    piece_copy(p, k + 1).start()

        def only_first(body):
            if z.scatter:
                pl.when(sec == 0)(body)

        for t in reversed(range(z.turns)):

            @pl.when(sec == 0)
            def _(t=t):
                for i in range(many):
                    relay_back(t * many + i).wait_recv()
                    given(t * many + i)

            back_ffn(t)
            back_middle(t)
            back_attention(t)
            if t == 0:

                @only_first
                def _():
                    pl.loop(0, groups)(piece_start)
                    pl.loop(0, ahead)(piece_first)

            back_second(t)

        @pl.when(sec == 1)
        def _():
            lax.fori_loop(0, batches, transposes, 0)

        lines = [sm[b, m : m + 1, :] for b in range(batches) for m in range(z.meshes)]
        for line in (6, 7):
            lines.append(sum(sm[b, line : line + 1, :] for b in range(batches)))
        lines.append(jnp.zeros((16 - len(lines), sm.shape[2]), F32))
        small = jnp.concatenate(lines, axis=0)

        def finish():
            @pl.loop(0, batches)
            def _(b):
                @pl.when(sec == 0)
                def _():
                    for copy in relay(b):
                        copy.wait_send()

                @pl.when(sec == 1)
                def _():
                    relay_back(b).wait_send()

                for copy in halos(b):
                    copy.wait_send()

        if not z.scatter:
            small_out[...] = small
            table_out[...] = emb[...]
            finish()
            return

        def ring_copy(k):
            return remote(msend.at[k], mrecv.at[k], m_s.at[k], m_r.at[k], (sec, mate(1 << k)))

        def ring_start(k, value):
            msend[k] = value.astype(LOW)
            ring_copy(k).start()

        def ring_end(k):
            ring_copy(k).wait_recv()
            value = msend[k].astype(F32) + mrecv[k].astype(F32)
            if k + 1 < z.rings:
                ring_start(k + 1, value)
            else:
                tot[...] = value

        ring_start(0, small)

        lags = [0, 3] + [7 + 4 * k for k in range(stages - 1)]
        begun, summed = (1 - sec) * groups, (1 - sec) * ahead

        @pl.loop(0, npiece + lags[-1])
        def _(p):
            @pl.when((p >= begun) & (p < npiece))
            def _():
                piece_start(p)

            @pl.when((p >= summed + lags[1]) & (p < npiece + lags[1]))
            def _():
                piece_first(p - lags[1])

            for k in range(1, stages):
                lag = lags[k + 1]

                @pl.when((p >= lag) & (p < npiece + lag))
                def _(k=k, lag=lag):
                    piece_step(p - lag, k)

            for k in range(z.rings):

                @pl.when(p == 9 + 3 * k)
                def _(k=k):
                    ring_end(k)

            @pl.when(p == 7 + 3 * z.rings)
            def _():
                finish()
                count = batches * z.meshes
                table = emb[pl.ds(pl.multiple_of(me * own, own), own), :]
                grad = jnp.zeros((own, 4 * width), F32)
                for k in range(count):
                    grad = grad + table[:, k : k + 1] * tot[k : k + 1, :]
                o_mod[0] = grad
                cols = 4 * width // shards
                mine = tot[:, pl.ds(pl.multiple_of(me * cols, cols), cols)]
                o_line[0:1, :] = jnp.sum(mine[0:count], axis=0, keepdims=True)
                o_line[1:2, :] = mine[count : count + 1]
                ratio = 128 // own
                line = tot[:, pl.ds(pl.multiple_of(me // ratio * 128, 128), 128)][count + 1 : count + 2]
                value = line
                for k in range(1, ratio):
                    rolled = jnp.concatenate([line[:, k * own :], line[:, : k * own]], axis=1)
                    value = jnp.where(me % ratio == k, rolled, value)
                o_line[2:3, :] = value

        for k in range(z.rings):
            ring_copy(k).wait_send()

    return kernel


def layout_of(z):
    own, groups = z.own, z.groups

    def kernel(
        lo, ig, piece, mod, line,
        o_lo, o_ig, o_qkv, o_out, o_up, o_upb, o_down, o_downb, o_mod, o_modb,
        sems,
    ):
        targets = [o_down.at[0, pl.ds(q * own, own), :] for q in range(groups)]
        targets += [o_up.at[0, :, pl.ds(q * TILE, TILE)] for q in range(groups)]
        targets += [o_out.at[0]] + [o_qkv.at[0, :, pl.ds(q * TILE, TILE)] for q in range(3)]
        moves = [(lo, o_lo), (ig, o_ig), (mod, o_mod)]
        moves += [(piece.at[k], target) for k, target in enumerate(targets)]
        copies = [pltpu.make_async_copy(a, b, sems.at[k]) for k, (a, b) in enumerate(moves)]
        for copy in copies:
            copy.start()
        o_modb[...] = line[0:1, :]
        o_upb[...] = line[1:2, :]
        o_downb[...] = line[2:3, 0:own]
        for copy in copies:
            copy.wait()

    return kernel


def body(
    inputs,
    cotangent,
    neighbours,
    mesh_ids,
    noise_sigma,
    w_qkv,
    w_out,
    w_up,
    b_up,
    w_down,
    b_down,
    w_mod,
    b_mod,
):
    shards = lax.axis_size("nodes")
    z = Sizes(inputs, neighbours, noise_sigma, w_up, shards)
    batches, rows, width, hidden, many = z.batches, z.rows, z.width, z.hidden, z.together
    own, npiece = z.own, z.pieces
    shape = jax.ShapeDtypeStruct
    stack = shape((1, batches, rows, width), LOW)
    outs = [stack, stack]
    sides = [(z.lefts, TILE, batches * rows), (z.rights, batches * rows, TILE)]
    if z.scatter:
        outs = [pltpu.VMEM(stack.shape, LOW)] * 2
        outs += [pltpu.VMEM((npiece, own, TILE), F32), pltpu.VMEM((1, own, 4 * width), F32), pltpu.VMEM((8, 128), F32)]
        scratch = [pltpu.VMEM(side, LOW) for side in sides]
    else:
        outs += [shape(side, LOW) for side in sides] + [shape((16, hidden), F32), shape((width, 128), F32)]
        scratch = []
    dma = pltpu.SemaphoreType.DMA
    scratch += [
        pltpu.VMEM((width, 3 * width), LOW),
        pltpu.VMEM((width, width), LOW),
        pltpu.VMEM((width, hidden), LOW),
        pltpu.VMEM((hidden, width), LOW),
        pltpu.VMEM((width, 4 * width), LOW),
        pltpu.VMEM((batches, z.ext, width), LOW),
        pltpu.VMEM((batches, rows, width), LOW),
        pltpu.VMEM((z.ext, 128), F32),
        pltpu.VMEM((16, rows), LOW),
        pltpu.VMEM((rows, z.window), F32),
        pltpu.VMEM((rows, z.window), LOW),
        pltpu.VMEM((rows, z.window), F32),
        pltpu.VMEM((batches, 8, 4 * width), F32),
        pltpu.VMEM((width, 128), F32),
        pltpu.VMEM((z.ext, width), LOW),
        pltpu.VMEM((batches, rows, width), LOW),
        pltpu.VMEM((batches, rows, width), F32),
        pltpu.VMEM((batches, rows, 128), F32),
        pltpu.VMEM((batches, rows, width), LOW),
        pltpu.VMEM((batches, z.window, 2 * width), LOW),
        pltpu.VMEM((many * HEADS, rows, z.window), F32),
        pltpu.VMEM((batches, HEADS, rows, z.window), F32),
        pltpu.VMEM((batches, HEADS, rows, z.window), LOW),
        pltpu.VMEM((batches, rows, width), LOW),
        pltpu.VMEM((batches, rows, width), LOW),
        pltpu.VMEM((batches, rows, width), F32),
        pltpu.VMEM((batches, rows, 128), F32),
        pltpu.VMEM((rows, width), F32),
        pltpu.VMEM((batches, rows, hidden), LOW),
        pltpu.VMEM((batches, rows, hidden), LOW),
        pltpu.VMEM((many * rows, width), LOW),
        pltpu.VMEM((many * rows, width), F32),
        pltpu.VMEM((many * HEADS, rows, z.window), LOW),
        pltpu.VMEM((many, rows, width), F32),
        pltpu.VMEM((many, rows, 2 * width), F32),
        pltpu.VMEM((batches, 2, REACH, 2 * width), LOW),
        pltpu.VMEM((batches, 2, REACH, 2 * width), LOW),
        pltpu.VMEM((batches, 8, hidden), F32),
        dma((7,)),
        dma((2,)),
        dma((2,)),
        dma((2,)),
        dma((2,)),
        dma((batches, 3)),
        dma((batches, 3)),
        dma((batches, 2)),
        dma((batches, 2)),
        dma((batches,)),
        dma((batches,)),
    ]
    if z.scatter:
        stages = len(z.bits)
        sizes = [TILE >> (k + 1) for k in range(stages)]
        scratch += [pltpu.VMEM((npiece, size, TILE), LOW) for size in sizes + sizes]
        scratch += [pltpu.VMEM((npiece, size, TILE), F32) for size in sizes[1:]]
        scratch += [
            pltpu.VMEM((4, sizes[0], TILE), LOW),
            pltpu.VMEM((z.rings, 16, hidden), LOW),
            pltpu.VMEM((z.rings, 16, hidden), LOW),
            pltpu.VMEM((16, hidden), F32),
            dma((npiece, stages)),
            dma((npiece, stages)),
            dma((z.rings,)),
            dma((z.rings,)),
        ]
    hbm = pl.BlockSpec(memory_space=pl.ANY)
    vmem = pl.BlockSpec(memory_space=pltpu.VMEM)
    smem = pl.BlockSpec(memory_space=pltpu.SMEM)
    got = pl.pallas_call(
        kernel_of(z),
        out_shape=outs,
        in_specs=[hbm, hbm, vmem, vmem, smem, hbm, hbm, hbm, vmem, hbm, vmem, hbm, vmem],
        out_specs=[vmem] * len(outs),
        scratch_shapes=scratch,
        compiler_params=pltpu.CompilerParams(
            collective_id=0, has_side_effects=True, vmem_limit_bytes=61 * 2**20
        ),
    )(
        inputs,
        cotangent,
        neighbours.T,
        mesh_ids.reshape(1, rows),
        noise_sigma.T,
        w_qkv,
        w_out,
        w_up,
        b_up,
        w_down,
        b_down,
        w_mod,
        b_mod,
    )
    if z.scatter:
        lo, ig, piece, mod, line = got
        return tuple(
            pl.pallas_call(
                layout_of(z),
                out_shape=[
                    stack,
                    stack,
                    shape((1, own, 3 * width), F32),
                    shape((1, own, width), F32),
                    shape((1, own, hidden), F32),
                    shape((1, hidden // shards), F32),
                    shape((1, hidden // shards, width), F32),
                    shape((1, own), F32),
                    shape((1, own, 4 * width), F32),
                    shape((1, 4 * width // shards), F32),
                ],
                in_specs=[vmem] * 5,
                out_specs=[hbm, hbm, hbm, hbm, hbm, vmem, hbm, vmem, hbm, vmem],
                scratch_shapes=[dma((npiece + 3,))],
                compiler_params=pltpu.CompilerParams(vmem_limit_bytes=2 * 2**20),
            )(lo, ig, piece, mod, line)
        )
    lo, ig, left_t, right_t, small, table = got
    groups = z.groups

    def summed(value):
        return lax.psum_scatter(value, "nodes", scatter_dimension=0, tiled=True)

    def wide_sum(left, first, last):
        return summed(jnp.concatenate([dot(left_t[left], right_t[r]) for r in range(first, last)], axis=1))[None]

    down = [dot(left_t[q], right_t[0]).reshape(TILE // 32, 32, TILE) for q in range(groups)]
    down = jnp.stack(down, axis=1)
    count = batches * z.meshes
    small = lax.psum(small, "nodes")
    me = lax.axis_index("nodes")
    mod = jnp.dot(table[:, :count], small[:count], precision=lax.Precision.HIGHEST)

    def mine(value):
        size = value.shape[0] // shards
        return lax.dynamic_slice_in_dim(value, me * size, size, axis=0)[None]

    return (
        lo,
        ig,
        wide_sum(groups + 2, 2 + groups, 5 + groups),
        wide_sum(groups + 1, 1 + groups, 2 + groups),
        wide_sum(groups, 1, 1 + groups),
        mine(small[count]),
        summed(down.reshape(hidden, width))[None],
        mine(small[count + 1, :width]),
        mine(mod),
        mine(jnp.sum(small[:count], axis=0)),
    )


def solution(mesh):
    return jax.shard_map(
        body,
        mesh=mesh,
        in_specs=(
            P(None, "nodes", None),
            P(None, "nodes", None),
            P("nodes", None),
            P("nodes"),
            P(),
            P("section", None, None),
            P("section", None, None),
            P("section", None, None),
            P("section", None),
            P("section", None, None),
            P("section", None),
            P("section", None, None),
            P("section", None),
        ),
        out_specs=(
            P("section", None, "nodes", None),
            P("section", None, "nodes", None),
            P("section", "nodes", None),
            P("section", "nodes", None),
            P("section", "nodes", None),
            P("section", "nodes"),
            P("section", "nodes", None),
            P("section", "nodes"),
            P("section", "nodes", None),
            P("section", "nodes"),
        ),
        check_vma=False,
    )
```

```python
import jax
import jax.numpy as jnp
from jax import lax
from jax.experimental import pallas as pl
from jax.experimental.pallas import tpu as pltpu
from jax.sharding import PartitionSpec as P

HEADS = 4
REACH = 32
EPSILON = 1e-06
MASKED = -1e9
ABSENT = -2e38
TILE = 512
TOGETHER = 2
MESH = pl.DeviceIdType.MESH
F32, LOW = jnp.float32, jnp.bfloat16


def dot(a, b):
    return lax.dot_general(a, b, (((1,), (0,)), ((), ())), preferred_element_type=F32)


def dot_nt(a, b):
    return lax.dot_general(a, b, (((1,), (1,)), ((), ())), preferred_element_type=F32)


def dot_tn(a, b):
    return lax.dot_general(a, b, (((0,), (0,)), ((), ())), preferred_element_type=F32)


class Sizes:
    def __init__(self, inputs, neighbours, noise, w_up, shards):
        self.batches, self.rows, self.width = inputs.shape
        self.together = TOGETHER if self.batches % TOGETHER == 0 else 1
        self.turns = self.batches // self.together
        self.slots = neighbours.shape[1]
        self.meshes = noise.shape[1]
        self.hidden = w_up.shape[2]
        self.shards = shards
        self.ext = self.rows + 2 * REACH
        self.window = (self.ext // 128 + 1) * 128
        self.groups = self.hidden // TILE
        self.own = self.width // shards
        self.scatter = self.own % 16 == 0
        self.pieces = 2 * self.groups + 4
        self.lefts = 3 + self.groups
        self.rights = 2 + self.groups + 3
        self.rings = max(shards.bit_length() - 1, 1)

        self.bits = [1 << k for k in range(shards.bit_length() - 1)]

    def left(self, p):
        n = self.groups
        return jnp.minimum(p, n) + lax.div(p, 2 * n) + lax.div(p, 2 * n + 1)

    def right(self, p):
        return jnp.maximum(p - (self.groups - 1), 0)


def kernel_of(z):
    batches, rows, width, ext, window = z.batches, z.rows, z.width, z.ext, z.window
    groups, shards, own, many = z.groups, z.shards, z.own, z.together
    head = width // HEADS
    score_scale = head ** (-0.5)
    log2e = 1.4426950408889634
    npiece = z.pieces
    half = TILE // 2
    stages = len(z.bits)
    g_out, g_q, g_k = 1 + groups, 2 + groups, 3 + groups

    def position(owner):
        if not z.scatter:
            return owner
        place = 0
        for bit in z.bits:
            place = 2 * place + owner // bit % 2
        return place

    def kernel(
        inputs, cotangent, neighbours, mesh_ids, sigma,
        w_qkv, w_out, w_up, b_up, w_down, b_down, w_mod, b_mod,
        lo, ig, *rest,
    ):
        if z.scatter:
            o_piece, o_mod, o_line, left_t, right_t = rest[:5]
            rest = rest[5:]
        else:
            left_t, right_t, small_out, table_out = rest[:4]
            rest = rest[4:]
        (
            wq, wo, wu, wd, wm, xext, dybuf, sel, pick, cnt, few, bias, mod, emb,
            n1, n1s, ua, ia, qb, kvext, sbuf, af, ca, obs, n2s, ub, ib, tb, fp, hs,
            ob, dbuf, cds, dx1, dkv, hsend, hrecv, sm,
            lsem, hx_s, hx_r, hm_s, hm_r, fx_s, fx_r, bh_s, bh_r, bx_s, bx_r,
        ) = rest[:49]
        rest = rest[49:]
        if z.scatter:
            gives, gets, keeps = rest[:stages], rest[stages : 2 * stages], rest[2 * stages : 3 * stages - 1]
            acc, msend, mrecv, tot, p_s, p_r, m_s, m_r = rest[3 * stages - 1 :]

        sec = lax.axis_index("section")
        me = lax.axis_index("nodes")
        up = lax.rem(me + 1, shards)
        down = lax.rem(me + shards - 1, shards)
        other = 1 - sec
        def local(src, dst, k):
            return pltpu.make_async_copy(src, dst, lsem.at[k])

        loads = [
            local(w_mod.at[0], wm, 0),
            local(w_qkv.at[0], wq, 1),
            local(w_out.at[0], wo, 2),
            local(w_up.at[0], wu, 3),
            local(w_down.at[0], wd, 4),
        ]
        own_rows = pl.ds(REACH, rows)
        first_load = local(inputs, xext.at[:, own_rows, :], 5)
        last_load = local(cotangent, dybuf, 6)
        loads[0].start()

        @pl.when(sec == 0)
        def _():
            first_load.start()

        for copy in loads[1:]:
            copy.start()

        @pl.when(sec == 1)
        def _():
            last_load.start()

        def side(bit):
            return lax.rem(lax.div(me, bit), 2)

        def mate(bit):
            return me + bit - 2 * bit * side(bit)

        barrier = pltpu.get_barrier_semaphore()
        mates = [(sec, up), (sec, down), (other, me), (other, up), (other, down)]
        if z.scatter:
            mates += [(sec, mate(bit)) for bit in z.bits[1:]]
        for peer in mates:
            pl.semaphore_signal(barrier, inc=1, device_id=peer, device_id_type=MESH)
        pl.semaphore_wait(barrier, len(mates))

        def remote(src, dst, s_sem, r_sem, peer):
            return pltpu.make_async_remote_copy(
                src_ref=src, dst_ref=dst, send_sem=s_sem, recv_sem=r_sem, device_id=peer, device_id_type=MESH
            )

        low_rows, top_rows = pl.ds(0, REACH), pl.ds(REACH + rows, REACH)
        head_rows, tail_rows = pl.ds(REACH, REACH), pl.ds(rows, REACH)
        x_down = remote(inputs.at[:, pl.ds(0, REACH), :], xext.at[:, top_rows, :], hx_s.at[0], hx_r.at[0], (sec, down))
        x_up = remote(inputs.at[:, pl.ds(rows - REACH, REACH), :], xext.at[:, low_rows, :], hx_s.at[1], hx_r.at[1], (sec, up))

        @pl.when(sec == 0)
        def _():
            x_down.start()
            x_up.start()

        ids = jnp.broadcast_to(mesh_ids[...].astype(F32), (128, rows))
        sel[own_rows, :] = ids.T
        sample = lax.broadcasted_iota(jnp.int32, (16, rows), 0).astype(F32)
        pick[...] = jnp.where(ids[0:16] == sample, 1.0, 0.0).astype(LOW)
        m_down = remote(sel.at[head_rows, :], sel.at[top_rows, :], hm_s.at[0], hm_r.at[0], (sec, down))
        m_up = remote(sel.at[tail_rows, :], sel.at[low_rows, :], hm_s.at[1], hm_r.at[1], (sec, up))
        m_down.start()
        m_up.start()

        kvext[:, ext:window, :] = jnp.zeros((batches, window - ext, 2 * width), LOW)
        sm[...] = jnp.zeros(sm.shape, F32)

        slots = neighbours[...].astype(F32)
        slots = jnp.concatenate([slots, jnp.zeros((128 - z.slots, rows), F32)], axis=0).T
        slots = jnp.where(slots >= 0, slots - (me * rows - REACH).astype(F32), float(ext))
        column = lax.broadcasted_iota(jnp.int32, (rows, window), 1).astype(F32)
        counts = jnp.zeros((rows, window), F32)
        for n in range(z.slots):
            counts = counts + jnp.where(slots[:, n : n + 1] == column, 1.0, 0.0)
        cnt[...] = counts
        few[...] = counts.astype(LOW)
        bias[...] = jnp.where(counts > 0, jnp.where(column == ext, MASKED * log2e, 0.0), ABSENT)

        row_no = lax.broadcasted_iota(jnp.int32, (16, width // 2), 0)
        level = jnp.ones((16, width // 2), F32)
        for b in range(batches):
            for m in range(z.meshes):
                level = jnp.where(row_no == b * z.meshes + m, sigma[m, b], level)
        place = lax.broadcasted_iota(jnp.int32, (16, width // 2), 1).astype(F32)
        frequency = 3.0 * jnp.exp(-jnp.log(100.0) * place / (width // 2))
        angles = jnp.log(level) * frequency
        embedded = jnp.concatenate([jnp.sin(angles), jnp.cos(angles)], axis=1).astype(LOW)
        padded = jnp.concatenate([embedded.astype(F32), jnp.zeros((112, width), F32)], axis=0)
        emb[...] = padded.T
        loads[0].wait()
        for g in range(4):
            cols = pl.ds(g * width, width)
            table = dot(embedded, wm[:, cols]) + b_mod[:, cols] + (1.0 - g % 2)
            for b in range(batches):
                mod[b, 0 : z.meshes, cols] = table[b * z.meshes : (b + 1) * z.meshes]

        def mod_rows(b, part, ids_rows):
            cols = pl.ds(part * width, width)
            value = jnp.broadcast_to(mod[b, 0:1, cols], (ids_rows.shape[0], width))
            for m in range(1, z.meshes):
                value = jnp.where(ids_rows > m - 0.5, mod[b, m : m + 1, cols], value)
            return value

        def wide(ids_rows):
            return jnp.concatenate([ids_rows] * (width // 128), axis=1)

        def unit(x):
            centred = x - jnp.mean(x, axis=-1, keepdims=True)
            inv = lax.rsqrt(jnp.mean(centred * centred, axis=-1, keepdims=True) + EPSILON)
            return centred * inv, inv

        def span_of(start, size):
            if isinstance(start, int):
                return pl.ds(start, size)
            return pl.ds(pl.multiple_of(start, size), size)

        def batch_cols(b):
            return span_of(b * rows, rows)

        def turn_cols(t):
            return span_of(t * many * rows, many * rows)

        def turn_of(ref, t):
            return ref[pl.ds(t * many, many)].reshape(many * rows, ref.shape[2])

        span = own if z.scatter else 32

        def transposes(b, carry):
            for first, ref in ((groups, n2s), (groups + 1, obs), (groups + 2, n1s)):
                turned = ref[b].T
                for owner in range(TILE // span):
                    at = position(owner) * span
                    left_t[first, at : at + span, batch_cols(b)] = turned[owner * span : (owner + 1) * span]
            run = groups * span
            for g in range(groups):
                turned = hs[b, :, g * TILE : (g + 1) * TILE].T
                for k in range(TILE // span):
                    at = g * TILE + k * span
                    owner, part = at // run, at % run // span
                    to = position(owner) * span
                    left_t[part, to : to + span, batch_cols(b)] = turned[k * span : (k + 1) * span]
            return carry

        heads = [slice(h * head, (h + 1) * head) for h in range(HEADS)]
        heads_v = [slice(width + h * head, width + (h + 1) * head) for h in range(HEADS)]
        tiles = [slice(g * TILE, (g + 1) * TILE) for g in range(groups)]
        thirds = [slice(g * width, (g + 1) * width) for g in range(3)]

        def forward(b):
            ids_rows = wide(sel[0:ext, :])
            u, inv = unit(xext[b].astype(F32))
            normed = (u * mod_rows(b, 0, ids_rows) + mod_rows(b, 1, ids_rows)).astype(LOW)
            n1[...] = normed
            n1s[b] = normed[REACH : REACH + rows]
            ua[b] = u[REACH : REACH + rows]
            ia[b] = jnp.broadcast_to(inv[REACH : REACH + rows], (rows, 128))
            kvext[b, 0:ext, thirds[0]] = dot(n1[...], wq[:, thirds[1]]).astype(LOW)
            qb[b] = dot(n1s[b], wq[:, thirds[0]]).astype(LOW)
            for h in range(HEADS):
                sbuf[h] = dot_nt(qb[b, :, heads[h]], kvext[b, :, heads[h]]) * (score_scale * log2e) + bias[...]
            kvext[b, 0:ext, thirds[1]] = dot(n1[...], wq[:, thirds[2]]).astype(LOW)
            for h in range(HEADS):
                s = sbuf[h]
                e = jnp.exp2(s - jnp.max(s, axis=-1, keepdims=True))
                a = e * (1.0 / jnp.sum(e * cnt[...], axis=-1, keepdims=True))
                af[b, h] = a
                ca[b, h] = a.astype(LOW) * few[...]
            for h in range(HEADS):
                obs[b, :, heads[h]] = dot(ca[b, h], kvext[b, :, heads_v[h]]).astype(LOW)

            x1 = xext[b, own_rows, :].astype(F32) + dot(obs[b], wo[...])
            u, inv = unit(x1)
            ub[b] = u
            ib[b] = jnp.broadcast_to(inv, (rows, 128))
            ids_rows = wide(sel[own_rows, :])
            n2s[b] = (u * mod_rows(b, 2, ids_rows) + mod_rows(b, 3, ids_rows)).astype(LOW)
            tb[...] = x1 + b_down[...]
            for gs in tiles:
                gate = dot(n2s[b], wu[:, gs]) + b_up[:, gs]
                s = 0.5 + 0.5 * jnp.tanh(0.5 * gate)
                hid = gate * s
                fp[b, :, gs] = (s + hid * (1.0 - s)).astype(LOW)
                hid = hid.astype(LOW)
                hs[b, :, gs] = hid
                tb[...] += dot(hid, wd[gs, :])
            lo[0, b] = tb[...].astype(LOW)

        def relay(b):
            return [
                remote(lo.at[0, b], xext.at[b, own_rows, :], fx_s.at[b, 0], fx_r.at[b, 0], (other, me)),
                remote(lo.at[0, b, pl.ds(0, REACH), :], xext.at[b, top_rows, :], fx_s.at[b, 1], fx_r.at[b, 1], (other, down)),
                remote(lo.at[0, b, pl.ds(rows - REACH, REACH), :], xext.at[b, low_rows, :], fx_s.at[b, 2], fx_r.at[b, 2], (other, up)),
            ]

        def norm_back(d, u, inv, scale):
            scaled = d * scale
            return inv * (
                scaled
                - jnp.mean(scaled, axis=-1, keepdims=True)
                - u * jnp.mean(scaled * u, axis=-1, keepdims=True)
            )

        def mod_sums(b, part, d, u):
            for k, value in enumerate((d * u, d)):
                total = dot(pick[...], value.astype(LOW))
                sm[b, 0 : z.meshes, (part + k) * width : (part + k + 1) * width] = total[0 : z.meshes]

        def halos(b):
            return [
                remote(hsend.at[b, 0], hrecv.at[b, 1], bh_s.at[b, 0], bh_r.at[b, 0], (sec, down)),
                remote(hsend.at[b, 1], hrecv.at[b, 0], bh_s.at[b, 1], bh_r.at[b, 1], (sec, up)),
            ]

        def given(b):
            at = batch_cols(b)
            dr = dybuf[b]
            right_t[0, at, :] = dr
            sm[b, 7:8, 0:width] = jnp.sum(dr.astype(F32), axis=0, keepdims=True)
            for g in range(groups):
                right_t[1 + g, at, :] = dot_nt(dr, wd[g * TILE : (g + 1) * TILE, :]).astype(LOW)

        def back_ffn(t):
            at = turn_cols(t)
            dn = jnp.zeros((many * rows, width), F32)
            for g in range(groups):
                gs = slice(g * TILE, (g + 1) * TILE)
                dg = right_t[1 + g, at, :].astype(F32) * turn_of(fp, t)[:, gs].astype(F32)
                sm[t * many, 6:7, gs] = jnp.sum(dg, axis=0, keepdims=True)
                dg = dg.astype(LOW)
                right_t[1 + g, at, :] = dg
                dn = dn + dot_nt(dg, wu[:, gs])
            dbuf[...] = dn

        def back_middle(t):
            at = turn_cols(t)
            ids_rows = wide(sel[own_rows, :])
            for i in range(many):
                b = t * many + i
                d = dbuf[i * rows : (i + 1) * rows]
                u = ub[b]
                grad = dybuf[b].astype(F32) + norm_back(d, u, ib[b][:, 0:1], mod_rows(b, 2, ids_rows))
                mod_sums(b, 2, d, u)
                dx1[i] = grad
                right_t[g_out, batch_cols(b), :] = grad.astype(LOW)
            ob[...] = dot_nt(right_t[g_out, at, :], wo[...]).astype(LOW)

        def back_attention(t):
            units = [(i, h) for i in range(many) for h in range(HEADS)]
            here = [slice(i * rows, (i + 1) * rows) for i in range(many)]
            for i, h in units:
                sbuf[i * HEADS + h] = dot_nt(ob[here[i], heads[h]], kvext[t * many + i, :, heads_v[h]])
            for i, h in units:
                b, k = t * many + i, i * HEADS + h
                a, da = af[b, h], sbuf[k]
                ds = a * (da - jnp.sum(a * cnt[...] * da, axis=-1, keepdims=True))
                cds[k] = ds.astype(LOW) * few[...]
            for i in range(many):
                b = t * many + i
                for h in range(HEADS):
                    dk = dot_tn(cds[i * HEADS + h], qb[b, :, heads[h]]) * score_scale
                    dv = dot_tn(ca[b, h], ob[here[i], heads[h]])
                    for part, cols in ((dk, heads[h]), (dv, heads_v[h])):
                        hsend[b, 0, :, cols] = part[0:REACH].astype(LOW)
                        dkv[i, :, cols] = part[REACH : REACH + rows]
                        hsend[b, 1, :, cols] = part[REACH + rows : ext].astype(LOW)
                for copy in halos(b):
                    copy.start()
            for i, h in units:
                b = t * many + i
                value = dot(cds[i * HEADS + h], kvext[b, :, heads[h]]) * score_scale
                right_t[g_q, batch_cols(b), heads[h]] = value.astype(LOW)

        def back_second(t):
            at = turn_cols(t)
            ids_rows = wide(sel[own_rows, :])
            edge = rows - REACH
            dbuf[...] = dot_nt(right_t[g_q, at, :], wq[:, 0:width])
            for i in range(many):
                b = t * many + i
                for copy in halos(b):
                    copy.wait_recv()
                dkv[i, 0:REACH, :] += hrecv[b, 0].astype(F32)
                dkv[i, edge:rows, :] += hrecv[b, 1].astype(F32)
                d = dbuf[i * rows : (i + 1) * rows]
                for g in range(2):
                    part = dkv[i, :, g * width : (g + 1) * width].astype(LOW)
                    right_t[g_k + g, batch_cols(b), :] = part
                    d = d + dot_nt(part, wq[:, (g + 1) * width : (g + 2) * width])
                u = ua[b]
                grad = dx1[i] + norm_back(d, u, ia[b][:, 0:1], mod_rows(b, 0, ids_rows))
                ig[0, b] = grad.astype(LOW)

                @pl.when(sec == 1)
                def _(b=b):
                    relay_back(b).start()

                mod_sums(b, 0, d, u)

        def relay_back(b):
            return remote(ig.at[0, b], dybuf.at[b], bx_s.at[b], bx_r.at[b], (other, me))

        for copy in loads[1:]:
            copy.wait()
        for copy in (m_down, m_up):
            copy.wait()

        @pl.when(sec == 0)
        def _():
            first_load.wait()
            x_down.wait()
            x_up.wait()

        @pl.when(sec == 1)
        def _():
            last_load.wait()

            @pl.loop(0, batches)
            def _(b):
                given(b)

        @pl.loop(0, batches)
        def _(b):
            @pl.when(sec == 1)
            def _():
                for copy in relay(b):
                    copy.wait_recv()

            forward(b)

            @pl.when(sec == 0)
            def _():
                for copy in relay(b):
                    copy.start()

        @pl.when(sec == 0)
        def _():
            lax.fori_loop(0, batches, transposes, 0)

        def rows_of(c, size):
            return pl.ds(pl.multiple_of(c * size, size), size)

        def turned(p):
            if stages <= 2:
                return 0 * p
            return lax.rem(p, 2) * side(1) + (1 - jnp.minimum(lax.rem(p, 4), 1)) * (1 - side(1))

        def bit_of(p, k):
            bits = list(z.bits)
            if stages > 2:
                bits[1], bits[2] = bits[2], bits[1]
            return z.bits[k] + (bits[k] - z.bits[k]) * turned(p)

        def piece_copy(p, k):
            return remote(gives[k].at[p], gets[k].at[p], p_s.at[p, k], p_r.at[p, k], (sec, mate(bit_of(p, k))))

        slots_held, ahead = 4, 2

        def piece_start(p):
            left = z.left(p)
            sides = [left_t[left, rows_of(c, half), :] for c in (1 - side(1), side(1))]
            value = dot(jnp.concatenate(sides, axis=0), right_t[z.right(p)])
            gives[0][p] = value[0:half].astype(LOW)
            piece_copy(p, 0).start()
            acc[lax.rem(p, slots_held)] = value[half : 2 * half].astype(LOW)

        def piece_first(p):
            piece_copy(p, 0).wait()
            here = side(bit_of(p, 1))
            run = half // 4
            for s, to in ((1 - here, gives[1]), (here, keeps[0])):
                for j in range(2):
                    at = rows_of((1 - turned(p)) * (2 * s + j) + turned(p) * (2 * j + s), run)
                    value = acc[lax.rem(p, slots_held), at, :].astype(F32) + gets[0][p, at, :].astype(F32)
                    to[p, j * run : (j + 1) * run, :] = value.astype(to.dtype)
                if to is gives[1]:
                    piece_copy(p, 1).start()

        def piece_step(p, k):
            size = half >> k
            piece_copy(p, k).wait()
            if k == stages - 1:
                o_piece[p] = keeps[k - 1][p] + gets[k][p].astype(F32)
                return
            here = side(bit_of(p, k + 1))
            for to, c in ((gives[k + 1], 1 - here), (keeps[k], here)):
                at = rows_of(c, size // 2)
                to[p] = (keeps[k - 1][p, at, :] + gets[k][p, at, :].astype(F32)).astype(to.dtype)
                if to is gives[k + 1]:
                    piece_copy(p, k + 1).start()

        def only_first(body):
            if z.scatter:
                pl.when(sec == 0)(body)

        for t in reversed(range(z.turns)):

            @pl.when(sec == 0)
            def _(t=t):
                for i in range(many):
                    relay_back(t * many + i).wait_recv()
                    given(t * many + i)

            back_ffn(t)
            back_middle(t)
            back_attention(t)
            if t == 0:

                @only_first
                def _():
                    pl.loop(0, groups)(piece_start)
                    pl.loop(0, ahead)(piece_first)

            back_second(t)

        @pl.when(sec == 1)
        def _():
            lax.fori_loop(0, batches, transposes, 0)

        lines = [sm[b, m : m + 1, :] for b in range(batches) for m in range(z.meshes)]
        for line in (6, 7):
            lines.append(sum(sm[b, line : line + 1, :] for b in range(batches)))
        lines.append(jnp.zeros((16 - len(lines), sm.shape[2]), F32))
        small = jnp.concatenate(lines, axis=0)

        def finish():
            @pl.loop(0, batches)
            def _(b):
                @pl.when(sec == 0)
                def _():
                    for copy in relay(b):
                        copy.wait_send()

                @pl.when(sec == 1)
                def _():
                    relay_back(b).wait_send()

                for copy in halos(b):
                    copy.wait_send()

        if not z.scatter:
            small_out[...] = small
            table_out[...] = emb[...]
            finish()
            return

        def ring_copy(k):
            return remote(msend.at[k], mrecv.at[k], m_s.at[k], m_r.at[k], (sec, mate(1 << k)))

        def ring_start(k, value):
            msend[k] = value.astype(LOW)
            ring_copy(k).start()

        def ring_end(k):
            ring_copy(k).wait_recv()
            value = msend[k].astype(F32) + mrecv[k].astype(F32)
            if k + 1 < z.rings:
                ring_start(k + 1, value)
            else:
                tot[...] = value

        ring_start(0, small)

        lags = [0, 3] + [7 + 4 * k for k in range(stages - 1)]
        begun, summed = (1 - sec) * groups, (1 - sec) * ahead

        @pl.loop(0, npiece + lags[-1])
        def _(p):
            @pl.when((p >= begun) & (p < npiece))
            def _():
                piece_start(p)

            @pl.when((p >= summed + lags[1]) & (p < npiece + lags[1]))
            def _():
                piece_first(p - lags[1])

            for k in range(1, stages):
                lag = lags[k + 1]

                @pl.when((p >= lag) & (p < npiece + lag))
                def _(k=k, lag=lag):
                    piece_step(p - lag, k)

            for k in range(z.rings):

                @pl.when(p == 9 + 3 * k)
                def _(k=k):
                    ring_end(k)

            @pl.when(p == 7 + 3 * z.rings)
            def _():
                finish()
                count = batches * z.meshes
                table = emb[pl.ds(pl.multiple_of(me * own, own), own), :]
                grad = jnp.zeros((own, 4 * width), F32)
                for k in range(count):
                    grad = grad + table[:, k : k + 1] * tot[k : k + 1, :]
                o_mod[0] = grad
                cols = 4 * width // shards
                mine = tot[:, pl.ds(pl.multiple_of(me * cols, cols), cols)]
                o_line[0:1, :] = jnp.sum(mine[0:count], axis=0, keepdims=True)
                o_line[1:2, :] = mine[count : count + 1]
                ratio = 128 // own
                line = tot[:, pl.ds(pl.multiple_of(me // ratio * 128, 128), 128)][count + 1 : count + 2]
                value = line
                for k in range(1, ratio):
                    rolled = jnp.concatenate([line[:, k * own :], line[:, : k * own]], axis=1)
                    value = jnp.where(me % ratio == k, rolled, value)
                o_line[2:3, :] = value

        for k in range(z.rings):
            ring_copy(k).wait_send()

    return kernel


def layout_of(z):
    own, groups = z.own, z.groups

    def kernel(
        lo, ig, piece, mod, line,
        o_lo, o_ig, o_qkv, o_out, o_up, o_upb, o_down, o_downb, o_mod, o_modb,
        sems,
    ):
        targets = [o_down.at[0, pl.ds(q * own, own), :] for q in range(groups)]
        targets += [o_up.at[0, :, pl.ds(q * TILE, TILE)] for q in range(groups)]
        targets += [o_out.at[0]] + [o_qkv.at[0, :, pl.ds(q * TILE, TILE)] for q in range(3)]
        moves = [(lo, o_lo), (ig, o_ig), (mod, o_mod)]
        moves += [(piece.at[k], target) for k, target in enumerate(targets)]
        copies = [pltpu.make_async_copy(a, b, sems.at[k]) for k, (a, b) in enumerate(moves)]
        for copy in copies:
            copy.start()
        o_modb[...] = line[0:1, :]
        o_upb[...] = line[1:2, :]
        o_downb[...] = line[2:3, 0:own]
        for copy in copies:
            copy.wait()

    return kernel


def body(
    inputs,
    cotangent,
    neighbours,
    mesh_ids,
    noise_sigma,
    w_qkv,
    w_out,
    w_up,
    b_up,
    w_down,
    b_down,
    w_mod,
    b_mod,
):
    shards = lax.axis_size("nodes")
    z = Sizes(inputs, neighbours, noise_sigma, w_up, shards)
    batches, rows, width, hidden, many = z.batches, z.rows, z.width, z.hidden, z.together
    own, npiece = z.own, z.pieces
    shape = jax.ShapeDtypeStruct
    stack = shape((1, batches, rows, width), LOW)
    outs = [stack, stack]
    sides = [(z.lefts, TILE, batches * rows), (z.rights, batches * rows, TILE)]
    if z.scatter:
        outs = [pltpu.VMEM(stack.shape, LOW)] * 2
        outs += [pltpu.VMEM((npiece, own, TILE), F32), pltpu.VMEM((1, own, 4 * width), F32), pltpu.VMEM((8, 128), F32)]
        scratch = [pltpu.VMEM(side, LOW) for side in sides]
    else:
        outs += [shape(side, LOW) for side in sides] + [shape((16, hidden), F32), shape((width, 128), F32)]
        scratch = []
    dma = pltpu.SemaphoreType.DMA
    scratch += [
        pltpu.VMEM((width, 3 * width), LOW),
        pltpu.VMEM((width, width), LOW),
        pltpu.VMEM((width, hidden), LOW),
        pltpu.VMEM((hidden, width), LOW),
        pltpu.VMEM((width, 4 * width), LOW),
        pltpu.VMEM((batches, z.ext, width), LOW),
        pltpu.VMEM((batches, rows, width), LOW),
        pltpu.VMEM((z.ext, 128), F32),
        pltpu.VMEM((16, rows), LOW),
        pltpu.VMEM((rows, z.window), F32),
        pltpu.VMEM((rows, z.window), LOW),
        pltpu.VMEM((rows, z.window), F32),
        pltpu.VMEM((batches, 8, 4 * width), F32),
        pltpu.VMEM((width, 128), F32),
        pltpu.VMEM((z.ext, width), LOW),
        pltpu.VMEM((batches, rows, width), LOW),
        pltpu.VMEM((batches, rows, width), F32),
        pltpu.VMEM((batches, rows, 128), F32),
        pltpu.VMEM((batches, rows, width), LOW),
        pltpu.VMEM((batches, z.window, 2 * width), LOW),
        pltpu.VMEM((many * HEADS, rows, z.window), F32),
        pltpu.VMEM((batches, HEADS, rows, z.window), F32),
        pltpu.VMEM((batches, HEADS, rows, z.window), LOW),
        pltpu.VMEM((batches, rows, width), LOW),
        pltpu.VMEM((batches, rows, width), LOW),
        pltpu.VMEM((batches, rows, width), F32),
        pltpu.VMEM((batches, rows, 128), F32),
        pltpu.VMEM((rows, width), F32),
        pltpu.VMEM((batches, rows, hidden), LOW),
        pltpu.VMEM((batches, rows, hidden), LOW),
        pltpu.VMEM((many * rows, width), LOW),
        pltpu.VMEM((many * rows, width), F32),
        pltpu.VMEM((many * HEADS, rows, z.window), LOW),
        pltpu.VMEM((many, rows, width), F32),
        pltpu.VMEM((many, rows, 2 * width), F32),
        pltpu.VMEM((batches, 2, REACH, 2 * width), LOW),
        pltpu.VMEM((batches, 2, REACH, 2 * width), LOW),
        pltpu.VMEM((batches, 8, hidden), F32),
        dma((7,)),
        dma((2,)),
        dma((2,)),
        dma((2,)),
        dma((2,)),
        dma((batches, 3)),
        dma((batches, 3)),
        dma((batches, 2)),
        dma((batches, 2)),
        dma((batches,)),
        dma((batches,)),
    ]
    if z.scatter:
        stages = len(z.bits)
        sizes = [TILE >> (k + 1) for k in range(stages)]
        scratch += [pltpu.VMEM((npiece, size, TILE), LOW) for size in sizes + sizes]
        scratch += [pltpu.VMEM((npiece, size, TILE), F32) for size in sizes[1:]]
        scratch += [
            pltpu.VMEM((4, sizes[0], TILE), LOW),
            pltpu.VMEM((z.rings, 16, hidden), LOW),
            pltpu.VMEM((z.rings, 16, hidden), LOW),
            pltpu.VMEM((16, hidden), F32),
            dma((npiece, stages)),
            dma((npiece, stages)),
            dma((z.rings,)),
            dma((z.rings,)),
        ]
    hbm = pl.BlockSpec(memory_space=pl.ANY)
    vmem = pl.BlockSpec(memory_space=pltpu.VMEM)
    smem = pl.BlockSpec(memory_space=pltpu.SMEM)
    got = pl.pallas_call(
        kernel_of(z),
        out_shape=outs,
        in_specs=[hbm, hbm, vmem, vmem, smem, hbm, hbm, hbm, vmem, hbm, vmem, hbm, vmem],
        out_specs=[vmem] * len(outs),
        scratch_shapes=scratch,
        compiler_params=pltpu.CompilerParams(
            collective_id=0, has_side_effects=True, vmem_limit_bytes=61 * 2**20
        ),
    )(
        inputs,
        cotangent,
        neighbours.T,
        mesh_ids.reshape(1, rows),
        noise_sigma.T,
        w_qkv,
        w_out,
        w_up,
        b_up,
        w_down,
        b_down,
        w_mod,
        b_mod,
    )
    if z.scatter:
        lo, ig, piece, mod, line = got
        return tuple(
            pl.pallas_call(
                layout_of(z),
                out_shape=[
                    stack,
                    stack,
                    shape((1, own, 3 * width), F32),
                    shape((1, own, width), F32),
                    shape((1, own, hidden), F32),
                    shape((1, hidden // shards), F32),
                    shape((1, hidden // shards, width), F32),
                    shape((1, own), F32),
                    shape((1, own, 4 * width), F32),
                    shape((1, 4 * width // shards), F32),
                ],
                in_specs=[vmem] * 5,
                out_specs=[hbm, hbm, hbm, hbm, hbm, vmem, hbm, vmem, hbm, vmem],
                scratch_shapes=[dma((npiece + 3,))],
                compiler_params=pltpu.CompilerParams(vmem_limit_bytes=2 * 2**20),
            )(lo, ig, piece, mod, line)
        )
    lo, ig, left_t, right_t, small, table = got
    groups = z.groups

    def summed(value):
        return lax.psum_scatter(value, "nodes", scatter_dimension=0, tiled=True)

    def wide_sum(left, first, last):
        return summed(jnp.concatenate([dot(left_t[left], right_t[r]) for r in range(first, last)], axis=1))[None]

    down = [dot(left_t[q], right_t[0]).reshape(TILE // 32, 32, TILE) for q in range(groups)]
    down = jnp.stack(down, axis=1)
    count = batches * z.meshes
    small = lax.psum(small, "nodes")
    me = lax.axis_index("nodes")
    mod = jnp.dot(table[:, :count], small[:count], precision=lax.Precision.HIGHEST)

    def mine(value):
        size = value.shape[0] // shards
        return lax.dynamic_slice_in_dim(value, me * size, size, axis=0)[None]

    return (
        lo,
        ig,
        wide_sum(groups + 2, 2 + groups, 5 + groups),
        wide_sum(groups + 1, 1 + groups, 2 + groups),
        wide_sum(groups, 1, 1 + groups),
        mine(small[count]),
        summed(down.reshape(hidden, width))[None],
        mine(small[count + 1, :width]),
        mine(mod),
        mine(jnp.sum(small[:count], axis=0)),
    )


def solution(mesh):
    return jax.shard_map(
        body,
        mesh=mesh,
        in_specs=(
            P(None, "nodes", None),
            P(None, "nodes", None),
            P("nodes", None),
            P("nodes"),
            P(),
            P("section", None, None),
            P("section", None, None),
            P("section", None, None),
            P("section", None),
            P("section", None, None),
            P("section", None),
            P("section", None, None),
            P("section", None),
        ),
        out_specs=(
            P("section", None, "nodes", None),
            P("section", None, "nodes", None),
            P("section", "nodes", None),
            P("section", "nodes", None),
            P("section", "nodes", None),
            P("section", "nodes"),
            P("section", "nodes", None),
            P("section", "nodes"),
            P("section", "nodes", None),
            P("section", "nodes"),
        ),
        check_vma=False,
    )
```

```python
import jax
import jax.numpy as jnp
from jax import lax
from jax.experimental import pallas as pl
from jax.experimental.pallas import tpu as pltpu
from jax.sharding import PartitionSpec as P

HEADS = 4
REACH = 32
EPSILON = 1e-06
MASKED = -1e9
ABSENT = -2e38
TILE = 512
TOGETHER = 2
MESH = pl.DeviceIdType.MESH
F32, LOW = jnp.float32, jnp.bfloat16


def dot(a, b):
    return lax.dot_general(a, b, (((1,), (0,)), ((), ())), preferred_element_type=F32)


def dot_nt(a, b):
    return lax.dot_general(a, b, (((1,), (1,)), ((), ())), preferred_element_type=F32)


def dot_tn(a, b):
    return lax.dot_general(a, b, (((0,), (0,)), ((), ())), preferred_element_type=F32)


class Sizes:
    def __init__(self, inputs, neighbours, noise, w_up, shards):
        self.batches, self.rows, self.width = inputs.shape
        self.together = TOGETHER if self.batches % TOGETHER == 0 else 1
        self.turns = self.batches // self.together
        self.slots = neighbours.shape[1]
        self.meshes = noise.shape[1]
        self.hidden = w_up.shape[2]
        self.shards = shards
        self.ext = self.rows + 2 * REACH
        self.window = (self.ext // 128 + 1) * 128
        self.groups = self.hidden // TILE
        self.own = self.width // shards
        self.scatter = self.own % 16 == 0
        self.pieces = 2 * self.groups + 4
        self.lefts = 3 + self.groups
        self.rights = 2 + self.groups + 3
        self.rings = max(shards.bit_length() - 1, 1)

        self.bits = [1 << k for k in range(shards.bit_length() - 1)]

    def left(self, p):
        n = self.groups
        return jnp.minimum(p, n) + lax.div(p, 2 * n) + lax.div(p, 2 * n + 1)

    def right(self, p):
        return jnp.maximum(p - (self.groups - 1), 0)


def kernel_of(z):
    batches, rows, width, ext, window = z.batches, z.rows, z.width, z.ext, z.window
    groups, shards, own, many = z.groups, z.shards, z.own, z.together
    head = width // HEADS
    score_scale = head ** (-0.5)
    log2e = 1.4426950408889634
    npiece = z.pieces
    half = TILE // 2
    stages = len(z.bits)
    g_out, g_q, g_k = 1 + groups, 2 + groups, 3 + groups

    def position(owner):
        if not z.scatter:
            return owner
        place = 0
        for bit in z.bits:
            place = 2 * place + owner // bit % 2
        return place

    def kernel(
        inputs, cotangent, neighbours, mesh_ids, sigma,
        w_qkv, w_out, w_up, b_up, w_down, b_down, w_mod, b_mod,
        lo, ig, *rest,
    ):
        if z.scatter:
            o_piece, o_mod, o_line, left_t, right_t = rest[:5]
            rest = rest[5:]
        else:
            left_t, right_t, small_out, table_out = rest[:4]
            rest = rest[4:]
        (
            wq, wo, wu, wd, wm, xext, dybuf, sel, pick, cnt, few, bias, mod, emb,
            n1, n1s, ua, ia, qb, kvext, sbuf, af, ca, obs, n2s, ub, ib, tb, fp, hs,
            ob, dbuf, cds, dx1, dkv, hsend, hrecv, sm,
            lsem, hx_s, hx_r, hm_s, hm_r, fx_s, fx_r, bh_s, bh_r, bx_s, bx_r,
        ) = rest[:49]
        rest = rest[49:]
        if z.scatter:
            gives, gets, keeps = rest[:stages], rest[stages : 2 * stages], rest[2 * stages : 3 * stages - 1]
            acc, msend, mrecv, tot, p_s, p_r, m_s, m_r = rest[3 * stages - 1 :]

        sec = lax.axis_index("section")
        me = lax.axis_index("nodes")
        up = lax.rem(me + 1, shards)
        down = lax.rem(me + shards - 1, shards)
        other = 1 - sec
        def local(src, dst, k):
            return pltpu.make_async_copy(src, dst, lsem.at[k])

        loads = [
            local(w_mod.at[0], wm, 0),
            local(w_qkv.at[0], wq, 1),
            local(w_out.at[0], wo, 2),
            local(w_up.at[0], wu, 3),
            local(w_down.at[0], wd, 4),
        ]
        own_rows = pl.ds(REACH, rows)
        first_load = local(inputs, xext.at[:, own_rows, :], 5)
        last_load = local(cotangent, dybuf, 6)
        loads[0].start()

        @pl.when(sec == 0)
        def _():
            first_load.start()

        for copy in loads[1:]:
            copy.start()

        @pl.when(sec == 1)
        def _():
            last_load.start()

        def side(bit):
            return lax.rem(lax.div(me, bit), 2)

        def mate(bit):
            return me + bit - 2 * bit * side(bit)

        barrier = pltpu.get_barrier_semaphore()
        mates = [(sec, up), (sec, down), (other, me), (other, up), (other, down)]
        if z.scatter:
            mates += [(sec, mate(bit)) for bit in z.bits[1:]]
        for peer in mates:
            pl.semaphore_signal(barrier, inc=1, device_id=peer, device_id_type=MESH)
        pl.semaphore_wait(barrier, len(mates))

        def remote(src, dst, s_sem, r_sem, peer):
            return pltpu.make_async_remote_copy(
                src_ref=src, dst_ref=dst, send_sem=s_sem, recv_sem=r_sem, device_id=peer, device_id_type=MESH
            )

        low_rows, top_rows = pl.ds(0, REACH), pl.ds(REACH + rows, REACH)
        head_rows, tail_rows = pl.ds(REACH, REACH), pl.ds(rows, REACH)
        x_down = remote(inputs.at[:, pl.ds(0, REACH), :], xext.at[:, top_rows, :], hx_s.at[0], hx_r.at[0], (sec, down))
        x_up = remote(inputs.at[:, pl.ds(rows - REACH, REACH), :], xext.at[:, low_rows, :], hx_s.at[1], hx_r.at[1], (sec, up))

        @pl.when(sec == 0)
        def _():
            x_down.start()
            x_up.start()

        ids = jnp.broadcast_to(mesh_ids[...].astype(F32), (128, rows))
        sel[own_rows, :] = ids.T
        sample = lax.broadcasted_iota(jnp.int32, (16, rows), 0).astype(F32)
        pick[...] = jnp.where(ids[0:16] == sample, 1.0, 0.0).astype(LOW)
        m_down = remote(sel.at[head_rows, :], sel.at[top_rows, :], hm_s.at[0], hm_r.at[0], (sec, down))
        m_up = remote(sel.at[tail_rows, :], sel.at[low_rows, :], hm_s.at[1], hm_r.at[1], (sec, up))
        m_down.start()
        m_up.start()

        kvext[:, ext:window, :] = jnp.zeros((batches, window - ext, 2 * width), LOW)
        sm[...] = jnp.zeros(sm.shape, F32)

        slots = neighbours[...].astype(F32)
        slots = jnp.concatenate([slots, jnp.zeros((128 - z.slots, rows), F32)], axis=0).T
        slots = jnp.where(slots >= 0, slots - (me * rows - REACH).astype(F32), float(ext))
        column = lax.broadcasted_iota(jnp.int32, (rows, window), 1).astype(F32)
        counts = jnp.zeros((rows, window), F32)
        for n in range(z.slots):
            counts = counts + jnp.where(slots[:, n : n + 1] == column, 1.0, 0.0)
        cnt[...] = counts
        few[...] = counts.astype(LOW)
        bias[...] = jnp.where(counts > 0, jnp.where(column == ext, MASKED * log2e, 0.0), ABSENT)

        row_no = lax.broadcasted_iota(jnp.int32, (16, width // 2), 0)
        level = jnp.ones((16, width // 2), F32)
        for b in range(batches):
            for m in range(z.meshes):
                level = jnp.where(row_no == b * z.meshes + m, sigma[m, b], level)
        place = lax.broadcasted_iota(jnp.int32, (16, width // 2), 1).astype(F32)
        frequency = 3.0 * jnp.exp(-jnp.log(100.0) * place / (width // 2))
        angles = jnp.log(level) * frequency
        embedded = jnp.concatenate([jnp.sin(angles), jnp.cos(angles)], axis=1).astype(LOW)
        padded = jnp.concatenate([embedded.astype(F32), jnp.zeros((112, width), F32)], axis=0)
        emb[...] = padded.T
        loads[0].wait()
        for g in range(4):
            cols = pl.ds(g * width, width)
            table = dot(embedded, wm[:, cols]) + b_mod[:, cols] + (1.0 - g % 2)
            for b in range(batches):
                mod[b, 0 : z.meshes, cols] = table[b * z.meshes : (b + 1) * z.meshes]

        def mod_rows(b, part, ids_rows):
            cols = pl.ds(part * width, width)
            value = jnp.broadcast_to(mod[b, 0:1, cols], (ids_rows.shape[0], width))
            for m in range(1, z.meshes):
                value = jnp.where(ids_rows > m - 0.5, mod[b, m : m + 1, cols], value)
            return value

        def wide(ids_rows):
            return jnp.concatenate([ids_rows] * (width // 128), axis=1)

        def unit(x):
            centred = x - jnp.mean(x, axis=-1, keepdims=True)
            inv = lax.rsqrt(jnp.mean(centred * centred, axis=-1, keepdims=True) + EPSILON)
            return centred * inv, inv

        def span_of(start, size):
            if isinstance(start, int):
                return pl.ds(start, size)
            return pl.ds(pl.multiple_of(start, size), size)

        def batch_cols(b):
            return span_of(b * rows, rows)

        def turn_cols(t):
            return span_of(t * many * rows, many * rows)

        def turn_of(ref, t):
            return ref[pl.ds(t * many, many)].reshape(many * rows, ref.shape[2])

        span = own if z.scatter else 32

        def transposes(b, carry):
            for first, ref in ((groups, n2s), (groups + 1, obs), (groups + 2, n1s)):
                turned = ref[b].T
                for owner in range(TILE // span):
                    at = position(owner) * span
                    left_t[first, at : at + span, batch_cols(b)] = turned[owner * span : (owner + 1) * span]
            run = groups * span
            for g in range(groups):
                turned = hs[b, :, g * TILE : (g + 1) * TILE].T
                for k in range(TILE // span):
                    at = g * TILE + k * span
                    owner, part = at // run, at % run // span
                    to = position(owner) * span
                    left_t[part, to : to + span, batch_cols(b)] = turned[k * span : (k + 1) * span]
            return carry

        heads = [slice(h * head, (h + 1) * head) for h in range(HEADS)]
        heads_v = [slice(width + h * head, width + (h + 1) * head) for h in range(HEADS)]
        tiles = [slice(g * TILE, (g + 1) * TILE) for g in range(groups)]
        thirds = [slice(g * width, (g + 1) * width) for g in range(3)]

        def forward(b):
            ids_rows = wide(sel[0:ext, :])
            u, inv = unit(xext[b].astype(F32))
            normed = (u * mod_rows(b, 0, ids_rows) + mod_rows(b, 1, ids_rows)).astype(LOW)
            n1[...] = normed
            n1s[b] = normed[REACH : REACH + rows]
            ua[b] = u[REACH : REACH + rows]
            ia[b] = jnp.broadcast_to(inv[REACH : REACH + rows], (rows, 128))
            kvext[b, 0:ext, thirds[0]] = dot(n1[...], wq[:, thirds[1]]).astype(LOW)
            qb[b] = dot(n1s[b], wq[:, thirds[0]]).astype(LOW)
            for h in range(HEADS):
                sbuf[h] = dot_nt(qb[b, :, heads[h]], kvext[b, :, heads[h]]) * (score_scale * log2e) + bias[...]
            kvext[b, 0:ext, thirds[1]] = dot(n1[...], wq[:, thirds[2]]).astype(LOW)
            for h in range(HEADS):
                s = sbuf[h]
                e = jnp.exp2(s - jnp.max(s, axis=-1, keepdims=True))
                a = e * (1.0 / jnp.sum(e * cnt[...], axis=-1, keepdims=True))
                af[b, h] = a
                ca[b, h] = a.astype(LOW) * few[...]
            for h in range(HEADS):
                obs[b, :, heads[h]] = dot(ca[b, h], kvext[b, :, heads_v[h]]).astype(LOW)

            x1 = xext[b, own_rows, :].astype(F32) + dot(obs[b], wo[...])
            u, inv = unit(x1)
            ub[b] = u
            ib[b] = jnp.broadcast_to(inv, (rows, 128))
            ids_rows = wide(sel[own_rows, :])
            n2s[b] = (u * mod_rows(b, 2, ids_rows) + mod_rows(b, 3, ids_rows)).astype(LOW)
            tb[...] = x1 + b_down[...]
            for gs in tiles:
                gate = dot(n2s[b], wu[:, gs]) + b_up[:, gs]
                s = 0.5 + 0.5 * jnp.tanh(0.5 * gate)
                hid = gate * s
                fp[b, :, gs] = (s + hid * (1.0 - s)).astype(LOW)
                hid = hid.astype(LOW)
                hs[b, :, gs] = hid
                tb[...] += dot(hid, wd[gs, :])
            lo[0, b] = tb[...].astype(LOW)

        def relay(b):
            return [
                remote(lo.at[0, b], xext.at[b, own_rows, :], fx_s.at[b, 0], fx_r.at[b, 0], (other, me)),
                remote(lo.at[0, b, pl.ds(0, REACH), :], xext.at[b, top_rows, :], fx_s.at[b, 1], fx_r.at[b, 1], (other, down)),
                remote(lo.at[0, b, pl.ds(rows - REACH, REACH), :], xext.at[b, low_rows, :], fx_s.at[b, 2], fx_r.at[b, 2], (other, up)),
            ]

        def norm_back(d, u, inv, scale):
            scaled = d * scale
            return inv * (
                scaled
                - jnp.mean(scaled, axis=-1, keepdims=True)
                - u * jnp.mean(scaled * u, axis=-1, keepdims=True)
            )

        def mod_sums(b, part, d, u):
            for k, value in enumerate((d * u, d)):
                total = dot(pick[...], value.astype(LOW))
                sm[b, 0 : z.meshes, (part + k) * width : (part + k + 1) * width] = total[0 : z.meshes]

        def halos(b):
            return [
                remote(hsend.at[b, 0], hrecv.at[b, 1], bh_s.at[b, 0], bh_r.at[b, 0], (sec, down)),
                remote(hsend.at[b, 1], hrecv.at[b, 0], bh_s.at[b, 1], bh_r.at[b, 1], (sec, up)),
            ]

        def given(b):
            at = batch_cols(b)
            dr = dybuf[b]
            right_t[0, at, :] = dr
            sm[b, 7:8, 0:width] = jnp.sum(dr.astype(F32), axis=0, keepdims=True)
            for g in range(groups):
                right_t[1 + g, at, :] = dot_nt(dr, wd[g * TILE : (g + 1) * TILE, :]).astype(LOW)

        def back_ffn(t):
            at = turn_cols(t)
            dn = jnp.zeros((many * rows, width), F32)
            for g in range(groups):
                gs = slice(g * TILE, (g + 1) * TILE)
                dg = right_t[1 + g, at, :].astype(F32) * turn_of(fp, t)[:, gs].astype(F32)
                sm[t * many, 6:7, gs] = jnp.sum(dg, axis=0, keepdims=True)
                dg = dg.astype(LOW)
                right_t[1 + g, at, :] = dg
                dn = dn + dot_nt(dg, wu[:, gs])
            dbuf[...] = dn

        def back_middle(t):
            at = turn_cols(t)
            ids_rows = wide(sel[own_rows, :])
            for i in range(many):
                b = t * many + i
                d = dbuf[i * rows : (i + 1) * rows]
                u = ub[b]
                grad = dybuf[b].astype(F32) + norm_back(d, u, ib[b][:, 0:1], mod_rows(b, 2, ids_rows))
                mod_sums(b, 2, d, u)
                dx1[i] = grad
                right_t[g_out, batch_cols(b), :] = grad.astype(LOW)
            ob[...] = dot_nt(right_t[g_out, at, :], wo[...]).astype(LOW)

        def back_attention(t):
            units = [(i, h) for i in range(many) for h in range(HEADS)]
            here = [slice(i * rows, (i + 1) * rows) for i in range(many)]
            for i, h in units:
                sbuf[i * HEADS + h] = dot_nt(ob[here[i], heads[h]], kvext[t * many + i, :, heads_v[h]])
            for i, h in units:
                b, k = t * many + i, i * HEADS + h
                a, da = af[b, h], sbuf[k]
                ds = a * (da - jnp.sum(a * cnt[...] * da, axis=-1, keepdims=True))
                cds[k] = ds.astype(LOW) * few[...]
            for i in range(many):
                b = t * many + i
                for h in range(HEADS):
                    dk = dot_tn(cds[i * HEADS + h], qb[b, :, heads[h]]) * score_scale
                    dv = dot_tn(ca[b, h], ob[here[i], heads[h]])
                    for part, cols in ((dk, heads[h]), (dv, heads_v[h])):
                        hsend[b, 0, :, cols] = part[0:REACH].astype(LOW)
                        dkv[i, :, cols] = part[REACH : REACH + rows]
                        hsend[b, 1, :, cols] = part[REACH + rows : ext].astype(LOW)
                for copy in halos(b):
                    copy.start()
            for i, h in units:
                b = t * many + i
                value = dot(cds[i * HEADS + h], kvext[b, :, heads[h]]) * score_scale
                right_t[g_q, batch_cols(b), heads[h]] = value.astype(LOW)

        def back_second(t):
            at = turn_cols(t)
            ids_rows = wide(sel[own_rows, :])
            edge = rows - REACH
            dbuf[...] = dot_nt(right_t[g_q, at, :], wq[:, 0:width])
            for i in range(many):
                b = t * many + i
                for copy in halos(b):
                    copy.wait_recv()
                dkv[i, 0:REACH, :] += hrecv[b, 0].astype(F32)
                dkv[i, edge:rows, :] += hrecv[b, 1].astype(F32)
                d = dbuf[i * rows : (i + 1) * rows]
                for g in range(2):
                    part = dkv[i, :, g * width : (g + 1) * width].astype(LOW)
                    right_t[g_k + g, batch_cols(b), :] = part
                    d = d + dot_nt(part, wq[:, (g + 1) * width : (g + 2) * width])
                u = ua[b]
                grad = dx1[i] + norm_back(d, u, ia[b][:, 0:1], mod_rows(b, 0, ids_rows))
                ig[0, b] = grad.astype(LOW)

                @pl.when(sec == 1)
                def _(b=b):
                    relay_back(b).start()

                mod_sums(b, 0, d, u)

        def relay_back(b):
            return remote(ig.at[0, b], dybuf.at[b], bx_s.at[b], bx_r.at[b], (other, me))

        for copy in loads[1:]:
            copy.wait()
        for copy in (m_down, m_up):
            copy.wait()

        @pl.when(sec == 0)
        def _():
            first_load.wait()
            x_down.wait()
            x_up.wait()

        @pl.when(sec == 1)
        def _():
            last_load.wait()

            @pl.loop(0, batches)
            def _(b):
                given(b)

        @pl.loop(0, batches)
        def _(b):
            @pl.when(sec == 1)
            def _():
                for copy in relay(b):
                    copy.wait_recv()

            forward(b)

            @pl.when(sec == 0)
            def _():
                for copy in relay(b):
                    copy.start()

        @pl.when(sec == 0)
        def _():
            lax.fori_loop(0, batches, transposes, 0)

        def rows_of(c, size):
            return pl.ds(pl.multiple_of(c * size, size), size)

        def turned(p):
            return 1 - jnp.minimum(lax.rem(p + 2 * side(1), 4), 1) if stages > 2 else 0 * p

        def bit_of(p, k):
            bits = list(z.bits)
            if stages > 2:
                bits[1], bits[2] = bits[2], bits[1]
            return z.bits[k] + (bits[k] - z.bits[k]) * turned(p)

        def piece_copy(p, k):
            return remote(gives[k].at[p], gets[k].at[p], p_s.at[p, k], p_r.at[p, k], (sec, mate(bit_of(p, k))))

        slots_held, ahead = 4, 2

        def piece_start(p):
            left = z.left(p)
            sides = [left_t[left, rows_of(c, half), :] for c in (1 - side(1), side(1))]
            value = dot(jnp.concatenate(sides, axis=0), right_t[z.right(p)])
            gives[0][p] = value[0:half].astype(LOW)
            piece_copy(p, 0).start()
            acc[lax.rem(p, slots_held)] = value[half : 2 * half].astype(LOW)

        def piece_first(p):
            piece_copy(p, 0).wait()
            here = side(bit_of(p, 1))
            run = half // 4
            for s, to in ((1 - here, gives[1]), (here, keeps[0])):
                for j in range(2):
                    at = rows_of((1 - turned(p)) * (2 * s + j) + turned(p) * (2 * j + s), run)
                    value = acc[lax.rem(p, slots_held), at, :].astype(F32) + gets[0][p, at, :].astype(F32)
                    to[p, j * run : (j + 1) * run, :] = value.astype(to.dtype)
                if to is gives[1]:
                    piece_copy(p, 1).start()

        def piece_step(p, k):
            size = half >> k
            piece_copy(p, k).wait()
            if k == stages - 1:
                o_piece[p] = keeps[k - 1][p] + gets[k][p].astype(F32)
                return
            here = side(bit_of(p, k + 1))
            for to, c in ((gives[k + 1], 1 - here), (keeps[k], here)):
                at = rows_of(c, size // 2)
                to[p] = (keeps[k - 1][p, at, :] + gets[k][p, at, :].astype(F32)).astype(to.dtype)
                if to is gives[k + 1]:
                    piece_copy(p, k + 1).start()

        def only_first(body):
            if z.scatter:
                pl.when(sec == 0)(body)

        for t in reversed(range(z.turns)):

            @pl.when(sec == 0)
            def _(t=t):
                for i in range(many):
                    relay_back(t * many + i).wait_recv()
                    given(t * many + i)

            back_ffn(t)
            back_middle(t)
            back_attention(t)
            if t == 0:

                @only_first
                def _():
                    pl.loop(0, groups)(piece_start)
                    pl.loop(0, ahead)(piece_first)

            back_second(t)

        @pl.when(sec == 1)
        def _():
            lax.fori_loop(0, batches, transposes, 0)

        lines = [sm[b, m : m + 1, :] for b in range(batches) for m in range(z.meshes)]
        for line in (6, 7):
            lines.append(sum(sm[b, line : line + 1, :] for b in range(batches)))
        lines.append(jnp.zeros((16 - len(lines), sm.shape[2]), F32))
        small = jnp.concatenate(lines, axis=0)

        def finish():
            @pl.loop(0, batches)
            def _(b):
                @pl.when(sec == 0)
                def _():
                    for copy in relay(b):
                        copy.wait_send()

                @pl.when(sec == 1)
                def _():
                    relay_back(b).wait_send()

                for copy in halos(b):
                    copy.wait_send()

        if not z.scatter:
            small_out[...] = small
            table_out[...] = emb[...]
            finish()
            return

        def ring_copy(k):
            return remote(msend.at[k], mrecv.at[k], m_s.at[k], m_r.at[k], (sec, mate(1 << k)))

        def ring_start(k, value):
            msend[k] = value.astype(LOW)
            ring_copy(k).start()

        def ring_end(k):
            ring_copy(k).wait_recv()
            value = msend[k].astype(F32) + mrecv[k].astype(F32)
            if k + 1 < z.rings:
                ring_start(k + 1, value)
            else:
                tot[...] = value

        ring_start(0, small)

        lags = [0, 3] + [7 + 4 * k for k in range(stages - 1)]
        begun, summed = (1 - sec) * groups, (1 - sec) * ahead

        @pl.loop(0, npiece + lags[-1])
        def _(p):
            @pl.when((p >= begun) & (p < npiece))
            def _():
                piece_start(p)

            @pl.when((p >= summed + lags[1]) & (p < npiece + lags[1]))
            def _():
                piece_first(p - lags[1])

            for k in range(1, stages):
                lag = lags[k + 1]

                @pl.when((p >= lag) & (p < npiece + lag))
                def _(k=k, lag=lag):
                    piece_step(p - lag, k)

            for k in range(z.rings):

                @pl.when(p == 9 + 3 * k)
                def _(k=k):
                    ring_end(k)

            @pl.when(p == 7 + 3 * z.rings)
            def _():
                finish()
                count = batches * z.meshes
                table = emb[pl.ds(pl.multiple_of(me * own, own), own), :]
                grad = jnp.zeros((own, 4 * width), F32)
                for k in range(count):
                    grad = grad + table[:, k : k + 1] * tot[k : k + 1, :]
                o_mod[0] = grad
                cols = 4 * width // shards
                mine = tot[:, pl.ds(pl.multiple_of(me * cols, cols), cols)]
                o_line[0:1, :] = jnp.sum(mine[0:count], axis=0, keepdims=True)
                o_line[1:2, :] = mine[count : count + 1]
                ratio = 128 // own
                line = tot[:, pl.ds(pl.multiple_of(me // ratio * 128, 128), 128)][count + 1 : count + 2]
                value = line
                for k in range(1, ratio):
                    rolled = jnp.concatenate([line[:, k * own :], line[:, : k * own]], axis=1)
                    value = jnp.where(me % ratio == k, rolled, value)
                o_line[2:3, :] = value

        for k in range(z.rings):
            ring_copy(k).wait_send()

    return kernel


def layout_of(z):
    own, groups = z.own, z.groups

    def kernel(
        lo, ig, piece, mod, line,
        o_lo, o_ig, o_qkv, o_out, o_up, o_upb, o_down, o_downb, o_mod, o_modb,
        sems,
    ):
        targets = [o_down.at[0, pl.ds(q * own, own), :] for q in range(groups)]
        targets += [o_up.at[0, :, pl.ds(q * TILE, TILE)] for q in range(groups)]
        targets += [o_out.at[0]] + [o_qkv.at[0, :, pl.ds(q * TILE, TILE)] for q in range(3)]
        moves = [(lo, o_lo), (ig, o_ig), (mod, o_mod)]
        moves += [(piece.at[k], target) for k, target in enumerate(targets)]
        copies = [pltpu.make_async_copy(a, b, sems.at[k]) for k, (a, b) in enumerate(moves)]
        for copy in copies:
            copy.start()
        o_modb[...] = line[0:1, :]
        o_upb[...] = line[1:2, :]
        o_downb[...] = line[2:3, 0:own]
        for copy in copies:
            copy.wait()

    return kernel


def body(
    inputs,
    cotangent,
    neighbours,
    mesh_ids,
    noise_sigma,
    w_qkv,
    w_out,
    w_up,
    b_up,
    w_down,
    b_down,
    w_mod,
    b_mod,
):
    shards = lax.axis_size("nodes")
    z = Sizes(inputs, neighbours, noise_sigma, w_up, shards)
    batches, rows, width, hidden, many = z.batches, z.rows, z.width, z.hidden, z.together
    own, npiece = z.own, z.pieces
    shape = jax.ShapeDtypeStruct
    stack = shape((1, batches, rows, width), LOW)
    outs = [stack, stack]
    sides = [(z.lefts, TILE, batches * rows), (z.rights, batches * rows, TILE)]
    if z.scatter:
        outs = [pltpu.VMEM(stack.shape, LOW)] * 2
        outs += [pltpu.VMEM((npiece, own, TILE), F32), pltpu.VMEM((1, own, 4 * width), F32), pltpu.VMEM((8, 128), F32)]
        scratch = [pltpu.VMEM(side, LOW) for side in sides]
    else:
        outs += [shape(side, LOW) for side in sides] + [shape((16, hidden), F32), shape((width, 128), F32)]
        scratch = []
    dma = pltpu.SemaphoreType.DMA
    scratch += [
        pltpu.VMEM((width, 3 * width), LOW),
        pltpu.VMEM((width, width), LOW),
        pltpu.VMEM((width, hidden), LOW),
        pltpu.VMEM((hidden, width), LOW),
        pltpu.VMEM((width, 4 * width), LOW),
        pltpu.VMEM((batches, z.ext, width), LOW),
        pltpu.VMEM((batches, rows, width), LOW),
        pltpu.VMEM((z.ext, 128), F32),
        pltpu.VMEM((16, rows), LOW),
        pltpu.VMEM((rows, z.window), F32),
        pltpu.VMEM((rows, z.window), LOW),
        pltpu.VMEM((rows, z.window), F32),
        pltpu.VMEM((batches, 8, 4 * width), F32),
        pltpu.VMEM((width, 128), F32),
        pltpu.VMEM((z.ext, width), LOW),
        pltpu.VMEM((batches, rows, width), LOW),
        pltpu.VMEM((batches, rows, width), F32),
        pltpu.VMEM((batches, rows, 128), F32),
        pltpu.VMEM((batches, rows, width), LOW),
        pltpu.VMEM((batches, z.window, 2 * width), LOW),
        pltpu.VMEM((many * HEADS, rows, z.window), F32),
        pltpu.VMEM((batches, HEADS, rows, z.window), F32),
        pltpu.VMEM((batches, HEADS, rows, z.window), LOW),
        pltpu.VMEM((batches, rows, width), LOW),
        pltpu.VMEM((batches, rows, width), LOW),
        pltpu.VMEM((batches, rows, width), F32),
        pltpu.VMEM((batches, rows, 128), F32),
        pltpu.VMEM((rows, width), F32),
        pltpu.VMEM((batches, rows, hidden), LOW),
        pltpu.VMEM((batches, rows, hidden), LOW),
        pltpu.VMEM((many * rows, width), LOW),
        pltpu.VMEM((many * rows, width), F32),
        pltpu.VMEM((many * HEADS, rows, z.window), LOW),
        pltpu.VMEM((many, rows, width), F32),
        pltpu.VMEM((many, rows, 2 * width), F32),
        pltpu.VMEM((batches, 2, REACH, 2 * width), LOW),
        pltpu.VMEM((batches, 2, REACH, 2 * width), LOW),
        pltpu.VMEM((batches, 8, hidden), F32),
        dma((7,)),
        dma((2,)),
        dma((2,)),
        dma((2,)),
        dma((2,)),
        dma((batches, 3)),
        dma((batches, 3)),
        dma((batches, 2)),
        dma((batches, 2)),
        dma((batches,)),
        dma((batches,)),
    ]
    if z.scatter:
        stages = len(z.bits)
        sizes = [TILE >> (k + 1) for k in range(stages)]
        scratch += [pltpu.VMEM((npiece, size, TILE), LOW) for size in sizes + sizes]
        scratch += [pltpu.VMEM((npiece, size, TILE), F32) for size in sizes[1:]]
        scratch += [
            pltpu.VMEM((4, sizes[0], TILE), LOW),
            pltpu.VMEM((z.rings, 16, hidden), LOW),
            pltpu.VMEM((z.rings, 16, hidden), LOW),
            pltpu.VMEM((16, hidden), F32),
            dma((npiece, stages)),
            dma((npiece, stages)),
            dma((z.rings,)),
            dma((z.rings,)),
        ]
    hbm = pl.BlockSpec(memory_space=pl.ANY)
    vmem = pl.BlockSpec(memory_space=pltpu.VMEM)
    smem = pl.BlockSpec(memory_space=pltpu.SMEM)
    got = pl.pallas_call(
        kernel_of(z),
        out_shape=outs,
        in_specs=[hbm, hbm, vmem, vmem, smem, hbm, hbm, hbm, vmem, hbm, vmem, hbm, vmem],
        out_specs=[vmem] * len(outs),
        scratch_shapes=scratch,
        compiler_params=pltpu.CompilerParams(
            collective_id=0, has_side_effects=True, vmem_limit_bytes=61 * 2**20
        ),
    )(
        inputs,
        cotangent,
        neighbours.T,
        mesh_ids.reshape(1, rows),
        noise_sigma.T,
        w_qkv,
        w_out,
        w_up,
        b_up,
        w_down,
        b_down,
        w_mod,
        b_mod,
    )
    if z.scatter:
        lo, ig, piece, mod, line = got
        return tuple(
            pl.pallas_call(
                layout_of(z),
                out_shape=[
                    stack,
                    stack,
                    shape((1, own, 3 * width), F32),
                    shape((1, own, width), F32),
                    shape((1, own, hidden), F32),
                    shape((1, hidden // shards), F32),
                    shape((1, hidden // shards, width), F32),
                    shape((1, own), F32),
                    shape((1, own, 4 * width), F32),
                    shape((1, 4 * width // shards), F32),
                ],
                in_specs=[vmem] * 5,
                out_specs=[hbm, hbm, hbm, hbm, hbm, vmem, hbm, vmem, hbm, vmem],
                scratch_shapes=[dma((npiece + 3,))],
                compiler_params=pltpu.CompilerParams(vmem_limit_bytes=2 * 2**20),
            )(lo, ig, piece, mod, line)
        )
    lo, ig, left_t, right_t, small, table = got
    groups = z.groups

    def summed(value):
        return lax.psum_scatter(value, "nodes", scatter_dimension=0, tiled=True)

    def wide_sum(left, first, last):
        return summed(jnp.concatenate([dot(left_t[left], right_t[r]) for r in range(first, last)], axis=1))[None]

    down = [dot(left_t[q], right_t[0]).reshape(TILE // 32, 32, TILE) for q in range(groups)]
    down = jnp.stack(down, axis=1)
    count = batches * z.meshes
    small = lax.psum(small, "nodes")
    me = lax.axis_index("nodes")
    mod = jnp.dot(table[:, :count], small[:count], precision=lax.Precision.HIGHEST)

    def mine(value):
        size = value.shape[0] // shards
        return lax.dynamic_slice_in_dim(value, me * size, size, axis=0)[None]

    return (
        lo,
        ig,
        wide_sum(groups + 2, 2 + groups, 5 + groups),
        wide_sum(groups + 1, 1 + groups, 2 + groups),
        wide_sum(groups, 1, 1 + groups),
        mine(small[count]),
        summed(down.reshape(hidden, width))[None],
        mine(small[count + 1, :width]),
        mine(mod),
        mine(jnp.sum(small[:count], axis=0)),
    )


def solution(mesh):
    return jax.shard_map(
        body,
        mesh=mesh,
        in_specs=(
            P(None, "nodes", None),
            P(None, "nodes", None),
            P("nodes", None),
            P("nodes"),
            P(),
            P("section", None, None),
            P("section", None, None),
            P("section", None, None),
            P("section", None),
            P("section", None, None),
            P("section", None),
            P("section", None, None),
            P("section", None),
        ),
        out_specs=(
            P("section", None, "nodes", None),
            P("section", None, "nodes", None),
            P("section", "nodes", None),
            P("section", "nodes", None),
            P("section", "nodes", None),
            P("section", "nodes"),
            P("section", "nodes", None),
            P("section", "nodes"),
            P("section", "nodes", None),
            P("section", "nodes"),
        ),
        check_vma=False,
    )
```

```python
import jax
import jax.numpy as jnp
from jax import lax
from jax.experimental import pallas as pl
from jax.experimental.pallas import tpu as pltpu
from jax.sharding import PartitionSpec as P

HEADS = 4
REACH = 32
EPSILON = 1e-06
MASKED = -1e9
ABSENT = -2e38
TILE = 512
TOGETHER = 2
MESH = pl.DeviceIdType.MESH
F32, LOW = jnp.float32, jnp.bfloat16


def dot(a, b):
    return lax.dot_general(a, b, (((1,), (0,)), ((), ())), preferred_element_type=F32)


def dot_nt(a, b):
    return lax.dot_general(a, b, (((1,), (1,)), ((), ())), preferred_element_type=F32)


def dot_tn(a, b):
    return lax.dot_general(a, b, (((0,), (0,)), ((), ())), preferred_element_type=F32)


class Sizes:
    def __init__(self, inputs, neighbours, noise, w_up, shards):
        self.batches, self.rows, self.width = inputs.shape
        self.together = TOGETHER if self.batches % TOGETHER == 0 else 1
        self.turns = self.batches // self.together
        self.slots = neighbours.shape[1]
        self.meshes = noise.shape[1]
        self.hidden = w_up.shape[2]
        self.shards = shards
        self.ext = self.rows + 2 * REACH
        self.window = (self.ext // 128 + 1) * 128
        self.groups = self.hidden // TILE
        self.own = self.width // shards
        self.scatter = self.own % 16 == 0
        self.pieces = 2 * self.groups + 4
        self.lefts = 3 + self.groups
        self.rights = 2 + self.groups + 3
        self.rings = max(shards.bit_length() - 1, 1)

        self.bits = [1 << k for k in range(shards.bit_length() - 1)]

    def left(self, p):
        n = self.groups
        return jnp.minimum(p, n) + lax.div(p, 2 * n) + lax.div(p, 2 * n + 1)

    def right(self, p):
        return jnp.maximum(p - (self.groups - 1), 0)


def kernel_of(z):
    batches, rows, width, ext, window = z.batches, z.rows, z.width, z.ext, z.window
    groups, shards, own, many = z.groups, z.shards, z.own, z.together
    head = width // HEADS
    score_scale = head ** (-0.5)
    log2e = 1.4426950408889634
    npiece = z.pieces
    half = TILE // 2
    stages = len(z.bits)
    g_out, g_q, g_k = 1 + groups, 2 + groups, 3 + groups

    def position(owner):
        if not z.scatter:
            return owner
        place = 0
        for bit in z.bits:
            place = 2 * place + owner // bit % 2
        return place

    def kernel(
        inputs, cotangent, neighbours, mesh_ids, sigma,
        w_qkv, w_out, w_up, b_up, w_down, b_down, w_mod, b_mod,
        lo, ig, *rest,
    ):
        if z.scatter:
            o_piece, o_mod, o_line, left_t, right_t = rest[:5]
            rest = rest[5:]
        else:
            left_t, right_t, small_out, table_out = rest[:4]
            rest = rest[4:]
        (
            wq, wo, wu, wd, wm, xext, dybuf, sel, pick, cnt, few, bias, mod, emb,
            n1, n1s, ua, ia, qb, kvext, sbuf, af, ca, obs, n2s, ub, ib, tb, fp, hs,
            ob, dbuf, cds, dx1, dkv, hsend, hrecv,
            lsem, hx_s, hx_r, hm_s, hm_r, fx_s, fx_r, bh_s, bh_r, bx_s, bx_r,
        ) = rest[:48]
        rest = rest[48:]
        if z.scatter:
            gives, gets, keeps = rest[:stages], rest[stages : 2 * stages], rest[2 * stages : 3 * stages - 1]
            acc, msend, mrecv, tot, p_s, p_r, m_s, m_r = rest[3 * stages - 1 :]

        sec = lax.axis_index("section")
        me = lax.axis_index("nodes")
        up = lax.rem(me + 1, shards)
        down = lax.rem(me + shards - 1, shards)
        other = 1 - sec
        def local(src, dst, k):
            return pltpu.make_async_copy(src, dst, lsem.at[k])

        loads = [
            local(w_mod.at[0], wm, 0),
            local(w_qkv.at[0], wq, 1),
            local(w_out.at[0], wo, 2),
            local(w_up.at[0], wu, 3),
            local(w_down.at[0], wd, 4),
        ]
        own_rows = pl.ds(REACH, rows)
        first_load = local(inputs, xext.at[:, own_rows, :], 5)
        last_load = local(cotangent, dybuf, 6)
        loads[0].start()

        @pl.when(sec == 0)
        def _():
            first_load.start()

        for copy in loads[1:]:
            copy.start()

        @pl.when(sec == 1)
        def _():
            last_load.start()

        def side(bit):
            return lax.rem(lax.div(me, bit), 2)

        def mate(bit):
            return me + bit - 2 * bit * side(bit)

        barrier = pltpu.get_barrier_semaphore()
        mates = [(sec, up), (sec, down), (other, me), (other, up), (other, down)]
        if z.scatter:
            mates += [(sec, mate(bit)) for bit in z.bits[1:]]
        for peer in mates:
            pl.semaphore_signal(barrier, inc=1, device_id=peer, device_id_type=MESH)
        pl.semaphore_wait(barrier, len(mates))

        def remote(src, dst, s_sem, r_sem, peer):
            return pltpu.make_async_remote_copy(
                src_ref=src, dst_ref=dst, send_sem=s_sem, recv_sem=r_sem, device_id=peer, device_id_type=MESH
            )

        low_rows, top_rows = pl.ds(0, REACH), pl.ds(REACH + rows, REACH)
        head_rows, tail_rows = pl.ds(REACH, REACH), pl.ds(rows, REACH)
        x_down = remote(inputs.at[:, pl.ds(0, REACH), :], xext.at[:, top_rows, :], hx_s.at[0], hx_r.at[0], (sec, down))
        x_up = remote(inputs.at[:, pl.ds(rows - REACH, REACH), :], xext.at[:, low_rows, :], hx_s.at[1], hx_r.at[1], (sec, up))

        @pl.when(sec == 0)
        def _():
            x_down.start()
            x_up.start()

        ids = jnp.broadcast_to(mesh_ids[...].astype(F32), (128, rows))
        sel[own_rows, :] = ids.T
        sample = lax.broadcasted_iota(jnp.int32, (16, rows), 0).astype(F32)
        pick[...] = jnp.where(ids[0:16] == sample, 1.0, 0.0).astype(LOW)
        m_down = remote(sel.at[head_rows, :], sel.at[top_rows, :], hm_s.at[0], hm_r.at[0], (sec, down))
        m_up = remote(sel.at[tail_rows, :], sel.at[low_rows, :], hm_s.at[1], hm_r.at[1], (sec, up))
        m_down.start()
        m_up.start()

        kvext[:, ext:window, :] = jnp.zeros((batches, window - ext, 2 * width), LOW)

        slots = neighbours[...].astype(F32)
        slots = jnp.concatenate([slots, jnp.zeros((128 - z.slots, rows), F32)], axis=0).T
        slots = jnp.where(slots >= 0, slots - (me * rows - REACH).astype(F32), float(ext))
        column = lax.broadcasted_iota(jnp.int32, (rows, window), 1).astype(F32)
        counts = jnp.zeros((rows, window), F32)
        for n in range(z.slots):
            counts = counts + jnp.where(slots[:, n : n + 1] == column, 1.0, 0.0)
        cnt[...] = counts
        few[...] = counts.astype(LOW)
        bias[...] = jnp.where(counts > 0, jnp.where(column == ext, MASKED * log2e, 0.0), ABSENT)

        row_no = lax.broadcasted_iota(jnp.int32, (16, width // 2), 0)
        level = jnp.ones((16, width // 2), F32)
        for b in range(batches):
            for m in range(z.meshes):
                level = jnp.where(row_no == b * z.meshes + m, sigma[m, b], level)
        place = lax.broadcasted_iota(jnp.int32, (16, width // 2), 1).astype(F32)
        frequency = 3.0 * jnp.exp(-jnp.log(100.0) * place / (width // 2))
        angles = jnp.log(level) * frequency
        embedded = jnp.concatenate([jnp.sin(angles), jnp.cos(angles)], axis=1).astype(LOW)
        padded = jnp.concatenate([embedded.astype(F32), jnp.zeros((112, width), F32)], axis=0)
        emb[...] = padded.T
        loads[0].wait()
        for g in range(4):
            cols = pl.ds(g * width, width)
            table = dot(embedded, wm[:, cols]) + b_mod[:, cols] + (1.0 - g % 2)
            for b in range(batches):
                mod[b, 0 : z.meshes, cols] = table[b * z.meshes : (b + 1) * z.meshes]

        def mod_rows(b, part, ids_rows):
            cols = pl.ds(part * width, width)
            value = jnp.broadcast_to(mod[b, 0:1, cols], (ids_rows.shape[0], width))
            for m in range(1, z.meshes):
                value = jnp.where(ids_rows > m - 0.5, mod[b, m : m + 1, cols], value)
            return value

        def wide(ids_rows):
            return jnp.concatenate([ids_rows] * (width // 128), axis=1)

        def unit(x):
            centred = x - jnp.mean(x, axis=-1, keepdims=True)
            inv = lax.rsqrt(jnp.mean(centred * centred, axis=-1, keepdims=True) + EPSILON)
            return centred * inv, inv

        def span_of(start, size):
            if isinstance(start, int):
                return pl.ds(start, size)
            return pl.ds(pl.multiple_of(start, size), size)

        def batch_cols(b):
            return span_of(b * rows, rows)

        def turn_cols(t):
            return span_of(t * many * rows, many * rows)

        def turn_of(ref, t):
            return ref[pl.ds(t * many, many)].reshape(many * rows, ref.shape[2])

        span = own if z.scatter else 32

        def transposes(b, carry):
            for first, ref in ((groups, n2s), (groups + 1, obs), (groups + 2, n1s)):
                turned = ref[b].T
                for owner in range(TILE // span):
                    at = position(owner) * span
                    left_t[first, at : at + span, batch_cols(b)] = turned[owner * span : (owner + 1) * span]
            run = groups * span
            for g in range(groups):
                turned = hs[b, :, g * TILE : (g + 1) * TILE].T
                for k in range(TILE // span):
                    at = g * TILE + k * span
                    owner, part = at // run, at % run // span
                    to = position(owner) * span
                    left_t[part, to : to + span, batch_cols(b)] = turned[k * span : (k + 1) * span]
            return carry

        heads = [slice(h * head, (h + 1) * head) for h in range(HEADS)]
        heads_v = [slice(width + h * head, width + (h + 1) * head) for h in range(HEADS)]
        tiles = [slice(g * TILE, (g + 1) * TILE) for g in range(groups)]
        thirds = [slice(g * width, (g + 1) * width) for g in range(3)]

        def forward(b):
            ids_rows = wide(sel[0:ext, :])
            u, inv = unit(xext[b].astype(F32))
            normed = (u * mod_rows(b, 0, ids_rows) + mod_rows(b, 1, ids_rows)).astype(LOW)
            n1[...] = normed
            n1s[b] = normed[REACH : REACH + rows]
            ua[b] = u[REACH : REACH + rows]
            ia[b] = jnp.broadcast_to(inv[REACH : REACH + rows], (rows, 128))
            kvext[b, 0:ext, thirds[0]] = dot(n1[...], wq[:, thirds[1]]).astype(LOW)
            qb[b] = dot(n1s[b], wq[:, thirds[0]]).astype(LOW)
            for h in range(HEADS):
                sbuf[h] = dot_nt(qb[b, :, heads[h]], kvext[b, :, heads[h]]) * (score_scale * log2e) + bias[...]
            kvext[b, 0:ext, thirds[1]] = dot(n1[...], wq[:, thirds[2]]).astype(LOW)
            for h in range(HEADS):
                s = sbuf[h]
                e = jnp.exp2(s - jnp.max(s, axis=-1, keepdims=True))
                a = e * (1.0 / jnp.sum(e * cnt[...], axis=-1, keepdims=True))
                af[b, h] = a
                ca[b, h] = a.astype(LOW) * few[...]
            for h in range(HEADS):
                obs[b, :, heads[h]] = dot(ca[b, h], kvext[b, :, heads_v[h]]).astype(LOW)

            x1 = xext[b, own_rows, :].astype(F32) + dot(obs[b], wo[...])
            u, inv = unit(x1)
            ub[b] = u
            ib[b] = jnp.broadcast_to(inv, (rows, 128))
            ids_rows = wide(sel[own_rows, :])
            n2s[b] = (u * mod_rows(b, 2, ids_rows) + mod_rows(b, 3, ids_rows)).astype(LOW)
            tb[...] = x1 + b_down[...]
            for gs in tiles:
                gate = dot(n2s[b], wu[:, gs]) + b_up[:, gs]
                s = 0.5 + 0.5 * jnp.tanh(0.5 * gate)
                hid = gate * s
                fp[b, :, gs] = (s + hid * (1.0 - s)).astype(LOW)
                hid = hid.astype(LOW)
                hs[b, :, gs] = hid
                tb[...] += dot(hid, wd[gs, :])
            lo[0, b] = tb[...].astype(LOW)

        def relay(b):
            return [
                remote(lo.at[0, b], xext.at[b, own_rows, :], fx_s.at[b, 0], fx_r.at[b, 0], (other, me)),
                remote(lo.at[0, b, pl.ds(0, REACH), :], xext.at[b, top_rows, :], fx_s.at[b, 1], fx_r.at[b, 1], (other, down)),
                remote(lo.at[0, b, pl.ds(rows - REACH, REACH), :], xext.at[b, low_rows, :], fx_s.at[b, 2], fx_r.at[b, 2], (other, up)),
            ]

        def norm_back(d, u, inv, scale):
            scaled = d * scale
            return inv * (
                scaled
                - jnp.mean(scaled, axis=-1, keepdims=True)
                - u * jnp.mean(scaled * u, axis=-1, keepdims=True)
            )

        def small_sums():
            lines = []
            for b in range(batches):
                sums = []
                for u, at in ((ua[b], width), (ub[b], 0)):
                    d = fp[b, :, at : at + width]
                    sums += [dot(pick[...], (d.astype(F32) * u).astype(LOW)), dot(pick[...], d)]
                lines.append(jnp.concatenate(sums, axis=1)[0 : z.meshes])
            ones = jnp.ones((16, batches * rows), LOW)
            ups = [dot(ones, right_t[1 + g])[0:1] for g in range(groups)]
            lines.append(jnp.concatenate(ups, axis=1))
            blank = jnp.zeros((1, z.hidden - width), F32)
            lines.append(jnp.concatenate([dot(ones, right_t[0])[0:1], blank], axis=1))
            lines.append(jnp.zeros((14 - batches * z.meshes, z.hidden), F32))
            return jnp.concatenate(lines, axis=0)

        def halos(b):
            return [
                remote(hsend.at[b, 0], hrecv.at[b, 1], bh_s.at[b, 0], bh_r.at[b, 0], (sec, down)),
                remote(hsend.at[b, 1], hrecv.at[b, 0], bh_s.at[b, 1], bh_r.at[b, 1], (sec, up)),
            ]

        def given(b):
            at = batch_cols(b)
            dr = dybuf[b]
            right_t[0, at, :] = dr
            for g in range(groups):
                right_t[1 + g, at, :] = dot_nt(dr, wd[g * TILE : (g + 1) * TILE, :]).astype(LOW)

        def back_ffn(t):
            at = turn_cols(t)
            dn = jnp.zeros((many * rows, width), F32)
            for g in range(groups):
                gs = slice(g * TILE, (g + 1) * TILE)
                dg = right_t[1 + g, at, :].astype(F32) * turn_of(fp, t)[:, gs].astype(F32)
                dg = dg.astype(LOW)
                right_t[1 + g, at, :] = dg
                dn = dn + dot_nt(dg, wu[:, gs])
            dbuf[...] = dn

        def back_middle(t):
            at = turn_cols(t)
            ids_rows = wide(sel[own_rows, :])
            for i in range(many):
                b = t * many + i
                d = dbuf[i * rows : (i + 1) * rows]
                u = ub[b]
                grad = dybuf[b].astype(F32) + norm_back(d, u, ib[b][:, 0:1], mod_rows(b, 2, ids_rows))
                fp[b, :, 0:width] = d.astype(LOW)
                dx1[i] = grad
                right_t[g_out, batch_cols(b), :] = grad.astype(LOW)
            ob[...] = dot_nt(right_t[g_out, at, :], wo[...]).astype(LOW)

        def back_attention(t):
            units = [(i, h) for i in range(many) for h in range(HEADS)]
            here = [slice(i * rows, (i + 1) * rows) for i in range(many)]
            for i, h in units:
                sbuf[i * HEADS + h] = dot_nt(ob[here[i], heads[h]], kvext[t * many + i, :, heads_v[h]])
            for i, h in units:
                b, k = t * many + i, i * HEADS + h
                a, da = af[b, h], sbuf[k]
                ds = a * (da - jnp.sum(a * cnt[...] * da, axis=-1, keepdims=True))
                cds[k] = ds.astype(LOW) * few[...]
            for i in range(many):
                b = t * many + i
                for h in range(HEADS):
                    dk = dot_tn(cds[i * HEADS + h], qb[b, :, heads[h]]) * score_scale
                    dv = dot_tn(ca[b, h], ob[here[i], heads[h]])
                    for part, cols in ((dk, heads[h]), (dv, heads_v[h])):
                        hsend[b, 0, :, cols] = part[0:REACH].astype(LOW)
                        dkv[i, :, cols] = part[REACH : REACH + rows]
                        hsend[b, 1, :, cols] = part[REACH + rows : ext].astype(LOW)
                for copy in halos(b):
                    copy.start()
            for i, h in units:
                b = t * many + i
                value = dot(cds[i * HEADS + h], kvext[b, :, heads[h]]) * score_scale
                right_t[g_q, batch_cols(b), heads[h]] = value.astype(LOW)

        def back_second(t):
            at = turn_cols(t)
            ids_rows = wide(sel[own_rows, :])
            edge = rows - REACH
            dbuf[...] = dot_nt(right_t[g_q, at, :], wq[:, 0:width])
            for i in range(many):
                b = t * many + i
                for copy in halos(b):
                    copy.wait_recv()
                dkv[i, 0:REACH, :] += hrecv[b, 0].astype(F32)
                dkv[i, edge:rows, :] += hrecv[b, 1].astype(F32)
                d = dbuf[i * rows : (i + 1) * rows]
                for g in range(2):
                    part = dkv[i, :, g * width : (g + 1) * width].astype(LOW)
                    right_t[g_k + g, batch_cols(b), :] = part
                    d = d + dot_nt(part, wq[:, (g + 1) * width : (g + 2) * width])
                u = ua[b]
                grad = dx1[i] + norm_back(d, u, ia[b][:, 0:1], mod_rows(b, 0, ids_rows))
                ig[0, b] = grad.astype(LOW)

                @pl.when(sec == 1)
                def _(b=b):
                    relay_back(b).start()

                fp[b, :, width : 2 * width] = d.astype(LOW)

        def relay_back(b):
            return remote(ig.at[0, b], dybuf.at[b], bx_s.at[b], bx_r.at[b], (other, me))

        for copy in loads[1:]:
            copy.wait()
        for copy in (m_down, m_up):
            copy.wait()

        @pl.when(sec == 0)
        def _():
            first_load.wait()
            x_down.wait()
            x_up.wait()

        @pl.when(sec == 1)
        def _():
            last_load.wait()

            @pl.loop(0, batches)
            def _(b):
                given(b)

        @pl.loop(0, batches)
        def _(b):
            @pl.when(sec == 1)
            def _():
                for copy in relay(b):
                    copy.wait_recv()

            forward(b)

            @pl.when(sec == 0)
            def _():
                for copy in relay(b):
                    copy.start()

        @pl.when(sec == 0)
        def _():
            lax.fori_loop(0, batches, transposes, 0)

        def rows_of(c, size):
            return pl.ds(pl.multiple_of(c * size, size), size)

        def turned(p):
            if stages <= 2:
                return 0 * p
            return lax.rem(p, 2) * side(1) + (1 - jnp.minimum(lax.rem(p, 4), 1)) * (1 - side(1))

        def bit_of(p, k):
            bits = list(z.bits)
            if stages > 2:
                bits[1], bits[2] = bits[2], bits[1]
            return z.bits[k] + (bits[k] - z.bits[k]) * turned(p)

        def piece_copy(p, k):
            return remote(gives[k].at[p], gets[k].at[p], p_s.at[p, k], p_r.at[p, k], (sec, mate(bit_of(p, k))))

        slots_held, ahead = 4, 2

        def piece_start(p):
            left = z.left(p)
            sides = [left_t[left, rows_of(c, half), :] for c in (1 - side(1), side(1))]
            value = dot(jnp.concatenate(sides, axis=0), right_t[z.right(p)])
            gives[0][p] = value[0:half].astype(LOW)
            piece_copy(p, 0).start()
            acc[lax.rem(p, slots_held)] = value[half : 2 * half].astype(LOW)

        def piece_first(p):
            piece_copy(p, 0).wait()
            here = side(bit_of(p, 1))
            run = half // 4
            for s, to in ((1 - here, gives[1]), (here, keeps[0])):
                for j in range(2):
                    at = rows_of((1 - turned(p)) * (2 * s + j) + turned(p) * (2 * j + s), run)
                    value = acc[lax.rem(p, slots_held), at, :].astype(F32) + gets[0][p, at, :].astype(F32)
                    to[p, j * run : (j + 1) * run, :] = value.astype(to.dtype)
                if to is gives[1]:
                    piece_copy(p, 1).start()

        def piece_step(p, k):
            size = half >> k
            piece_copy(p, k).wait()
            if k == stages - 1:
                o_piece[p] = keeps[k - 1][p] + gets[k][p].astype(F32)
                return
            here = side(bit_of(p, k + 1))
            for to, c in ((gives[k + 1], 1 - here), (keeps[k], here)):
                at = rows_of(c, size // 2)
                to[p] = (keeps[k - 1][p, at, :] + gets[k][p, at, :].astype(F32)).astype(to.dtype)
                if to is gives[k + 1]:
                    piece_copy(p, k + 1).start()

        def only_first(body):
            if z.scatter:
                pl.when(sec == 0)(body)

        for t in reversed(range(z.turns)):

            @pl.when(sec == 0)
            def _(t=t):
                for i in range(many):
                    relay_back(t * many + i).wait_recv()
                    given(t * many + i)

            back_ffn(t)
            back_middle(t)
            back_attention(t)
            if t == 0:

                @only_first
                def _():
                    pl.loop(0, groups)(piece_start)
                    pl.loop(0, ahead)(piece_first)

            back_second(t)

        @pl.when(sec == 1)
        def _():
            lax.fori_loop(0, batches, transposes, 0)

        def finish():
            @pl.loop(0, batches)
            def _(b):
                @pl.when(sec == 0)
                def _():
                    for copy in relay(b):
                        copy.wait_send()

                @pl.when(sec == 1)
                def _():
                    relay_back(b).wait_send()

                for copy in halos(b):
                    copy.wait_send()

        if not z.scatter:
            small_out[...] = small_sums()
            table_out[...] = emb[...]
            finish()
            return

        def ring_copy(k):
            return remote(msend.at[k], mrecv.at[k], m_s.at[k], m_r.at[k], (sec, mate(1 << k)))

        def ring_start(k, value):
            msend[k] = value.astype(LOW)
            ring_copy(k).start()

        def ring_end(k):
            ring_copy(k).wait_recv()
            value = msend[k].astype(F32) + mrecv[k].astype(F32)
            if k + 1 < z.rings:
                ring_start(k + 1, value)
            else:
                tot[...] = value

        lags = [0, 3] + [7 + 4 * k for k in range(stages - 1)]
        begun, summed = (1 - sec) * groups, (1 - sec) * ahead

        @pl.loop(0, npiece + lags[-1])
        def _(p):
            @pl.when((p >= begun) & (p < npiece))
            def _():
                piece_start(p)

            @pl.when((p >= summed + lags[1]) & (p < npiece + lags[1]))
            def _():
                piece_first(p - lags[1])

            for k in range(1, stages):
                lag = lags[k + 1]

                @pl.when((p >= lag) & (p < npiece + lag))
                def _(k=k, lag=lag):
                    piece_step(p - lag, k)

            @pl.when(p == 6)
            def _():
                ring_start(0, small_sums())

            for k in range(z.rings):

                @pl.when(p == 9 + 3 * k)
                def _(k=k):
                    ring_end(k)

            @pl.when(p == 7 + 3 * z.rings)
            def _():
                finish()
                count = batches * z.meshes
                table = emb[pl.ds(pl.multiple_of(me * own, own), own), :]
                grad = jnp.zeros((own, 4 * width), F32)
                for k in range(count):
                    grad = grad + table[:, k : k + 1] * tot[k : k + 1, :]
                o_mod[0] = grad
                cols = 4 * width // shards
                mine = tot[:, pl.ds(pl.multiple_of(me * cols, cols), cols)]
                o_line[0:1, :] = jnp.sum(mine[0:count], axis=0, keepdims=True)
                o_line[1:2, :] = mine[count : count + 1]
                ratio = 128 // own
                line = tot[:, pl.ds(pl.multiple_of(me // ratio * 128, 128), 128)][count + 1 : count + 2]
                value = line
                for k in range(1, ratio):
                    rolled = jnp.concatenate([line[:, k * own :], line[:, : k * own]], axis=1)
                    value = jnp.where(me % ratio == k, rolled, value)
                o_line[2:3, :] = value

        for k in range(z.rings):
            ring_copy(k).wait_send()

    return kernel


def layout_of(z):
    own, groups = z.own, z.groups

    def kernel(
        lo, ig, piece, mod, line,
        o_lo, o_ig, o_qkv, o_out, o_up, o_upb, o_down, o_downb, o_mod, o_modb,
        sems,
    ):
        targets = [o_down.at[0, pl.ds(q * own, own), :] for q in range(groups)]
        targets += [o_up.at[0, :, pl.ds(q * TILE, TILE)] for q in range(groups)]
        targets += [o_out.at[0]] + [o_qkv.at[0, :, pl.ds(q * TILE, TILE)] for q in range(3)]
        moves = [(lo, o_lo), (ig, o_ig), (mod, o_mod)]
        moves += [(piece.at[k], target) for k, target in enumerate(targets)]
        copies = [pltpu.make_async_copy(a, b, sems.at[k]) for k, (a, b) in enumerate(moves)]
        for copy in copies:
            copy.start()
        o_modb[...] = line[0:1, :]
        o_upb[...] = line[1:2, :]
        o_downb[...] = line[2:3, 0:own]
        for copy in copies:
            copy.wait()

    return kernel


def body(
    inputs,
    cotangent,
    neighbours,
    mesh_ids,
    noise_sigma,
    w_qkv,
    w_out,
    w_up,
    b_up,
    w_down,
    b_down,
    w_mod,
    b_mod,
):
    shards = lax.axis_size("nodes")
    z = Sizes(inputs, neighbours, noise_sigma, w_up, shards)
    batches, rows, width, hidden, many = z.batches, z.rows, z.width, z.hidden, z.together
    own, npiece = z.own, z.pieces
    shape = jax.ShapeDtypeStruct
    stack = shape((1, batches, rows, width), LOW)
    outs = [stack, stack]
    sides = [(z.lefts, TILE, batches * rows), (z.rights, batches * rows, TILE)]
    if z.scatter:
        outs = [pltpu.VMEM(stack.shape, LOW)] * 2
        outs += [pltpu.VMEM((npiece, own, TILE), F32), pltpu.VMEM((1, own, 4 * width), F32), pltpu.VMEM((8, 128), F32)]
        scratch = [pltpu.VMEM(side, LOW) for side in sides]
    else:
        outs += [shape(side, LOW) for side in sides] + [shape((16, hidden), F32), shape((width, 128), F32)]
        scratch = []
    dma = pltpu.SemaphoreType.DMA
    scratch += [
        pltpu.VMEM((width, 3 * width), LOW),
        pltpu.VMEM((width, width), LOW),
        pltpu.VMEM((width, hidden), LOW),
        pltpu.VMEM((hidden, width), LOW),
        pltpu.VMEM((width, 4 * width), LOW),
        pltpu.VMEM((batches, z.ext, width), LOW),
        pltpu.VMEM((batches, rows, width), LOW),
        pltpu.VMEM((z.ext, 128), F32),
        pltpu.VMEM((16, rows), LOW),
        pltpu.VMEM((rows, z.window), F32),
        pltpu.VMEM((rows, z.window), LOW),
        pltpu.VMEM((rows, z.window), F32),
        pltpu.VMEM((batches, 8, 4 * width), F32),
        pltpu.VMEM((width, 128), F32),
        pltpu.VMEM((z.ext, width), LOW),
        pltpu.VMEM((batches, rows, width), LOW),
        pltpu.VMEM((batches, rows, width), F32),
        pltpu.VMEM((batches, rows, 128), F32),
        pltpu.VMEM((batches, rows, width), LOW),
        pltpu.VMEM((batches, z.window, 2 * width), LOW),
        pltpu.VMEM((many * HEADS, rows, z.window), F32),
        pltpu.VMEM((batches, HEADS, rows, z.window), F32),
        pltpu.VMEM((batches, HEADS, rows, z.window), LOW),
        pltpu.VMEM((batches, rows, width), LOW),
        pltpu.VMEM((batches, rows, width), LOW),
        pltpu.VMEM((batches, rows, width), F32),
        pltpu.VMEM((batches, rows, 128), F32),
        pltpu.VMEM((rows, width), F32),
        pltpu.VMEM((batches, rows, hidden), LOW),
        pltpu.VMEM((batches, rows, hidden), LOW),
        pltpu.VMEM((many * rows, width), LOW),
        pltpu.VMEM((many * rows, width), F32),
        pltpu.VMEM((many * HEADS, rows, z.window), LOW),
        pltpu.VMEM((many, rows, width), F32),
        pltpu.VMEM((many, rows, 2 * width), F32),
        pltpu.VMEM((batches, 2, REACH, 2 * width), LOW),
        pltpu.VMEM((batches, 2, REACH, 2 * width), LOW),
        dma((7,)),
        dma((2,)),
        dma((2,)),
        dma((2,)),
        dma((2,)),
        dma((batches, 3)),
        dma((batches, 3)),
        dma((batches, 2)),
        dma((batches, 2)),
        dma((batches,)),
        dma((batches,)),
    ]
    if z.scatter:
        stages = len(z.bits)
        sizes = [TILE >> (k + 1) for k in range(stages)]
        scratch += [pltpu.VMEM((npiece, size, TILE), LOW) for size in sizes + sizes]
        scratch += [pltpu.VMEM((npiece, size, TILE), F32) for size in sizes[1:]]
        scratch += [
            pltpu.VMEM((4, sizes[0], TILE), LOW),
            pltpu.VMEM((z.rings, 16, hidden), LOW),
            pltpu.VMEM((z.rings, 16, hidden), LOW),
            pltpu.VMEM((16, hidden), F32),
            dma((npiece, stages)),
            dma((npiece, stages)),
            dma((z.rings,)),
            dma((z.rings,)),
        ]
    hbm = pl.BlockSpec(memory_space=pl.ANY)
    vmem = pl.BlockSpec(memory_space=pltpu.VMEM)
    smem = pl.BlockSpec(memory_space=pltpu.SMEM)
    got = pl.pallas_call(
        kernel_of(z),
        out_shape=outs,
        in_specs=[hbm, hbm, vmem, vmem, smem, hbm, hbm, hbm, vmem, hbm, vmem, hbm, vmem],
        out_specs=[vmem] * len(outs),
        scratch_shapes=scratch,
        compiler_params=pltpu.CompilerParams(
            collective_id=0, has_side_effects=True, vmem_limit_bytes=61 * 2**20
        ),
    )(
        inputs,
        cotangent,
        neighbours.T,
        mesh_ids.reshape(1, rows),
        noise_sigma.T,
        w_qkv,
        w_out,
        w_up,
        b_up,
        w_down,
        b_down,
        w_mod,
        b_mod,
    )
    if z.scatter:
        lo, ig, piece, mod, line = got
        return tuple(
            pl.pallas_call(
                layout_of(z),
                out_shape=[
                    stack,
                    stack,
                    shape((1, own, 3 * width), F32),
                    shape((1, own, width), F32),
                    shape((1, own, hidden), F32),
                    shape((1, hidden // shards), F32),
                    shape((1, hidden // shards, width), F32),
                    shape((1, own), F32),
                    shape((1, own, 4 * width), F32),
                    shape((1, 4 * width // shards), F32),
                ],
                in_specs=[vmem] * 5,
                out_specs=[hbm, hbm, hbm, hbm, hbm, vmem, hbm, vmem, hbm, vmem],
                scratch_shapes=[dma((npiece + 3,))],
                compiler_params=pltpu.CompilerParams(vmem_limit_bytes=2 * 2**20),
            )(lo, ig, piece, mod, line)
        )
    lo, ig, left_t, right_t, small, table = got
    groups = z.groups

    def summed(value):
        return lax.psum_scatter(value, "nodes", scatter_dimension=0, tiled=True)

    def wide_sum(left, first, last):
        return summed(jnp.concatenate([dot(left_t[left], right_t[r]) for r in range(first, last)], axis=1))[None]

    down = [dot(left_t[q], right_t[0]).reshape(TILE // 32, 32, TILE) for q in range(groups)]
    down = jnp.stack(down, axis=1)
    count = batches * z.meshes
    small = lax.psum(small, "nodes")
    me = lax.axis_index("nodes")
    mod = jnp.dot(table[:, :count], small[:count], precision=lax.Precision.HIGHEST)

    def mine(value):
        size = value.shape[0] // shards
        return lax.dynamic_slice_in_dim(value, me * size, size, axis=0)[None]

    return (
        lo,
        ig,
        wide_sum(groups + 2, 2 + groups, 5 + groups),
        wide_sum(groups + 1, 1 + groups, 2 + groups),
        wide_sum(groups, 1, 1 + groups),
        mine(small[count]),
        summed(down.reshape(hidden, width))[None],
        mine(small[count + 1, :width]),
        mine(mod),
        mine(jnp.sum(small[:count], axis=0)),
    )


def solution(mesh):
    return jax.shard_map(
        body,
        mesh=mesh,
        in_specs=(
            P(None, "nodes", None),
            P(None, "nodes", None),
            P("nodes", None),
            P("nodes"),
            P(),
            P("section", None, None),
            P("section", None, None),
            P("section", None, None),
            P("section", None),
            P("section", None, None),
            P("section", None),
            P("section", None, None),
            P("section", None),
        ),
        out_specs=(
            P("section", None, "nodes", None),
            P("section", None, "nodes", None),
            P("section", "nodes", None),
            P("section", "nodes", None),
            P("section", "nodes", None),
            P("section", "nodes"),
            P("section", "nodes", None),
            P("section", "nodes"),
            P("section", "nodes", None),
            P("section", "nodes"),
        ),
        check_vma=False,
    )
```

```python
import jax
import jax.numpy as jnp
from jax import lax
from jax.experimental import pallas as pl
from jax.experimental.pallas import tpu as pltpu
from jax.sharding import PartitionSpec as P

HEADS = 4
REACH = 32
EPSILON = 1e-06
MASKED = -1e9
ABSENT = -2e38
TILE = 512
TOGETHER = 2
MESH = pl.DeviceIdType.MESH
F32, LOW = jnp.float32, jnp.bfloat16


def dot(a, b):
    return lax.dot_general(a, b, (((1,), (0,)), ((), ())), preferred_element_type=F32)


def dot_nt(a, b):
    return lax.dot_general(a, b, (((1,), (1,)), ((), ())), preferred_element_type=F32)


def dot_tn(a, b):
    return lax.dot_general(a, b, (((0,), (0,)), ((), ())), preferred_element_type=F32)


class Sizes:
    def __init__(self, inputs, neighbours, noise, w_up, shards):
        self.batches, self.rows, self.width = inputs.shape
        self.together = TOGETHER if self.batches % TOGETHER == 0 else 1
        self.turns = self.batches // self.together
        self.slots = neighbours.shape[1]
        self.meshes = noise.shape[1]
        self.hidden = w_up.shape[2]
        self.shards = shards
        self.ext = self.rows + 2 * REACH
        self.window = (self.ext // 128 + 1) * 128
        self.groups = self.hidden // TILE
        self.own = self.width // shards
        self.scatter = self.own % 16 == 0
        self.pieces = 2 * self.groups + 4
        self.lefts = 3 + self.groups
        self.rights = 2 + self.groups + 3
        self.rings = max(shards.bit_length() - 1, 1)

        self.bits = [1 << k for k in range(shards.bit_length() - 1)]

    def left(self, p):
        n = self.groups
        return jnp.minimum(p, n) + lax.div(p, 2 * n) + lax.div(p, 2 * n + 1)

    def right(self, p):
        return jnp.maximum(p - (self.groups - 1), 0)


def kernel_of(z):
    batches, rows, width, ext, window = z.batches, z.rows, z.width, z.ext, z.window
    groups, shards, own, many = z.groups, z.shards, z.own, z.together
    head = width // HEADS
    score_scale = head ** (-0.5)
    log2e = 1.4426950408889634
    npiece = z.pieces
    half = TILE // 2
    stages = len(z.bits)
    g_out, g_q, g_k = 1 + groups, 2 + groups, 3 + groups

    def position(owner):
        if not z.scatter:
            return owner
        place = 0
        for bit in z.bits:
            place = 2 * place + owner // bit % 2
        return place

    def kernel(
        inputs, cotangent, neighbours, mesh_ids, sigma,
        w_qkv, w_out, w_up, b_up, w_down, b_down, w_mod, b_mod,
        lo, ig, *rest,
    ):
        if z.scatter:
            o_piece, o_mod, o_line, left_t, right_t = rest[:5]
            rest = rest[5:]
        else:
            left_t, right_t, small_out, table_out = rest[:4]
            rest = rest[4:]
        (
            wq, wo, wu, wd, wm, xext, dybuf, sel, pick, cnt, few, bias, mod, emb,
            n1, n1s, ua, ia, qb, kvext, sbuf, af, ca, obs, n2s, ub, ib, tb, fp, hs,
            ob, dbuf, cds, dx1, dkv, hsend, hrecv,
            lsem, hx_s, hx_r, hm_s, hm_r, fx_s, fx_r, bh_s, bh_r, bx_s, bx_r,
        ) = rest[:48]
        rest = rest[48:]
        if z.scatter:
            gives, gets, keeps = rest[:stages], rest[stages : 2 * stages], rest[2 * stages : 3 * stages - 1]
            acc, msend, mrecv, tot, p_s, p_r, m_s, m_r = rest[3 * stages - 1 :]

        sec = lax.axis_index("section")
        me = lax.axis_index("nodes")
        up = lax.rem(me + 1, shards)
        down = lax.rem(me + shards - 1, shards)
        other = 1 - sec
        def local(src, dst, k):
            return pltpu.make_async_copy(src, dst, lsem.at[k])

        loads = [
            local(w_mod.at[0], wm, 0),
            local(w_qkv.at[0], wq, 1),
            local(w_out.at[0], wo, 2),
            local(w_up.at[0], wu, 3),
            local(w_down.at[0], wd, 4),
        ]
        own_rows = pl.ds(REACH, rows)
        first_load = local(inputs, xext.at[:, own_rows, :], 5)
        last_load = local(cotangent, dybuf, 6)
        loads[0].start()

        @pl.when(sec == 0)
        def _():
            first_load.start()

        for copy in loads[1:]:
            copy.start()

        @pl.when(sec == 1)
        def _():
            last_load.start()

        def side(bit):
            return lax.rem(lax.div(me, bit), 2)

        def mate(bit):
            return me + bit - 2 * bit * side(bit)

        barrier = pltpu.get_barrier_semaphore()
        mates = [(sec, up), (sec, down), (other, me), (other, up), (other, down)]
        if z.scatter:
            mates += [(sec, mate(bit)) for bit in z.bits[1:]]
        for peer in mates:
            pl.semaphore_signal(barrier, inc=1, device_id=peer, device_id_type=MESH)
        pl.semaphore_wait(barrier, len(mates))

        def remote(src, dst, s_sem, r_sem, peer):
            return pltpu.make_async_remote_copy(
                src_ref=src, dst_ref=dst, send_sem=s_sem, recv_sem=r_sem, device_id=peer, device_id_type=MESH
            )

        low_rows, top_rows = pl.ds(0, REACH), pl.ds(REACH + rows, REACH)
        head_rows, tail_rows = pl.ds(REACH, REACH), pl.ds(rows, REACH)
        x_down = remote(inputs.at[:, pl.ds(0, REACH), :], xext.at[:, top_rows, :], hx_s.at[0], hx_r.at[0], (sec, down))
        x_up = remote(inputs.at[:, pl.ds(rows - REACH, REACH), :], xext.at[:, low_rows, :], hx_s.at[1], hx_r.at[1], (sec, up))

        @pl.when(sec == 0)
        def _():
            x_down.start()
            x_up.start()

        ids = jnp.broadcast_to(mesh_ids[...].astype(F32), (128, rows))
        sel[own_rows, :] = ids.T
        sample = lax.broadcasted_iota(jnp.int32, (16, rows), 0).astype(F32)
        pick[...] = jnp.where(ids[0:16] == sample, 1.0, 0.0).astype(LOW)
        m_down = remote(sel.at[head_rows, :], sel.at[top_rows, :], hm_s.at[0], hm_r.at[0], (sec, down))
        m_up = remote(sel.at[tail_rows, :], sel.at[low_rows, :], hm_s.at[1], hm_r.at[1], (sec, up))
        m_down.start()
        m_up.start()

        kvext[:, ext:window, :] = jnp.zeros((batches, window - ext, 2 * width), LOW)

        slots = neighbours[...].astype(F32)
        slots = jnp.concatenate([slots, jnp.zeros((128 - z.slots, rows), F32)], axis=0).T
        slots = jnp.where(slots >= 0, slots - (me * rows - REACH).astype(F32), float(ext))
        column = lax.broadcasted_iota(jnp.int32, (rows, window), 1).astype(F32)
        counts = jnp.zeros((rows, window), F32)
        for n in range(z.slots):
            counts = counts + jnp.where(slots[:, n : n + 1] == column, 1.0, 0.0)
        cnt[...] = counts
        few[...] = counts.astype(LOW)
        bias[...] = jnp.where(counts > 0, jnp.where(column == ext, MASKED * log2e, 0.0), ABSENT)

        row_no = lax.broadcasted_iota(jnp.int32, (16, width // 2), 0)
        level = jnp.ones((16, width // 2), F32)
        for b in range(batches):
            for m in range(z.meshes):
                level = jnp.where(row_no == b * z.meshes + m, sigma[m, b], level)
        place = lax.broadcasted_iota(jnp.int32, (16, width // 2), 1).astype(F32)
        frequency = 3.0 * jnp.exp(-jnp.log(100.0) * place / (width // 2))
        angles = jnp.log(level) * frequency
        embedded = jnp.concatenate([jnp.sin(angles), jnp.cos(angles)], axis=1).astype(LOW)
        padded = jnp.concatenate([embedded.astype(F32), jnp.zeros((112, width), F32)], axis=0)
        emb[...] = padded.T
        loads[0].wait()
        for g in range(4):
            cols = pl.ds(g * width, width)
            table = dot(embedded, wm[:, cols]) + b_mod[:, cols] + (1.0 - g % 2)
            for b in range(batches):
                mod[b, 0 : z.meshes, cols] = table[b * z.meshes : (b + 1) * z.meshes]

        def mod_rows(b, part, ids_rows):
            cols = pl.ds(part * width, width)
            value = jnp.broadcast_to(mod[b, 0:1, cols], (ids_rows.shape[0], width))
            for m in range(1, z.meshes):
                value = jnp.where(ids_rows > m - 0.5, mod[b, m : m + 1, cols], value)
            return value

        def wide(ids_rows):
            return jnp.concatenate([ids_rows] * (width // 128), axis=1)

        def unit(x):
            centred = x - jnp.mean(x, axis=-1, keepdims=True)
            inv = lax.rsqrt(jnp.mean(centred * centred, axis=-1, keepdims=True) + EPSILON)
            return centred * inv, inv

        def span_of(start, size):
            if isinstance(start, int):
                return pl.ds(start, size)
            return pl.ds(pl.multiple_of(start, size), size)

        def batch_cols(b):
            return span_of(b * rows, rows)

        def turn_cols(t):
            return span_of(t * many * rows, many * rows)

        def turn_of(ref, t):
            return ref[pl.ds(t * many, many)].reshape(many * rows, ref.shape[2])

        span = own if z.scatter else 32

        def transposes(b, carry):
            for first, ref in ((groups, n2s), (groups + 1, obs), (groups + 2, n1s)):
                turned = ref[b].T
                for owner in range(TILE // span):
                    at = position(owner) * span
                    left_t[first, at : at + span, batch_cols(b)] = turned[owner * span : (owner + 1) * span]
            run = groups * span
            for g in range(groups):
                turned = hs[b, :, g * TILE : (g + 1) * TILE].T
                for k in range(TILE // span):
                    at = g * TILE + k * span
                    owner, part = at // run, at % run // span
                    to = position(owner) * span
                    left_t[part, to : to + span, batch_cols(b)] = turned[k * span : (k + 1) * span]
            return carry

        heads = [slice(h * head, (h + 1) * head) for h in range(HEADS)]
        heads_v = [slice(width + h * head, width + (h + 1) * head) for h in range(HEADS)]
        tiles = [slice(g * TILE, (g + 1) * TILE) for g in range(groups)]
        thirds = [slice(g * width, (g + 1) * width) for g in range(3)]

        def forward(b):
            ids_rows = wide(sel[0:ext, :])
            u, inv = unit(xext[b].astype(F32))
            normed = (u * mod_rows(b, 0, ids_rows) + mod_rows(b, 1, ids_rows)).astype(LOW)
            n1[...] = normed
            n1s[b] = normed[REACH : REACH + rows]
            ua[b] = u[REACH : REACH + rows]
            ia[b] = jnp.broadcast_to(inv[REACH : REACH + rows], (rows, 128))
            kvext[b, 0:ext, thirds[0]] = dot(n1[...], wq[:, thirds[1]]).astype(LOW)
            qb[b] = dot(n1s[b], wq[:, thirds[0]]).astype(LOW)
            for h in range(HEADS):
                sbuf[h] = dot_nt(qb[b, :, heads[h]], kvext[b, :, heads[h]]) * (score_scale * log2e) + bias[...]
            kvext[b, 0:ext, thirds[1]] = dot(n1[...], wq[:, thirds[2]]).astype(LOW)
            for h in range(HEADS):
                s = sbuf[h]
                e = jnp.exp2(s - jnp.max(s, axis=-1, keepdims=True))
                a = e * (1.0 / jnp.sum(e * cnt[...], axis=-1, keepdims=True))
                af[b, h] = a
                ca[b, h] = a.astype(LOW) * few[...]
            for h in range(HEADS):
                obs[b, :, heads[h]] = dot(ca[b, h], kvext[b, :, heads_v[h]]).astype(LOW)

            x1 = xext[b, own_rows, :].astype(F32) + dot(obs[b], wo[...])
            u, inv = unit(x1)
            ub[b] = u
            ib[b] = jnp.broadcast_to(inv, (rows, 128))
            ids_rows = wide(sel[own_rows, :])
            n2s[b] = (u * mod_rows(b, 2, ids_rows) + mod_rows(b, 3, ids_rows)).astype(LOW)
            tb[...] = x1 + b_down[...]
            for gs in tiles:
                gate = dot(n2s[b], wu[:, gs]) + b_up[:, gs]
                s = 0.5 + 0.5 * jnp.tanh(0.5 * gate)
                hid = gate * s
                fp[b, :, gs] = (s + hid * (1.0 - s)).astype(LOW)
                hid = hid.astype(LOW)
                hs[b, :, gs] = hid
                tb[...] += dot(hid, wd[gs, :])
            lo[0, b] = tb[...].astype(LOW)

        def relay(b):
            return [
                remote(lo.at[0, b], xext.at[b, own_rows, :], fx_s.at[b, 0], fx_r.at[b, 0], (other, me)),
                remote(lo.at[0, b, pl.ds(0, REACH), :], xext.at[b, top_rows, :], fx_s.at[b, 1], fx_r.at[b, 1], (other, down)),
                remote(lo.at[0, b, pl.ds(rows - REACH, REACH), :], xext.at[b, low_rows, :], fx_s.at[b, 2], fx_r.at[b, 2], (other, up)),
            ]

        def norm_back(d, u, inv, scale):
            scaled = d * scale
            return inv * (
                scaled
                - jnp.mean(scaled, axis=-1, keepdims=True)
                - u * jnp.mean(scaled * u, axis=-1, keepdims=True)
            )

        def small_sums():
            lines = []
            for b in range(batches):
                sums = []
                for u, at in ((ua[b], width), (ub[b], 0)):
                    d = fp[b, :, at : at + width]
                    sums += [dot(pick[...], (d.astype(F32) * u).astype(LOW)), dot(pick[...], d)]
                lines.append(jnp.concatenate(sums, axis=1)[0 : z.meshes])
            ones = jnp.ones((16, batches * rows), LOW)
            ups = [dot(ones, right_t[1 + g])[0:1] for g in range(groups)]
            lines.append(jnp.concatenate(ups, axis=1))
            blank = jnp.zeros((1, z.hidden - width), F32)
            lines.append(jnp.concatenate([dot(ones, right_t[0])[0:1], blank], axis=1))
            lines.append(jnp.zeros((14 - batches * z.meshes, z.hidden), F32))
            return jnp.concatenate(lines, axis=0)

        def halos(b):
            return [
                remote(hsend.at[b, 0], hrecv.at[b, 1], bh_s.at[b, 0], bh_r.at[b, 0], (sec, down)),
                remote(hsend.at[b, 1], hrecv.at[b, 0], bh_s.at[b, 1], bh_r.at[b, 1], (sec, up)),
            ]

        def given(b):
            at = batch_cols(b)
            dr = dybuf[b]
            right_t[0, at, :] = dr
            for g in range(groups):
                right_t[1 + g, at, :] = dot_nt(dr, wd[g * TILE : (g + 1) * TILE, :]).astype(LOW)

        def back_ffn(t):
            at = turn_cols(t)
            dn = jnp.zeros((many * rows, width), F32)
            for g in range(groups):
                gs = slice(g * TILE, (g + 1) * TILE)
                dg = right_t[1 + g, at, :].astype(F32) * turn_of(fp, t)[:, gs].astype(F32)
                dg = dg.astype(LOW)
                right_t[1 + g, at, :] = dg
                dn = dn + dot_nt(dg, wu[:, gs])
            dbuf[...] = dn

        def back_middle(t):
            at = turn_cols(t)
            ids_rows = wide(sel[own_rows, :])
            for i in range(many):
                b = t * many + i
                d = dbuf[i * rows : (i + 1) * rows]
                u = ub[b]
                grad = dybuf[b].astype(F32) + norm_back(d, u, ib[b][:, 0:1], mod_rows(b, 2, ids_rows))
                fp[b, :, 0:width] = d.astype(LOW)
                dx1[i] = grad
                right_t[g_out, batch_cols(b), :] = grad.astype(LOW)
            ob[...] = dot_nt(right_t[g_out, at, :], wo[...]).astype(LOW)

        def back_attention(t):
            units = [(i, h) for i in range(many) for h in range(HEADS)]
            here = [slice(i * rows, (i + 1) * rows) for i in range(many)]
            for i, h in units:
                sbuf[i * HEADS + h] = dot_nt(ob[here[i], heads[h]], kvext[t * many + i, :, heads_v[h]])
            for i, h in units:
                b, k = t * many + i, i * HEADS + h
                a, da = af[b, h], sbuf[k]
                ds = a * (da - jnp.sum(a * cnt[...] * da, axis=-1, keepdims=True))
                cds[k] = ds.astype(LOW) * few[...]
            for i in range(many):
                b = t * many + i
                for h in range(HEADS):
                    dk = dot_tn(cds[i * HEADS + h], qb[b, :, heads[h]]) * score_scale
                    dv = dot_tn(ca[b, h], ob[here[i], heads[h]])
                    for part, cols in ((dk, heads[h]), (dv, heads_v[h])):
                        hsend[b, 0, :, cols] = part[0:REACH].astype(LOW)
                        dkv[i, :, cols] = part[REACH : REACH + rows]
                        hsend[b, 1, :, cols] = part[REACH + rows : ext].astype(LOW)
                for copy in halos(b):
                    copy.start()
            for i, h in units:
                b = t * many + i
                value = dot(cds[i * HEADS + h], kvext[b, :, heads[h]]) * score_scale
                right_t[g_q, batch_cols(b), heads[h]] = value.astype(LOW)

        def back_second(t):
            at = turn_cols(t)
            ids_rows = wide(sel[own_rows, :])
            edge = rows - REACH
            dbuf[...] = dot_nt(right_t[g_q, at, :], wq[:, 0:width])
            for i in range(many):
                b = t * many + i
                for copy in halos(b):
                    copy.wait_recv()
                dkv[i, 0:REACH, :] += hrecv[b, 0].astype(F32)
                dkv[i, edge:rows, :] += hrecv[b, 1].astype(F32)
                d = dbuf[i * rows : (i + 1) * rows]
                for g in range(2):
                    part = dkv[i, :, g * width : (g + 1) * width].astype(LOW)
                    right_t[g_k + g, batch_cols(b), :] = part
                    d = d + dot_nt(part, wq[:, (g + 1) * width : (g + 2) * width])
                u = ua[b]
                grad = dx1[i] + norm_back(d, u, ia[b][:, 0:1], mod_rows(b, 0, ids_rows))
                ig[0, b] = grad.astype(LOW)

                @pl.when(sec == 1)
                def _(b=b):
                    relay_back(b).start()

                fp[b, :, width : 2 * width] = d.astype(LOW)

        def relay_back(b):
            return remote(ig.at[0, b], dybuf.at[b], bx_s.at[b], bx_r.at[b], (other, me))

        for copy in loads[1:]:
            copy.wait()
        for copy in (m_down, m_up):
            copy.wait()

        @pl.when(sec == 0)
        def _():
            first_load.wait()
            x_down.wait()
            x_up.wait()

        @pl.when(sec == 1)
        def _():
            last_load.wait()

            @pl.loop(0, batches)
            def _(b):
                given(b)

        @pl.loop(0, batches)
        def _(b):
            @pl.when(sec == 1)
            def _():
                for copy in relay(b):
                    copy.wait_recv()

            forward(b)

            @pl.when(sec == 0)
            def _():
                for copy in relay(b):
                    copy.start()

        @pl.when(sec == 0)
        def _():
            lax.fori_loop(0, batches, transposes, 0)

        def rows_of(c, size):
            return pl.ds(pl.multiple_of(c * size, size), size)

        def turned(p):
            if stages <= 2:
                return 0 * p
            return lax.rem(p, 2) * side(1) + (1 - jnp.minimum(lax.rem(p, 4), 1)) * (1 - side(1))

        def bit_of(p, k):
            bits = list(z.bits)
            if stages > 2:
                bits[1], bits[2] = bits[2], bits[1]
            return z.bits[k] + (bits[k] - z.bits[k]) * turned(p)

        def piece_copy(p, k):
            return remote(gives[k].at[p], gets[k].at[p], p_s.at[p, k], p_r.at[p, k], (sec, mate(bit_of(p, k))))

        slots_held, ahead = 4, 3

        def piece_start(p):
            left = z.left(p)
            sides = [left_t[left, rows_of(c, half), :] for c in (1 - side(1), side(1))]
            value = dot(jnp.concatenate(sides, axis=0), right_t[z.right(p)])
            gives[0][p] = value[0:half].astype(LOW)
            piece_copy(p, 0).start()
            acc[lax.rem(p, slots_held)] = value[half : 2 * half].astype(LOW)

        def piece_first(p):
            piece_copy(p, 0).wait()
            here = side(bit_of(p, 1))
            run = half // 4
            for s, to in ((1 - here, gives[1]), (here, keeps[0])):
                for j in range(2):
                    at = rows_of((1 - turned(p)) * (2 * s + j) + turned(p) * (2 * j + s), run)
                    value = acc[lax.rem(p, slots_held), at, :].astype(F32) + gets[0][p, at, :].astype(F32)
                    to[p, j * run : (j + 1) * run, :] = value.astype(to.dtype)
                if to is gives[1]:
                    piece_copy(p, 1).start()

        def piece_step(p, k):
            size = half >> k
            piece_copy(p, k).wait()
            if k == stages - 1:
                o_piece[p] = keeps[k - 1][p] + gets[k][p].astype(F32)
                return
            here = side(bit_of(p, k + 1))
            for to, c in ((gives[k + 1], 1 - here), (keeps[k], here)):
                at = rows_of(c, size // 2)
                to[p] = (keeps[k - 1][p, at, :] + gets[k][p, at, :].astype(F32)).astype(to.dtype)
                if to is gives[k + 1]:
                    piece_copy(p, k + 1).start()

        def only_first(body):
            if z.scatter:
                pl.when(sec == 0)(body)

        for t in reversed(range(z.turns)):

            @pl.when(sec == 0)
            def _(t=t):
                for i in range(many):
                    relay_back(t * many + i).wait_recv()
                    given(t * many + i)

            back_ffn(t)
            back_middle(t)
            back_attention(t)
            if t == 0:

                @only_first
                def _():
                    pl.loop(0, groups)(piece_start)
                    pl.loop(0, ahead)(piece_first)

            back_second(t)

        @pl.when(sec == 1)
        def _():
            lax.fori_loop(0, batches, transposes, 0)

        def finish():
            @pl.loop(0, batches)
            def _(b):
                @pl.when(sec == 0)
                def _():
                    for copy in relay(b):
                        copy.wait_send()

                @pl.when(sec == 1)
                def _():
                    relay_back(b).wait_send()

                for copy in halos(b):
                    copy.wait_send()

        if not z.scatter:
            small_out[...] = small_sums()
            table_out[...] = emb[...]
            finish()
            return

        def ring_copy(k):
            return remote(msend.at[k], mrecv.at[k], m_s.at[k], m_r.at[k], (sec, mate(1 << k)))

        def ring_start(k, value):
            msend[k] = value.astype(LOW)
            ring_copy(k).start()

        def ring_end(k):
            ring_copy(k).wait_recv()
            value = msend[k].astype(F32) + mrecv[k].astype(F32)
            if k + 1 < z.rings:
                ring_start(k + 1, value)
            else:
                tot[...] = value

        lags = [0, 3] + [8 + 5 * k for k in range(stages - 1)]
        begun, summed = (1 - sec) * groups, (1 - sec) * ahead

        @pl.loop(0, npiece + lags[-1])
        def _(p):
            @pl.when((p >= begun) & (p < npiece))
            def _():
                piece_start(p)

            @pl.when((p >= summed + lags[1]) & (p < npiece + lags[1]))
            def _():
                piece_first(p - lags[1])

            for k in range(1, stages):
                lag = lags[k + 1]

                @pl.when((p >= lag) & (p < npiece + lag))
                def _(k=k, lag=lag):
                    piece_step(p - lag, k)

            @pl.when(p == 6)
            def _():
                ring_start(0, small_sums())

            for k in range(z.rings):

                @pl.when(p == 9 + 3 * k)
                def _(k=k):
                    ring_end(k)

            @pl.when(p == 7 + 3 * z.rings)
            def _():
                finish()
                count = batches * z.meshes
                table = emb[pl.ds(pl.multiple_of(me * own, own), own), :]
                grad = jnp.zeros((own, 4 * width), F32)
                for k in range(count):
                    grad = grad + table[:, k : k + 1] * tot[k : k + 1, :]
                o_mod[0] = grad
                cols = 4 * width // shards
                mine = tot[:, pl.ds(pl.multiple_of(me * cols, cols), cols)]
                o_line[0:1, :] = jnp.sum(mine[0:count], axis=0, keepdims=True)
                o_line[1:2, :] = mine[count : count + 1]
                ratio = 128 // own
                line = tot[:, pl.ds(pl.multiple_of(me // ratio * 128, 128), 128)][count + 1 : count + 2]
                value = line
                for k in range(1, ratio):
                    rolled = jnp.concatenate([line[:, k * own :], line[:, : k * own]], axis=1)
                    value = jnp.where(me % ratio == k, rolled, value)
                o_line[2:3, :] = value

        for k in range(z.rings):
            ring_copy(k).wait_send()

    return kernel


def layout_of(z):
    own, groups = z.own, z.groups

    def kernel(
        lo, ig, piece, mod, line,
        o_lo, o_ig, o_qkv, o_out, o_up, o_upb, o_down, o_downb, o_mod, o_modb,
        sems,
    ):
        targets = [o_down.at[0, pl.ds(q * own, own), :] for q in range(groups)]
        targets += [o_up.at[0, :, pl.ds(q * TILE, TILE)] for q in range(groups)]
        targets += [o_out.at[0]] + [o_qkv.at[0, :, pl.ds(q * TILE, TILE)] for q in range(3)]
        moves = [(lo, o_lo), (ig, o_ig), (mod, o_mod)]
        moves += [(piece.at[k], target) for k, target in enumerate(targets)]
        copies = [pltpu.make_async_copy(a, b, sems.at[k]) for k, (a, b) in enumerate(moves)]
        for copy in copies:
            copy.start()
        o_modb[...] = line[0:1, :]
        o_upb[...] = line[1:2, :]
        o_downb[...] = line[2:3, 0:own]
        for copy in copies:
            copy.wait()

    return kernel


def body(
    inputs,
    cotangent,
    neighbours,
    mesh_ids,
    noise_sigma,
    w_qkv,
    w_out,
    w_up,
    b_up,
    w_down,
    b_down,
    w_mod,
    b_mod,
):
    shards = lax.axis_size("nodes")
    z = Sizes(inputs, neighbours, noise_sigma, w_up, shards)
    batches, rows, width, hidden, many = z.batches, z.rows, z.width, z.hidden, z.together
    own, npiece = z.own, z.pieces
    shape = jax.ShapeDtypeStruct
    stack = shape((1, batches, rows, width), LOW)
    outs = [stack, stack]
    sides = [(z.lefts, TILE, batches * rows), (z.rights, batches * rows, TILE)]
    if z.scatter:
        outs = [pltpu.VMEM(stack.shape, LOW)] * 2
        outs += [pltpu.VMEM((npiece, own, TILE), F32), pltpu.VMEM((1, own, 4 * width), F32), pltpu.VMEM((8, 128), F32)]
        scratch = [pltpu.VMEM(side, LOW) for side in sides]
    else:
        outs += [shape(side, LOW) for side in sides] + [shape((16, hidden), F32), shape((width, 128), F32)]
        scratch = []
    dma = pltpu.SemaphoreType.DMA
    scratch += [
        pltpu.VMEM((width, 3 * width), LOW),
        pltpu.VMEM((width, width), LOW),
        pltpu.VMEM((width, hidden), LOW),
        pltpu.VMEM((hidden, width), LOW),
        pltpu.VMEM((width, 4 * width), LOW),
        pltpu.VMEM((batches, z.ext, width), LOW),
        pltpu.VMEM((batches, rows, width), LOW),
        pltpu.VMEM((z.ext, 128), F32),
        pltpu.VMEM((16, rows), LOW),
        pltpu.VMEM((rows, z.window), F32),
        pltpu.VMEM((rows, z.window), LOW),
        pltpu.VMEM((rows, z.window), F32),
        pltpu.VMEM((batches, 8, 4 * width), F32),
        pltpu.VMEM((width, 128), F32),
        pltpu.VMEM((z.ext, width), LOW),
        pltpu.VMEM((batches, rows, width), LOW),
        pltpu.VMEM((batches, rows, width), F32),
        pltpu.VMEM((batches, rows, 128), F32),
        pltpu.VMEM((batches, rows, width), LOW),
        pltpu.VMEM((batches, z.window, 2 * width), LOW),
        pltpu.VMEM((many * HEADS, rows, z.window), F32),
        pltpu.VMEM((batches, HEADS, rows, z.window), F32),
        pltpu.VMEM((batches, HEADS, rows, z.window), LOW),
        pltpu.VMEM((batches, rows, width), LOW),
        pltpu.VMEM((batches, rows, width), LOW),
        pltpu.VMEM((batches, rows, width), F32),
        pltpu.VMEM((batches, rows, 128), F32),
        pltpu.VMEM((rows, width), F32),
        pltpu.VMEM((batches, rows, hidden), LOW),
        pltpu.VMEM((batches, rows, hidden), LOW),
        pltpu.VMEM((many * rows, width), LOW),
        pltpu.VMEM((many * rows, width), F32),
        pltpu.VMEM((many * HEADS, rows, z.window), LOW),
        pltpu.VMEM((many, rows, width), F32),
        pltpu.VMEM((many, rows, 2 * width), F32),
        pltpu.VMEM((batches, 2, REACH, 2 * width), LOW),
        pltpu.VMEM((batches, 2, REACH, 2 * width), LOW),
        dma((7,)),
        dma((2,)),
        dma((2,)),
        dma((2,)),
        dma((2,)),
        dma((batches, 3)),
        dma((batches, 3)),
        dma((batches, 2)),
        dma((batches, 2)),
        dma((batches,)),
        dma((batches,)),
    ]
    if z.scatter:
        stages = len(z.bits)
        sizes = [TILE >> (k + 1) for k in range(stages)]
        scratch += [pltpu.VMEM((npiece, size, TILE), LOW) for size in sizes + sizes]
        scratch += [pltpu.VMEM((npiece, size, TILE), F32) for size in sizes[1:]]
        scratch += [
            pltpu.VMEM((4, sizes[0], TILE), LOW),
            pltpu.VMEM((z.rings, 16, hidden), LOW),
            pltpu.VMEM((z.rings, 16, hidden), LOW),
            pltpu.VMEM((16, hidden), F32),
            dma((npiece, stages)),
            dma((npiece, stages)),
            dma((z.rings,)),
            dma((z.rings,)),
        ]
    hbm = pl.BlockSpec(memory_space=pl.ANY)
    vmem = pl.BlockSpec(memory_space=pltpu.VMEM)
    smem = pl.BlockSpec(memory_space=pltpu.SMEM)
    got = pl.pallas_call(
        kernel_of(z),
        out_shape=outs,
        in_specs=[hbm, hbm, vmem, vmem, smem, hbm, hbm, hbm, vmem, hbm, vmem, hbm, vmem],
        out_specs=[vmem] * len(outs),
        scratch_shapes=scratch,
        compiler_params=pltpu.CompilerParams(
            collective_id=0, has_side_effects=True, vmem_limit_bytes=61 * 2**20
        ),
    )(
        inputs,
        cotangent,
        neighbours.T,
        mesh_ids.reshape(1, rows),
        noise_sigma.T,
        w_qkv,
        w_out,
        w_up,
        b_up,
        w_down,
        b_down,
        w_mod,
        b_mod,
    )
    if z.scatter:
        lo, ig, piece, mod, line = got
        return tuple(
            pl.pallas_call(
                layout_of(z),
                out_shape=[
                    stack,
                    stack,
                    shape((1, own, 3 * width), F32),
                    shape((1, own, width), F32),
                    shape((1, own, hidden), F32),
                    shape((1, hidden // shards), F32),
                    shape((1, hidden // shards, width), F32),
                    shape((1, own), F32),
                    shape((1, own, 4 * width), F32),
                    shape((1, 4 * width // shards), F32),
                ],
                in_specs=[vmem] * 5,
                out_specs=[hbm, hbm, hbm, hbm, hbm, vmem, hbm, vmem, hbm, vmem],
                scratch_shapes=[dma((npiece + 3,))],
                compiler_params=pltpu.CompilerParams(vmem_limit_bytes=2 * 2**20),
            )(lo, ig, piece, mod, line)
        )
    lo, ig, left_t, right_t, small, table = got
    groups = z.groups

    def summed(value):
        return lax.psum_scatter(value, "nodes", scatter_dimension=0, tiled=True)

    def wide_sum(left, first, last):
        return summed(jnp.concatenate([dot(left_t[left], right_t[r]) for r in range(first, last)], axis=1))[None]

    down = [dot(left_t[q], right_t[0]).reshape(TILE // 32, 32, TILE) for q in range(groups)]
    down = jnp.stack(down, axis=1)
    count = batches * z.meshes
    small = lax.psum(small, "nodes")
    me = lax.axis_index("nodes")
    mod = jnp.dot(table[:, :count], small[:count], precision=lax.Precision.HIGHEST)

    def mine(value):
        size = value.shape[0] // shards
        return lax.dynamic_slice_in_dim(value, me * size, size, axis=0)[None]

    return (
        lo,
        ig,
        wide_sum(groups + 2, 2 + groups, 5 + groups),
        wide_sum(groups + 1, 1 + groups, 2 + groups),
        wide_sum(groups, 1, 1 + groups),
        mine(small[count]),
        summed(down.reshape(hidden, width))[None],
        mine(small[count + 1, :width]),
        mine(mod),
        mine(jnp.sum(small[:count], axis=0)),
    )


def solution(mesh):
    return jax.shard_map(
        body,
        mesh=mesh,
        in_specs=(
            P(None, "nodes", None),
            P(None, "nodes", None),
            P("nodes", None),
            P("nodes"),
            P(),
            P("section", None, None),
            P("section", None, None),
            P("section", None, None),
            P("section", None),
            P("section", None, None),
            P("section", None),
            P("section", None, None),
            P("section", None),
        ),
        out_specs=(
            P("section", None, "nodes", None),
            P("section", None, "nodes", None),
            P("section", "nodes", None),
            P("section", "nodes", None),
            P("section", "nodes", None),
            P("section", "nodes"),
            P("section", "nodes", None),
            P("section", "nodes"),
            P("section", "nodes", None),
            P("section", "nodes"),
        ),
        check_vma=False,
    )
```
